32 devices in a mesh: dp: 8 (over z, y), rep: 4 (over x, core).
Axes of the slice: x: 2, y: 2, z: 4, core: 2. Of those that a mesh axis runs over, the one named last changes fastest.
Arguments:
- latents: float32 [2, 32, 4096], P(None, ('dp', 'rep')), may hold values from -5 to 5
- noise_field: float32 [2, 32, 4096], P(None, ('dp', 'rep')), may hold values from -12 to 12
- timesteps: int32 [2, 32], P(None, ('dp', 'rep')), may hold values from 0 to 999
- labels: int32 [2, 32], P(None, ('dp', 'rep')), may hold values from 0 to 31
- drop_mask: int32 [2, 32], P(None, ('dp', 'rep')), may hold values 0 or 1
- roster: float32 [2, 1000], replicated, may hold values from 0.1 to 1
- w_qkv: float32 [2, 768, 2304], P(None, 'dp'), may hold values from -1 to 1
- w_proj: float32 [2, 768, 768], P(None, 'dp'), may hold values from -2 to 2
- w_fc1: float32 [2, 768, 3072], P(None, 'dp'), may hold values from -1 to 1
- w_fc2: float32 [2, 3072, 768], P(None, 'dp'), may hold values from -1 to 1
- w_mod: float32 [768, 10752], P('dp'), may hold values from -1 to 1
- row_qkv: float32 [2, 768], P(None, 'dp'), may hold values from 1.8119812e-07 to 7.2479247e-07
- col_qkv: float32 [2, 2304], replicated, may hold values from 1.8119812e-07 to 7.2479247e-07
- row_proj: float32 [2, 768], P(None, 'dp'), may hold values from 1.8119812e-07 to 7.2479247e-07
- col_proj: float32 [2, 768], replicated, may hold values from 1.8119812e-07 to 7.2479247e-07
- row_fc1: float32 [2, 768], P(None, 'dp'), may hold values from 1.8119812e-07 to 7.2479247e-07
- col_fc1: float32 [2, 3072], replicated, may hold values from 1.8119812e-07 to 7.2479247e-07
- row_fc2: float32 [2, 3072], P(None, 'dp'), may hold values from 1.8119812e-07 to 7.2479247e-07
- col_fc2: float32 [2, 768], replicated, may hold values from 1.8119812e-07 to 7.2479247e-07
- row_mod: float32 [768], P('dp'), may hold values from 1.8119812e-07 to 7.2479247e-07
- col_mod: float32 [10752], replicated, may hold values from 1.8119812e-07 to 7.2479247e-07
- small: float32 [861712], replicated, may hold values from -8 to 8
- small_second: float32 [861712], replicated, may hold values from 1.8119812e-07 to 7.2479247e-07
Outputs:
- loss_total: float32 [], replicated
- qkv_new: float32 [2, 768, 2304], P(None, 'dp')
- qkv_grad: float32 [2, 768, 2304], P(None, 'dp')
- qkv_row: float32 [2, 768], P(None, 'dp')
- qkv_col: float32 [2, 2304], replicated
- qkv_low: bfloat16 [2, 768, 2304], P(None, 'dp')
- proj_new: float32 [2, 768, 768], P(None, 'dp')
- proj_grad: float32 [2, 768, 768], P(None, 'dp')
- proj_row: float32 [2, 768], P(None, 'dp')
- proj_col: float32 [2, 768], replicated
- proj_low: bfloat16 [2, 768, 768], P(None, 'dp')
- fc1_new: float32 [2, 768, 3072], P(None, 'dp')
- fc1_grad: float32 [2, 768, 3072], P(None, 'dp')
- fc1_row: float32 [2, 768], P(None, 'dp')
- fc1_col: float32 [2, 3072], replicated
- fc1_low: bfloat16 [2, 768, 3072], P(None, 'dp')
- fc2_new: float32 [2, 3072, 768], P(None, 'dp')
- fc2_grad: float32 [2, 3072, 768], P(None, 'dp')
- fc2_row: float32 [2, 3072], P(None, 'dp')
- fc2_col: float32 [2, 768], replicated
- fc2_low: bfloat16 [2, 3072, 768], P(None, 'dp')
- mod_new: float32 [768, 10752], P('dp')
- mod_grad: float32 [768, 10752], P('dp')
- mod_row: float32 [768], P('dp')
- mod_col: float32 [10752], replicated
- mod_low: bfloat16 [768, 10752], P('dp')
- small_grad: float32 [861712], replicated
- small_second_new: float32 [861712], replicated
- small_new: float32 [861712], replicated
- small_low: bfloat16 [861712], replicated
The draws below stay inside these ranges and needn't reach their ends.
All inputs are finite; a program needn't handle non-finite values. No bound on the sum of `drop_mask` on one device may be relied on, other than what follows from the above.
Results may differ from the reference program's by a relative error of at most 0.0039.
The reference program's roundings to bfloat16 on the way count: a program that leaves them out, or rounds other values in their place, can miss the bound.
Values may be sent and summed in bfloat16 or wider, within the bound.
A program may use at most 384 MiB of HBM per device.

```python
import math
import jax
import jax.numpy as jnp
from jax import lax

D = 768
HEADS = 12
FF = 3072
FREQ = 256
CLASSES = 32
GRID = 16
PATCH = 2
CHAN = 4
LAYERS = 2
MICRO = 2
STEPS_T = 1000
STEP = 10
IMG_DEV = 1
IMAGES = 32
TOKENS_IMG = 256
LAT = 32
PDIM = 16
MOD = 10752
SMALL = 861712
N_REP = 4


def ramp_columns(base, top):
    col_count = base.shape[-1]
    factor = 1.0 + (top - 1.0) * jnp.arange(col_count, dtype=jnp.float32) / max(col_count - 1, 1)
    return base * factor * (2.0 / (1.0 + top))


def base_normal(key, dims):
    return jax.random.truncated_normal(key, -4.0, 4.0, dims, jnp.float32)


def draw_w_qkv(key, part):
    key = jax.random.fold_in(key, 11)
    dims = (LAYERS, D, 3 * D)
    return ramp_columns(base_normal(key, dims), 3.0) * (0.6 / math.sqrt(D))


def draw_w_proj(key, part):
    key = jax.random.fold_in(key, 12)
    dims = (LAYERS, D, D)
    return ramp_columns(base_normal(key, dims), 3.0) * (3.0 / math.sqrt(D))


def draw_w_fc1(key, part):
    key = jax.random.fold_in(key, 13)
    dims = (LAYERS, D, FF)
    return ramp_columns(base_normal(key, dims), 3.0) * (1.0 / math.sqrt(D))


def draw_w_fc2(key, part):
    key = jax.random.fold_in(key, 14)
    dims = (LAYERS, FF, D)
    return ramp_columns(base_normal(key, dims), 3.0) * (1.0 / math.sqrt(FF))


def draw_w_mod(key, part):
    key = jax.random.fold_in(key, 15)
    dims = (D, MOD)
    return ramp_columns(base_normal(key, dims), 3.0) * (1.0 / math.sqrt(D))


def device_ramp(top):
    index = jnp.arange(IMAGES, dtype=jnp.int32)
    rep_place = (index // IMG_DEV % N_REP).astype(jnp.float32) / max(N_REP - 1, 1)
    dp_count = IMAGES // (IMG_DEV * N_REP)
    dp_place = (index // (IMG_DEV * N_REP)).astype(jnp.float32) / max(dp_count - 1, 1)
    return jnp.exp(math.log(top) * (dp_place + rep_place - 1.0))


def draw_noise_field(key, part):
    key = jax.random.fold_in(key, 17)
    dims = (MICRO, IMAGES, LAT * LAT * CHAN)
    return base_normal(key, dims) * device_ramp(3.0)[None, :, None]


def draw_small(key, part):
    key = jax.random.fold_in(key, 23)
    plan = [(PDIM * D, D, 1.0 / math.sqrt(PDIM)), (D, 0, 0.5), (FREQ * D, D, 1.0 / math.sqrt(FREQ)), (D, 0, 0.5), (D * D, D, 1.0 / math.sqrt(D)), (D, 0, 0.5), ((CLASSES + 1) * D, D, 1.0), (MOD, 0, 0.5), (D * PDIM, PDIM, 1.0 / math.sqrt(D)), (PDIM, 0, 0.5), (LAYERS * (4 * D + FF), 0, 0.3)]
    pieces = []
    for position, entry in enumerate(plan):
        piece_size, col_count, spread = entry
        sub_key = jax.random.fold_in(key, position)
        base = base_normal(sub_key, (piece_size,))
        top = 3.0
        if col_count > 0:
            base = ramp_columns(base.reshape(-1, col_count), top).reshape(-1)
        pieces.append(base * spread)
    return jnp.concatenate(pieces)


def set_ends(result, rng, least, high):
    place = [jax.random.randint(jax.random.fold_in(rng, axis), (), 0, length) for axis, length in enumerate(result.shape)]
    longest = result.shape.index(max(result.shape))
    neighbour = place[:longest] + [(place[longest] + 1) % result.shape[longest]] + place[longest + 1:]
    return result.at[tuple(place)].set(least).at[tuple(neighbour)].set(high)


def level_of(key, shape, split, least, largest):
    def one(axis_at, shards_of):
        steps = jax.random.uniform(jax.random.fold_in(jax.random.fold_in(key, 6), axis_at), (shards_of,), jnp.float32, least / len(split), largest / len(split))
        return jnp.repeat(jnp.exp(steps), shape[axis_at] // shards_of).reshape((-1,) + (1,) * (len(shape) - axis_at - 1))

    gain = one(*split[0])
    for cut in split[1:]:
        gain = gain * one(*cut)
    return gain


def noise(rng, extent, width, limit, shards=(), kind=jnp.bfloat16):
    values = width * jax.random.normal(rng, extent, jnp.float32)
    if shards:
        values = values * level_of(rng, extent, shards, -0.22, 0.18)
    return jnp.clip(values, -limit, limit).astype(kind)


def setup_inputs(seed: int = 0) -> dict:
    streams_of = jax.random.split(jax.random.key(seed), 24)
    return {
        "latents": noise(streams_of[0], (MICRO, IMAGES, LAT * LAT * CHAN), 1.0, 5.0, ((1, 32),), jnp.float32),
        "noise_field": draw_noise_field(jax.random.fold_in(streams_of[23], 71), 0),
        "timesteps": set_ends(jax.random.randint(streams_of[2], (MICRO, IMAGES), 0, STEPS_T), jax.random.fold_in(streams_of[2], 1), 0, STEPS_T - 1).astype(jnp.int32),
        "labels": set_ends(jax.random.randint(streams_of[3], (MICRO, IMAGES), 0, CLASSES), jax.random.fold_in(streams_of[3], 1), 0, CLASSES - 1).astype(jnp.int32),
        "drop_mask": set_ends((jax.random.randint(streams_of[4], (MICRO, IMAGES), 0, 10) < 1).astype(jnp.int32), jax.random.fold_in(streams_of[4], 1), 0, 1),
        "roster": jnp.clip(jax.random.uniform(streams_of[5], (2, STEPS_T), jnp.float32, 0.1, 1.0), 0.1, 1.0),
        "w_qkv": draw_w_qkv(jax.random.fold_in(streams_of[23], 71), 0),
        "w_proj": draw_w_proj(jax.random.fold_in(streams_of[23], 71), 0),
        "w_fc1": draw_w_fc1(jax.random.fold_in(streams_of[23], 71), 0),
        "w_fc2": draw_w_fc2(jax.random.fold_in(streams_of[23], 71), 0),
        "w_mod": draw_w_mod(jax.random.fold_in(streams_of[23], 71), 0),
        "row_qkv": jnp.clip(jnp.exp(math.log(7.24792471373803e-07) - 1.3862944 * jax.random.uniform(streams_of[11], (LAYERS, D), jnp.float32) ** level_of(streams_of[11], (LAYERS, D), ((1, 8),), -0.2, 0.2)), 1.8119811784345075e-07, 7.24792471373803e-07),
        "col_qkv": jnp.clip(jnp.exp(jax.random.uniform(streams_of[12], (LAYERS, 3 * D), jnp.float32, math.log(1.8119811784345075e-07), math.log(7.24792471373803e-07))), 1.8119811784345075e-07, 7.24792471373803e-07),
        "row_proj": jnp.clip(jnp.exp(math.log(7.24792471373803e-07) - 1.3862944 * jax.random.uniform(streams_of[13], (LAYERS, D), jnp.float32) ** level_of(streams_of[13], (LAYERS, D), ((1, 8),), -0.2, 0.2)), 1.8119811784345075e-07, 7.24792471373803e-07),
        "col_proj": jnp.clip(jnp.exp(jax.random.uniform(streams_of[14], (LAYERS, D), jnp.float32, math.log(1.8119811784345075e-07), math.log(7.24792471373803e-07))), 1.8119811784345075e-07, 7.24792471373803e-07),
        "row_fc1": jnp.clip(jnp.exp(math.log(7.24792471373803e-07) - 1.3862944 * jax.random.uniform(streams_of[15], (LAYERS, D), jnp.float32) ** level_of(streams_of[15], (LAYERS, D), ((1, 8),), -0.2, 0.2)), 1.8119811784345075e-07, 7.24792471373803e-07),
        "col_fc1": jnp.clip(jnp.exp(jax.random.uniform(streams_of[16], (LAYERS, FF), jnp.float32, math.log(1.8119811784345075e-07), math.log(7.24792471373803e-07))), 1.8119811784345075e-07, 7.24792471373803e-07),
        "row_fc2": jnp.clip(jnp.exp(math.log(7.24792471373803e-07) - 1.3862944 * jax.random.uniform(streams_of[17], (LAYERS, FF), jnp.float32) ** level_of(streams_of[17], (LAYERS, FF), ((1, 8),), -0.2, 0.2)), 1.8119811784345075e-07, 7.24792471373803e-07),
        "col_fc2": jnp.clip(jnp.exp(jax.random.uniform(streams_of[18], (LAYERS, D), jnp.float32, math.log(1.8119811784345075e-07), math.log(7.24792471373803e-07))), 1.8119811784345075e-07, 7.24792471373803e-07),
        "row_mod": jnp.clip(jnp.exp(math.log(7.24792471373803e-07) - 1.3862944 * jax.random.uniform(streams_of[19], (D,), jnp.float32) ** level_of(streams_of[19], (D,), ((0, 8),), -0.2, 0.2)), 1.8119811784345075e-07, 7.24792471373803e-07),
        "col_mod": jnp.clip(jnp.exp(jax.random.uniform(streams_of[20], (MOD,), jnp.float32, math.log(1.8119811784345075e-07), math.log(7.24792471373803e-07))), 1.8119811784345075e-07, 7.24792471373803e-07),
        "small": draw_small(jax.random.fold_in(streams_of[23], 71), 0),
        "small_second": jnp.clip(jnp.exp(jax.random.uniform(streams_of[22], (SMALL,), jnp.float32, math.log(1.8119811784345075e-07), math.log(7.24792471373803e-07))), 1.8119811784345075e-07, 7.24792471373803e-07),
    }


@jax.custom_vjp
def low(v):
    return lax.optimization_barrier(v.astype(jnp.bfloat16)).astype(jnp.float32)

@jax.custom_vjp
def low_back(v):
    return v

def low_keep(v):
    return (low(v), None)

def low_pass(kept, grad):
    return (grad,)

def back_keep(v):
    return (v, None)

def back_low(kept, grad):
    return (low(grad),)
low.defvjp(low_keep, low_pass)
low_back.defvjp(back_keep, back_low)
HIGHEST = lax.Precision.HIGHEST
EPS_NORM = 1e-06
EPS_ONE = 1e-30
CLIP = 0.5
RATE = 0.6

def matmul_hi(left, right):
    return jnp.matmul(left, right, precision=HIGHEST)

def layout():
    return [('patch_w', (PDIM, D)), ('patch_b', (D,)), ('time1_w', (FREQ, D)), ('time1_b', (D,)), ('time2_w', (D, D)), ('time2_b', (D,)), ('class_tab', (CLASSES + 1, D)), ('mod_b', (MOD,)), ('head_w', (D, PDIM)), ('head_b', (PDIM,)), ('block_b', (LAYERS, 4 * D + FF))]

def unpack(small):
    pieces = {}
    offset = 0
    for piece_name, piece_dims in layout():
        piece_size = math.prod(piece_dims)
        pieces[piece_name] = small[offset:offset + piece_size].reshape(piece_dims)
        offset += piece_size
    return pieces

def position_table():
    quarter = D // 4
    omega = jnp.exp(-math.log(10000.0) * jnp.arange(quarter, dtype=jnp.float32) / quarter)
    places = jnp.arange(GRID * GRID, dtype=jnp.int32)
    across = (places // GRID).astype(jnp.float32)[:, None] * omega
    downward = (places % GRID).astype(jnp.float32)[:, None] * omega
    return jnp.concatenate([jnp.sin(across), jnp.cos(across), jnp.sin(downward), jnp.cos(downward)], axis=1)

def time_features(timesteps):
    half_count = FREQ // 2
    frequency = jnp.exp(-math.log(10000.0) * jnp.arange(half_count, dtype=jnp.float32) / half_count)
    angles = timesteps.astype(jnp.float32)[:, None] * frequency
    return jnp.concatenate([jnp.cos(angles), jnp.sin(angles)], axis=1)

def patchify(flat):
    number = flat.shape[0]
    blocks = flat.reshape(number, GRID, PATCH, GRID, PATCH, CHAN).transpose(0, 1, 3, 2, 4, 5)
    return blocks.reshape(number, GRID * GRID, PDIM)

def layer_norm(values):
    centered = values - lax.optimization_barrier(jnp.mean(values, axis=-1, keepdims=True))
    return centered * lax.rsqrt(lax.optimization_barrier(jnp.mean(centered * centered, axis=-1, keepdims=True)) + EPS_NORM)

def block(residual, modulation, params, pieces, layer_index):
    number, seq_tokens = (residual.shape[0], residual.shape[1])
    spans = [modulation[:, None, D * i:D * (i + 1)] for i in range(6)]
    biases = pieces['block_b'][layer_index]
    blank_bias = jnp.zeros((D,), biases.dtype)
    qkv_bias = jnp.concatenate([biases[:D], blank_bias, biases[D:2 * D]])
    mixed = low(layer_norm(residual) * (1.0 + spans[1]) + spans[0])
    projected = low_back(low(matmul_hi(mixed, low(params['w_qkv'][layer_index])) + qkv_bias))
    projected = projected.reshape(number, seq_tokens, 3, HEADS, D // HEADS)
    scaling = 1.0 / math.sqrt(D // HEADS)
    scores = low_back(jnp.einsum('bqhd,bkhd->bhqk', projected[:, :, 0], projected[:, :, 1], precision=HIGHEST) * scaling)
    attention = low(jax.nn.softmax(scores, axis=-1))
    attended = jnp.einsum('bhqk,bkhd->bqhd', attention, projected[:, :, 2], precision=HIGHEST)
    attended = low_back(low(attended)).reshape(number, seq_tokens, D)
    branch = low_back(matmul_hi(attended, low(params['w_proj'][layer_index])) + biases[2 * D:3 * D])
    residual = residual + spans[2] * branch
    mixed = low(layer_norm(residual) * (1.0 + spans[4]) + spans[3])
    hidden = low_back(matmul_hi(mixed, low(params['w_fc1'][layer_index])) + biases[3 * D:3 * D + FF])
    activated = low(jax.nn.gelu(hidden, approximate=True))
    branch = low_back(matmul_hi(activated, low(params['w_fc2'][layer_index])) + biases[3 * D + FF:])
    return residual + spans[5] * branch

def group_total(params, latent, noise_part, timesteps, labels, drop_mask, roster, places):
    pieces = unpack(params['small'])
    picker = (timesteps[:, None] == jnp.arange(STEPS_T)[None, :]).astype(jnp.float32)
    factors = matmul_hi(picker, roster.T)
    noised = factors[:, 0:1] * latent + factors[:, 1:2] * noise_part
    tokens = patchify(noised)
    target = patchify(noise_part)
    residual = low_back(matmul_hi(low(tokens), low(pieces['patch_w'])) + pieces['patch_b']) + places
    hidden = low_back(matmul_hi(low(time_features(timesteps)), low(pieces['time1_w'])) + pieces['time1_b'])
    time_out = matmul_hi(low(jax.nn.silu(hidden)), low(pieces['time2_w'])) + pieces['time2_b']
    chosen = jnp.where(drop_mask == 1, CLASSES, labels)
    onehot = (chosen[:, None] == jnp.arange(CLASSES + 1)[None, :]).astype(jnp.float32)
    condition = low_back(time_out + matmul_hi(onehot, pieces['class_tab']))
    modulation = low_back(matmul_hi(low(jax.nn.silu(condition)), low(params['w_mod'])) + pieces['mod_b'])
    for layer_index in range(LAYERS):
        residual = block(residual, modulation[:, 6 * D * layer_index:6 * D * (layer_index + 1)], params, pieces, layer_index)
    shifts = modulation[:, None, 6 * D * LAYERS:6 * D * LAYERS + D]
    scales = modulation[:, None, 6 * D * LAYERS + D:]
    final_in = low(layer_norm(residual) * (1.0 + scales) + shifts)
    output = low_back(matmul_hi(final_in, low(pieces['head_w'])) + pieces['head_b'])
    error = output - target
    return jnp.sum(error * error)

def factored(weight, grad, row, col):
    beta = 1.0 - STEP ** (-0.8)
    square = grad * grad + EPS_ONE
    row_new = beta * row + (1.0 - beta) * lax.optimization_barrier(jnp.mean(square, axis=1))
    col_new = beta * col + (1.0 - beta) * lax.optimization_barrier(jnp.mean(square, axis=0))
    estimate = row_new[:, None] * col_new[None, :] / jnp.mean(row_new)
    update = grad * lax.rsqrt(estimate)
    update = update / jnp.maximum(1.0, jnp.sqrt(jnp.mean(update * update)) / CLIP)
    rate = RATE * jnp.maximum(0.001, jnp.sqrt(jnp.mean(weight * weight)))
    return (weight - rate * update, row_new, col_new)

def finish(weight, grad, row, col):
    new_weight, row_new, col_new = jax.vmap(factored)(weight, grad, row, col)
    return (new_weight, grad, row_new, col_new, new_weight.astype(jnp.bfloat16))

def reference(latents, noise_field, timesteps, labels, drop_mask, roster, w_qkv, w_proj, w_fc1, w_fc2, w_mod, row_qkv, col_qkv, row_proj, col_proj, row_fc1, col_fc1, row_fc2, col_fc2, row_mod, col_mod, small, small_second):
    places = position_table()
    group = math.gcd(IMAGES, max(1, 4096 // TOKENS_IMG))
    blocks_n = MICRO * IMAGES // group

    def regroup(values):
        return values.reshape((blocks_n, group) + values.shape[2:])
    data = (regroup(latents), regroup(noise_field), regroup(timesteps), regroup(labels), regroup(drop_mask))
    params = {'w_qkv': w_qkv, 'w_proj': w_proj, 'w_fc1': w_fc1, 'w_fc2': w_fc2, 'w_mod': w_mod, 'small': small}

    def total_fn(params):
        checked = jax.checkpoint(group_total)

        def step_fn(carry, batch):
            latent, noise_part, steps_part, label_part, drop_part = batch
            return (carry + checked(params, latent, noise_part, steps_part, label_part, drop_part, roster, places), None)
        total, _ = lax.scan(step_fn, jnp.zeros((), jnp.float32), data)
        return total
    loss_total, pull = jax.vjp(total_fn, params)
    grads = pull(jnp.ones_like(loss_total) / (MICRO * IMAGES * TOKENS_IMG * PDIM))[0]
    qkv_new, qkv_grad, qkv_row, qkv_col, qkv_low = finish(w_qkv, grads['w_qkv'], row_qkv, col_qkv)
    proj_new, proj_grad, proj_row, proj_col, proj_low = finish(w_proj, grads['w_proj'], row_proj, col_proj)
    fc1_new, fc1_grad, fc1_row, fc1_col, fc1_low = finish(w_fc1, grads['w_fc1'], row_fc1, col_fc1)
    fc2_new, fc2_grad, fc2_row, fc2_col, fc2_low = finish(w_fc2, grads['w_fc2'], row_fc2, col_fc2)
    mod_grad = grads['w_mod']
    mod_new, mod_row, mod_col = factored(w_mod, mod_grad, row_mod, col_mod)
    mod_low = mod_new.astype(jnp.bfloat16)
    small_grad = grads['small']
    beta = 1.0 - STEP ** (-0.8)
    small_second_new = beta * small_second + (1.0 - beta) * (small_grad * small_grad + EPS_ONE)
    update = small_grad * lax.rsqrt(small_second_new)
    update = update / jnp.maximum(1.0, jnp.sqrt(jnp.mean(update * update)) / CLIP)
    small_new = small - RATE * jnp.maximum(0.001, jnp.sqrt(jnp.mean(small * small))) * update
    small_low = small_new.astype(jnp.bfloat16)
    return (loss_total, qkv_new, qkv_grad, qkv_row, qkv_col, qkv_low, proj_new, proj_grad, proj_row, proj_col, proj_low, fc1_new, fc1_grad, fc1_row, fc1_col, fc1_low, fc2_new, fc2_grad, fc2_row, fc2_col, fc2_low, mod_new, mod_grad, mod_row, mod_col, mod_low, small_grad, small_second_new, small_new, small_low)
```

```python
from functools import partial
import math

import jax
import jax.numpy as jnp
from jax import lax
from jax.sharding import PartitionSpec as P

D = 768
HEADS = 12
FF = 3072
FREQ = 256
CLASSES = 32
GRID = 16
PATCH = 2
CHAN = 4
LAYERS = 2
MICRO = 2
STEPS_T = 1000
STEP = 10
PDIM = 16
MOD = 10752


HIGHEST = lax.Precision.HIGHEST
EPS_NORM = 1e-06
EPS_ONE = 1e-30
CLIP = 0.5
RATE = 0.6


def product(left, right):
    return jnp.dot(left, right, preferred_element_type=jnp.float32)


def layout():
    return [
        ("patch_w", (PDIM, D)),
        ("patch_b", (D,)),
        ("time1_w", (FREQ, D)),
        ("time1_b", (D,)),
        ("time2_w", (D, D)),
        ("time2_b", (D,)),
        ("class_tab", (CLASSES + 1, D)),
        ("mod_b", (MOD,)),
        ("head_w", (D, PDIM)),
        ("head_b", (PDIM,)),
        ("block_b", (LAYERS, 4 * D + FF)),
    ]


def unpack(small):
    pieces = {}
    offset = 0
    for piece_name, piece_dims in layout():
        piece_size = math.prod(piece_dims)
        pieces[piece_name] = small[offset : offset + piece_size].reshape(piece_dims)
        offset += piece_size
    return pieces


def position_table():
    quarter = D // 4
    omega = jnp.exp(-math.log(10000.0) * jnp.arange(quarter, dtype=jnp.float32) / quarter)
    places = jnp.arange(GRID * GRID, dtype=jnp.int32)
    across = (places // GRID).astype(jnp.float32)[:, None] * omega
    downward = (places % GRID).astype(jnp.float32)[:, None] * omega
    return jnp.concatenate(
        [jnp.sin(across), jnp.cos(across), jnp.sin(downward), jnp.cos(downward)], axis=1
    )


def time_features(timesteps):
    half_count = FREQ // 2
    frequency = jnp.exp(-math.log(10000.0) * jnp.arange(half_count, dtype=jnp.float32) / half_count)
    angles = timesteps.astype(jnp.float32)[:, None] * frequency
    return jnp.concatenate([jnp.cos(angles), jnp.sin(angles)], axis=1)


def patchify(flat):
    number = flat.shape[0]
    blocks = flat.reshape(number, GRID, PATCH, GRID, PATCH, CHAN).transpose(0, 1, 3, 2, 4, 5)
    return blocks.reshape(number, GRID * GRID, PDIM)


def norm_rows(values):
    centered = values - jnp.mean(values, axis=-1, keepdims=True)
    inverse = lax.rsqrt(jnp.mean(centered * centered, axis=-1, keepdims=True) + EPS_NORM)
    return (centered * inverse, inverse)


def norm_back(grad, normed, inverse):
    return inverse * (
        grad
        - jnp.mean(grad, axis=-1, keepdims=True)
        - normed * jnp.mean(grad * normed, axis=-1, keepdims=True)
    )


def layer_forward(residual, spans, weights, biases):
    number, seq_tokens = (residual.shape[0], residual.shape[1])
    scaling = 1.0 / math.sqrt(D // HEADS)
    blank_bias = jnp.zeros((D,), jnp.float32)
    qkv_bias = jnp.concatenate([biases[:D], blank_bias, biases[D : 2 * D]])
    normed_a, inverse_a = norm_rows(residual)
    mixed_a = (normed_a * (1.0 + spans[1]) + spans[0]).astype(jnp.bfloat16)
    projected = (product(mixed_a.reshape(-1, D), weights[0]) + qkv_bias).astype(jnp.bfloat16)
    projected = projected.reshape(number, seq_tokens, 3, HEADS, D // HEADS)
    scores = (
        jnp.einsum(
            "bqhd,bkhd->bhqk",
            projected[:, :, 0],
            projected[:, :, 1],
            preferred_element_type=jnp.float32,
        )
        * scaling
    )
    total_lse = jax.nn.logsumexp(scores, axis=-1, keepdims=True)
    attention = jnp.exp(scores - total_lse).astype(jnp.bfloat16)
    attended = jnp.einsum(
        "bhqk,bkhd->bqhd", attention, projected[:, :, 2], preferred_element_type=jnp.float32
    )
    attended = attended.astype(jnp.bfloat16).reshape(-1, D)
    branch_a = product(attended, weights[1]) + biases[2 * D : 3 * D]
    middle = residual + spans[2] * branch_a.reshape(number, seq_tokens, D)
    normed_b, inverse_b = norm_rows(middle)
    mixed_b = (normed_b * (1.0 + spans[4]) + spans[3]).astype(jnp.bfloat16)
    hidden = product(mixed_b.reshape(-1, D), weights[2]) + biases[3 * D : 3 * D + FF]
    activated = jax.nn.gelu(hidden, approximate=True).astype(jnp.bfloat16)
    branch_b = product(activated, weights[3]) + biases[3 * D + FF :]
    result = middle + spans[5] * branch_b.reshape(number, seq_tokens, D)
    kept = (
        normed_a,
        inverse_a,
        mixed_a,
        projected,
        total_lse,
        attended,
        branch_a,
        normed_b,
        inverse_b,
        mixed_b,
        hidden,
        activated,
        branch_b,
    )
    return (result, kept)


def layer_backward(grad_out, spans, weights, kept):
    (
        normed_a,
        inverse_a,
        mixed_a,
        projected,
        total_lse,
        attended,
        branch_a,
        normed_b,
        inverse_b,
        mixed_b,
        hidden,
        activated,
        branch_b,
    ) = kept
    number, seq_tokens = (grad_out.shape[0], grad_out.shape[1])
    scaling = 1.0 / math.sqrt(D // HEADS)
    grad_b = (spans[5] * grad_out).reshape(-1, D).astype(jnp.bfloat16)
    gate_b = jnp.sum(grad_out * branch_b.reshape(number, seq_tokens, D), axis=1)
    grad_fc2 = product(activated.T, grad_b)
    bias_fc2 = jnp.sum(grad_b.astype(jnp.float32), axis=0)
    _, gelu_pull = jax.vjp(partial(jax.nn.gelu, approximate=True), hidden)
    grad_hidden = gelu_pull(product(grad_b, weights[3].T))[0].astype(jnp.bfloat16)
    grad_fc1 = product(mixed_b.reshape(-1, D).T, grad_hidden)
    bias_fc1 = jnp.sum(grad_hidden.astype(jnp.float32), axis=0)
    grad_mixed = product(grad_hidden, weights[2].T).reshape(number, seq_tokens, D)
    shift_b = jnp.sum(grad_mixed, axis=1)
    scale_b = jnp.sum(grad_mixed * normed_b, axis=1)
    grad_mid = grad_out + norm_back(grad_mixed * (1.0 + spans[4]), normed_b, inverse_b)
    grad_a = (spans[2] * grad_mid).reshape(-1, D).astype(jnp.bfloat16)
    gate_a = jnp.sum(grad_mid * branch_a.reshape(number, seq_tokens, D), axis=1)
    grad_proj = product(attended.T, grad_a)
    bias_proj = jnp.sum(grad_a.astype(jnp.float32), axis=0)
    grad_att = (
        product(grad_a, weights[1].T)
        .astype(jnp.bfloat16)
        .reshape(number, seq_tokens, HEADS, D // HEADS)
    )
    query, keys, values = (projected[:, :, 0], projected[:, :, 1], projected[:, :, 2])
    scores = (
        jnp.einsum("bqhd,bkhd->bhqk", query, keys, preferred_element_type=jnp.float32) * scaling
    )
    attention = jnp.exp(scores - total_lse)
    grad_values = jnp.einsum(
        "bhqk,bqhd->bkhd",
        attention.astype(jnp.bfloat16),
        grad_att,
        preferred_element_type=jnp.float32,
    )
    grad_weights = jnp.einsum(
        "bqhd,bkhd->bhqk", grad_att, values, preferred_element_type=jnp.float32
    )
    inner = jnp.sum(attention * grad_weights, axis=-1, keepdims=True)
    grad_scores = (attention * (grad_weights - inner)).astype(jnp.bfloat16)
    grad_query = (
        jnp.einsum("bhqk,bkhd->bqhd", grad_scores, keys, preferred_element_type=jnp.float32)
        * scaling
    )
    grad_keys = (
        jnp.einsum("bhqk,bqhd->bkhd", grad_scores, query, preferred_element_type=jnp.float32)
        * scaling
    )
    grad_projected = (
        jnp.stack([grad_query, grad_keys, grad_values], axis=2)
        .reshape(-1, 3 * D)
        .astype(jnp.bfloat16)
    )
    grad_qkv = product(mixed_a.reshape(-1, D).T, grad_projected)
    bias_sums = jnp.sum(grad_projected.astype(jnp.float32), axis=0)
    grad_mixed_a = product(grad_projected, weights[0].T).reshape(number, seq_tokens, D)
    shift_a = jnp.sum(grad_mixed_a, axis=1)
    scale_a = jnp.sum(grad_mixed_a * normed_a, axis=1)
    grad_in = grad_mid + norm_back(grad_mixed_a * (1.0 + spans[1]), normed_a, inverse_a)
    grad_spans = jnp.concatenate([shift_a, scale_a, gate_a, shift_b, scale_b, gate_b], axis=-1)
    grad_bias = jnp.concatenate([bias_sums[:D], bias_sums[2 * D :], bias_proj, bias_fc1, bias_fc2])
    return (grad_in, (grad_qkv, grad_proj, grad_fc1, grad_fc2), grad_bias, grad_spans)


def local(
    latents,
    noise_field,
    timesteps,
    labels,
    drop_mask,
    roster,
    w_qkv,
    w_proj,
    w_fc1,
    w_fc2,
    w_mod,
    row_qkv,
    col_qkv,
    row_proj,
    col_proj,
    row_fc1,
    col_fc1,
    row_fc2,
    col_fc2,
    row_mod,
    col_mod,
    small,
    small_second,
):
    pieces = unpack(small)
    dp_size, rep_size = lax.axis_size("dp"), lax.axis_size("rep")
    everyone = dp_size * rep_size
    number = latents.shape[0] * latents.shape[1]
    count_all = number * everyone * GRID * GRID * PDIM
    rows_mod = w_mod.shape[0]
    first_row = lax.axis_index("dp") * rows_mod
    places = position_table()
    patch_low = pieces["patch_w"].astype(jnp.bfloat16)
    time1_low = pieces["time1_w"].astype(jnp.bfloat16)
    time2_low = pieces["time2_w"].astype(jnp.bfloat16)
    head_low = pieces["head_w"].astype(jnp.bfloat16)
    mod_shard = w_mod.astype(jnp.bfloat16)

    own_ids = jnp.stack([timesteps, labels, drop_mask]).reshape(3, number)
    all_ids = lax.all_gather(own_ids, ("dp", "rep"), axis=0, tiled=False)
    all_ids = all_ids.transpose(1, 0, 2).reshape(3, everyone * number)
    features = time_features(all_ids[0]).astype(jnp.bfloat16)
    hidden_t = product(features, time1_low) + pieces["time1_b"]
    silu_t = jax.nn.silu(hidden_t).astype(jnp.bfloat16)
    chosen = jnp.where(all_ids[2] == 1, CLASSES, all_ids[1])
    onehot = (chosen[:, None] == jnp.arange(CLASSES + 1)[None, :]).astype(jnp.float32)
    condition = (
        product(silu_t, time2_low)
        + pieces["time2_b"]
        + jnp.dot(onehot, pieces["class_tab"], precision=HIGHEST)
    )
    silu_c = jax.nn.silu(condition).astype(jnp.bfloat16)
    silu_rows = lax.dynamic_slice_in_dim(silu_c, first_row, rows_mod, axis=1)
    group_rows = lax.dynamic_index_in_dim(
        silu_rows.reshape(dp_size, rep_size, number, rows_mod),
        lax.axis_index("rep"),
        axis=1,
        keepdims=False,
    ).reshape(dp_size * number, rows_mod)
    modulation = (
        lax.psum_scatter(product(group_rows, mod_shard), "dp", scatter_dimension=0, tiled=True)
        + pieces["mod_b"]
    )

    picker = (timesteps.reshape(-1)[:, None] == jnp.arange(STEPS_T)[None, :]).astype(jnp.float32)
    factors = jnp.dot(picker, roster.T, precision=HIGHEST)
    noise_flat = noise_field.reshape(number, -1)
    noised = factors[:, 0:1] * latents.reshape(number, -1) + factors[:, 1:2] * noise_flat
    tokens = patchify(noised).astype(jnp.bfloat16)
    target = patchify(noise_flat).reshape(-1, PDIM)
    residual = (product(tokens.reshape(-1, PDIM), patch_low) + pieces["patch_b"]).reshape(
        number, GRID * GRID, D
    ) + places
    kept_all = []
    gathered_all = []
    spans_all = []
    for layer_index in range(LAYERS):
        weights = tuple(
            lax.all_gather(w[layer_index].astype(jnp.bfloat16), "dp", axis=0, tiled=True)
            for w in (w_qkv, w_proj, w_fc1, w_fc2)
        )
        spans = [
            modulation[:, None, D * (6 * layer_index + i) : D * (6 * layer_index + i + 1)]
            for i in range(6)
        ]
        residual, kept = layer_forward(residual, spans, weights, pieces["block_b"][layer_index])
        kept_all.append(kept)
        gathered_all.append(weights)
        spans_all.append(spans)
    final_shift = modulation[:, None, 6 * D * LAYERS : 6 * D * LAYERS + D]
    final_scale = modulation[:, None, 6 * D * LAYERS + D :]
    normed_f, inverse_f = norm_rows(residual)
    final_in = (normed_f * (1.0 + final_scale) + final_shift).astype(jnp.bfloat16).reshape(-1, D)
    output = product(final_in, head_low) + pieces["head_b"]
    error = output - target
    loss_own = jnp.sum(error * error)
    grad_output = (error * (2.0 / count_all)).astype(jnp.bfloat16)
    grad_head = product(final_in.T, grad_output)
    grad_head_b = jnp.sum(grad_output.astype(jnp.float32), axis=0)
    grad_final = product(grad_output, head_low.T).reshape(number, GRID * GRID, D)
    final_grads = [jnp.sum(grad_final, axis=1), jnp.sum(grad_final * normed_f, axis=1)]
    grad_res = norm_back(grad_final * (1.0 + final_scale), normed_f, inverse_f)
    layer_spans = [None] * LAYERS
    bias_grads = [None] * LAYERS
    block_grads = [None] * LAYERS
    for layer_index in reversed(range(LAYERS)):
        grad_res, grads, grad_bias, grad_spans = layer_backward(
            grad_res, spans_all[layer_index], gathered_all[layer_index], kept_all[layer_index]
        )
        layer_spans[layer_index] = grad_spans
        bias_grads[layer_index] = grad_bias
        block_grads[layer_index] = tuple(
            lax.psum_scatter(g, "dp", scatter_dimension=0, tiled=True) for g in grads
        )
    grad_qkv, grad_proj, grad_fc1, grad_fc2 = lax.psum(
        tuple(jnp.stack([block_grads[i][k] for i in range(LAYERS)]) for k in range(4)), "rep"
    )

    own_mod = jnp.concatenate(layer_spans + final_grads, axis=-1).astype(jnp.bfloat16)
    grad_mod = lax.all_gather(own_mod, ("dp", "rep"), axis=0, tiled=True)
    grad_wmod = product(silu_rows.T, grad_mod)
    grad_mod_b = jnp.sum(grad_mod.astype(jnp.float32), axis=0)
    cond_rows = lax.all_gather(product(grad_mod, mod_shard.T), "dp", axis=1, tiled=True)
    _, silu_pull = jax.vjp(jax.nn.silu, condition)
    grad_cond = silu_pull(cond_rows)[0].astype(jnp.bfloat16)
    grad_class = jnp.dot(onehot.T, grad_cond.astype(jnp.float32), precision=HIGHEST)
    grad_time2 = product(silu_t.T, grad_cond)
    grad_time2_b = jnp.sum(grad_cond.astype(jnp.float32), axis=0)
    _, silu_time_pull = jax.vjp(jax.nn.silu, hidden_t)
    grad_hidden_t = silu_time_pull(product(grad_cond, time2_low.T))[0].astype(jnp.bfloat16)
    grad_time1 = product(features.T, grad_hidden_t)
    grad_time1_b = jnp.sum(grad_hidden_t.astype(jnp.float32), axis=0)
    grad_start = grad_res.reshape(-1, D).astype(jnp.bfloat16)
    grad_patch = product(tokens.reshape(-1, PDIM).T, grad_start)
    grad_patch_b = jnp.sum(grad_start.astype(jnp.float32), axis=0)
    summed = lax.psum(
        jnp.concatenate(
            [
                grad_patch.reshape(-1),
                grad_patch_b,
                grad_head.reshape(-1),
                jnp.stack(bias_grads).reshape(-1),
                grad_head_b,
                loss_own[None],
            ]
        ),
        ("dp", "rep"),
    )
    cut_patch = (PDIM + 1) * D
    cut_head = cut_patch + D * PDIM
    cut_bias = cut_head + LAYERS * (4 * D + FF)
    loss_total = summed[cut_bias + PDIM]
    small_grad = jnp.concatenate(
        [
            summed[:cut_patch],
            grad_time1.reshape(-1),
            grad_time1_b,
            grad_time2.reshape(-1),
            grad_time2_b,
            grad_class.reshape(-1),
            grad_mod_b,
            summed[cut_patch:cut_head],
            summed[cut_bias : cut_bias + PDIM],
            summed[cut_head:cut_bias],
        ]
    )
    beta = 1.0 - STEP ** (-0.8)
    rows_dp = lax.axis_size("dp")
    kinds = [
        (w_qkv, grad_qkv, row_qkv, col_qkv),
        (w_proj, grad_proj, row_proj, col_proj),
        (w_fc1, grad_fc1, row_fc1, col_fc1),
        (w_fc2, grad_fc2, row_fc2, col_fc2),
        (w_mod[None], grad_wmod[None], row_mod[None], col_mod[None]),
    ]
    firsts = []
    for weight, grad, row, col in kinds:
        square = grad * grad
        row_new = beta * row + (1.0 - beta) * jnp.mean(square + EPS_ONE, axis=-1)
        firsts.append(
            (
                row_new,
                jnp.sum(square + EPS_ONE, axis=-2),
                jnp.sum(square / row_new[:, :, None], axis=-2),
                jnp.sum(row_new, axis=-1),
                jnp.sum(weight * weight, axis=(-2, -1)),
            )
        )
    shared = lax.psum(
        jnp.concatenate([entry[k].reshape(-1) for k in range(1, 5) for entry in firsts]), "dp"
    )
    parts = []
    offset = 0
    for k in range(1, 5):
        for entry in firsts:
            parts.append(shared[offset : offset + entry[k].size].reshape(entry[k].shape))
            offset += entry[k].size
    seconds = []
    for index, kind in enumerate(kinds):
        weight, grad, row, col = kind
        rows_all = weight.shape[1] * rows_dp
        col_count = weight.shape[2]
        col_sum, over_rows, row_sum, weight_sq = (parts[index + len(kinds) * k] for k in range(4))
        row_mean = row_sum / rows_all
        weight_rms = jnp.sqrt(weight_sq / (rows_all * col_count))
        col_new = beta * col + (1.0 - beta) * col_sum / rows_all
        update_sq = row_mean * jnp.sum(over_rows / col_new, axis=-1)
        estimate = firsts[index][0][:, :, None] * col_new[:, None, :] / row_mean[:, None, None]
        update = grad * lax.rsqrt(estimate)
        seconds.append((update, col_new, weight_rms, update_sq / (rows_all * col_count)))
    results = []
    for kind, first, second in zip(kinds, firsts, seconds):
        weight, grad = (kind[0], kind[1])
        update, col_new, weight_rms, update_ms = second
        update_rms = jnp.sqrt(update_ms)
        update = update / jnp.maximum(1.0, update_rms / CLIP)[:, None, None]
        new_weight = weight - (RATE * jnp.maximum(0.001, weight_rms))[:, None, None] * update
        results.append((new_weight, grad, first[0], col_new, new_weight.astype(jnp.bfloat16)))
    square = small_grad * small_grad + EPS_ONE
    small_second_new = beta * small_second + (1.0 - beta) * square
    update = small_grad * lax.rsqrt(small_second_new)
    update = update / jnp.maximum(1.0, jnp.sqrt(jnp.mean(update * update)) / CLIP)
    small_new = small - RATE * jnp.maximum(0.001, jnp.sqrt(jnp.mean(small * small))) * update
    mod_result = results[4]
    return (
        loss_total,
        results[0][0],
        results[0][1],
        results[0][2],
        results[0][3],
        results[0][4],
        results[1][0],
        results[1][1],
        results[1][2],
        results[1][3],
        results[1][4],
        results[2][0],
        results[2][1],
        results[2][2],
        results[2][3],
        results[2][4],
        results[3][0],
        results[3][1],
        results[3][2],
        results[3][3],
        results[3][4],
        mod_result[0][0],
        mod_result[1][0],
        mod_result[2][0],
        mod_result[3][0],
        mod_result[4][0],
        small_grad,
        small_second_new,
        small_new,
        small_new.astype(jnp.bfloat16),
    )


def solution(mesh):
    in_specs = (
        P(None, ("dp", "rep"), None),
        P(None, ("dp", "rep"), None),
        P(None, ("dp", "rep")),
        P(None, ("dp", "rep")),
        P(None, ("dp", "rep")),
        P(),
        P(None, "dp", None),
        P(None, "dp", None),
        P(None, "dp", None),
        P(None, "dp", None),
        P("dp", None),
        P(None, "dp"),
        P(),
        P(None, "dp"),
        P(),
        P(None, "dp"),
        P(),
        P(None, "dp"),
        P(),
        P("dp"),
        P(),
        P(),
        P(),
    )
    out_specs = (
        P(),
        P(None, "dp", None),
        P(None, "dp", None),
        P(None, "dp"),
        P(),
        P(None, "dp", None),
        P(None, "dp", None),
        P(None, "dp", None),
        P(None, "dp"),
        P(),
        P(None, "dp", None),
        P(None, "dp", None),
        P(None, "dp", None),
        P(None, "dp"),
        P(),
        P(None, "dp", None),
        P(None, "dp", None),
        P(None, "dp", None),
        P(None, "dp"),
        P(),
        P(None, "dp", None),
        P("dp", None),
        P("dp", None),
        P("dp"),
        P(),
        P("dp", None),
        P(),
        P(),
        P(),
        P(),
    )
    return jax.shard_map(local, mesh=mesh, in_specs=in_specs, out_specs=out_specs, check_vma=False)
```

```python
from functools import partial
import math

import jax
import jax.numpy as jnp
from jax import lax
from jax.experimental import pallas as pl
from jax.experimental.pallas import tpu as pltpu
from jax.sharding import PartitionSpec as P

D = 768
HEADS = 12
FF = 3072
FREQ = 256
CLASSES = 32
GRID = 16
PATCH = 2
CHAN = 4
LAYERS = 2
MICRO = 2
STEPS_T = 1000
STEP = 10
PDIM = 16
MOD = 10752


HIGHEST = lax.Precision.HIGHEST
EPS_NORM = 1e-06
EPS_ONE = 1e-30
CLIP = 0.5
RATE = 0.6


def product(left, right):
    return jnp.dot(left, right, preferred_element_type=jnp.float32)


def layout():
    return [
        ("patch_w", (PDIM, D)),
        ("patch_b", (D,)),
        ("time1_w", (FREQ, D)),
        ("time1_b", (D,)),
        ("time2_w", (D, D)),
        ("time2_b", (D,)),
        ("class_tab", (CLASSES + 1, D)),
        ("mod_b", (MOD,)),
        ("head_w", (D, PDIM)),
        ("head_b", (PDIM,)),
        ("block_b", (LAYERS, 4 * D + FF)),
    ]


def unpack(small):
    pieces = {}
    offset = 0
    for piece_name, piece_dims in layout():
        piece_size = math.prod(piece_dims)
        pieces[piece_name] = small[offset : offset + piece_size].reshape(piece_dims)
        offset += piece_size
    return pieces


def position_table():
    quarter = D // 4
    omega = jnp.exp(-math.log(10000.0) * jnp.arange(quarter, dtype=jnp.float32) / quarter)
    places = jnp.arange(GRID * GRID, dtype=jnp.int32)
    across = (places // GRID).astype(jnp.float32)[:, None] * omega
    downward = (places % GRID).astype(jnp.float32)[:, None] * omega
    return jnp.concatenate(
        [jnp.sin(across), jnp.cos(across), jnp.sin(downward), jnp.cos(downward)], axis=1
    )


def time_features(timesteps):
    half_count = FREQ // 2
    frequency = jnp.exp(-math.log(10000.0) * jnp.arange(half_count, dtype=jnp.float32) / half_count)
    angles = timesteps.astype(jnp.float32)[:, None] * frequency
    return jnp.concatenate([jnp.cos(angles), jnp.sin(angles)], axis=1)


def patchify(flat):
    number = flat.shape[0]
    blocks = flat.reshape(number, GRID, PATCH, GRID, PATCH, CHAN).transpose(0, 1, 3, 2, 4, 5)
    return blocks.reshape(number, GRID * GRID, PDIM)


def norm_rows(values):
    centered = values - jnp.mean(values, axis=-1, keepdims=True)
    inverse = lax.rsqrt(jnp.mean(centered * centered, axis=-1, keepdims=True) + EPS_NORM)
    return (centered * inverse, inverse)


def norm_back(grad, normed, inverse):
    return inverse * (
        grad
        - jnp.mean(grad, axis=-1, keepdims=True)
        - normed * jnp.mean(grad * normed, axis=-1, keepdims=True)
    )


def layer_forward(residual, spans, weights, biases):
    number, seq_tokens = (residual.shape[0], residual.shape[1])
    scaling = 1.0 / math.sqrt(D // HEADS)
    blank_bias = jnp.zeros((D,), jnp.float32)
    qkv_bias = jnp.concatenate([biases[:D], blank_bias, biases[D : 2 * D]])
    normed_a, inverse_a = norm_rows(residual)
    mixed_a = (normed_a * (1.0 + spans[1]) + spans[0]).astype(jnp.bfloat16)
    projected = (product(mixed_a.reshape(-1, D), weights[0]) + qkv_bias).astype(jnp.bfloat16)
    projected = projected.reshape(number, seq_tokens, 3, HEADS, D // HEADS)
    scores = (
        jnp.einsum(
            "bqhd,bkhd->bhqk",
            projected[:, :, 0],
            projected[:, :, 1],
            preferred_element_type=jnp.float32,
        )
        * scaling
    )
    total_lse = jax.nn.logsumexp(scores, axis=-1, keepdims=True)
    attention = jnp.exp(scores - total_lse).astype(jnp.bfloat16)
    attended = jnp.einsum(
        "bhqk,bkhd->bqhd", attention, projected[:, :, 2], preferred_element_type=jnp.float32
    )
    attended = attended.astype(jnp.bfloat16).reshape(-1, D)
    branch_a = product(attended, weights[1]) + biases[2 * D : 3 * D]
    middle = residual + spans[2] * branch_a.reshape(number, seq_tokens, D)
    normed_b, inverse_b = norm_rows(middle)
    mixed_b = (normed_b * (1.0 + spans[4]) + spans[3]).astype(jnp.bfloat16)
    hidden = product(mixed_b.reshape(-1, D), weights[2]) + biases[3 * D : 3 * D + FF]
    activated = jax.nn.gelu(hidden, approximate=True).astype(jnp.bfloat16)
    branch_b = product(activated, weights[3]) + biases[3 * D + FF :]
    result = middle + spans[5] * branch_b.reshape(number, seq_tokens, D)
    kept = (
        normed_a,
        inverse_a,
        mixed_a,
        projected,
        total_lse,
        attended,
        branch_a,
        normed_b,
        inverse_b,
        mixed_b,
        hidden,
        activated,
        branch_b,
    )
    return (result, kept)


def layer_backward(grad_out, spans, weights, kept):
    (
        normed_a,
        inverse_a,
        mixed_a,
        projected,
        total_lse,
        attended,
        branch_a,
        normed_b,
        inverse_b,
        mixed_b,
        hidden,
        activated,
        branch_b,
    ) = kept
    number, seq_tokens = (grad_out.shape[0], grad_out.shape[1])
    scaling = 1.0 / math.sqrt(D // HEADS)
    grad_b = (spans[5] * grad_out).reshape(-1, D).astype(jnp.bfloat16)
    gate_b = jnp.sum(grad_out * branch_b.reshape(number, seq_tokens, D), axis=1)
    grad_fc2 = product(activated.T, grad_b)
    bias_fc2 = jnp.sum(grad_b.astype(jnp.float32), axis=0)
    _, gelu_pull = jax.vjp(partial(jax.nn.gelu, approximate=True), hidden)
    grad_hidden = gelu_pull(product(grad_b, weights[3].T))[0].astype(jnp.bfloat16)
    grad_fc1 = product(mixed_b.reshape(-1, D).T, grad_hidden)
    bias_fc1 = jnp.sum(grad_hidden.astype(jnp.float32), axis=0)
    grad_mixed = product(grad_hidden, weights[2].T).reshape(number, seq_tokens, D)
    shift_b = jnp.sum(grad_mixed, axis=1)
    scale_b = jnp.sum(grad_mixed * normed_b, axis=1)
    grad_mid = grad_out + norm_back(grad_mixed * (1.0 + spans[4]), normed_b, inverse_b)
    grad_a = (spans[2] * grad_mid).reshape(-1, D).astype(jnp.bfloat16)
    gate_a = jnp.sum(grad_mid * branch_a.reshape(number, seq_tokens, D), axis=1)
    grad_proj = product(attended.T, grad_a)
    bias_proj = jnp.sum(grad_a.astype(jnp.float32), axis=0)
    grad_att = (
        product(grad_a, weights[1].T)
        .astype(jnp.bfloat16)
        .reshape(number, seq_tokens, HEADS, D // HEADS)
    )
    query, keys, values = (projected[:, :, 0], projected[:, :, 1], projected[:, :, 2])
    scores = (
        jnp.einsum("bqhd,bkhd->bhqk", query, keys, preferred_element_type=jnp.float32) * scaling
    )
    attention = jnp.exp(scores - total_lse)
    grad_values = jnp.einsum(
        "bhqk,bqhd->bkhd",
        attention.astype(jnp.bfloat16),
        grad_att,
        preferred_element_type=jnp.float32,
    )
    grad_weights = jnp.einsum(
        "bqhd,bkhd->bhqk", grad_att, values, preferred_element_type=jnp.float32
    )
    inner = jnp.sum(attention * grad_weights, axis=-1, keepdims=True)
    grad_scores = (attention * (grad_weights - inner)).astype(jnp.bfloat16)
    grad_query = (
        jnp.einsum("bhqk,bkhd->bqhd", grad_scores, keys, preferred_element_type=jnp.float32)
        * scaling
    )
    grad_keys = (
        jnp.einsum("bhqk,bqhd->bkhd", grad_scores, query, preferred_element_type=jnp.float32)
        * scaling
    )
    grad_projected = (
        jnp.stack([grad_query, grad_keys, grad_values], axis=2)
        .reshape(-1, 3 * D)
        .astype(jnp.bfloat16)
    )
    grad_qkv = product(mixed_a.reshape(-1, D).T, grad_projected)
    bias_sums = jnp.sum(grad_projected.astype(jnp.float32), axis=0)
    grad_mixed_a = product(grad_projected, weights[0].T).reshape(number, seq_tokens, D)
    shift_a = jnp.sum(grad_mixed_a, axis=1)
    scale_a = jnp.sum(grad_mixed_a * normed_a, axis=1)
    grad_in = grad_mid + norm_back(grad_mixed_a * (1.0 + spans[1]), normed_a, inverse_a)
    grad_spans = jnp.concatenate([shift_a, scale_a, gate_a, shift_b, scale_b, gate_b], axis=-1)
    grad_bias = jnp.concatenate([bias_sums[:D], bias_sums[2 * D :], bias_proj, bias_fc1, bias_fc2])
    return (grad_in, (grad_qkv, grad_proj, grad_fc1, grad_fc2), grad_bias, grad_spans)


MESH_IDS = pl.DeviceIdType.MESH
Z_SIZE, Y_SIZE, X_SIZE, C_SIZE = 4, 2, 2, 2
LANES = 128


def place():
    dp, rep = lax.axis_index("dp"), lax.axis_index("rep")
    return (dp // Y_SIZE, dp % Y_SIZE, rep // C_SIZE, rep % C_SIZE)


def device(z, y, x, c):
    return (z * Y_SIZE + y, x * C_SIZE + c)


def meet(peers):
    barrier = pltpu.get_barrier_semaphore()
    for peer in peers:
        pl.semaphore_signal(barrier, inc=1, device_id=peer, device_id_type=MESH_IDS)
    pl.semaphore_wait(barrier, len(peers))


def push(source, target, send, receive, peer):
    return pltpu.make_async_remote_copy(
        src_ref=source,
        dst_ref=target,
        send_sem=send,
        recv_sem=receive,
        device_id=peer,
        device_id_type=MESH_IDS,
    )


def ids_kernel(own, full, send, receive, local):
    dp, rep = lax.axis_index("dp"), lax.axis_index("rep")
    dps, reps = Z_SIZE * Y_SIZE, X_SIZE * C_SIZE
    offsets = [(i, j) for i in range(dps) for j in range(reps) if i or j]
    peers = [((dp + i) % dps, (rep + j) % reps) for i, j in offsets]
    meet(peers)
    mine = dp * reps + rep
    copies = [
        push(own, full.at[mine], send.at[n], receive.at[n], peer) for n, peer in enumerate(peers)
    ]
    for copy in copies:
        copy.start()
    keep = pltpu.make_async_copy(own, full.at[mine], local)
    keep.start()
    keep.wait()
    for copy in copies:
        copy.wait()


def gather_ids(own):
    count = Z_SIZE * Y_SIZE * X_SIZE * C_SIZE
    return pl.pallas_call(
        ids_kernel,
        out_shape=jax.ShapeDtypeStruct((count,) + own.shape, own.dtype),
        in_specs=[pl.BlockSpec(memory_space=pltpu.VMEM)],
        out_specs=pl.BlockSpec(memory_space=pltpu.VMEM),
        scratch_shapes=[
            pltpu.SemaphoreType.DMA((count - 1,)),
            pltpu.SemaphoreType.DMA((count - 1,)),
            pltpu.SemaphoreType.DMA,
        ],
        compiler_params=pltpu.CompilerParams(collective_id=1, has_side_effects=True),
        name="gather_ids",
    )(own)


def gather_kernel(groups, packed, parts, full, summed, part_in, z_s, z_r, y_s, y_r, x_s, x_r, c_s, c_r, p_s, p_r, local):
    z, y, x, c = place()
    dp = z * Y_SIZE + y
    dps = Z_SIZE * Y_SIZE
    part_peers = [((dp + k) % dps, x * C_SIZE + c) for k in range(1, dps)]
    across_y, across_x, sibling = device(z, 1 - y, x, c), device(z, y, 1 - x, c), device(z, y, x, 1 - c)
    meet(part_peers + [across_x, sibling])
    part_copies = [
        push(parts.at[peer[0]], part_in.at[dp], p_s.at[k], p_r.at[k], peer)
        for k, peer in enumerate(part_peers)
    ]
    for copy in part_copies:
        copy.start()
    keeps = []
    for layer in range(LAYERS):
        keep = pltpu.make_async_copy(packed.at[layer], full.at[layer, dp], local.at[layer])
        keep.start()
        keeps.append(keep)
    started = []

    def rows(group, third, count):
        layer, first, size = groups[group]
        step = size // 6
        return pl.ds(pl.multiple_of(first + c * 3 * step + third * step, 16), count * step)

    def source(k, other):
        return ((z - k) % Z_SIZE) * Y_SIZE + (1 - y if other else y)

    def piece(group, owner, third, count):
        return full.at[groups[group][0], owner, rows(group, third, count)]

    def go(source_ref, target_ref, send, receive, peer):
        copy = push(source_ref, target_ref, send, receive, peer)
        copy.start()
        started.append(copy)

    def first_hop(group):
        own = packed.at[groups[group][0], rows(group, x, 2)]
        target = piece(group, dp, x, 2)
        go(own, target, y_s.at[group, 0], y_r.at[group, 0], across_y)
        for k in range(1, Z_SIZE):
            peer = device((z + k) % Z_SIZE, y, x, c)
            go(own, target, z_s.at[group, k - 1], z_r.at[group, k - 1], peer)

    def arrive(ref, send, receive, peer):
        push(ref, ref, send, receive, peer).wait_recv()

    def spread(group, index, owner):
        third = piece(group, owner, 2 * x, 1)
        go(third, third, x_s.at[group, index], x_r.at[group, index], across_x)
        both = piece(group, owner, x, 2)
        go(both, both, c_s.at[group, index], c_r.at[group, index], sibling)

    def on_z(group, k):
        ref = piece(group, source(k, False), x, 2)
        arrive(ref, z_s.at[group, k - 1], z_r.at[group, k - 1], across_y)
        go(ref, ref, y_s.at[group, k], y_r.at[group, k], across_y)
        spread(group, k - 1, source(k, False))

    def on_y(group, k):
        ref = piece(group, source(k, True), x, 2)
        arrive(ref, y_s.at[group, k], y_r.at[group, k], across_y)
        spread(group, Z_SIZE - 1 + k, source(k, True))

    def on_x(group, index):
        owner = source(index + 1, False) if index < Z_SIZE - 1 else source(index - Z_SIZE + 1, True)
        ref = piece(group, owner, 2 - 2 * x, 1)
        arrive(ref, x_s.at[group, index], x_r.at[group, index], across_x)
        slot = index + 2 * Z_SIZE - 1
        go(ref, ref, c_s.at[group, slot], c_r.at[group, slot], sibling)

    def on_c(group):
        layer, first, size = groups[group]
        step = size // 6
        other = 1 - c
        for index in range(2 * Z_SIZE - 1):
            owner = source(index + 1, False) if index < Z_SIZE - 1 else source(index - Z_SIZE + 1, True)
            for slot, third, count in ((index, x, 2), (index + 2 * Z_SIZE - 1, 2 - 2 * x, 1)):
                start = pl.multiple_of(first + other * 3 * step + third * step, 16)
                ref = full.at[layer, owner, pl.ds(start, count * step)]
                arrive(ref, c_s.at[group, slot], c_r.at[group, slot], sibling)

    first_hop(0)
    count = len(groups)
    for group in range(count + 1):
        if group + 1 < count:
            first_hop(group + 1)
        events = []
        if group < count:
            events = [(on_y, group, 0)]
            for k in range(1, Z_SIZE):
                events += [(on_z, group, k), (on_y, group, k)]
        for index in range(2 * Z_SIZE - 1):
            if events:
                step, *where = events[index]
                step(*where)
            if group > 0:
                on_x(group - 1, index)
        if group == 0:
            for copy in part_copies:
                copy.wait()
            total = jnp.where(dp == 0, parts[0], part_in[0])
            for k in range(1, dps):
                total = total + jnp.where(dp == k, parts[k], part_in[k])
            summed[...] = total
    for group in range(count):
        on_c(group)
    for copy in started:
        copy.wait_send()
    for keep in keeps:
        keep.wait()


def gather_weights(packed, parts, groups):
    layers, height, width = packed.shape
    dps = Z_SIZE * Y_SIZE
    count = len(groups)
    dma = pltpu.SemaphoreType.DMA
    return pl.pallas_call(
        partial(gather_kernel, groups),
        out_shape=(
            jax.ShapeDtypeStruct((layers, dps, height, width), packed.dtype),
            jax.ShapeDtypeStruct(parts.shape[1:], parts.dtype),
        ),
        in_specs=[pl.BlockSpec(memory_space=pl.ANY), pl.BlockSpec(memory_space=pltpu.VMEM)],
        out_specs=(pl.BlockSpec(memory_space=pl.ANY), pl.BlockSpec(memory_space=pltpu.VMEM)),
        scratch_shapes=[
            pltpu.VMEM(parts.shape, parts.dtype),
            dma((count, Z_SIZE - 1)),
            dma((count, Z_SIZE - 1)),
            dma((count, Z_SIZE)),
            dma((count, Z_SIZE)),
            dma((count, 2 * Z_SIZE - 1)),
            dma((count, 2 * Z_SIZE - 1)),
            dma((count, 4 * Z_SIZE - 2)),
            dma((count, 4 * Z_SIZE - 2)),
            dma((dps - 1,)),
            dma((dps - 1,)),
            dma((layers,)),
        ],
        compiler_params=pltpu.CompilerParams(
            collective_id=2, has_side_effects=True, vmem_limit_bytes=16 * 2**20
        ),
        name="gather_weights",
    )(packed, parts)


def scatter_kernel(
    groups, grads, mods, smalls, finals, mods_all, small_out,
    held, from_c, from_x, from_y, from_z, to_x, from_fin, small_c, small_x, small_y, small_z,
    c_s, c_r, x_s, x_r, y_s, y_r, z_s, z_r, e_s, e_r, f_s, f_r, m_s, m_r, v_s, v_r, local,
):
    z, y, x, c = place()
    dps = Z_SIZE * Y_SIZE
    z_peers = [device((z + k) % Z_SIZE, y, x, c) for k in range(1, Z_SIZE)]
    across_y, across_x, sibling = device(z, 1 - y, x, c), device(z, y, 1 - x, c), device(z, y, x, 1 - c)
    count = len(groups)
    meet(z_peers + [across_y, across_x, sibling])
    started = []

    def go(source_ref, target_ref, send, receive, peer):
        copy = push(source_ref, target_ref, send, receive, peer)
        copy.start()
        started.append(copy)

    def arrive(ref, send, receive, peer):
        push(ref, ref, send, receive, peer).wait_recv()

    sizes = [size // 2 for _, _, size in groups]
    starts = [sum(sizes[:g]) for g in range(count)]

    def half(group):
        return pl.ds(starts[group], sizes[group])

    def two(group):
        step = sizes[group] // 3
        return pl.ds(pl.multiple_of(starts[group] + x * step, 16), 2 * step)

    def tight(group):
        return pl.ds(starts[group] // 3 * 2, sizes[group] // 3 * 2)

    def third(group):
        return pl.ds(starts[group] // 3, sizes[group] // 3)

    def begin(group):
        layer, first, size = groups[group]
        theirs = pl.ds(pl.multiple_of(first + (1 - c) * (size // 2), 16), size // 2)
        ours = pl.ds(pl.multiple_of(first + c * (size // 2), 16), size // 2)
        for j in range(Y_SIZE):
            side = y if j else 1 - y
            go(grads.at[layer, :, side, theirs], from_c.at[:, side, half(group)], c_s.at[group, j], c_r.at[group, j], sibling)
            pltpu.make_async_copy(grads.at[layer, :, side, ours], held.at[:, side, half(group)], local.at[group, j]).start()

    def add(target, extra, send=None):
        def body(owner, carry):
            total = target[owner].astype(jnp.float32) + extra[owner].astype(jnp.float32)
            total = total.astype(jnp.bfloat16)
            if send is None:
                target[owner] = total
            else:
                send[owner] = total
            return carry
        lax.fori_loop(0, Z_SIZE, body, 0)

    def on_c(group):
        layer, first, size = groups[group]
        step = sizes[group] // 3
        theirs = pl.ds(pl.multiple_of(starts[group] + (2 - 2 * x) * step, 16), step)
        for j in range(Y_SIZE):
            side = y if j else 1 - y
            mine = held.at[:, side, half(group)]
            pltpu.make_async_copy(mine, mine, local.at[group, j]).wait()
            arrive(mine, c_s.at[group, j], c_r.at[group, j], sibling)
            add(held.at[:, side, theirs], from_c.at[:, side, theirs], to_x.at[:, side, third(group)])
            go(to_x.at[:, side, third(group)], from_x.at[:, side, third(group)], x_s.at[group, j], x_r.at[group, j], across_x)
            add(held.at[:, side, two(group)], from_c.at[:, side, two(group)])

    def on_x(group):
        step = sizes[group] // 3
        ours = pl.ds(pl.multiple_of(starts[group] + 2 * x * step, 16), step)
        for j in range(Y_SIZE):
            side = y if j else 1 - y
            got = from_x.at[:, side, third(group)]
            arrive(got, x_s.at[group, j], x_r.at[group, j], across_x)
            add(held.at[:, side, ours], got)
            if j == 0:
                go(held.at[:, side, two(group)], from_y.at[:, tight(group)], y_s.at[group], y_r.at[group], across_y)

    def on_y(group):
        got = from_y.at[:, tight(group)]
        arrive(got, y_s.at[group], y_r.at[group], across_y)
        add(held.at[:, y, two(group)], got)
        for k in range(1, Z_SIZE):
            go(
                held.at[(z + k) % Z_SIZE, y, two(group)], from_z.at[k - 1, tight(group)],
                z_s.at[group, k - 1], z_r.at[group, k - 1], z_peers[k - 1],
            )

    def on_z(group):
        total = held[z, y, two(group)].astype(jnp.float32)
        for k in range(1, Z_SIZE):
            arrive(from_z.at[k - 1, tight(group)], z_s.at[group, k - 1], z_r.at[group, k - 1], across_y)
            total = total + from_z[k - 1, tight(group)].astype(jnp.float32)
        held[z, y, two(group)] = total.astype(jnp.bfloat16)
        go(held.at[z, y, two(group)], from_fin.at[tight(group)], e_s.at[group], e_r.at[group], across_x)

    def on_fin(group):
        layer, first, size = groups[group]
        step = sizes[group] // 3
        arrive(from_fin.at[tight(group)], e_s.at[group], e_r.at[group], across_x)
        base = pl.multiple_of(starts[group] // 3 * 2, 16)
        out = pl.multiple_of(first + c * (size // 2), 16)
        mine = pl.multiple_of(starts[group] + 2 * x * step, 16)
        middle = starts[group] + step
        finals[layer, pl.ds(pl.multiple_of(out + 2 * x * step, 16), step)] = held[z, y, pl.ds(mine, step)].astype(jnp.float32)
        finals[layer, pl.ds(pl.multiple_of(out + (2 - 2 * x) * step, 16), step)] = from_fin[
            pl.ds(pl.multiple_of(base + (1 - x) * step, 16), step)
        ].astype(jnp.float32)
        finals[layer, pl.ds(pl.multiple_of(out + step, 16), step)] = held[z, y, pl.ds(middle, step)].astype(
            jnp.float32
        ) + from_fin[pl.ds(pl.multiple_of(base + x * step, 16), step)].astype(jnp.float32)
        ref = finals.at[layer, pl.ds(out, size // 2)]
        go(ref, ref, f_s.at[group], f_r.at[group], sibling)

    def on_last(group):
        layer, first, size = groups[group]
        ref = finals.at[layer, pl.ds(pl.multiple_of(first + (1 - c) * (size // 2), 16), size // 2)]
        arrive(ref, f_s.at[group], f_r.at[group], sibling)

    slot = x * C_SIZE + c

    def mods_first():
        keep = pltpu.make_async_copy(mods, mods_all.at[z, y, slot], local.at[count, 0])
        keep.start()
        keep.wait()
        own = mods_all.at[z, y, slot]
        for k in range(1, Z_SIZE):
            go(own, own, m_s.at[k - 1], m_r.at[k - 1], z_peers[k - 1])

    def mods_y():
        for k in range(1, Z_SIZE):
            arrive(mods_all.at[(z - k) % Z_SIZE, y, slot], m_s.at[k - 1], m_r.at[k - 1], across_y)
        ref = mods_all.at[:, y, slot]
        go(ref, ref, m_s.at[3], m_r.at[3], across_y)

    def mods_x():
        arrive(mods_all.at[:, 1 - y, slot], m_s.at[3], m_r.at[3], across_y)
        ref = mods_all.at[:, :, slot]
        go(ref, ref, m_s.at[4], m_r.at[4], across_x)

    def mods_c():
        arrive(mods_all.at[:, :, (1 - x) * C_SIZE + c], m_s.at[4], m_r.at[4], across_x)
        for k in range(X_SIZE):
            ref = mods_all.at[:, :, k * C_SIZE + c]
            go(ref, ref, m_s.at[5 + k], m_r.at[5 + k], sibling)

    def mods_end():
        for k in range(X_SIZE):
            arrive(mods_all.at[:, :, k * C_SIZE + 1 - c], m_s.at[5 + k], m_r.at[5 + k], sibling)

    span = small_c.shape[0]
    mine_v = pl.ds(pl.multiple_of(c * span, 8), span)
    other_v = pl.ds(pl.multiple_of((1 - c) * span, 8), span)

    def small_first():
        go(smalls.at[other_v], small_c, v_s.at[0], v_r.at[0], sibling)

    def small_to_x():
        arrive(small_c, v_s.at[0], v_r.at[0], sibling)
        small_c[...] = small_c[...] + smalls[mine_v]
        go(small_c, small_x, v_s.at[1], v_r.at[1], across_x)

    def small_to_y():
        arrive(small_x, v_s.at[1], v_r.at[1], across_x)
        small_x[...] = small_x[...] + small_c[...]
        go(small_x, small_y, v_s.at[2], v_r.at[2], across_y)

    def small_to_z():
        arrive(small_y, v_s.at[2], v_r.at[2], across_y)
        small_z[z] = small_y[...] + small_x[...]
        for k in range(1, Z_SIZE):
            go(small_z.at[z], small_z.at[z], v_s.at[2 + k], v_r.at[2 + k], z_peers[k - 1])

    def small_to_c():
        for k in range(1, Z_SIZE):
            arrive(small_z.at[(z - k) % Z_SIZE], v_s.at[2 + k], v_r.at[2 + k], across_y)
        small_out[mine_v] = (small_z[0] + small_z[1]) + (small_z[2] + small_z[3])
        go(small_out.at[mine_v], small_out.at[mine_v], v_s.at[6], v_r.at[6], sibling)

    def small_end():
        arrive(small_out.at[other_v], v_s.at[6], v_r.at[6], sibling)

    extra = [
        [small_first, mods_first], [small_to_x, mods_y], [small_to_y, mods_x], [small_to_z, mods_c],
        [small_to_c, mods_end], [small_end],
    ]
    for group in range(count):
        begin(group)
    stages = [on_c, on_x, on_y, on_z, on_fin, on_last]
    for step in range(max(count + len(stages) - 1, len(extra))):
        for index, stage in enumerate(stages):
            if 0 <= step - index < count:
                stage(step - index)
        if step < len(extra):
            for stage in extra[step]:
                stage()
    for copy in started:
        copy.wait_send()


def scatter_grads(grads, mods, smalls, groups):
    layers, owners, height, width = grads.shape
    grads = grads.reshape(layers, Z_SIZE, Y_SIZE, height, width)
    rows = sum(size for _, _, size in groups) // 2
    count = len(groups)
    dma = pltpu.SemaphoreType.DMA
    low, wide = jnp.bfloat16, jnp.float32
    span = smalls.shape[0] // 2
    vmem = pl.BlockSpec(memory_space=pltpu.VMEM)
    finals, mods_all, small_out = pl.pallas_call(
        partial(scatter_kernel, groups),
        out_shape=(
            jax.ShapeDtypeStruct((layers, height, width), wide),
            jax.ShapeDtypeStruct((Z_SIZE, Y_SIZE, X_SIZE * C_SIZE) + mods.shape, mods.dtype),
            jax.ShapeDtypeStruct(smalls.shape, wide),
        ),
        in_specs=[pl.BlockSpec(memory_space=pl.ANY), vmem, vmem],
        out_specs=(vmem, vmem, vmem),
        scratch_shapes=[
            pltpu.VMEM((Z_SIZE, Y_SIZE, rows, width), low),
            pltpu.VMEM((Z_SIZE, Y_SIZE, rows, width), low),
            pltpu.VMEM((Z_SIZE, Y_SIZE, rows // 3, width), low),
            pltpu.VMEM((Z_SIZE, rows // 3 * 2, width), low),
            pltpu.VMEM((Z_SIZE - 1, rows // 3 * 2, width), low),
            pltpu.VMEM((Z_SIZE, Y_SIZE, rows // 3, width), low),
            pltpu.VMEM((rows // 3 * 2, width), low),
            pltpu.VMEM((span, LANES), wide),
            pltpu.VMEM((span, LANES), wide),
            pltpu.VMEM((span, LANES), wide),
            pltpu.VMEM((Z_SIZE, span, LANES), wide),
            dma((count, 2)), dma((count, 2)),
            dma((count, 2)), dma((count, 2)),
            dma((count,)), dma((count,)),
            dma((count, Z_SIZE - 1)), dma((count, Z_SIZE - 1)),
            dma((count,)), dma((count,)),
            dma((count,)), dma((count,)),
            dma((7,)), dma((7,)),
            dma((7,)), dma((7,)),
            dma((count + 1, 2)),
        ],
        compiler_params=pltpu.CompilerParams(
            collective_id=3, has_side_effects=True, vmem_limit_bytes=62 * 2**20
        ),
        name="scatter_grads",
    )(grads, mods, smalls)
    return finals, mods_all, small_out


def pack_shard(w_qkv, w_proj, w_fc1, w_fc2):
    pieces = [w_qkv[:, D * i : D * (i + 1)] for i in range(3)] + [w_proj]
    pieces += [w_fc1[:, D * i : D * (i + 1)] for i in range(FF // D)] + [w_fc2]
    return jnp.concatenate(pieces, axis=0).astype(jnp.bfloat16)


def square(full, index):
    rows = D // full.shape[0]
    return full[:, rows * index : rows * (index + 1)].reshape(D, D)


def unpack_full(full):
    rows = D // full.shape[0]
    count = FF // D
    return (
        jnp.concatenate([square(full, i) for i in range(3)], axis=1),
        square(full, 3),
        jnp.concatenate([square(full, 4 + i) for i in range(count)], axis=1),
        full[:, rows * (4 + count) :].reshape(FF, D),
    )


def pack_grads(grads, owners):
    def split(block):
        return block.astype(jnp.bfloat16).reshape(owners, -1, D)

    pieces = [split(grads[0][:, D * i : D * (i + 1)]) for i in range(3)] + [split(grads[1])]
    pieces += [split(grads[2][:, D * i : D * (i + 1)]) for i in range(FF // D)] + [split(grads[3])]
    return jnp.concatenate(pieces, axis=1)


def unpack_shard(packed, rows):
    count = FF // D
    blocks = [packed[:, rows * i : rows * (i + 1)] for i in range(4 + count)]
    return (
        jnp.concatenate(blocks[:3], axis=-1),
        blocks[3],
        jnp.concatenate(blocks[4:], axis=-1),
        packed[:, rows * (4 + count) :],
    )


def local(
    latents,
    noise_field,
    timesteps,
    labels,
    drop_mask,
    roster,
    w_qkv,
    w_proj,
    w_fc1,
    w_fc2,
    w_mod,
    row_qkv,
    col_qkv,
    row_proj,
    col_proj,
    row_fc1,
    col_fc1,
    row_fc2,
    col_fc2,
    row_mod,
    col_mod,
    small,
    small_second,
):
    pieces = unpack(small)
    dp_size, rep_size = lax.axis_size("dp"), lax.axis_size("rep")
    everyone = dp_size * rep_size
    number = latents.shape[0] * latents.shape[1]
    count_all = number * everyone * GRID * GRID * PDIM
    rows_mod = w_mod.shape[0]
    first_row = lax.axis_index("dp") * rows_mod
    places = position_table()
    patch_low = pieces["patch_w"].astype(jnp.bfloat16)
    time1_low = pieces["time1_w"].astype(jnp.bfloat16)
    time2_low = pieces["time2_w"].astype(jnp.bfloat16)
    head_low = pieces["head_w"].astype(jnp.bfloat16)
    mod_shard = w_mod.astype(jnp.bfloat16)

    own_ids = jnp.stack([timesteps, labels, drop_mask]).reshape(3, number)
    direct = (dp_size, rep_size) == (Z_SIZE * Y_SIZE, X_SIZE * C_SIZE) and rows_mod % 96 == 0
    if direct:
        tile = jnp.pad(own_ids, ((0, 8 - 3), (0, LANES - number))).astype(jnp.float32)
        all_ids = gather_ids(tile)[:, :3, :number].astype(jnp.int32)
    else:
        all_ids = lax.all_gather(own_ids, ("dp", "rep"), axis=0, tiled=False)
    all_ids = all_ids.transpose(1, 0, 2).reshape(3, everyone * number)
    features = time_features(all_ids[0]).astype(jnp.bfloat16)
    hidden_t = product(features, time1_low) + pieces["time1_b"]
    silu_t = jax.nn.silu(hidden_t).astype(jnp.bfloat16)
    chosen = jnp.where(all_ids[2] == 1, CLASSES, all_ids[1])
    onehot = (chosen[:, None] == jnp.arange(CLASSES + 1)[None, :]).astype(jnp.float32)
    condition = (
        product(silu_t, time2_low)
        + pieces["time2_b"]
        + jnp.dot(onehot, pieces["class_tab"], precision=HIGHEST)
    )
    silu_c = jax.nn.silu(condition).astype(jnp.bfloat16)
    silu_rows = lax.dynamic_slice_in_dim(silu_c, first_row, rows_mod, axis=1)
    group_rows = lax.dynamic_index_in_dim(
        silu_rows.reshape(dp_size, rep_size, number, rows_mod),
        lax.axis_index("rep"),
        axis=1,
        keepdims=False,
    ).reshape(dp_size * number, rows_mod)
    mod_part = product(group_rows, mod_shard)
    if direct:
        packed = jnp.stack(
            [pack_shard(w_qkv[i], w_proj[i], w_fc1[i], w_fc2[i]) for i in range(LAYERS)]
        )
        heights = [(0, 384), (384, 384), (768, 384)]
        groups = [(i, first, size) for i in range(LAYERS) for first, size in heights]
        mod_part = mod_part.reshape(dp_size, -1, LANES)
        packed_full, mod_sum = gather_weights(packed, mod_part, groups)
        mod_sum = mod_sum.reshape(number, MOD)
    else:
        mod_sum = lax.psum_scatter(mod_part, "dp", scatter_dimension=0, tiled=True)
    modulation = mod_sum + pieces["mod_b"]

    picker = (timesteps.reshape(-1)[:, None] == jnp.arange(STEPS_T)[None, :]).astype(jnp.float32)
    factors = jnp.dot(picker, roster.T, precision=HIGHEST)
    noise_flat = noise_field.reshape(number, -1)
    noised = factors[:, 0:1] * latents.reshape(number, -1) + factors[:, 1:2] * noise_flat
    tokens = patchify(noised).astype(jnp.bfloat16)
    target = patchify(noise_flat).reshape(-1, PDIM)
    residual = (product(tokens.reshape(-1, PDIM), patch_low) + pieces["patch_b"]).reshape(
        number, GRID * GRID, D
    ) + places
    kept_all = []
    gathered_all = []
    spans_all = []
    for layer_index in range(LAYERS):
        if direct:
            weights = unpack_full(packed_full[layer_index])
        else:
            weights = tuple(
                lax.all_gather(w[layer_index].astype(jnp.bfloat16), "dp", axis=0, tiled=True)
                for w in (w_qkv, w_proj, w_fc1, w_fc2)
            )
        spans = [
            modulation[:, None, D * (6 * layer_index + i) : D * (6 * layer_index + i + 1)]
            for i in range(6)
        ]
        residual, kept = layer_forward(residual, spans, weights, pieces["block_b"][layer_index])
        kept_all.append(kept)
        gathered_all.append(weights)
        spans_all.append(spans)
    final_shift = modulation[:, None, 6 * D * LAYERS : 6 * D * LAYERS + D]
    final_scale = modulation[:, None, 6 * D * LAYERS + D :]
    normed_f, inverse_f = norm_rows(residual)
    final_in = (normed_f * (1.0 + final_scale) + final_shift).astype(jnp.bfloat16).reshape(-1, D)
    output = product(final_in, head_low) + pieces["head_b"]
    error = output - target
    loss_own = jnp.sum(error * error)
    grad_output = (error * (2.0 / count_all)).astype(jnp.bfloat16)
    grad_head = product(final_in.T, grad_output)
    grad_head_b = jnp.sum(grad_output.astype(jnp.float32), axis=0)
    grad_final = product(grad_output, head_low.T).reshape(number, GRID * GRID, D)
    final_grads = [jnp.sum(grad_final, axis=1), jnp.sum(grad_final * normed_f, axis=1)]
    grad_res = norm_back(grad_final * (1.0 + final_scale), normed_f, inverse_f)
    layer_spans = [None] * LAYERS
    bias_grads = [None] * LAYERS
    block_grads = [None] * LAYERS
    for layer_index in reversed(range(LAYERS)):
        grad_res, grads, grad_bias, grad_spans = layer_backward(
            grad_res, spans_all[layer_index], gathered_all[layer_index], kept_all[layer_index]
        )
        layer_spans[layer_index] = grad_spans
        bias_grads[layer_index] = grad_bias
        if direct:
            block_grads[layer_index] = pack_grads(grads, dp_size)
        else:
            block_grads[layer_index] = tuple(
                lax.psum_scatter(g, "dp", scatter_dimension=0, tiled=True) for g in grads
            )

    grad_start = grad_res.reshape(-1, D).astype(jnp.bfloat16)
    grad_patch = product(tokens.reshape(-1, PDIM).T, grad_start)
    grad_patch_b = jnp.sum(grad_start.astype(jnp.float32), axis=0)
    own_sums = jnp.concatenate(
        [
            grad_patch.reshape(-1),
            grad_patch_b,
            grad_head.reshape(-1),
            jnp.stack(bias_grads).reshape(-1),
            grad_head_b,
            loss_own[None],
        ]
    )
    own_mod = jnp.concatenate(layer_spans + final_grads, axis=-1).astype(jnp.bfloat16)
    if direct:
        order = [(i, first, size) for i in reversed(range(LAYERS)) for first, size in heights[::-1]]
        mod_rows = number * MOD // LANES
        mod_tile = jnp.pad(own_mod.reshape(mod_rows, LANES), ((0, -mod_rows % 16), (0, 0)))
        sum_tile = jnp.pad(own_sums, (0, -own_sums.size % (16 * LANES))).reshape(-1, LANES)
        finals, mod_all, sum_all = scatter_grads(jnp.stack(block_grads), mod_tile, sum_tile, order)
        grad_qkv, grad_proj, grad_fc1, grad_fc2 = unpack_shard(finals, rows_mod)
        grad_mod = mod_all.reshape(everyone, -1, LANES)[:, :mod_rows].reshape(-1, MOD)
        summed = sum_all.reshape(-1)
    else:
        grad_qkv, grad_proj, grad_fc1, grad_fc2 = lax.psum(
            tuple(jnp.stack([block_grads[i][k] for i in range(LAYERS)]) for k in range(4)), "rep"
        )
        grad_mod = lax.all_gather(own_mod, ("dp", "rep"), axis=0, tiled=True)
        summed = lax.psum(own_sums, ("dp", "rep"))

    grad_wmod = product(silu_rows.T, grad_mod)
    grad_mod_b = jnp.sum(grad_mod.astype(jnp.float32), axis=0)
    cond_rows = lax.all_gather(product(grad_mod, mod_shard.T), "dp", axis=1, tiled=True)
    _, silu_pull = jax.vjp(jax.nn.silu, condition)
    grad_cond = silu_pull(cond_rows)[0].astype(jnp.bfloat16)
    grad_class = jnp.dot(onehot.T, grad_cond.astype(jnp.float32), precision=HIGHEST)
    grad_time2 = product(silu_t.T, grad_cond)
    grad_time2_b = jnp.sum(grad_cond.astype(jnp.float32), axis=0)
    _, silu_time_pull = jax.vjp(jax.nn.silu, hidden_t)
    grad_hidden_t = silu_time_pull(product(grad_cond, time2_low.T))[0].astype(jnp.bfloat16)
    grad_time1 = product(features.T, grad_hidden_t)
    grad_time1_b = jnp.sum(grad_hidden_t.astype(jnp.float32), axis=0)
    cut_patch = (PDIM + 1) * D
    cut_head = cut_patch + D * PDIM
    cut_bias = cut_head + LAYERS * (4 * D + FF)
    loss_total = summed[cut_bias + PDIM]
    small_grad = jnp.concatenate(
        [
            summed[:cut_patch],
            grad_time1.reshape(-1),
            grad_time1_b,
            grad_time2.reshape(-1),
            grad_time2_b,
            grad_class.reshape(-1),
            grad_mod_b,
            summed[cut_patch:cut_head],
            summed[cut_bias : cut_bias + PDIM],
            summed[cut_head:cut_bias],
        ]
    )
    beta = 1.0 - STEP ** (-0.8)
    rows_dp = lax.axis_size("dp")
    kinds = [
        (w_qkv, grad_qkv, row_qkv, col_qkv),
        (w_proj, grad_proj, row_proj, col_proj),
        (w_fc1, grad_fc1, row_fc1, col_fc1),
        (w_fc2, grad_fc2, row_fc2, col_fc2),
        (w_mod[None], grad_wmod[None], row_mod[None], col_mod[None]),
    ]
    firsts = []
    for weight, grad, row, col in kinds:
        square = grad * grad
        row_new = beta * row + (1.0 - beta) * jnp.mean(square + EPS_ONE, axis=-1)
        firsts.append(
            (
                row_new,
                jnp.sum(square + EPS_ONE, axis=-2),
                jnp.sum(square / row_new[:, :, None], axis=-2),
                jnp.sum(row_new, axis=-1),
                jnp.sum(weight * weight, axis=(-2, -1)),
            )
        )
    shared = lax.psum(
        jnp.concatenate([entry[k].reshape(-1) for k in range(1, 5) for entry in firsts]), "dp"
    )
    parts = []
    offset = 0
    for k in range(1, 5):
        for entry in firsts:
            parts.append(shared[offset : offset + entry[k].size].reshape(entry[k].shape))
            offset += entry[k].size
    seconds = []
    for index, kind in enumerate(kinds):
        weight, grad, row, col = kind
        rows_all = weight.shape[1] * rows_dp
        col_count = weight.shape[2]
        col_sum, over_rows, row_sum, weight_sq = (parts[index + len(kinds) * k] for k in range(4))
        row_mean = row_sum / rows_all
        weight_rms = jnp.sqrt(weight_sq / (rows_all * col_count))
        col_new = beta * col + (1.0 - beta) * col_sum / rows_all
        update_sq = row_mean * jnp.sum(over_rows / col_new, axis=-1)
        estimate = firsts[index][0][:, :, None] * col_new[:, None, :] / row_mean[:, None, None]
        update = grad * lax.rsqrt(estimate)
        seconds.append((update, col_new, weight_rms, update_sq / (rows_all * col_count)))
    results = []
    for kind, first, second in zip(kinds, firsts, seconds):
        weight, grad = (kind[0], kind[1])
        update, col_new, weight_rms, update_ms = second
        update_rms = jnp.sqrt(update_ms)
        update = update / jnp.maximum(1.0, update_rms / CLIP)[:, None, None]
        new_weight = weight - (RATE * jnp.maximum(0.001, weight_rms))[:, None, None] * update
        results.append((new_weight, grad, first[0], col_new, new_weight.astype(jnp.bfloat16)))
    square = small_grad * small_grad + EPS_ONE
    small_second_new = beta * small_second + (1.0 - beta) * square
    update = small_grad * lax.rsqrt(small_second_new)
    update = update / jnp.maximum(1.0, jnp.sqrt(jnp.mean(update * update)) / CLIP)
    small_new = small - RATE * jnp.maximum(0.001, jnp.sqrt(jnp.mean(small * small))) * update
    mod_result = results[4]
    return (
        loss_total,
        results[0][0],
        results[0][1],
        results[0][2],
        results[0][3],
        results[0][4],
        results[1][0],
        results[1][1],
        results[1][2],
        results[1][3],
        results[1][4],
        results[2][0],
        results[2][1],
        results[2][2],
        results[2][3],
        results[2][4],
        results[3][0],
        results[3][1],
        results[3][2],
        results[3][3],
        results[3][4],
        mod_result[0][0],
        mod_result[1][0],
        mod_result[2][0],
        mod_result[3][0],
        mod_result[4][0],
        small_grad,
        small_second_new,
        small_new,
        small_new.astype(jnp.bfloat16),
    )


def solution(mesh):
    in_specs = (
        P(None, ("dp", "rep"), None),
        P(None, ("dp", "rep"), None),
        P(None, ("dp", "rep")),
        P(None, ("dp", "rep")),
        P(None, ("dp", "rep")),
        P(),
        P(None, "dp", None),
        P(None, "dp", None),
        P(None, "dp", None),
        P(None, "dp", None),
        P("dp", None),
        P(None, "dp"),
        P(),
        P(None, "dp"),
        P(),
        P(None, "dp"),
        P(),
        P(None, "dp"),
        P(),
        P("dp"),
        P(),
        P(),
        P(),
    )
    out_specs = (
        P(),
        P(None, "dp", None),
        P(None, "dp", None),
        P(None, "dp"),
        P(),
        P(None, "dp", None),
        P(None, "dp", None),
        P(None, "dp", None),
        P(None, "dp"),
        P(),
        P(None, "dp", None),
        P(None, "dp", None),
        P(None, "dp", None),
        P(None, "dp"),
        P(),
        P(None, "dp", None),
        P(None, "dp", None),
        P(None, "dp", None),
        P(None, "dp"),
        P(),
        P(None, "dp", None),
        P("dp", None),
        P("dp", None),
        P("dp"),
        P(),
        P("dp", None),
        P(),
        P(),
        P(),
        P(),
    )
    return jax.shard_map(local, mesh=mesh, in_specs=in_specs, out_specs=out_specs, check_vma=False)
```

```python
from functools import partial
import math

import jax
import jax.numpy as jnp
from jax import lax
from jax.experimental import pallas as pl
from jax.experimental.pallas import tpu as pltpu
from jax.sharding import PartitionSpec as P

D = 768
HEADS = 12
FF = 3072
FREQ = 256
CLASSES = 32
GRID = 16
PATCH = 2
CHAN = 4
LAYERS = 2
MICRO = 2
STEPS_T = 1000
STEP = 10
PDIM = 16
MOD = 10752


HIGHEST = lax.Precision.HIGHEST
EPS_NORM = 1e-06
EPS_ONE = 1e-30
CLIP = 0.5
RATE = 0.6


def product(left, right):
    return jnp.dot(left, right, preferred_element_type=jnp.float32)


def layout():
    return [
        ("patch_w", (PDIM, D)),
        ("patch_b", (D,)),
        ("time1_w", (FREQ, D)),
        ("time1_b", (D,)),
        ("time2_w", (D, D)),
        ("time2_b", (D,)),
        ("class_tab", (CLASSES + 1, D)),
        ("mod_b", (MOD,)),
        ("head_w", (D, PDIM)),
        ("head_b", (PDIM,)),
        ("block_b", (LAYERS, 4 * D + FF)),
    ]


def unpack(small):
    pieces = {}
    offset = 0
    for piece_name, piece_dims in layout():
        piece_size = math.prod(piece_dims)
        pieces[piece_name] = small[offset : offset + piece_size].reshape(piece_dims)
        offset += piece_size
    return pieces


def position_table():
    quarter = D // 4
    omega = jnp.exp(-math.log(10000.0) * jnp.arange(quarter, dtype=jnp.float32) / quarter)
    places = jnp.arange(GRID * GRID, dtype=jnp.int32)
    across = (places // GRID).astype(jnp.float32)[:, None] * omega
    downward = (places % GRID).astype(jnp.float32)[:, None] * omega
    return jnp.concatenate(
        [jnp.sin(across), jnp.cos(across), jnp.sin(downward), jnp.cos(downward)], axis=1
    )


def time_features(timesteps):
    half_count = FREQ // 2
    frequency = jnp.exp(-math.log(10000.0) * jnp.arange(half_count, dtype=jnp.float32) / half_count)
    angles = timesteps.astype(jnp.float32)[:, None] * frequency
    return jnp.concatenate([jnp.cos(angles), jnp.sin(angles)], axis=1)


def patchify(flat):
    number = flat.shape[0]
    blocks = flat.reshape(number, GRID, PATCH, GRID, PATCH, CHAN).transpose(0, 1, 3, 2, 4, 5)
    return blocks.reshape(number, GRID * GRID, PDIM)


def norm_rows(values):
    centered = values - jnp.mean(values, axis=-1, keepdims=True)
    inverse = lax.rsqrt(jnp.mean(centered * centered, axis=-1, keepdims=True) + EPS_NORM)
    return (centered * inverse, inverse)


def norm_back(grad, normed, inverse):
    return inverse * (
        grad
        - jnp.mean(grad, axis=-1, keepdims=True)
        - normed * jnp.mean(grad * normed, axis=-1, keepdims=True)
    )


def layer_forward(residual, spans, weights, biases):
    number, seq_tokens = (residual.shape[0], residual.shape[1])
    scaling = 1.0 / math.sqrt(D // HEADS)
    blank_bias = jnp.zeros((D,), jnp.float32)
    qkv_bias = jnp.concatenate([biases[:D], blank_bias, biases[D : 2 * D]])
    normed_a, inverse_a = norm_rows(residual)
    mixed_a = (normed_a * (1.0 + spans[1]) + spans[0]).astype(jnp.bfloat16)
    projected = (product(mixed_a.reshape(-1, D), weights[0]) + qkv_bias).astype(jnp.bfloat16)
    projected = projected.reshape(number, seq_tokens, 3, HEADS, D // HEADS)
    scores = (
        jnp.einsum(
            "bqhd,bkhd->bhqk",
            projected[:, :, 0],
            projected[:, :, 1],
            preferred_element_type=jnp.float32,
        )
        * scaling
    )
    total_lse = jax.nn.logsumexp(scores, axis=-1, keepdims=True)
    attention = jnp.exp(scores - total_lse).astype(jnp.bfloat16)
    attended = jnp.einsum(
        "bhqk,bkhd->bqhd", attention, projected[:, :, 2], preferred_element_type=jnp.float32
    )
    attended = attended.astype(jnp.bfloat16).reshape(-1, D)
    branch_a = product(attended, weights[1]) + biases[2 * D : 3 * D]
    middle = residual + spans[2] * branch_a.reshape(number, seq_tokens, D)
    normed_b, inverse_b = norm_rows(middle)
    mixed_b = (normed_b * (1.0 + spans[4]) + spans[3]).astype(jnp.bfloat16)
    hidden = product(mixed_b.reshape(-1, D), weights[2]) + biases[3 * D : 3 * D + FF]
    activated = jax.nn.gelu(hidden, approximate=True).astype(jnp.bfloat16)
    branch_b = product(activated, weights[3]) + biases[3 * D + FF :]
    result = middle + spans[5] * branch_b.reshape(number, seq_tokens, D)
    kept = (
        normed_a,
        inverse_a,
        mixed_a,
        projected,
        total_lse,
        attended,
        branch_a,
        normed_b,
        inverse_b,
        mixed_b,
        hidden,
        activated,
        branch_b,
    )
    return (result, kept)


def layer_backward(grad_out, spans, weights, kept):
    (
        normed_a,
        inverse_a,
        mixed_a,
        projected,
        total_lse,
        attended,
        branch_a,
        normed_b,
        inverse_b,
        mixed_b,
        hidden,
        activated,
        branch_b,
    ) = kept
    number, seq_tokens = (grad_out.shape[0], grad_out.shape[1])
    scaling = 1.0 / math.sqrt(D // HEADS)
    grad_b = (spans[5] * grad_out).reshape(-1, D).astype(jnp.bfloat16)
    gate_b = jnp.sum(grad_out * branch_b.reshape(number, seq_tokens, D), axis=1)
    grad_fc2 = product(activated.T, grad_b)
    bias_fc2 = jnp.sum(grad_b.astype(jnp.float32), axis=0)
    _, gelu_pull = jax.vjp(partial(jax.nn.gelu, approximate=True), hidden)
    grad_hidden = gelu_pull(product(grad_b, weights[3].T))[0].astype(jnp.bfloat16)
    grad_fc1 = product(mixed_b.reshape(-1, D).T, grad_hidden)
    bias_fc1 = jnp.sum(grad_hidden.astype(jnp.float32), axis=0)
    grad_mixed = product(grad_hidden, weights[2].T).reshape(number, seq_tokens, D)
    shift_b = jnp.sum(grad_mixed, axis=1)
    scale_b = jnp.sum(grad_mixed * normed_b, axis=1)
    grad_mid = grad_out + norm_back(grad_mixed * (1.0 + spans[4]), normed_b, inverse_b)
    grad_a = (spans[2] * grad_mid).reshape(-1, D).astype(jnp.bfloat16)
    gate_a = jnp.sum(grad_mid * branch_a.reshape(number, seq_tokens, D), axis=1)
    grad_proj = product(attended.T, grad_a)
    bias_proj = jnp.sum(grad_a.astype(jnp.float32), axis=0)
    grad_att = (
        product(grad_a, weights[1].T)
        .astype(jnp.bfloat16)
        .reshape(number, seq_tokens, HEADS, D // HEADS)
    )
    query, keys, values = (projected[:, :, 0], projected[:, :, 1], projected[:, :, 2])
    scores = (
        jnp.einsum("bqhd,bkhd->bhqk", query, keys, preferred_element_type=jnp.float32) * scaling
    )
    attention = jnp.exp(scores - total_lse)
    grad_values = jnp.einsum(
        "bhqk,bqhd->bkhd",
        attention.astype(jnp.bfloat16),
        grad_att,
        preferred_element_type=jnp.float32,
    )
    grad_weights = jnp.einsum(
        "bqhd,bkhd->bhqk", grad_att, values, preferred_element_type=jnp.float32
    )
    inner = jnp.sum(attention * grad_weights, axis=-1, keepdims=True)
    grad_scores = (attention * (grad_weights - inner)).astype(jnp.bfloat16)
    grad_query = (
        jnp.einsum("bhqk,bkhd->bqhd", grad_scores, keys, preferred_element_type=jnp.float32)
        * scaling
    )
    grad_keys = (
        jnp.einsum("bhqk,bqhd->bkhd", grad_scores, query, preferred_element_type=jnp.float32)
        * scaling
    )
    grad_projected = (
        jnp.stack([grad_query, grad_keys, grad_values], axis=2)
        .reshape(-1, 3 * D)
        .astype(jnp.bfloat16)
    )
    grad_qkv = product(mixed_a.reshape(-1, D).T, grad_projected)
    bias_sums = jnp.sum(grad_projected.astype(jnp.float32), axis=0)
    grad_mixed_a = product(grad_projected, weights[0].T).reshape(number, seq_tokens, D)
    shift_a = jnp.sum(grad_mixed_a, axis=1)
    scale_a = jnp.sum(grad_mixed_a * normed_a, axis=1)
    grad_in = grad_mid + norm_back(grad_mixed_a * (1.0 + spans[1]), normed_a, inverse_a)
    grad_spans = jnp.concatenate([shift_a, scale_a, gate_a, shift_b, scale_b, gate_b], axis=-1)
    grad_bias = jnp.concatenate([bias_sums[:D], bias_sums[2 * D :], bias_proj, bias_fc1, bias_fc2])
    return (grad_in, (grad_qkv, grad_proj, grad_fc1, grad_fc2), grad_bias, grad_spans)


MESH_IDS = pl.DeviceIdType.MESH
Z_SIZE, Y_SIZE, X_SIZE, C_SIZE = 4, 2, 2, 2
LANES = 128


def place():
    dp, rep = lax.axis_index("dp"), lax.axis_index("rep")
    return (dp // Y_SIZE, dp % Y_SIZE, rep // C_SIZE, rep % C_SIZE)


def device(z, y, x, c):
    return (z * Y_SIZE + y, x * C_SIZE + c)


def meet(peers):
    barrier = pltpu.get_barrier_semaphore()
    for peer in peers:
        pl.semaphore_signal(barrier, inc=1, device_id=peer, device_id_type=MESH_IDS)
    pl.semaphore_wait(barrier, len(peers))


def push(source, target, send, receive, peer):
    return pltpu.make_async_remote_copy(
        src_ref=source,
        dst_ref=target,
        send_sem=send,
        recv_sem=receive,
        device_id=peer,
        device_id_type=MESH_IDS,
    )


def ids_kernel(own, full, send, receive, local):
    dp, rep = lax.axis_index("dp"), lax.axis_index("rep")
    dps, reps = Z_SIZE * Y_SIZE, X_SIZE * C_SIZE
    offsets = [(i, j) for i in range(dps) for j in range(reps) if i or j]
    peers = [((dp + i) % dps, (rep + j) % reps) for i, j in offsets]
    meet(peers)
    mine = dp * reps + rep
    copies = [
        push(own, full.at[mine], send.at[n], receive.at[n], peer) for n, peer in enumerate(peers)
    ]
    for copy in copies:
        copy.start()
    keep = pltpu.make_async_copy(own, full.at[mine], local)
    keep.start()
    keep.wait()
    for copy in copies:
        copy.wait()


def gather_ids(own):
    count = Z_SIZE * Y_SIZE * X_SIZE * C_SIZE
    return pl.pallas_call(
        ids_kernel,
        out_shape=jax.ShapeDtypeStruct((count,) + own.shape, own.dtype),
        in_specs=[pl.BlockSpec(memory_space=pltpu.VMEM)],
        out_specs=pl.BlockSpec(memory_space=pltpu.VMEM),
        scratch_shapes=[
            pltpu.SemaphoreType.DMA((count - 1,)),
            pltpu.SemaphoreType.DMA((count - 1,)),
            pltpu.SemaphoreType.DMA,
        ],
        compiler_params=pltpu.CompilerParams(collective_id=1, has_side_effects=True),
        name="gather_ids",
    )(own)


def gather_kernel(groups, packed, parts, full, summed, part_in, z_s, z_r, y_s, y_r, x_s, x_r, c_s, c_r, p_s, p_r, local):
    z, y, x, c = place()
    dp = z * Y_SIZE + y
    dps = Z_SIZE * Y_SIZE
    part_peers = [((dp + k) % dps, x * C_SIZE + c) for k in range(1, dps)]
    across_y, across_x, sibling = device(z, 1 - y, x, c), device(z, y, 1 - x, c), device(z, y, x, 1 - c)
    meet(part_peers + [across_x, sibling])
    part_copies = [
        push(parts.at[peer[0]], part_in.at[dp], p_s.at[k], p_r.at[k], peer)
        for k, peer in enumerate(part_peers)
    ]
    for copy in part_copies:
        copy.start()
    keeps = []
    for layer in range(LAYERS):
        keep = pltpu.make_async_copy(packed.at[layer], full.at[layer, dp], local.at[layer])
        keep.start()
        keeps.append(keep)
    started = []

    def rows(group, third, count):
        layer, first, size = groups[group]
        step = size // 6
        return pl.ds(pl.multiple_of(first + c * 3 * step + third * step, 16), count * step)

    def source(k, other):
        return ((z - k) % Z_SIZE) * Y_SIZE + (1 - y if other else y)

    def piece(group, owner, third, count):
        return full.at[groups[group][0], owner, rows(group, third, count)]

    def go(source_ref, target_ref, send, receive, peer):
        copy = push(source_ref, target_ref, send, receive, peer)
        copy.start()
        started.append(copy)

    def first_hop(group):
        own = packed.at[groups[group][0], rows(group, x, 2)]
        target = piece(group, dp, x, 2)
        go(own, target, y_s.at[group, 0], y_r.at[group, 0], across_y)
        for k in range(1, Z_SIZE):
            peer = device((z + k) % Z_SIZE, y, x, c)
            go(own, target, z_s.at[group, k - 1], z_r.at[group, k - 1], peer)

    def arrive(ref, send, receive, peer):
        push(ref, ref, send, receive, peer).wait_recv()

    def spread(group, index, owner):
        third = piece(group, owner, 2 * x, 1)
        go(third, third, x_s.at[group, index], x_r.at[group, index], across_x)
        both = piece(group, owner, x, 2)
        go(both, both, c_s.at[group, index], c_r.at[group, index], sibling)

    def on_z(group, k):
        ref = piece(group, source(k, False), x, 2)
        arrive(ref, z_s.at[group, k - 1], z_r.at[group, k - 1], across_y)
        go(ref, ref, y_s.at[group, k], y_r.at[group, k], across_y)
        spread(group, k - 1, source(k, False))

    def on_y(group, k):
        ref = piece(group, source(k, True), x, 2)
        arrive(ref, y_s.at[group, k], y_r.at[group, k], across_y)
        spread(group, Z_SIZE - 1 + k, source(k, True))

    def on_x(group, index):
        owner = source(index + 1, False) if index < Z_SIZE - 1 else source(index - Z_SIZE + 1, True)
        ref = piece(group, owner, 2 - 2 * x, 1)
        arrive(ref, x_s.at[group, index], x_r.at[group, index], across_x)
        slot = index + 2 * Z_SIZE - 1
        go(ref, ref, c_s.at[group, slot], c_r.at[group, slot], sibling)

    def on_c(group):
        layer, first, size = groups[group]
        step = size // 6
        other = 1 - c
        for index in range(2 * Z_SIZE - 1):
            owner = source(index + 1, False) if index < Z_SIZE - 1 else source(index - Z_SIZE + 1, True)
            for slot, third, count in ((index, x, 2), (index + 2 * Z_SIZE - 1, 2 - 2 * x, 1)):
                start = pl.multiple_of(first + other * 3 * step + third * step, 16)
                ref = full.at[layer, owner, pl.ds(start, count * step)]
                arrive(ref, c_s.at[group, slot], c_r.at[group, slot], sibling)

    first_hop(0)
    count = len(groups)
    for group in range(count + 1):
        if group + 1 < count:
            first_hop(group + 1)
        events = []
        if group < count:
            events = [(on_y, group, 0)]
            for k in range(1, Z_SIZE):
                events += [(on_z, group, k), (on_y, group, k)]
        for index in range(2 * Z_SIZE - 1):
            if events:
                step, *where = events[index]
                step(*where)
            if group > 0:
                on_x(group - 1, index)
        if group == 0:
            for copy in part_copies:
                copy.wait()
            total = jnp.where(dp == 0, parts[0], part_in[0])
            for k in range(1, dps):
                total = total + jnp.where(dp == k, parts[k], part_in[k])
            summed[...] = total
    for group in range(count):
        on_c(group)
    for copy in started:
        copy.wait_send()
    for keep in keeps:
        keep.wait()


def gather_weights(packed, parts, groups):
    layers, height, width = packed.shape
    dps = Z_SIZE * Y_SIZE
    count = len(groups)
    dma = pltpu.SemaphoreType.DMA
    return pl.pallas_call(
        partial(gather_kernel, groups),
        out_shape=(
            jax.ShapeDtypeStruct((layers, dps, height, width), packed.dtype),
            jax.ShapeDtypeStruct(parts.shape[1:], parts.dtype),
        ),
        in_specs=[pl.BlockSpec(memory_space=pl.ANY), pl.BlockSpec(memory_space=pltpu.VMEM)],
        out_specs=(pl.BlockSpec(memory_space=pl.ANY), pl.BlockSpec(memory_space=pltpu.VMEM)),
        scratch_shapes=[
            pltpu.VMEM(parts.shape, parts.dtype),
            dma((count, Z_SIZE - 1)),
            dma((count, Z_SIZE - 1)),
            dma((count, Z_SIZE)),
            dma((count, Z_SIZE)),
            dma((count, 2 * Z_SIZE - 1)),
            dma((count, 2 * Z_SIZE - 1)),
            dma((count, 4 * Z_SIZE - 2)),
            dma((count, 4 * Z_SIZE - 2)),
            dma((dps - 1,)),
            dma((dps - 1,)),
            dma((layers,)),
        ],
        compiler_params=pltpu.CompilerParams(
            collective_id=2, has_side_effects=True, vmem_limit_bytes=16 * 2**20
        ),
        name="gather_weights",
    )(packed, parts)


GELU_A, GELU_B = 0.79788456, 0.044715
FF_BLOCKS = FF // D
TILE = 256
ROWS = 64


def centre(values):
    centered = values - jnp.mean(values, axis=-1, keepdims=True)
    inverse = lax.rsqrt(jnp.mean(centered * centered, axis=-1, keepdims=True) + EPS_NORM)
    return centered * inverse, inverse


def dot_nn(left, right):
    return lax.dot_general(left, right, (((1,), (0,)), ((), ())), preferred_element_type=jnp.float32)


def dot_nt(left, right):
    return lax.dot_general(left, right, (((1,), (1,)), ((), ())), preferred_element_type=jnp.float32)


def dot_tn(left, right):
    return lax.dot_general(left, right, (((0,), (0,)), ((), ())), preferred_element_type=jnp.float32)


def each(count, body):
    if count <= 3:
        for i in range(count):
            body(i)
        return
    lax.fori_loop(0, count, lambda i, carry: (body(i), carry)[1], 0)


def row_blocks(tokens, body, step=ROWS):
    each(tokens // step, lambda i: body(pl.ds(pl.multiple_of(i * step, step), step), i // (GRID * GRID // step)))


def modulate(source, mods, shift, scale, target, tokens):
    def body(rows, image):
        normed, _ = centre(source[rows])
        target[rows] = (normed * (1.0 + mods[image, scale]) + mods[image, shift]).astype(jnp.bfloat16)

    row_blocks(tokens, body)


def block_at(i, size):
    return pl.ds(i * size if isinstance(i, int) else pl.multiple_of(i * size, size), size)


def columns(i):
    return block_at(i, TILE)


def head_lanes(head):
    lane = lax.broadcasted_iota(jnp.int32, (GRID * GRID, 2 * D // HEADS), 1)
    return lane // (D // HEADS) == head


def softmax(query, keys):
    scores = dot_nt(query, keys) * (1.0 / math.sqrt(D // HEADS))
    powers = jnp.exp(scores - jnp.max(scores, axis=-1, keepdims=True))
    return powers * (1.0 / jnp.sum(powers, axis=-1, keepdims=True))


def pick(lanes, values):
    return jnp.where(lanes, values, jnp.zeros_like(values))


def attention_forward(projected, attended, images):
    pairs = HEADS // 2
    size, width = GRID * GRID, 2 * D // HEADS

    def body(i, image):
        rows, lanes = block_at(image, size), block_at(i, width)
        query, keys, values = (projected[p, rows, lanes] for p in range(3))
        first = head_lanes(0)
        outs = []
        for own in (first, jnp.logical_not(first)):
            weights = softmax(pick(own, query), keys).astype(jnp.bfloat16)
            outs.append(dot_nn(weights, values))
        attended[rows, lanes] = jnp.where(first, outs[0], outs[1]).astype(jnp.bfloat16)

    each(pairs, lambda i: [body(i, image) for image in range(images)])


def attention_backward(projected, grad_attended, grad_projected, image, first_pair, pairs):
    size, width = GRID * GRID, 2 * D // HEADS
    scaling = 1.0 / math.sqrt(D // HEADS)

    def body(i):
        rows, lanes = block_at(image, size), block_at(first_pair + i, width)
        query, keys, values = (projected[p, rows, lanes] for p in range(3))
        grad_out = grad_attended[rows, lanes]
        first = head_lanes(0)
        outs = []
        for own in (first, jnp.logical_not(first)):
            weights = softmax(pick(own, query), keys)
            grad_values = dot_tn(weights.astype(jnp.bfloat16), grad_out)
            grad_weights = dot_nt(pick(own, grad_out), values)
            inner = jnp.sum(weights * grad_weights, axis=-1, keepdims=True)
            grad_scores = (weights * (grad_weights - inner)).astype(jnp.bfloat16)
            outs.append(
                (dot_nn(grad_scores, keys) * scaling, dot_tn(grad_scores, query) * scaling, grad_values)
            )
        for p in range(3):
            grad_projected[p, rows, lanes] = jnp.where(first, outs[0][p], outs[1][p]).astype(jnp.bfloat16)

    each(pairs, body)


def whole(block):
    return block.reshape(D, block.shape[-1])


def forward_kernel(
    start, mods, biases, full, out, x_h, proj_h, att_h, branch_a_h, middle_h, branch_b_h,
    w_in, w_out, x_v, proj_v, att_v, branch_a, middle, branch_b, mixed, active, w_sem, save_sem,
):
    tokens = start.shape[0]
    images = mods.shape[0]
    shard = w_in.shape[3]
    deep = w_out.shape[3]
    count = 4 + FF_BLOCKS

    def load(layer, index):
        if index < count:
            return pltpu.make_async_copy(
                full.at[layer, :, pl.ds(index * shard, shard)], w_in.at[layer, index], w_sem.at[layer, index]
            )
        block = index - count
        per = D // deep
        return pltpu.make_async_copy(
            full.at[layer, pl.ds(block * per, per), pl.ds(count * shard, deep)],
            w_out.at[layer, block],
            w_sem.at[layer, index],
        )

    order = [0, 1, 2, 3] + [i for b in range(FF_BLOCKS) for i in (4 + b, count + b)]
    for layer in range(LAYERS):
        for index in order:
            load(layer, index).start()
    x_v[0] = start[...]

    def one_layer(layer):
        saves = []

        def save(source, target, index):
            copy = pltpu.make_async_copy(source.at[layer], target.at[layer], save_sem.at[layer, index])
            copy.start()
            saves.append(copy)

        base = 6 * layer
        x, projected, attended = x_v.at[layer], proj_v.at[layer], att_v.at[layer]
        mid = middle.at[layer]
        save(x_v, x_h, 0)
        modulate(x, mods, base, base + 1, mixed, tokens)
        for p in range(3):
            load(layer, p).wait()

            def project(i, p=p):
                value = dot_nn(mixed[...], whole(w_in[layer, p, :, :, columns(i)]))
                if p != 1:
                    value = value + biases[layer, p // 2, :, columns(i)]
                projected[p, :, columns(i)] = value.astype(jnp.bfloat16)

            each(D // TILE, project)
        save(proj_v, proj_h, 1)
        attention_forward(projected, attended, images)
        save(att_v, att_h, 2)
        load(layer, 3).wait()

        def first_branch(i):
            value = dot_nn(attended[...], whole(w_in[layer, 3, :, :, columns(i)]))
            value = value + biases[layer, 2, :, columns(i)]
            branch_a[layer, :, columns(i)] = value
            for image in range(images):
                rows = pl.ds(image * GRID * GRID, GRID * GRID)
                part = value[image * GRID * GRID : (image + 1) * GRID * GRID]
                mid[rows, columns(i)] = x[rows, columns(i)] + mods[image, base + 2, :, columns(i)] * part

        each(D // TILE, first_branch)
        save(branch_a, branch_a_h, 3)
        save(middle, middle_h, 4)
        modulate(mid, mods, base + 3, base + 4, mixed, tokens)
        for block in range(FF_BLOCKS):
            load(layer, 4 + block).wait()

            def expand(i, block=block):
                hidden = dot_nn(mixed[...], whole(w_in[layer, 4 + block, :, :, columns(i)]))
                hidden = hidden + biases[layer, 3 + block, :, columns(i)]
                inner = jnp.tanh(GELU_A * (hidden + GELU_B * hidden * hidden * hidden))
                active[:, columns(i)] = (0.5 * hidden * (1.0 + inner)).astype(jnp.bfloat16)

            each(D // TILE, expand)
            load(layer, count + block).wait()

            def contract(i, block=block):
                value = dot_nn(active[...], whole(w_out[layer, block, :, :, columns(i)]))
                if block == 0:
                    branch_b[layer, :, columns(i)] = value + biases[layer, 3 + FF_BLOCKS, :, columns(i)]
                else:
                    branch_b[layer, :, columns(i)] += value

            each(D // TILE, contract)
        save(branch_b, branch_b_h, 5)

        def finish(rows, image):
            value = mid[rows] + mods[image, base + 5] * branch_b[layer, rows]
            out[rows] = value

            @pl.when(layer + 1 < LAYERS)
            def _():
                x_v[layer + 1, rows] = value

        row_blocks(tokens, finish)
        for copy in saves:
            copy.wait()

    each(LAYERS, one_layer)


def run_forward(start, mods, biases, full):
    tokens = start.shape[0]
    layers, owners, height, width = full.shape
    shard, deep = D // owners, FF // owners
    wide, low = jnp.float32, jnp.bfloat16
    keep = [
        ((tokens, D), wide), ((3, tokens, D), low), ((tokens, D), low),
        ((tokens, D), wide), ((tokens, D), wide), ((tokens, D), wide),
    ]
    vmem, anywhere = pl.BlockSpec(memory_space=pltpu.VMEM), pl.BlockSpec(memory_space=pl.ANY)
    kept = [jax.ShapeDtypeStruct((layers,) + shape, kind) for shape, kind in keep]
    return pl.pallas_call(
        forward_kernel,
        out_shape=[jax.ShapeDtypeStruct((tokens, D), wide)] + kept,
        in_specs=[vmem, vmem, vmem, anywhere],
        out_specs=[vmem] + [anywhere] * len(keep),
        scratch_shapes=[
            pltpu.VMEM((layers, 4 + FF_BLOCKS, owners, shard, D), low),
            pltpu.VMEM((layers, FF_BLOCKS, D // deep, deep, D), low),
        ]
        + [pltpu.VMEM(entry.shape, entry.dtype) for entry in kept]
        + [
            pltpu.VMEM((tokens, D), low),
            pltpu.VMEM((tokens, D), low),
            pltpu.SemaphoreType.DMA((layers, 4 + 2 * FF_BLOCKS)),
            pltpu.SemaphoreType.DMA((layers, len(keep))),
        ],
        compiler_params=pltpu.CompilerParams(vmem_limit_bytes=62 * 2**20),
        name="blocks_forward",
    )(start, mods, biases, full)


class Pace:
    RATE = 48e3
    LATENCY = 2.2

    def __init__(self):
        self.now = 0.0
        self.free = {}
        self.entries = []

    def send(self, link, count):
        rate = 10 * self.RATE if link == "c" else self.RATE
        self.free[link] = max(self.now, self.free.get(link, 0.0)) + count / rate
        return self.free[link] + self.LATENCY

    def add(self, ready, run):
        self.entries.append([ready, len(self.entries), run])

    def serve(self, entry):
        cost, ready = entry[2]()
        self.now += cost
        if ready is None:
            self.entries.remove(entry)
        else:
            entry[0] = ready

    def spend(self, cost):
        self.now += cost
        while self.entries:
            entry = min(self.entries, key=lambda e: e[:2])
            if entry[0] > self.now:
                return
            self.serve(entry)

    def drain(self):
        while self.entries:
            entry = min(self.entries, key=lambda e: e[:2])
            self.now = max(self.now, entry[0])
            self.serve(entry)


class Reduction:
    COSTS = (0.6, 0.4, 0.8, 0.5, 0.4, 0.1)

    def __init__(self, pace, groups, shard, spot, buffers, semaphores, credits, finals):
        self.pace, self.groups, self.shard, self.spot = pace, groups, shard, spot
        self.held, self.from_c, self.from_x, self.from_y, self.from_z, self.from_fin = buffers
        self.sems, self.credits, self.finals = semaphores, credits, finals
        z, y, x, c = spot
        self.z_peers = [device((z + k) % Z_SIZE, y, x, c) for k in range(1, Z_SIZE)]
        self.z_before = [device((z - k) % Z_SIZE, y, x, c) for k in range(1, Z_SIZE)]
        self.across_y, self.across_x = device(z, 1 - y, x, c), device(z, y, 1 - x, c)
        self.sibling = device(z, y, x, 1 - c)
        self.started, self.kept, self.filled, self.busy = {}, {}, {}, {}
        self.at_half = [first for first, _, _ in groups]
        self.halves = [rows for _, rows, _ in groups]
        self.parts = [part for _, _, part in groups]
        most = [rows - part for _, rows, part in groups]
        self.at_part = [sum(self.parts[:g]) for g in range(len(groups))]
        self.at_most = [sum(most[:g]) for g in range(len(groups))]

    def peers(self):
        return self.z_peers + [self.across_y, self.across_x, self.sibling]

    def go(self, key, source, target, sems, peer):
        copy = push(source, target, sems[0], sems[1], peer)
        copy.start()
        self.started.setdefault(key, []).append(copy)

    def arrive(self, ref, sems):
        push(ref, ref, sems[0], sems[1], self.across_y).wait_recv()

    def sem(self, name, layer, *index):
        send, receive = self.sems[name]
        return send.at[(layer,) + index], receive.at[(layer,) + index]

    def give(self, layer, name, peer, *index):
        if layer == LAYERS - 1:
            pl.semaphore_signal(
                self.credits[name].at[index], inc=1, device_id=peer, device_id_type=MESH_IDS
            )

    def take(self, layer, name, *index):
        if layer != LAYERS - 1:
            pl.semaphore_wait(self.credits[name].at[index], 1)

    def put(self, layer, group, stage, first, squares, owner_z, slot):
        c = self.spot[3]
        half = self.shard // 2
        if (layer, group) not in self.filled:
            while (layer + 1, group) in self.busy:
                self.pace.spend(0.5)
            for copy in self.started.pop((layer + 1, group), []):
                copy.wait_send()
            self.take(layer, "c", group)
            self.filled[layer, group] = []
        rows = pl.ds(first, squares * half)
        theirs = stage.at[:, :, :, pl.ds(pl.multiple_of((1 - c) * half, 16), half)]
        ours = stage.at[:, :, :, pl.ds(pl.multiple_of(c * half, 16), half)]
        zs = stage.shape[0]

        def view(ref):
            pieces = ref.reshape(Z_SIZE, Y_SIZE, ref.shape[2] // half, half, D)
            return pieces.at[pl.ds(owner_z, zs), :, pl.ds(first // half, squares)]

        sems = self.sem("c", layer, group, slot)
        send = push(theirs, view(self.from_c), sems[0], sems[1], self.sibling)
        keep = pltpu.make_async_copy(ours, view(self.held), self.sems["keep"].at[layer, group, slot])
        send.start()
        keep.start()
        self.filled[layer, group].append((slot, owner_z, zs, rows))
        self.kept[layer, group, slot] = keep
        self.ready = self.pace.send("c", zs * Y_SIZE * squares * half * D * 2)

        def free():
            send.wait_send()
            self.keep_wait(layer, group, slot)

        return free

    def begin(self, layer, group):
        stages = [self.on_c, self.on_x, self.on_y, self.on_z, self.on_fin, self.on_last]
        costs = list(self.COSTS)
        self.busy[layer, group] = True

        def run():
            ready = stages.pop(0)(layer, group)
            if not stages:
                del self.busy[layer, group]
            return costs.pop(0), ready

        self.pace.add(self.ready, run)

    def keep_wait(self, *key):
        keep = self.kept.pop(key, None)
        if keep is not None:
            keep.wait()

    def add(self, target, extra):
        def body(owner):
            total = target[owner].astype(jnp.float32) + extra[owner].astype(jnp.float32)
            target[owner] = total.astype(jnp.bfloat16)

        each(Z_SIZE, body)

    def on_c(self, layer, group):
        z, y, x, c = self.spot
        half, part = self.halves[group], self.parts[group]
        first = self.at_half[group]
        for slot, owner_z, zs, rows in self.filled[layer, group]:
            self.keep_wait(layer, group, slot)
            self.arrive(self.from_c.at[pl.ds(owner_z, zs), :, rows], self.sem("c", layer, group, slot))
        theirs = pl.ds(pl.multiple_of(first + (1 - x) * (half - part), 16), part)
        ours = pl.ds(pl.multiple_of(first + x * part, 16), half - part)
        for side in range(Y_SIZE):
            self.add(self.held.at[:, side, theirs], self.from_c.at[:, side, theirs])
        target = self.from_x.at[:, :, pl.ds(self.at_part[group], part)]
        self.take(layer, "x", group)
        self.go((layer, group), self.held.at[:, :, theirs], target, self.sem("x", layer, group), self.across_x)
        for side in range(Y_SIZE):
            self.add(self.held.at[:, side, ours], self.from_c.at[:, side, ours])
        self.give(layer, "c", self.sibling, group)
        return self.pace.send("x", 8 * part * D * 2)

    def on_x(self, layer, group):
        z, y, x, c = self.spot
        half, part = self.halves[group], self.parts[group]
        first = self.at_half[group]
        got = self.from_x.at[:, :, pl.ds(self.at_part[group], part)]
        self.arrive(got, self.sem("x", layer, group))
        ours = pl.ds(pl.multiple_of(first + x * (half - part), 16), part)
        for side in (1 - y, y):
            self.add(self.held.at[:, side, ours], self.from_x.at[:, side, pl.ds(self.at_part[group], part)])
        self.give(layer, "x", self.across_x, group)
        most = pl.ds(pl.multiple_of(first + x * part, 16), half - part)
        self.take(layer, "y", group)
        self.go(
            (layer, group), self.held.at[:, 1 - y, most], self.from_y.at[:, pl.ds(self.at_most[group], half - part)],
            self.sem("y", layer, group), self.across_y,
        )
        return self.pace.send("y", 4 * (half - part) * D * 2)

    def on_y(self, layer, group):
        z, y, x, c = self.spot
        half, part = self.halves[group], self.parts[group]
        got = self.from_y.at[:, pl.ds(self.at_most[group], half - part)]
        self.arrive(got, self.sem("y", layer, group))
        most = pl.ds(pl.multiple_of(self.at_half[group] + x * part, 16), half - part)
        self.add(self.held.at[:, y, most], got)
        self.give(layer, "y", self.across_y, group)
        for k in range(1, Z_SIZE):
            self.take(layer, "z", group, k - 1)
            self.go(
                (layer, group), self.held.at[(z + k) % Z_SIZE, y, most],
                self.from_z.at[k - 1, pl.ds(self.at_most[group], half - part)],
                self.sem("z", layer, group, k - 1), self.z_peers[k - 1],
            )
        return self.pace.send("z", 4 * (half - part) * D * 2)

    def on_z(self, layer, group):
        z, y, x, c = self.spot
        half, part = self.halves[group], self.parts[group]
        most = pl.ds(pl.multiple_of(self.at_half[group] + x * part, 16), half - part)
        got = pl.ds(self.at_most[group], half - part)
        for k in range(1, Z_SIZE):
            self.arrive(self.from_z.at[k - 1, got], self.sem("z", layer, group, k - 1))
        total = self.held[z, y, most].astype(jnp.float32)
        for k in range(1, Z_SIZE):
            total = total + self.from_z[k - 1, got].astype(jnp.float32)
        self.held[z, y, most] = total.astype(jnp.bfloat16)
        for k in range(1, Z_SIZE):
            self.give(layer, "z", self.z_before[k - 1], group, k - 1)
        self.take(layer, "e", group)
        self.go((layer, group), self.held.at[z, y, most], self.from_fin.at[got], self.sem("e", layer, group), self.across_x)
        return self.pace.send("x", (half - part) * D * 2)

    def on_fin(self, layer, group):
        z, y, x, c = self.spot
        half, part = self.halves[group], self.parts[group]
        middle = half - 2 * part
        base, start = self.at_most[group], self.at_half[group]
        self.arrive(self.from_fin.at[pl.ds(base, half - part)], self.sem("e", layer, group))
        wide = jnp.float32

        def span(begin, size):
            return pl.ds(pl.multiple_of(begin, 16), size)

        ours, theirs = span(start + x * (half - part), part), span(start + (1 - x) * (half - part), part)
        both = span(start + part, middle)
        self.finals[layer, c, ours] = self.held[z, y, ours].astype(wide)
        self.finals[layer, c, theirs] = self.from_fin[span(base + (1 - x) * middle, part)].astype(wide)
        self.finals[layer, c, both] = self.held[z, y, both].astype(wide) + self.from_fin[
            span(base + x * part, middle)
        ].astype(wide)
        self.give(layer, "e", self.across_x, group)
        ref = self.finals.at[layer, c, pl.ds(start, half)]
        self.go((layer, group), ref, ref, self.sem("f", layer, group), self.sibling)
        return self.pace.send("c", half * D * 4)

    def on_last(self, layer, group):
        c = self.spot[3]
        ref = self.finals.at[layer, 1 - c, pl.ds(self.at_half[group], self.halves[group])]
        self.arrive(ref, self.sem("f", layer, group))
        return None

    def finish(self):
        for copies in self.started.values():
            for copy in copies:
                copy.wait_send()


class Sums:
    def __init__(self, reduction, own, total, small_c, small_x, small_y, small_z, mods, mods_all, sems, mod_sems, local):
        self.r = reduction
        self.own, self.total = own, total
        self.small_c, self.small_x, self.small_y, self.small_z = small_c, small_x, small_y, small_z
        self.mods, self.mods_all, self.v, self.m, self.local = mods, mods_all, sems, mod_sems, local
        self.stages = [self.first, self.to_x, self.to_y, self.to_z, self.to_c, self.last]

    def sem(self, pair, index):
        return pair[0].at[index], pair[1].at[index]

    def go(self, ref, target, pair, index, peer):
        self.r.go("sums", ref, target, self.sem(pair, index), peer)

    def arrive(self, ref, pair, index):
        self.r.arrive(ref, self.sem(pair, index))

    def run(self):
        self.stages.pop(0)()
        return 1.0, self.r.pace.now + 7.0 if self.stages else None

    def halves(self):
        span = self.small_c.shape[0]
        c = self.r.spot[3]
        return [pl.ds(pl.multiple_of(i * span, 8), span) for i in (c, 1 - c)]

    def first(self):
        z, y, x, c = self.r.spot
        mine, other = self.halves()
        self.go(self.own.at[other], self.small_c, self.v, 0, self.r.sibling)
        own = self.mods_all.at[z, y, x * C_SIZE + c]
        keep = pltpu.make_async_copy(self.mods, own, self.local)
        keep.start()
        for k in range(1, Z_SIZE):
            self.go(self.mods, own, self.m, k - 1, self.r.z_peers[k - 1])
        keep.wait()

    def to_x(self):
        z, y, x, c = self.r.spot
        mine, other = self.halves()
        self.arrive(self.small_c, self.v, 0)
        self.small_c[...] = self.small_c[...] + self.own[mine]
        self.go(self.small_c, self.small_x, self.v, 1, self.r.across_x)
        slot = x * C_SIZE + c
        for k in range(1, Z_SIZE):
            self.arrive(self.mods_all.at[(z - k) % Z_SIZE, y, slot], self.m, k - 1)
        ref = self.mods_all.at[:, y, slot]
        self.go(ref, ref, self.m, 3, self.r.across_y)

    def to_y(self):
        z, y, x, c = self.r.spot
        self.arrive(self.small_x, self.v, 1)
        self.small_x[...] = self.small_x[...] + self.small_c[...]
        self.go(self.small_x, self.small_y, self.v, 2, self.r.across_y)
        slot = x * C_SIZE + c
        self.arrive(self.mods_all.at[:, 1 - y, slot], self.m, 3)
        ref = self.mods_all.at[:, :, slot]
        self.go(ref, ref, self.m, 4, self.r.across_x)

    def to_z(self):
        z, y, x, c = self.r.spot
        self.arrive(self.small_y, self.v, 2)
        self.small_z[z] = self.small_y[...] + self.small_x[...]
        own = self.small_z.at[z]
        for k in range(1, Z_SIZE):
            self.go(own, own, self.v, 2 + k, self.r.z_peers[k - 1])
        self.arrive(self.mods_all.at[:, :, (1 - x) * C_SIZE + c], self.m, 4)
        for k in range(X_SIZE):
            ref = self.mods_all.at[:, :, k * C_SIZE + c]
            self.go(ref, ref, self.m, 5 + k, self.r.sibling)

    def to_c(self):
        z, y, x, c = self.r.spot
        mine, other = self.halves()
        for k in range(1, Z_SIZE):
            self.arrive(self.small_z.at[(z - k) % Z_SIZE], self.v, 2 + k)
        self.total[mine] = (self.small_z[0] + self.small_z[1]) + (self.small_z[2] + self.small_z[3])
        self.go(self.total.at[mine], self.total.at[mine], self.v, 6, self.r.sibling)
        for k in range(X_SIZE):
            self.arrive(self.mods_all.at[:, :, k * C_SIZE + 1 - c], self.m, 5 + k)

    def last(self):
        mine, other = self.halves()
        self.arrive(self.total.at[other], self.v, 6)


def backward_kernel(
    groups, grad_out, mods, biases, tokens_t, head_sums, head_mods, full,
    x_h, proj_h, att_h, branch_a_h, middle_h, branch_b_h,
    finals, mods_all, sums_out,
    w_v, grad_x, x_v, proj_v, att_v, branch, middle, mixed, grad_b, active, grad_hidden, grad_mixed,
    grad_projected, stage, mods_acc, mods_tile, mods_low, sums,
    held, from_c, from_x, from_y, from_z, from_fin, small_c, small_x, small_y, small_z,
    w_sem, load_sem, keep_sem, c_s, c_r, x_s, x_r, y_s, y_r, z_s, z_r, e_s, e_r, f_s, f_r,
    v_s, v_r, m_s, m_r, local, cred_c, cred_x, cred_y, cred_z, cred_e,
):
    tokens = grad_out.shape[0]
    images = mods.shape[0]
    owners = full.shape[1]
    shard, deep = D // owners, FF // owners
    count = 4 + FF_BLOCKS
    per = D // deep
    slots = w_v.shape[0]
    spot = place()
    pace = Pace()
    reduction = Reduction(
        pace, groups, shard, spot, (held, from_c, from_x, from_y, from_z, from_fin),
        {"c": (c_s, c_r), "x": (x_s, x_r), "y": (y_s, y_r), "z": (z_s, z_r), "e": (e_s, e_r), "f": (f_s, f_r), "keep": keep_sem},
        {"c": cred_c, "x": cred_x, "y": cred_y, "z": cred_z, "e": cred_e}, finals,
    )
    order = [i for b in range(FF_BLOCKS) for i in (4 + b, count + b)] + [3, 0, 1, 2]
    order = [(layer, index) for layer in reversed(range(LAYERS)) for index in order]

    def load(at):
        layer, index = order[at]
        slot = at % slots
        target = w_v.at[slot]
        if index < count:
            return pltpu.make_async_copy(
                full.at[layer, :, pl.ds(index * shard, shard)], target.reshape(owners, shard, D), w_sem.at[slot]
            )
        return pltpu.make_async_copy(
            full.at[layer, pl.ds((index - count) * per, per), pl.ds(count * shard, deep)],
            target.reshape(per, deep, D),
            w_sem.at[slot],
        )

    def fetch(at):
        if at < len(order):
            load(at).start()

    def weight(at):
        load(at).wait()
        return w_v.at[at % slots]

    def total(values):
        return jnp.sum(values, axis=0, keepdims=True)

    for at in range(slots):
        fetch(at)
    reduction_peers = reduction.peers()
    meet(reduction_peers)
    sums[...] = jnp.zeros_like(sums)
    sums[pl.ds(PDIM, 2 * PDIM)] = head_sums[...]
    mods_acc[...] = jnp.zeros_like(mods_acc)
    for image in range(images):
        for k in range(2):
            mods_acc[image, 6 * LAYERS + k] = head_mods[image, k]
    grad_x[...] = grad_out[...]
    busy = [[], []]
    turn = [0]

    def weight_grad(layer, left, right, index):
        slot = turn[0] % 2
        turn[0] += 1
        for wait in busy[slot]:
            wait()

        def body(i):
            cut = block_at(i, D // 2)
            value = dot_tn(left[:, cut], right[...]).astype(jnp.bfloat16)
            stage[slot, cut] = value

        each(2, body)
        half = shard // 2
        if index < count:
            group = next(g for g, entry in enumerate(groups) if entry[0] <= index * half < entry[0] + entry[1])
            view = stage.at[slot].reshape(Z_SIZE, Y_SIZE, 1, shard, D)
            busy[slot] = [
                reduction.put(layer, group, view, index * half, 1, 0, (index * half - groups[group][0]) // half)
            ]
            if index * half == groups[group][0] + groups[group][1] - half:
                reduction.begin(layer, group)
        else:
            block = index - count
            busy[slot] = []
            for group, (first, rows, _) in enumerate(groups):
                if first >= count * half:
                    squares = rows // half
                    view = stage.at[slot].reshape(1, Y_SIZE, deep // shard, shard, D)
                    view = view.at[:, :, pl.ds((first - count * half) // half, squares)]
                    busy[slot].append(reduction.put(layer, group, view, first, squares, block, block))
                    if block == FF_BLOCKS - 1:
                        reduction.begin(layer, group)
        pace.spend(1.3)

    for layer in reversed(range(LAYERS)):
        base = 6 * layer
        at = (LAYERS - 1 - layer) * (count + FF_BLOCKS)
        bias_row = 3 * PDIM + layer * (4 + FF_BLOCKS)

        def bias_add(k, values, cut=slice(None), bias_row=bias_row):
            sums[pl.ds(bias_row + k, 1), cut] += total(values)

        saved = [
            (branch_b_h, branch), (middle_h, middle), (att_h, att_v), (proj_h, proj_v), (x_h, x_v), (branch_a_h, branch),
        ]
        copies = [
            pltpu.make_async_copy(source.at[layer], target, load_sem.at[i])
            for i, (source, target) in enumerate(saved)
        ]
        for copy in copies[:-1]:
            copy.start()
        copies[0].wait()
        copies[1].wait()

        def enter(rows, image, base=base, bias_add=bias_add):
            grad = grad_x[rows]
            low = (mods[image, base + 5] * grad).astype(jnp.bfloat16)
            grad_b[rows] = low
            bias_add(3 + FF_BLOCKS, low.astype(jnp.float32))
            mods_acc[image, base + 5] += total(grad * branch[rows])
            normed, _ = centre(middle[rows])
            mixed[rows] = (normed * (1.0 + mods[image, base + 4]) + mods[image, base + 3]).astype(jnp.bfloat16)

        row_blocks(tokens, enter)
        pace.spend(1.8)
        copies[-1].start()
        for block in range(FF_BLOCKS):
            w_one, w_two = weight(at), weight(at + 1)

            def expand(i, block=block, w_one=w_one, w_two=w_two, layer=layer, bias_add=bias_add):
                hidden = dot_nn(mixed[...], w_one[:, columns(i)]) + biases[layer, 3 + block, :, columns(i)]
                square = hidden * hidden
                inner = jnp.tanh(GELU_A * (hidden + GELU_B * hidden * square))
                active[:, columns(i)] = (0.5 * hidden * (1.0 + inner)).astype(jnp.bfloat16)
                slope = 0.5 * (1.0 + inner) + 0.5 * hidden * (1.0 - inner * inner) * (
                    GELU_A * (1.0 + 3.0 * GELU_B * square)
                )
                low = (slope * dot_nt(grad_b[...], w_two[columns(i)])).astype(jnp.bfloat16)
                grad_hidden[:, columns(i)] = low
                bias_add(3 + block, low.astype(jnp.float32), columns(i))

            each(D // TILE, expand)
            pace.spend(3.6)
            weight_grad(layer, active, grad_b, count + block)

            def back(i, block=block, w_one=w_one):
                value = dot_nt(grad_hidden[...], w_one[columns(i)])
                if block == 0:
                    grad_mixed[:, columns(i)] = value
                else:
                    grad_mixed[:, columns(i)] += value

            each(D // TILE, back)
            pace.spend(1.0)
            fetch(at + slots)
            fetch(at + slots + 1)
            weight_grad(layer, mixed, grad_hidden, 4 + block)
            at += 2
        for copy in copies[2:]:
            copy.wait()

        def leave(rows, image, base=base, bias_add=bias_add):
            grad = grad_mixed[rows]
            normed, inverse = centre(middle[rows])
            mods_acc[image, base + 3] += total(grad)
            mods_acc[image, base + 4] += total(grad * normed)
            grad = grad * (1.0 + mods[image, base + 4])
            grad = grad_x[rows] + inverse * (
                grad - jnp.mean(grad, axis=-1, keepdims=True) - normed * jnp.mean(grad * normed, axis=-1, keepdims=True)
            )
            middle[rows] = grad
            low = (mods[image, base + 2] * grad).astype(jnp.bfloat16)
            grad_b[rows] = low
            bias_add(2, low.astype(jnp.float32))
            mods_acc[image, base + 2] += total(grad * branch[rows])
            normed, _ = centre(x_v[rows])
            mixed[rows] = (normed * (1.0 + mods[image, base + 1]) + mods[image, base]).astype(jnp.bfloat16)

        row_blocks(tokens, leave)
        pace.spend(2.6)
        w_proj = weight(at)

        def through(i, w_proj=w_proj):
            active[:, columns(i)] = dot_nt(grad_b[...], w_proj[columns(i)]).astype(jnp.bfloat16)

        each(D // TILE, through)
        pace.spend(0.9)
        fetch(at + slots)
        weight_grad(layer, att_v, grad_b, 3)
        for image in range(images):
            for pair in range(0, HEADS // 2, 2):
                attention_backward(proj_v, active, grad_projected, image, pair, 2)
                pace.spend(2.1)
        for p in range(3):
            w_part = weight(at + 1 + p)

            def into(i, p=p, w_part=w_part):
                value = dot_nt(grad_projected[p], w_part[columns(i)])
                if p == 0:
                    grad_mixed[:, columns(i)] = value
                else:
                    grad_mixed[:, columns(i)] += value

            weight_grad(layer, mixed, grad_projected.at[p], p)
            each(D // TILE, into)
            pace.spend(1.0)
            fetch(at + 1 + p + slots)

        def last(rows, image, base=base, bias_add=bias_add):
            grad = grad_mixed[rows]
            normed, inverse = centre(x_v[rows])
            mods_acc[image, base] += total(grad)
            mods_acc[image, base + 1] += total(grad * normed)
            grad = grad * (1.0 + mods[image, base + 1])
            grad_x[rows] = middle[rows] + inverse * (
                grad - jnp.mean(grad, axis=-1, keepdims=True) - normed * jnp.mean(grad * normed, axis=-1, keepdims=True)
            )
            bias_add(0, grad_projected[0, rows].astype(jnp.float32))
            bias_add(1, grad_projected[2, rows].astype(jnp.float32))

        row_blocks(tokens, last)
        pace.spend(2.2)

    def patch(rows, image):
        low = grad_x[rows].astype(jnp.bfloat16)
        grad_b[rows] = low
        sums[pl.ds(2 * PDIM + 8, 1)] += total(low.astype(jnp.float32))

    row_blocks(tokens, patch)
    sums[pl.ds(0, PDIM)] = dot_nn(tokens_t[...], grad_b[...])
    mods_tile[...] = jnp.zeros_like(mods_tile)
    entries = mods.shape[1]
    for image in range(images):
        for k in range(entries):
            mods_tile[pl.ds(image * entries + k, 1)] = mods_acc[image, k]
    mods_low[...] = mods_tile[...].astype(jnp.bfloat16)
    small = Sums(
        reduction, sums, sums_out, small_c, small_x, small_y, small_z, mods_low, mods_all, (v_s, v_r), (m_s, m_r), local
    )
    pace.add(pace.now, small.run)
    pace.drain()
    reduction.finish()
    for waits in busy:
        for wait in waits:
            wait()


def run_backward(grad_out, mods, biases, tokens_t, head_sums, head_mods, full, kept):
    tokens = grad_out.shape[0]
    images, entries = mods.shape[:2]
    layers, owners, height, width = full.shape
    shard = D // owners
    count = 4 + FF_BLOCKS
    piece = shard // 2
    sizes = [(2, 1), (1, 1), (1, 1), (2, 2), (2, 1), (2, 2), (2, 1)]
    groups = []
    for squares, thirds in sizes:
        first = sum(group[1] for group in groups)
        groups.append((first, squares * piece, thirds * piece // 3))
    half = height // 2
    part = sum(group[2] for group in groups)
    most = half - part
    wide, low = jnp.float32, jnp.bfloat16
    vmem, anywhere = pl.BlockSpec(memory_space=pltpu.VMEM), pl.BlockSpec(memory_space=pl.ANY)
    rows = (tokens, D)
    dma, regular = pltpu.SemaphoreType.DMA, pltpu.SemaphoreType.REGULAR
    number = len(groups)
    sum_rows = 3 * PDIM + LAYERS * count
    mod_rows = -(-images * entries // 16) * 16
    pair = [dma((layers, number))] * 2
    return pl.pallas_call(
        partial(backward_kernel, groups),
        out_shape=[
            jax.ShapeDtypeStruct((layers, 2, half, width), wide),
            jax.ShapeDtypeStruct((Z_SIZE, Y_SIZE, X_SIZE * C_SIZE, mod_rows, D), low),
            jax.ShapeDtypeStruct((sum_rows, D), wide),
        ],
        in_specs=[vmem] * 6 + [anywhere] * 7,
        out_specs=[vmem] * 3,
        scratch_shapes=[
            pltpu.VMEM((4, D, D), low),
            pltpu.VMEM(rows, wide),
            pltpu.VMEM(rows, wide),
            pltpu.VMEM((3,) + rows, low),
            pltpu.VMEM(rows, low),
            pltpu.VMEM(rows, wide),
            pltpu.VMEM(rows, wide),
            pltpu.VMEM(rows, low),
            pltpu.VMEM(rows, low),
            pltpu.VMEM(rows, low),
            pltpu.VMEM(rows, low),
            pltpu.VMEM(rows, wide),
            pltpu.VMEM((3,) + rows, low),
            pltpu.VMEM((2, D, D), low),
            pltpu.VMEM((images, entries, 1, D), wide),
            pltpu.VMEM((mod_rows, D), wide),
            pltpu.VMEM((mod_rows, D), low),
            pltpu.VMEM((sum_rows, D), wide),
            pltpu.VMEM((Z_SIZE, Y_SIZE, half, D), low),
            pltpu.VMEM((Z_SIZE, Y_SIZE, half, D), low),
            pltpu.VMEM((Z_SIZE, Y_SIZE, part, D), low),
            pltpu.VMEM((Z_SIZE, most, D), low),
            pltpu.VMEM((Z_SIZE - 1, most, D), low),
            pltpu.VMEM((most, D), low),
            pltpu.VMEM((sum_rows // 2, D), wide),
            pltpu.VMEM((sum_rows // 2, D), wide),
            pltpu.VMEM((sum_rows // 2, D), wide),
            pltpu.VMEM((Z_SIZE, sum_rows // 2, D), wide),
            dma((4,)),
            dma((6,)),
            dma((layers, number, FF_BLOCKS)),
            dma((layers, number, FF_BLOCKS)),
            dma((layers, number, FF_BLOCKS)),
            *pair,
            *pair,
            dma((layers, number, Z_SIZE - 1)),
            dma((layers, number, Z_SIZE - 1)),
            *pair,
            *pair,
            dma((7,)),
            dma((7,)),
            dma((7,)),
            dma((7,)),
            dma,
            regular((number,)),
            regular((number,)),
            regular((number,)),
            regular((number, Z_SIZE - 1)),
            regular((number,)),
        ],
        compiler_params=pltpu.CompilerParams(
            collective_id=3, has_side_effects=True, vmem_limit_bytes=63 * 2**20
        ),
        name="blocks_backward",
    )(grad_out, mods, biases, tokens_t, head_sums, head_mods, full, *kept)


def pack_shard(w_qkv, w_proj, w_fc1, w_fc2):
    pieces = [w_qkv[:, D * i : D * (i + 1)] for i in range(3)] + [w_proj]
    pieces += [w_fc1[:, D * i : D * (i + 1)] for i in range(FF // D)] + [w_fc2]
    return jnp.concatenate(pieces, axis=0).astype(jnp.bfloat16)


def unpack_shard(packed, rows):
    count = FF // D
    blocks = [packed[:, rows * i : rows * (i + 1)] for i in range(4 + count)]
    return (
        jnp.concatenate(blocks[:3], axis=-1),
        blocks[3],
        jnp.concatenate(blocks[4:], axis=-1),
        packed[:, rows * (4 + count) :],
    )


def local(
    latents,
    noise_field,
    timesteps,
    labels,
    drop_mask,
    roster,
    w_qkv,
    w_proj,
    w_fc1,
    w_fc2,
    w_mod,
    row_qkv,
    col_qkv,
    row_proj,
    col_proj,
    row_fc1,
    col_fc1,
    row_fc2,
    col_fc2,
    row_mod,
    col_mod,
    small,
    small_second,
):
    pieces = unpack(small)
    dp_size, rep_size = lax.axis_size("dp"), lax.axis_size("rep")
    everyone = dp_size * rep_size
    number = latents.shape[0] * latents.shape[1]
    count_all = number * everyone * GRID * GRID * PDIM
    rows_mod = w_mod.shape[0]
    first_row = lax.axis_index("dp") * rows_mod
    places = position_table()
    patch_low = pieces["patch_w"].astype(jnp.bfloat16)
    time1_low = pieces["time1_w"].astype(jnp.bfloat16)
    time2_low = pieces["time2_w"].astype(jnp.bfloat16)
    head_low = pieces["head_w"].astype(jnp.bfloat16)
    mod_shard = w_mod.astype(jnp.bfloat16)

    own_ids = jnp.stack([timesteps, labels, drop_mask]).reshape(3, number)
    direct = (dp_size, rep_size) == (Z_SIZE * Y_SIZE, X_SIZE * C_SIZE) and rows_mod % 96 == 0
    if direct:
        tile = jnp.pad(own_ids, ((0, 8 - 3), (0, LANES - number))).astype(jnp.float32)
        all_ids = gather_ids(tile)[:, :3, :number].astype(jnp.int32)
    else:
        all_ids = lax.all_gather(own_ids, ("dp", "rep"), axis=0, tiled=False)
    all_ids = all_ids.transpose(1, 0, 2).reshape(3, everyone * number)
    features = time_features(all_ids[0]).astype(jnp.bfloat16)
    hidden_t = product(features, time1_low) + pieces["time1_b"]
    silu_t = jax.nn.silu(hidden_t).astype(jnp.bfloat16)
    chosen = jnp.where(all_ids[2] == 1, CLASSES, all_ids[1])
    onehot = (chosen[:, None] == jnp.arange(CLASSES + 1)[None, :]).astype(jnp.float32)
    condition = (
        product(silu_t, time2_low)
        + pieces["time2_b"]
        + jnp.dot(onehot, pieces["class_tab"], precision=HIGHEST)
    )
    silu_c = jax.nn.silu(condition).astype(jnp.bfloat16)
    silu_rows = lax.dynamic_slice_in_dim(silu_c, first_row, rows_mod, axis=1)
    group_rows = lax.dynamic_index_in_dim(
        silu_rows.reshape(dp_size, rep_size, number, rows_mod),
        lax.axis_index("rep"),
        axis=1,
        keepdims=False,
    ).reshape(dp_size * number, rows_mod)
    mod_part = product(group_rows, mod_shard)
    if direct:
        packed = jnp.stack(
            [pack_shard(w_qkv[i], w_proj[i], w_fc1[i], w_fc2[i]) for i in range(LAYERS)]
        )
        heights = [(0, 384), (384, 384), (768, 384)]
        groups = [(i, first, size) for i in range(LAYERS) for first, size in heights]
        mod_part = mod_part.reshape(dp_size, -1, LANES)
        packed_full, mod_sum = gather_weights(packed, mod_part, groups)
        mod_sum = mod_sum.reshape(number, MOD)
    else:
        mod_sum = lax.psum_scatter(mod_part, "dp", scatter_dimension=0, tiled=True)
    modulation = mod_sum + pieces["mod_b"]

    picker = (timesteps.reshape(-1)[:, None] == jnp.arange(STEPS_T)[None, :]).astype(jnp.float32)
    factors = jnp.dot(picker, roster.T, precision=HIGHEST)
    noise_flat = noise_field.reshape(number, -1)
    noised = factors[:, 0:1] * latents.reshape(number, -1) + factors[:, 1:2] * noise_flat
    tokens = patchify(noised).astype(jnp.bfloat16)
    target = patchify(noise_flat).reshape(-1, PDIM)
    residual = (product(tokens.reshape(-1, PDIM), patch_low) + pieces["patch_b"]).reshape(
        number, GRID * GRID, D
    ) + places
    if direct:
        mods = modulation.reshape(number, -1, 1, D)
        biases = pieces["block_b"].reshape(LAYERS, -1, 1, D)
        residual, *kept_blocks = run_forward(residual.reshape(-1, D), mods, biases, packed_full)
        residual = residual.reshape(number, GRID * GRID, D)
    kept_all = []
    gathered_all = []
    spans_all = []
    for layer_index in range(LAYERS):
        if direct:
            break
        weights = tuple(
            lax.all_gather(w[layer_index].astype(jnp.bfloat16), "dp", axis=0, tiled=True)
            for w in (w_qkv, w_proj, w_fc1, w_fc2)
        )
        spans = [
            modulation[:, None, D * (6 * layer_index + i) : D * (6 * layer_index + i + 1)]
            for i in range(6)
        ]
        residual, kept = layer_forward(residual, spans, weights, pieces["block_b"][layer_index])
        kept_all.append(kept)
        gathered_all.append(weights)
        spans_all.append(spans)
    final_shift = modulation[:, None, 6 * D * LAYERS : 6 * D * LAYERS + D]
    final_scale = modulation[:, None, 6 * D * LAYERS + D :]
    normed_f, inverse_f = norm_rows(residual)
    final_in = (normed_f * (1.0 + final_scale) + final_shift).astype(jnp.bfloat16).reshape(-1, D)
    output = product(final_in, head_low) + pieces["head_b"]
    error = output - target
    loss_own = jnp.sum(error * error)
    grad_output = (error * (2.0 / count_all)).astype(jnp.bfloat16)
    grad_head = product(final_in.T, grad_output)
    grad_head_b = jnp.sum(grad_output.astype(jnp.float32), axis=0)
    grad_final = product(grad_output, head_low.T).reshape(number, GRID * GRID, D)
    final_grads = [jnp.sum(grad_final, axis=1), jnp.sum(grad_final * normed_f, axis=1)]
    grad_res = norm_back(grad_final * (1.0 + final_scale), normed_f, inverse_f)
    if direct:
        head_row = jnp.pad(jnp.append(grad_head_b, loss_own), (0, D - PDIM - 1))[None]
        head_sums = jnp.concatenate([grad_head.T, head_row, jnp.zeros((PDIM - 1, D), jnp.float32)])
        head_mods = jnp.stack(final_grads, axis=1)[:, :, None]
        finals, mod_all, sums = run_backward(
            grad_res.reshape(-1, D), mods, biases, tokens.reshape(-1, PDIM).T, head_sums, head_mods, packed_full, kept_blocks
        )
        finals = finals.reshape(LAYERS, C_SIZE, -1, rows_mod // C_SIZE, D).transpose(0, 2, 1, 3, 4)
        grad_qkv, grad_proj, grad_fc1, grad_fc2 = unpack_shard(finals.reshape(LAYERS, -1, D), rows_mod)
        grad_mod = mod_all.reshape(everyone, -1, D)[:, : number * (MOD // D)].reshape(-1, MOD)
        sum_patch = jnp.concatenate([sums[:PDIM], sums[2 * PDIM + 8 :][:1]]).reshape(-1)
        sum_head = jnp.append(sums[PDIM : 2 * PDIM].T.reshape(-1), sums[2 * PDIM, :PDIM])
        sum_bias = sums[3 * PDIM :].reshape(-1)
        loss_total = sums[2 * PDIM, PDIM]
    else:
        layer_spans = [None] * LAYERS
        bias_grads = [None] * LAYERS
        block_grads = [None] * LAYERS
        for layer_index in reversed(range(LAYERS)):
            grad_res, grads, grad_bias, grad_spans = layer_backward(
                grad_res, spans_all[layer_index], gathered_all[layer_index], kept_all[layer_index]
            )
            layer_spans[layer_index] = grad_spans
            bias_grads[layer_index] = grad_bias
            block_grads[layer_index] = tuple(
                lax.psum_scatter(g, "dp", scatter_dimension=0, tiled=True) for g in grads
            )

        grad_start = grad_res.reshape(-1, D).astype(jnp.bfloat16)
        grad_patch = product(tokens.reshape(-1, PDIM).T, grad_start)
        grad_patch_b = jnp.sum(grad_start.astype(jnp.float32), axis=0)
        own_sums = jnp.concatenate(
            [
                grad_patch.reshape(-1),
                grad_patch_b,
                grad_head.reshape(-1),
                jnp.stack(bias_grads).reshape(-1),
                grad_head_b,
                loss_own[None],
            ]
        )
        own_mod = jnp.concatenate(layer_spans + final_grads, axis=-1).astype(jnp.bfloat16)
        grad_qkv, grad_proj, grad_fc1, grad_fc2 = lax.psum(
            tuple(jnp.stack([block_grads[i][k] for i in range(LAYERS)]) for k in range(4)), "rep"
        )
        grad_mod = lax.all_gather(own_mod, ("dp", "rep"), axis=0, tiled=True)
        summed = lax.psum(own_sums, ("dp", "rep"))
        cut_patch = (PDIM + 1) * D
        cut_head = cut_patch + D * PDIM
        cut_bias = cut_head + LAYERS * (4 * D + FF)
        loss_total = summed[cut_bias + PDIM]
        sum_patch = summed[:cut_patch]
        sum_head = jnp.append(summed[cut_patch:cut_head], summed[cut_bias : cut_bias + PDIM])
        sum_bias = summed[cut_head:cut_bias]

    grad_wmod = product(silu_rows.T, grad_mod)
    grad_mod_b = jnp.sum(grad_mod.astype(jnp.float32), axis=0)
    cond_rows = lax.all_gather(product(grad_mod, mod_shard.T), "dp", axis=1, tiled=True)
    _, silu_pull = jax.vjp(jax.nn.silu, condition)
    grad_cond = silu_pull(cond_rows)[0].astype(jnp.bfloat16)
    grad_class = jnp.dot(onehot.T, grad_cond.astype(jnp.float32), precision=HIGHEST)
    grad_time2 = product(silu_t.T, grad_cond)
    grad_time2_b = jnp.sum(grad_cond.astype(jnp.float32), axis=0)
    _, silu_time_pull = jax.vjp(jax.nn.silu, hidden_t)
    grad_hidden_t = silu_time_pull(product(grad_cond, time2_low.T))[0].astype(jnp.bfloat16)
    grad_time1 = product(features.T, grad_hidden_t)
    grad_time1_b = jnp.sum(grad_hidden_t.astype(jnp.float32), axis=0)
    small_grad = jnp.concatenate(
        [
            sum_patch,
            grad_time1.reshape(-1),
            grad_time1_b,
            grad_time2.reshape(-1),
            grad_time2_b,
            grad_class.reshape(-1),
            grad_mod_b,
            sum_head,
            sum_bias,
        ]
    )
    beta = 1.0 - STEP ** (-0.8)
    rows_dp = lax.axis_size("dp")
    kinds = [
        (w_qkv, grad_qkv, row_qkv, col_qkv),
        (w_proj, grad_proj, row_proj, col_proj),
        (w_fc1, grad_fc1, row_fc1, col_fc1),
        (w_fc2, grad_fc2, row_fc2, col_fc2),
        (w_mod[None], grad_wmod[None], row_mod[None], col_mod[None]),
    ]
    firsts = []
    for weight, grad, row, col in kinds:
        square = grad * grad
        row_new = beta * row + (1.0 - beta) * jnp.mean(square + EPS_ONE, axis=-1)
        firsts.append(
            (
                row_new,
                jnp.sum(square + EPS_ONE, axis=-2),
                jnp.sum(square / row_new[:, :, None], axis=-2),
                jnp.sum(row_new, axis=-1),
                jnp.sum(weight * weight, axis=(-2, -1)),
            )
        )
    shared = lax.psum(
        jnp.concatenate([entry[k].reshape(-1) for k in range(1, 5) for entry in firsts]), "dp"
    )
    parts = []
    offset = 0
    for k in range(1, 5):
        for entry in firsts:
            parts.append(shared[offset : offset + entry[k].size].reshape(entry[k].shape))
            offset += entry[k].size
    seconds = []
    for index, kind in enumerate(kinds):
        weight, grad, row, col = kind
        rows_all = weight.shape[1] * rows_dp
        col_count = weight.shape[2]
        col_sum, over_rows, row_sum, weight_sq = (parts[index + len(kinds) * k] for k in range(4))
        row_mean = row_sum / rows_all
        weight_rms = jnp.sqrt(weight_sq / (rows_all * col_count))
        col_new = beta * col + (1.0 - beta) * col_sum / rows_all
        update_sq = row_mean * jnp.sum(over_rows / col_new, axis=-1)
        estimate = firsts[index][0][:, :, None] * col_new[:, None, :] / row_mean[:, None, None]
        update = grad * lax.rsqrt(estimate)
        seconds.append((update, col_new, weight_rms, update_sq / (rows_all * col_count)))
    results = []
    for kind, first, second in zip(kinds, firsts, seconds):
        weight, grad = (kind[0], kind[1])
        update, col_new, weight_rms, update_ms = second
        update_rms = jnp.sqrt(update_ms)
        update = update / jnp.maximum(1.0, update_rms / CLIP)[:, None, None]
        new_weight = weight - (RATE * jnp.maximum(0.001, weight_rms))[:, None, None] * update
        results.append((new_weight, grad, first[0], col_new, new_weight.astype(jnp.bfloat16)))
    square = small_grad * small_grad + EPS_ONE
    small_second_new = beta * small_second + (1.0 - beta) * square
    update = small_grad * lax.rsqrt(small_second_new)
    update = update / jnp.maximum(1.0, jnp.sqrt(jnp.mean(update * update)) / CLIP)
    small_new = small - RATE * jnp.maximum(0.001, jnp.sqrt(jnp.mean(small * small))) * update
    mod_result = results[4]
    return (
        loss_total,
        results[0][0],
        results[0][1],
        results[0][2],
        results[0][3],
        results[0][4],
        results[1][0],
        results[1][1],
        results[1][2],
        results[1][3],
        results[1][4],
        results[2][0],
        results[2][1],
        results[2][2],
        results[2][3],
        results[2][4],
        results[3][0],
        results[3][1],
        results[3][2],
        results[3][3],
        results[3][4],
        mod_result[0][0],
        mod_result[1][0],
        mod_result[2][0],
        mod_result[3][0],
        mod_result[4][0],
        small_grad,
        small_second_new,
        small_new,
        small_new.astype(jnp.bfloat16),
    )


def solution(mesh):
    in_specs = (
        P(None, ("dp", "rep"), None),
        P(None, ("dp", "rep"), None),
        P(None, ("dp", "rep")),
        P(None, ("dp", "rep")),
        P(None, ("dp", "rep")),
        P(),
        P(None, "dp", None),
        P(None, "dp", None),
        P(None, "dp", None),
        P(None, "dp", None),
        P("dp", None),
        P(None, "dp"),
        P(),
        P(None, "dp"),
        P(),
        P(None, "dp"),
        P(),
        P(None, "dp"),
        P(),
        P("dp"),
        P(),
        P(),
        P(),
    )
    out_specs = (
        P(),
        P(None, "dp", None),
        P(None, "dp", None),
        P(None, "dp"),
        P(),
        P(None, "dp", None),
        P(None, "dp", None),
        P(None, "dp", None),
        P(None, "dp"),
        P(),
        P(None, "dp", None),
        P(None, "dp", None),
        P(None, "dp", None),
        P(None, "dp"),
        P(),
        P(None, "dp", None),
        P(None, "dp", None),
        P(None, "dp", None),
        P(None, "dp"),
        P(),
        P(None, "dp", None),
        P("dp", None),
        P("dp", None),
        P("dp"),
        P(),
        P("dp", None),
        P(),
        P(),
        P(),
        P(),
    )
    return jax.shard_map(local, mesh=mesh, in_specs=in_specs, out_specs=out_specs, check_vma=False)
```

```python
from functools import partial
import math

import jax
import jax.numpy as jnp
from jax import lax
from jax.experimental import pallas as pl
from jax.experimental.pallas import tpu as pltpu
from jax.sharding import PartitionSpec as P

D = 768
HEADS = 12
FF = 3072
FREQ = 256
CLASSES = 32
GRID = 16
PATCH = 2
CHAN = 4
LAYERS = 2
MICRO = 2
STEPS_T = 1000
STEP = 10
PDIM = 16
MOD = 10752


HIGHEST = lax.Precision.HIGHEST
EPS_NORM = 1e-06
EPS_ONE = 1e-30
CLIP = 0.5
RATE = 0.6


def product(left, right):
    return jnp.dot(left, right, preferred_element_type=jnp.float32)


def layout():
    return [
        ("patch_w", (PDIM, D)),
        ("patch_b", (D,)),
        ("time1_w", (FREQ, D)),
        ("time1_b", (D,)),
        ("time2_w", (D, D)),
        ("time2_b", (D,)),
        ("class_tab", (CLASSES + 1, D)),
        ("mod_b", (MOD,)),
        ("head_w", (D, PDIM)),
        ("head_b", (PDIM,)),
        ("block_b", (LAYERS, 4 * D + FF)),
    ]


def unpack(small):
    pieces = {}
    offset = 0
    for piece_name, piece_dims in layout():
        piece_size = math.prod(piece_dims)
        pieces[piece_name] = small[offset : offset + piece_size].reshape(piece_dims)
        offset += piece_size
    return pieces


def position_table():
    quarter = D // 4
    omega = jnp.exp(-math.log(10000.0) * jnp.arange(quarter, dtype=jnp.float32) / quarter)
    places = jnp.arange(GRID * GRID, dtype=jnp.int32)
    across = (places // GRID).astype(jnp.float32)[:, None] * omega
    downward = (places % GRID).astype(jnp.float32)[:, None] * omega
    return jnp.concatenate(
        [jnp.sin(across), jnp.cos(across), jnp.sin(downward), jnp.cos(downward)], axis=1
    )


def time_features(timesteps):
    half_count = FREQ // 2
    frequency = jnp.exp(-math.log(10000.0) * jnp.arange(half_count, dtype=jnp.float32) / half_count)
    angles = timesteps.astype(jnp.float32)[:, None] * frequency
    return jnp.concatenate([jnp.cos(angles), jnp.sin(angles)], axis=1)


def patchify(flat):
    number = flat.shape[0]
    blocks = flat.reshape(number, GRID, PATCH, GRID, PATCH, CHAN).transpose(0, 1, 3, 2, 4, 5)
    return blocks.reshape(number, GRID * GRID, PDIM)


def norm_rows(values):
    centered = values - jnp.mean(values, axis=-1, keepdims=True)
    inverse = lax.rsqrt(jnp.mean(centered * centered, axis=-1, keepdims=True) + EPS_NORM)
    return (centered * inverse, inverse)


def norm_back(grad, normed, inverse):
    return inverse * (
        grad
        - jnp.mean(grad, axis=-1, keepdims=True)
        - normed * jnp.mean(grad * normed, axis=-1, keepdims=True)
    )


def layer_forward(residual, spans, weights, biases):
    number, seq_tokens = (residual.shape[0], residual.shape[1])
    scaling = 1.0 / math.sqrt(D // HEADS)
    blank_bias = jnp.zeros((D,), jnp.float32)
    qkv_bias = jnp.concatenate([biases[:D], blank_bias, biases[D : 2 * D]])
    normed_a, inverse_a = norm_rows(residual)
    mixed_a = (normed_a * (1.0 + spans[1]) + spans[0]).astype(jnp.bfloat16)
    projected = (product(mixed_a.reshape(-1, D), weights[0]) + qkv_bias).astype(jnp.bfloat16)
    projected = projected.reshape(number, seq_tokens, 3, HEADS, D // HEADS)
    scores = (
        jnp.einsum(
            "bqhd,bkhd->bhqk",
            projected[:, :, 0],
            projected[:, :, 1],
            preferred_element_type=jnp.float32,
        )
        * scaling
    )
    total_lse = jax.nn.logsumexp(scores, axis=-1, keepdims=True)
    attention = jnp.exp(scores - total_lse).astype(jnp.bfloat16)
    attended = jnp.einsum(
        "bhqk,bkhd->bqhd", attention, projected[:, :, 2], preferred_element_type=jnp.float32
    )
    attended = attended.astype(jnp.bfloat16).reshape(-1, D)
    branch_a = product(attended, weights[1]) + biases[2 * D : 3 * D]
    middle = residual + spans[2] * branch_a.reshape(number, seq_tokens, D)
    normed_b, inverse_b = norm_rows(middle)
    mixed_b = (normed_b * (1.0 + spans[4]) + spans[3]).astype(jnp.bfloat16)
    hidden = product(mixed_b.reshape(-1, D), weights[2]) + biases[3 * D : 3 * D + FF]
    activated = jax.nn.gelu(hidden, approximate=True).astype(jnp.bfloat16)
    branch_b = product(activated, weights[3]) + biases[3 * D + FF :]
    result = middle + spans[5] * branch_b.reshape(number, seq_tokens, D)
    kept = (
        normed_a,
        inverse_a,
        mixed_a,
        projected,
        total_lse,
        attended,
        branch_a,
        normed_b,
        inverse_b,
        mixed_b,
        hidden,
        activated,
        branch_b,
    )
    return (result, kept)


def layer_backward(grad_out, spans, weights, kept):
    (
        normed_a,
        inverse_a,
        mixed_a,
        projected,
        total_lse,
        attended,
        branch_a,
        normed_b,
        inverse_b,
        mixed_b,
        hidden,
        activated,
        branch_b,
    ) = kept
    number, seq_tokens = (grad_out.shape[0], grad_out.shape[1])
    scaling = 1.0 / math.sqrt(D // HEADS)
    grad_b = (spans[5] * grad_out).reshape(-1, D).astype(jnp.bfloat16)
    gate_b = jnp.sum(grad_out * branch_b.reshape(number, seq_tokens, D), axis=1)
    grad_fc2 = product(activated.T, grad_b)
    bias_fc2 = jnp.sum(grad_b.astype(jnp.float32), axis=0)
    _, gelu_pull = jax.vjp(partial(jax.nn.gelu, approximate=True), hidden)
    grad_hidden = gelu_pull(product(grad_b, weights[3].T))[0].astype(jnp.bfloat16)
    grad_fc1 = product(mixed_b.reshape(-1, D).T, grad_hidden)
    bias_fc1 = jnp.sum(grad_hidden.astype(jnp.float32), axis=0)
    grad_mixed = product(grad_hidden, weights[2].T).reshape(number, seq_tokens, D)
    shift_b = jnp.sum(grad_mixed, axis=1)
    scale_b = jnp.sum(grad_mixed * normed_b, axis=1)
    grad_mid = grad_out + norm_back(grad_mixed * (1.0 + spans[4]), normed_b, inverse_b)
    grad_a = (spans[2] * grad_mid).reshape(-1, D).astype(jnp.bfloat16)
    gate_a = jnp.sum(grad_mid * branch_a.reshape(number, seq_tokens, D), axis=1)
    grad_proj = product(attended.T, grad_a)
    bias_proj = jnp.sum(grad_a.astype(jnp.float32), axis=0)
    grad_att = (
        product(grad_a, weights[1].T)
        .astype(jnp.bfloat16)
        .reshape(number, seq_tokens, HEADS, D // HEADS)
    )
    query, keys, values = (projected[:, :, 0], projected[:, :, 1], projected[:, :, 2])
    scores = (
        jnp.einsum("bqhd,bkhd->bhqk", query, keys, preferred_element_type=jnp.float32) * scaling
    )
    attention = jnp.exp(scores - total_lse)
    grad_values = jnp.einsum(
        "bhqk,bqhd->bkhd",
        attention.astype(jnp.bfloat16),
        grad_att,
        preferred_element_type=jnp.float32,
    )
    grad_weights = jnp.einsum(
        "bqhd,bkhd->bhqk", grad_att, values, preferred_element_type=jnp.float32
    )
    inner = jnp.sum(attention * grad_weights, axis=-1, keepdims=True)
    grad_scores = (attention * (grad_weights - inner)).astype(jnp.bfloat16)
    grad_query = (
        jnp.einsum("bhqk,bkhd->bqhd", grad_scores, keys, preferred_element_type=jnp.float32)
        * scaling
    )
    grad_keys = (
        jnp.einsum("bhqk,bqhd->bkhd", grad_scores, query, preferred_element_type=jnp.float32)
        * scaling
    )
    grad_projected = (
        jnp.stack([grad_query, grad_keys, grad_values], axis=2)
        .reshape(-1, 3 * D)
        .astype(jnp.bfloat16)
    )
    grad_qkv = product(mixed_a.reshape(-1, D).T, grad_projected)
    bias_sums = jnp.sum(grad_projected.astype(jnp.float32), axis=0)
    grad_mixed_a = product(grad_projected, weights[0].T).reshape(number, seq_tokens, D)
    shift_a = jnp.sum(grad_mixed_a, axis=1)
    scale_a = jnp.sum(grad_mixed_a * normed_a, axis=1)
    grad_in = grad_mid + norm_back(grad_mixed_a * (1.0 + spans[1]), normed_a, inverse_a)
    grad_spans = jnp.concatenate([shift_a, scale_a, gate_a, shift_b, scale_b, gate_b], axis=-1)
    grad_bias = jnp.concatenate([bias_sums[:D], bias_sums[2 * D :], bias_proj, bias_fc1, bias_fc2])
    return (grad_in, (grad_qkv, grad_proj, grad_fc1, grad_fc2), grad_bias, grad_spans)


MESH_IDS = pl.DeviceIdType.MESH
Z_SIZE, Y_SIZE, X_SIZE, C_SIZE = 4, 2, 2, 2
LANES = 128


def place():
    dp, rep = lax.axis_index("dp"), lax.axis_index("rep")
    return (dp // Y_SIZE, dp % Y_SIZE, rep // C_SIZE, rep % C_SIZE)


def device(z, y, x, c):
    return (z * Y_SIZE + y, x * C_SIZE + c)


def meet(peers):
    barrier = pltpu.get_barrier_semaphore()
    for peer in peers:
        pl.semaphore_signal(barrier, inc=1, device_id=peer, device_id_type=MESH_IDS)
    pl.semaphore_wait(barrier, len(peers))


def push(source, target, send, receive, peer):
    return pltpu.make_async_remote_copy(
        src_ref=source,
        dst_ref=target,
        send_sem=send,
        recv_sem=receive,
        device_id=peer,
        device_id_type=MESH_IDS,
    )


GELU_A, GELU_B = 0.79788456, 0.044715
FF_BLOCKS = FF // D
TILE = 256
ROWS = 64


def centre(values):
    centered = values - jnp.mean(values, axis=-1, keepdims=True)
    inverse = lax.rsqrt(jnp.mean(centered * centered, axis=-1, keepdims=True) + EPS_NORM)
    return centered * inverse, inverse


def dot_nn(left, right):
    return lax.dot_general(left, right, (((1,), (0,)), ((), ())), preferred_element_type=jnp.float32)


def dot_nt(left, right):
    return lax.dot_general(left, right, (((1,), (1,)), ((), ())), preferred_element_type=jnp.float32)


def dot_tn(left, right):
    return lax.dot_general(left, right, (((0,), (0,)), ((), ())), preferred_element_type=jnp.float32)


def each(count, body):
    if count <= 3:
        for i in range(count):
            body(i)
        return
    lax.fori_loop(0, count, lambda i, carry: (body(i), carry)[1], 0)


def row_blocks(tokens, body, step=ROWS):
    each(tokens // step, lambda i: body(pl.ds(pl.multiple_of(i * step, step), step), i // (GRID * GRID // step)))


def modulate(source, mods, shift, scale, target, tokens):
    def body(rows, image):
        normed, _ = centre(source[rows])
        target[rows] = (normed * (1.0 + mods[image, scale]) + mods[image, shift]).astype(jnp.bfloat16)

    row_blocks(tokens, body)


def block_at(i, size):
    return pl.ds(i * size if isinstance(i, int) else pl.multiple_of(i * size, size), size)


def columns(i):
    return block_at(i, TILE)


def head_lanes(head):
    lane = lax.broadcasted_iota(jnp.int32, (GRID * GRID, 2 * D // HEADS), 1)
    return lane // (D // HEADS) == head


def softmax(query, keys):
    scores = dot_nt(query, keys) * (1.0 / math.sqrt(D // HEADS))
    powers = jnp.exp(scores - jnp.max(scores, axis=-1, keepdims=True))
    return powers * (1.0 / jnp.sum(powers, axis=-1, keepdims=True))


def pick(lanes, values):
    return jnp.where(lanes, values, jnp.zeros_like(values))


def attention_forward(projected, attended, images, first_pair, pairs):
    size, width = GRID * GRID, 2 * D // HEADS

    def body(i, image):
        rows, lanes = block_at(image, size), block_at(first_pair + i, width)
        query, keys, values = (projected[p, rows, lanes] for p in range(3))
        first = head_lanes(0)
        outs = []
        for own in (first, jnp.logical_not(first)):
            weights = softmax(pick(own, query), keys).astype(jnp.bfloat16)
            outs.append(dot_nn(weights, values))
        attended[rows, lanes] = jnp.where(first, outs[0], outs[1]).astype(jnp.bfloat16)

    each(pairs, lambda i: [body(i, image) for image in range(images)])


def attention_backward(projected, grad_attended, grad_projected, image, first_pair, pairs):
    size, width = GRID * GRID, 2 * D // HEADS
    scaling = 1.0 / math.sqrt(D // HEADS)

    def body(i):
        rows, lanes = block_at(image, size), block_at(first_pair + i, width)
        query, keys, values = (projected[p, rows, lanes] for p in range(3))
        grad_out = grad_attended[rows, lanes]
        first = head_lanes(0)
        outs = []
        for own in (first, jnp.logical_not(first)):
            weights = softmax(pick(own, query), keys)
            grad_values = dot_tn(weights.astype(jnp.bfloat16), grad_out)
            grad_weights = dot_nt(pick(own, grad_out), values)
            inner = jnp.sum(weights * grad_weights, axis=-1, keepdims=True)
            grad_scores = (weights * (grad_weights - inner)).astype(jnp.bfloat16)
            outs.append(
                (dot_nn(grad_scores, keys) * scaling, dot_tn(grad_scores, query) * scaling, grad_values)
            )
        for p in range(3):
            grad_projected[p, rows, lanes] = jnp.where(first, outs[0][p], outs[1][p]).astype(jnp.bfloat16)

    each(pairs, body)


def whole(block):
    return block.reshape(D, block.shape[-1])


class Pace:
    RATE = 48e3
    LATENCY = 2.2

    def __init__(self):
        self.now = 0.0
        self.free = {}
        self.entries = []

    def send(self, link, count):
        rate = 10 * self.RATE if link == "c" else self.RATE
        self.free[link] = max(self.now, self.free.get(link, 0.0)) + count / rate
        return self.free[link] + self.LATENCY

    def add(self, ready, run):
        self.entries.append([ready, len(self.entries), run])

    def serve(self, entry):
        cost, ready = entry[2]()
        self.now += cost
        if ready is None:
            self.entries.remove(entry)
        else:
            entry[0] = ready

    def spend(self, cost):
        self.now += cost
        while self.entries:
            entry = min(self.entries, key=lambda e: e[:2])
            if entry[0] > self.now:
                return
            self.serve(entry)

    def next(self):
        entry = min(self.entries, key=lambda e: e[:2])
        self.now = max(self.now, entry[0])
        self.serve(entry)

    def until(self, done):
        while not done():
            self.next()

    def drain(self):
        while self.entries:
            self.next()


class Gather:
    def __init__(self, pace, groups, spot, packed, full, semaphores, prepare, loads):
        self.pace, self.groups, self.spot = pace, groups, spot
        self.packed = packed
        layers, owners, height, width = full.shape
        self.full = full.reshape(layers, Z_SIZE, Y_SIZE, height, width)
        self.sems, self.prepare, self.loads = semaphores, prepare, loads
        z, y, x, c = spot
        self.z_peers = [device((z + k) % Z_SIZE, y, x, c) for k in range(1, Z_SIZE)]
        self.across_y, self.across_x = device(z, 1 - y, x, c), device(z, y, 1 - x, c)
        self.sibling = device(z, y, x, 1 - c)
        self.done, self.copies, self.keeps = set(), [], {}
        self.waiting = list(range(len(groups)))

    def rows(self, group, third, count, core):
        _, first, size = self.groups[group]
        step = size // 6
        return pl.ds(pl.multiple_of(first + core * 3 * step + third * step, 16), count * step)

    def size(self, group, count):
        return self.groups[group][2] // 6 * count * D * 2

    def sem(self, name, group, *index):
        send, receive = self.sems[name]
        return send.at[(group,) + index], receive.at[(group,) + index]

    def go(self, source, target, sems, peer):
        copy = push(source, target, sems[0], sems[1], peer)
        copy.start()
        self.copies.append(copy)

    def arrive(self, ref, sems):
        push(ref, ref, sems[0], sems[1], self.across_y).wait_recv()

    def start(self):
        z, y, x, c = self.spot
        group = self.waiting.pop(0)
        layer = self.groups[group][0]
        self.prepare(group)
        own = self.packed.at[layer, self.rows(group, x, 2, c)]
        target = self.full.at[layer, z, y, self.rows(group, x, 2, c)]
        for k in range(1, Z_SIZE):
            self.go(own, target, self.sem("z", group, k - 1), self.z_peers[k - 1])
        keep = pltpu.make_async_copy(own, target, self.sems["keep"].at[group])
        keep.start()
        self.keeps[group] = keep
        stages = [self.on_z, self.on_y, self.on_x, self.on_c]
        self.pace.add(
            self.pace.send("z", 4 * self.size(group, 2)), lambda: (0.6, stages.pop(0)(group, layer))
        )
        return 1.4, self.pace.free["z"] - 9.0 if self.waiting else None

    def on_z(self, group, layer):
        z, y, x, c = self.spot
        self.keeps[group].wait()
        both, third = self.rows(group, x, 2, c), self.rows(group, 2 * x, 1, c)
        for k in range(1, Z_SIZE):
            self.arrive(self.full.at[layer, (z - k) % Z_SIZE, y, both], self.sem("z", group, k - 1))
        ref = self.full.at[layer, :, y, both]
        self.go(ref, ref, self.sem("y", group), self.across_y)
        part = self.full.at[layer, :, y, third]
        self.go(part, part, self.sem("x", group, 0), self.across_x)
        self.go(ref, ref, self.sem("c", group, 0), self.sibling)
        self.x_ready = self.pace.send("x", 4 * self.size(group, 1))
        return self.pace.send("y", 4 * self.size(group, 2))

    def on_y(self, group, layer):
        z, y, x, c = self.spot
        ref = self.full.at[layer, :, 1 - y, self.rows(group, x, 2, c)]
        self.arrive(ref, self.sem("y", group))
        part = self.full.at[layer, :, 1 - y, self.rows(group, 2 * x, 1, c)]
        self.go(part, part, self.sem("x", group, 1), self.across_x)
        self.go(ref, ref, self.sem("c", group, 1), self.sibling)
        return self.pace.send("x", 4 * self.size(group, 1))

    def on_x(self, group, layer):
        z, y, x, c = self.spot
        third = self.rows(group, 2 - 2 * x, 1, c)
        for k, side in enumerate((y, 1 - y)):
            self.arrive(self.full.at[layer, :, side, third], self.sem("x", group, k))
        ref = self.full.at[layer, :, :, third]
        self.go(ref, ref, self.sem("c", group, 2), self.sibling)
        return self.pace.send("c", 8 * self.size(group, 1))

    def on_c(self, group, layer):
        z, y, x, c = self.spot
        for k, side in enumerate((y, 1 - y)):
            self.arrive(self.full.at[layer, :, side, self.rows(group, x, 2, 1 - c)], self.sem("c", group, k))
        third = self.rows(group, 2 - 2 * x, 1, 1 - c)
        self.arrive(self.full.at[layer, :, :, third], self.sem("c", group, 2))
        self.done.add(group)
        self.loads(group)
        return None

    def finish(self):
        for copy in self.copies:
            copy.wait_send()


def silu(values):
    return values / (1.0 + jnp.exp(-values))


def conditions(ids, time1_w, time1_b, time2_w, time2_b, class_tab, hidden_t, condition):
    rows, half = ids.shape[0], FREQ // 2
    k = lax.broadcasted_iota(jnp.int32, (1, half), 1).astype(jnp.float32)
    angles = ids[:, 0:1] * jnp.exp(-math.log(10000.0) * k / half)
    features = jnp.concatenate([jnp.cos(angles), jnp.sin(angles)], axis=1).astype(jnp.bfloat16)
    hidden = dot_nn(features, time1_w[...]) + time1_b
    hidden_t[...] = hidden
    chosen = jnp.where(ids[:, 2:3] == 1.0, float(CLASSES), ids[:, 1:2])
    lane = lax.broadcasted_iota(jnp.int32, (rows, class_tab.shape[0]), 1).astype(jnp.float32)
    picked = jnp.dot(
        (lane == chosen).astype(jnp.float32), class_tab, precision=HIGHEST, preferred_element_type=jnp.float32
    )
    condition[...] = dot_nn(silu(hidden).astype(jnp.bfloat16), time2_w[...]) + time2_b + picked


def forward_kernel(
    groups, places_of, picked, places, ids, w_qkv, w_proj, w_fc1, w_fc2, w_mod, small, biases,
    out, full, mods, ids_all, hidden_t, condition, x_h, proj_h, att_h, branch_a_h, middle_h, branch_b_h,
    w_in, w_out, x_v, proj_v, att_v, branch_a, middle, branch_b, mixed, active,
    mod_part, mod_y, mod_z, packed, raw, time1_w, time2_w, raw_sem, out_sem,
    w_sem, save_sem, i_s, i_r, z_s, z_r, y_s, y_r, x_s, x_r, c_s, c_r, keep_sem, my_s, my_r, mz_s, mz_r,
):
    tokens = picked.shape[0]
    images, entries = mods.shape[:2]
    shard, deep = w_in.shape[3], w_out.shape[3]
    ways = D // LANES
    count = 4 + FF_BLOCKS
    spot = place()
    z, y, x, c = spot
    dps, reps = Z_SIZE * Y_SIZE, X_SIZE * C_SIZE
    dp, rep = z * Y_SIZE + y, x * C_SIZE + c
    pace = Pace()

    def load(layer, index):
        if index < count:
            return pltpu.make_async_copy(
                full.at[layer, :, pl.ds(index * shard, shard)], w_in.at[layer, index], w_sem.at[layer, index]
            )
        block = index - count
        per = D // deep
        return pltpu.make_async_copy(
            full.at[layer, pl.ds(block * per, per), pl.ds(count * shard, deep)],
            w_out.at[layer, block],
            w_sem.at[layer, index],
        )

    def loads(group):
        layer, first, size = groups[group]
        for index in range(count):
            if first <= index * shard < first + size:
                load(layer, index).start()
        ends = {g for g, (at, begin, _) in enumerate(groups) if at == layer and begin >= count * shard}
        if group in ends and ends <= gather.done:
            for block in range(FF_BLOCKS):
                load(layer, count + block).start()

    def square(layer, index):
        if index < 3:
            return w_qkv.at[layer, :, pl.ds(index * D, D)]
        if index == 3:
            return w_proj.at[layer]
        if index < count:
            return w_fc1.at[layer, :, pl.ds((index - 4) * D, D)]
        return w_fc2.at[layer, pl.ds((index - count) * shard, shard)]

    def fetch(group):
        if group < len(groups):
            layer, first, size = groups[group]
            slot = group % raw.shape[0]
            for k in range(size // shard):
                pltpu.make_async_copy(square(layer, first // shard + k), raw.at[slot, k], raw_sem.at[slot, k]).start()

    def prepare(group):
        layer, first, size = groups[group]
        slot = group % raw.shape[0]
        for k in range(size // shard):
            pltpu.make_async_copy(square(layer, first // shard + k), raw.at[slot, k], raw_sem.at[slot, k]).wait()
            packed[layer, pl.ds(first + k * shard, shard)] = raw[slot, k].astype(jnp.bfloat16)
        fetch(group + raw.shape[0])

    gather = Gather(
        pace, groups, spot, packed, full,
        {"z": (z_s, z_r), "y": (y_s, y_r), "x": (x_s, x_r), "c": (c_s, c_r), "keep": keep_sem}, prepare, loads,
    )
    for group in range(raw.shape[0]):
        fetch(group)

    def rows_of(name, k, first=0, size=None):
        at, height = places_of[name]
        return small[pl.ds((at + first) * ways + k, size or height, stride=ways)]

    def piece(name):
        return jnp.concatenate([rows_of(name, k) for k in range(ways)], axis=1)
    offsets = [(i, j) for i in range(dps) for j in range(reps) if i or j]
    everyone = [((dp + i) % dps, (rep + j) % reps) for i, j in offsets]
    meet(everyone)
    mine = dp * reps + rep
    id_copies = [push(ids, ids_all.at[mine], i_s.at[n], i_r.at[n], peer) for n, peer in enumerate(everyone)]
    for copy in id_copies:
        copy.start()
    ids_all[mine] = ids[...]
    ready = []

    def mods_start():
        for copy in id_copies:
            copy.wait_recv()
        for k in range(ways):
            lanes = pl.ds(k * LANES, LANES)
            time1_w[:, lanes] = rows_of("time1_w", k).astype(jnp.bfloat16)
            time2_w[:, lanes] = rows_of("time2_w", k).astype(jnp.bfloat16)
        conditions(
            ids_all[...].reshape(dps * reps * 8, LANES), time1_w, piece("time1_b"), time2_w, piece("time2_b"),
            piece("class_tab"), hidden_t, condition,
        )
        chosen = [condition[pl.ds(pl.multiple_of((d * reps + rep) * 8, 8), 8)] for d in range(dps)]
        group_c = silu(jnp.concatenate(chosen, axis=0)).astype(jnp.bfloat16)
        rows_mod = w_mod.shape[0]
        entry = lax.broadcasted_iota(jnp.int32, (D, rows_mod), 0)
        lane = lax.broadcasted_iota(jnp.int32, (D, rows_mod), 1)
        select = (entry == lane + dp * rows_mod).astype(jnp.bfloat16)
        own = dot_nn(group_c, select).astype(jnp.bfloat16)
        for k in range(entries):
            value = dot_nn(own, w_mod[:, k * D : (k + 1) * D].astype(jnp.bfloat16))
            for d in range(dps):
                for image in range(images):
                    row = 8 * d + image
                    mod_part[d // Y_SIZE, d % Y_SIZE, pl.ds(image * entries + k, 1)] = value[row : row + 1]
        gather.go(mod_part.at[:, 1 - y], mod_y, (my_s, my_r), gather.across_y)
        return 9.0, pace.send("y", 4 * mod_part.shape[2] * D * 4)

    def mods_across():
        gather.arrive(mod_y, (my_s, my_r))
        for k in range(Z_SIZE):
            mod_y[k] = mod_y[k] + mod_part[k, y]
        for k in range(1, Z_SIZE):
            peer = (z + k) % Z_SIZE
            gather.go(mod_y.at[peer], mod_z.at[z], (mz_s.at[k - 1], mz_r.at[k - 1]), gather.z_peers[k - 1])
        return 1.5, pace.send("z", 4 * mod_part.shape[2] * D * 4)

    def mods_end():
        mod_z[z] = mod_y[z]
        for k in range(1, Z_SIZE):
            gather.arrive(mod_z.at[(z - k) % Z_SIZE], (mz_s.at[k - 1], mz_r.at[k - 1]))
        value = (mod_z[0] + mod_z[1]) + (mod_z[2] + mod_z[3])
        shift = piece("mod_b")
        for image in range(images):
            for k in range(entries):
                row = image * entries + k
                mods[image, k] = value[row : row + 1] + shift[k : k + 1]
        ready.append(True)
        return 1.0, None

    steps = [mods_start, mods_across, mods_end]
    pace.now = 8.0
    for _ in range(2):
        gather.start()
    pace.add(pace.now + 3.0, lambda: steps.pop(0)())
    pace.add(pace.free["z"] - 9.0, gather.start)

    def need(layer, which):
        index = min(which, count)
        last = (index if index < count else count + deep // shard - 1) * shard
        first = min(last, index * shard)
        wanted = {
            g for g, (at, begin, size) in enumerate(groups) if at == layer and first < begin + size and begin <= last
        }
        pace.until(lambda: wanted <= gather.done)
        load(layer, which).wait()

    patch_w = piece("patch_w").astype(jnp.bfloat16)
    strip = PDIM // PATCH
    weights = jnp.concatenate([patch_w[u * strip : (u + 1) * strip] for u in range(PATCH) for _ in range(GRID)], axis=0)
    shift = piece("patch_b")
    for image in range(images):
        rows = pl.ds(image * GRID * GRID, GRID * GRID)
        x_v[rows] = dot_nn(picked[rows], weights) + shift + places[...]
    pace.spend(1.5)
    saves = {}

    def save(layer, source, target, index):
        copy = pltpu.make_async_copy(source, target.at[layer], save_sem.at[layer, index])
        copy.start()
        saves[index] = copy

    def reuse(index):
        copy = saves.pop(index, None)
        if copy is not None:
            copy.wait()

    for layer in range(LAYERS):
        base = 6 * layer
        save(layer, x_v, x_h, 0)
        pace.until(lambda: ready)
        modulate(x_v, mods, base, base + 1, mixed, tokens)
        pace.spend(1.0)
        reuse(1)
        for p in range(3):
            need(layer, p)

            def project(i, p=p, layer=layer):
                value = dot_nn(mixed[...], whole(w_in[layer, p, :, :, columns(i)]))
                if p != 1:
                    value = value + biases[layer, p // 2, :, columns(i)]
                proj_v[p, :, columns(i)] = value.astype(jnp.bfloat16)

            each(D // TILE, project)
            pace.spend(1.1)
        save(layer, proj_v, proj_h, 1)
        reuse(2)
        for pair in range(0, HEADS // 2, 2):
            attention_forward(proj_v, att_v, images, pair, 2)
            pace.spend(2.3)
        save(layer, att_v, att_h, 2)
        reuse(3)
        reuse(4)
        need(layer, 3)

        def first_branch(i, layer=layer, base=base):
            value = dot_nn(att_v[...], whole(w_in[layer, 3, :, :, columns(i)]))
            value = value + biases[layer, 2, :, columns(i)]
            branch_a[:, columns(i)] = value
            for image in range(images):
                rows = pl.ds(image * GRID * GRID, GRID * GRID)
                part = value[image * GRID * GRID : (image + 1) * GRID * GRID]
                middle[rows, columns(i)] = x_v[rows, columns(i)] + mods[image, base + 2, :, columns(i)] * part

        each(D // TILE, first_branch)
        save(layer, branch_a, branch_a_h, 3)
        save(layer, middle, middle_h, 4)
        modulate(middle, mods, base + 3, base + 4, mixed, tokens)
        pace.spend(2.3)
        for block in range(FF_BLOCKS):
            need(layer, 4 + block)

            def expand(i, block=block, layer=layer):
                hidden = dot_nn(mixed[...], whole(w_in[layer, 4 + block, :, :, columns(i)]))
                hidden = hidden + biases[layer, 3 + block, :, columns(i)]
                inner = jnp.tanh(GELU_A * (hidden + GELU_B * hidden * hidden * hidden))
                active[block, :, columns(i)] = (0.5 * hidden * (1.0 + inner)).astype(jnp.bfloat16)

            each(D // TILE, expand)
            pace.spend(2.2)
        reuse(5)
        for block in range(FF_BLOCKS):
            need(layer, count + block)

            def contract(i, block=block, layer=layer):
                value = dot_nn(active[block], whole(w_out[layer, block, :, :, columns(i)]))
                if block == 0:
                    branch_b[:, columns(i)] = value + biases[layer, 3 + FF_BLOCKS, :, columns(i)]
                else:
                    branch_b[:, columns(i)] += value

            each(D // TILE, contract)
            pace.spend(1.1)
        save(layer, branch_b, branch_b_h, 5)
        reuse(0)

        def finish(rows, image, base=base):
            x_v[rows] = middle[rows] + mods[image, base + 5] * branch_b[rows]

        row_blocks(tokens, finish)
        pace.spend(1.0)
    last = pltpu.make_async_copy(x_v, out, out_sem)
    last.start()
    pace.drain()
    for copy in saves.values():
        copy.wait()
    last.wait()
    gather.finish()
    for copy in id_copies:
        copy.wait_send()


def run_forward(picked, places, ids, w_qkv, w_proj, w_fc1, w_fc2, w_mod, small, places_of, biases, images):
    tokens = picked.shape[0]
    layers = w_qkv.shape[0]
    owners, everyone = Z_SIZE * Y_SIZE, Z_SIZE * Y_SIZE * X_SIZE * C_SIZE
    shard, deep = D // owners, FF // owners
    height, width = (4 + FF_BLOCKS) * shard + deep, D
    wide, low = jnp.float32, jnp.bfloat16
    entries = MOD // D
    mod_rows = -(-images * entries // 8) * 8
    keep = [
        ((tokens, D), wide), ((3, tokens, D), low), ((tokens, D), low),
        ((tokens, D), wide), ((tokens, D), wide), ((tokens, D), wide),
    ]
    groups = [(layer, first, 2 * shard) for layer in range(layers) for first in range(0, height, 2 * shard)]
    number = len(groups)
    dma = pltpu.SemaphoreType.DMA
    vmem, anywhere = pl.BlockSpec(memory_space=pltpu.VMEM), pl.BlockSpec(memory_space=pl.ANY)
    outs = [
        jax.ShapeDtypeStruct((tokens, D), wide),
        jax.ShapeDtypeStruct((layers, owners, height, width), low),
        jax.ShapeDtypeStruct((images, entries, 1, D), wide),
        jax.ShapeDtypeStruct((everyone,) + ids.shape, wide),
        jax.ShapeDtypeStruct((everyone * ids.shape[0], D), wide),
        jax.ShapeDtypeStruct((everyone * ids.shape[0], D), wide),
    ]
    return pl.pallas_call(
        partial(forward_kernel, groups, places_of),
        out_shape=outs + [jax.ShapeDtypeStruct((layers,) + shape, kind) for shape, kind in keep],
        in_specs=[vmem] * 3 + [anywhere] * 4 + [vmem] * 3,
        out_specs=[anywhere, anywhere, vmem, vmem, vmem, vmem] + [anywhere] * len(keep),
        scratch_shapes=[
            pltpu.VMEM((layers, 4 + FF_BLOCKS, owners, shard, D), low),
            pltpu.VMEM((layers, FF_BLOCKS, D // deep, deep, D), low),
        ]
        + [pltpu.VMEM(shape, kind) for shape, kind in keep]
        + [
            pltpu.VMEM((tokens, D), low),
            pltpu.VMEM((FF_BLOCKS, tokens, D), low),
            pltpu.VMEM((Z_SIZE, Y_SIZE, mod_rows, D), wide),
            pltpu.VMEM((Z_SIZE, mod_rows, D), wide),
            pltpu.VMEM((Z_SIZE, mod_rows, D), wide),
            pltpu.VMEM((layers, height, width), low),
            pltpu.VMEM((3, 2, shard, D), wide),
            pltpu.VMEM((FREQ, D), low),
            pltpu.VMEM((D, D), low),
            dma((3, 2)),
            dma,
            dma((layers, 4 + 2 * FF_BLOCKS)),
            dma((layers, len(keep))),
            dma((everyone - 1,)),
            dma((everyone - 1,)),
            dma((number, Z_SIZE - 1)),
            dma((number, Z_SIZE - 1)),
            dma((number,)),
            dma((number,)),
            dma((number, 2)),
            dma((number, 2)),
            dma((number, 3)),
            dma((number, 3)),
            dma((number,)),
            dma,
            dma,
            dma((Z_SIZE - 1,)),
            dma((Z_SIZE - 1,)),
        ],
        compiler_params=pltpu.CompilerParams(
            collective_id=2, has_side_effects=True, vmem_limit_bytes=63 * 2**20
        ),
        name="blocks_forward",
    )(picked, places, ids, w_qkv, w_proj, w_fc1, w_fc2, w_mod, small, biases)


class Reduction:
    COSTS = (0.6, 0.4, 0.8, 0.5, 0.4, 0.1)

    def __init__(self, pace, groups, shard, spot, buffers, semaphores, credits, finals):
        self.pace, self.groups, self.shard, self.spot = pace, groups, shard, spot
        self.held, self.from_c, self.from_x, self.from_y, self.from_z, self.from_fin = buffers
        self.sems, self.credits, self.finals = semaphores, credits, finals
        z, y, x, c = spot
        self.z_peers = [device((z + k) % Z_SIZE, y, x, c) for k in range(1, Z_SIZE)]
        self.z_before = [device((z - k) % Z_SIZE, y, x, c) for k in range(1, Z_SIZE)]
        self.across_y, self.across_x = device(z, 1 - y, x, c), device(z, y, 1 - x, c)
        self.sibling = device(z, y, x, 1 - c)
        self.started, self.kept, self.filled, self.busy = {}, {}, {}, {}
        self.at_half = [first for first, _, _ in groups]
        self.halves = [rows for _, rows, _ in groups]
        self.parts = [part for _, _, part in groups]
        most = [rows - part for _, rows, part in groups]
        self.at_part = [sum(self.parts[:g]) for g in range(len(groups))]
        self.at_most = [sum(most[:g]) for g in range(len(groups))]

    def peers(self):
        return self.z_peers + [self.across_y, self.across_x, self.sibling]

    def go(self, key, source, target, sems, peer):
        copy = push(source, target, sems[0], sems[1], peer)
        copy.start()
        self.started.setdefault(key, []).append(copy)

    def arrive(self, ref, sems):
        push(ref, ref, sems[0], sems[1], self.across_y).wait_recv()

    def sem(self, name, layer, *index):
        send, receive = self.sems[name]
        return send.at[(layer,) + index], receive.at[(layer,) + index]

    def give(self, layer, name, peer, *index):
        if layer == LAYERS - 1:
            pl.semaphore_signal(
                self.credits[name].at[index], inc=1, device_id=peer, device_id_type=MESH_IDS
            )

    def take(self, layer, name, *index):
        if layer != LAYERS - 1:
            pl.semaphore_wait(self.credits[name].at[index], 1)

    def put(self, layer, group, stage, first, squares, owner_z, slot):
        c = self.spot[3]
        half = self.shard // 2
        if (layer, group) not in self.filled:
            while (layer + 1, group) in self.busy:
                self.pace.spend(0.5)
            for copy in self.started.pop((layer + 1, group), []):
                copy.wait_send()
            self.take(layer, "c", group)
            self.filled[layer, group] = []
        rows = pl.ds(first, squares * half)
        theirs = stage.at[:, :, :, pl.ds(pl.multiple_of((1 - c) * half, 16), half)]
        ours = stage.at[:, :, :, pl.ds(pl.multiple_of(c * half, 16), half)]
        zs = stage.shape[0]

        def view(ref):
            pieces = ref.reshape(Z_SIZE, Y_SIZE, ref.shape[2] // half, half, D)
            return pieces.at[pl.ds(owner_z, zs), :, pl.ds(first // half, squares)]

        sems = self.sem("c", layer, group, slot)
        send = push(theirs, view(self.from_c), sems[0], sems[1], self.sibling)
        keep = pltpu.make_async_copy(ours, view(self.held), self.sems["keep"].at[layer, group, slot])
        send.start()
        keep.start()
        self.filled[layer, group].append((slot, owner_z, zs, rows))
        self.kept[layer, group, slot] = keep
        self.ready = self.pace.send("c", zs * Y_SIZE * squares * half * D * 2)

        def free():
            send.wait_send()
            self.keep_wait(layer, group, slot)

        return free

    def begin(self, layer, group):
        stages = [self.on_c, self.on_x, self.on_y, self.on_z, self.on_fin, self.on_last]
        costs = list(self.COSTS)
        self.busy[layer, group] = True

        def run():
            ready = stages.pop(0)(layer, group)
            if not stages:
                del self.busy[layer, group]
            return costs.pop(0), ready

        self.pace.add(self.ready, run)

    def keep_wait(self, *key):
        keep = self.kept.pop(key, None)
        if keep is not None:
            keep.wait()

    def add(self, target, extra):
        def body(owner):
            total = target[owner].astype(jnp.float32) + extra[owner].astype(jnp.float32)
            target[owner] = total.astype(jnp.bfloat16)

        each(Z_SIZE, body)

    def on_c(self, layer, group):
        z, y, x, c = self.spot
        half, part = self.halves[group], self.parts[group]
        first = self.at_half[group]
        for slot, owner_z, zs, rows in self.filled[layer, group]:
            self.keep_wait(layer, group, slot)
            self.arrive(self.from_c.at[pl.ds(owner_z, zs), :, rows], self.sem("c", layer, group, slot))
        theirs = pl.ds(pl.multiple_of(first + (1 - x) * (half - part), 16), part)
        ours = pl.ds(pl.multiple_of(first + x * part, 16), half - part)
        for side in range(Y_SIZE):
            self.add(self.held.at[:, side, theirs], self.from_c.at[:, side, theirs])
        target = self.from_x.at[:, :, pl.ds(self.at_part[group], part)]
        self.take(layer, "x", group)
        self.go((layer, group), self.held.at[:, :, theirs], target, self.sem("x", layer, group), self.across_x)
        for side in range(Y_SIZE):
            self.add(self.held.at[:, side, ours], self.from_c.at[:, side, ours])
        self.give(layer, "c", self.sibling, group)
        return self.pace.send("x", 8 * part * D * 2)

    def on_x(self, layer, group):
        z, y, x, c = self.spot
        half, part = self.halves[group], self.parts[group]
        first = self.at_half[group]
        got = self.from_x.at[:, :, pl.ds(self.at_part[group], part)]
        self.arrive(got, self.sem("x", layer, group))
        ours = pl.ds(pl.multiple_of(first + x * (half - part), 16), part)
        for side in (1 - y, y):
            self.add(self.held.at[:, side, ours], self.from_x.at[:, side, pl.ds(self.at_part[group], part)])
        self.give(layer, "x", self.across_x, group)
        most = pl.ds(pl.multiple_of(first + x * part, 16), half - part)
        self.take(layer, "y", group)
        self.go(
            (layer, group), self.held.at[:, 1 - y, most], self.from_y.at[:, pl.ds(self.at_most[group], half - part)],
            self.sem("y", layer, group), self.across_y,
        )
        return self.pace.send("y", 4 * (half - part) * D * 2)

    def on_y(self, layer, group):
        z, y, x, c = self.spot
        half, part = self.halves[group], self.parts[group]
        got = self.from_y.at[:, pl.ds(self.at_most[group], half - part)]
        self.arrive(got, self.sem("y", layer, group))
        most = pl.ds(pl.multiple_of(self.at_half[group] + x * part, 16), half - part)
        self.add(self.held.at[:, y, most], got)
        self.give(layer, "y", self.across_y, group)
        for k in range(1, Z_SIZE):
            self.take(layer, "z", group, k - 1)
            self.go(
                (layer, group), self.held.at[(z + k) % Z_SIZE, y, most],
                self.from_z.at[k - 1, pl.ds(self.at_most[group], half - part)],
                self.sem("z", layer, group, k - 1), self.z_peers[k - 1],
            )
        return self.pace.send("z", 4 * (half - part) * D * 2)

    def on_z(self, layer, group):
        z, y, x, c = self.spot
        half, part = self.halves[group], self.parts[group]
        most = pl.ds(pl.multiple_of(self.at_half[group] + x * part, 16), half - part)
        got = pl.ds(self.at_most[group], half - part)
        for k in range(1, Z_SIZE):
            self.arrive(self.from_z.at[k - 1, got], self.sem("z", layer, group, k - 1))
        total = self.held[z, y, most].astype(jnp.float32)
        for k in range(1, Z_SIZE):
            total = total + self.from_z[k - 1, got].astype(jnp.float32)
        self.held[z, y, most] = total.astype(jnp.bfloat16)
        for k in range(1, Z_SIZE):
            self.give(layer, "z", self.z_before[k - 1], group, k - 1)
        self.take(layer, "e", group)
        self.go((layer, group), self.held.at[z, y, most], self.from_fin.at[got], self.sem("e", layer, group), self.across_x)
        return self.pace.send("x", (half - part) * D * 2)

    def on_fin(self, layer, group):
        z, y, x, c = self.spot
        half, part = self.halves[group], self.parts[group]
        middle = half - 2 * part
        base, start = self.at_most[group], self.at_half[group]
        self.arrive(self.from_fin.at[pl.ds(base, half - part)], self.sem("e", layer, group))
        wide = jnp.float32

        def span(begin, size):
            return pl.ds(pl.multiple_of(begin, 16), size)

        ours, theirs = span(start + x * (half - part), part), span(start + (1 - x) * (half - part), part)
        both = span(start + part, middle)
        self.finals[layer, c, ours] = self.held[z, y, ours].astype(wide)
        self.finals[layer, c, theirs] = self.from_fin[span(base + (1 - x) * middle, part)].astype(wide)
        self.finals[layer, c, both] = self.held[z, y, both].astype(wide) + self.from_fin[
            span(base + x * part, middle)
        ].astype(wide)
        self.give(layer, "e", self.across_x, group)
        ref = self.finals.at[layer, c, pl.ds(start, half)]
        self.go((layer, group), ref, ref, self.sem("f", layer, group), self.sibling)
        return self.pace.send("c", half * D * 4)

    def on_last(self, layer, group):
        c = self.spot[3]
        ref = self.finals.at[layer, 1 - c, pl.ds(self.at_half[group], self.halves[group])]
        self.arrive(ref, self.sem("f", layer, group))
        return None

    def finish(self):
        for copies in self.started.values():
            for copy in copies:
                copy.wait_send()


class Sums:
    def __init__(self, reduction, own, total, small_c, small_x, small_y, small_z, mods, mods_all, sems, mod_sems, local):
        self.r = reduction
        self.own, self.total = own, total
        self.small_c, self.small_x, self.small_y, self.small_z = small_c, small_x, small_y, small_z
        self.mods, self.mods_all, self.v, self.m, self.local = mods, mods_all, sems, mod_sems, local
        self.stages = [self.first, self.to_x, self.to_y, self.to_z, self.to_c, self.last]

    def sem(self, pair, index):
        return pair[0].at[index], pair[1].at[index]

    def go(self, ref, target, pair, index, peer):
        self.r.go("sums", ref, target, self.sem(pair, index), peer)

    def arrive(self, ref, pair, index):
        self.r.arrive(ref, self.sem(pair, index))

    def run(self):
        self.stages.pop(0)()
        return 1.0, self.r.pace.now + 7.0 if self.stages else None

    def halves(self):
        span = self.small_c.shape[0]
        c = self.r.spot[3]
        return [pl.ds(pl.multiple_of(i * span, 8), span) for i in (c, 1 - c)]

    def first(self):
        z, y, x, c = self.r.spot
        mine, other = self.halves()
        self.go(self.own.at[other], self.small_c, self.v, 0, self.r.sibling)
        own = self.mods_all.at[z, y, x * C_SIZE + c]
        keep = pltpu.make_async_copy(self.mods, own, self.local)
        keep.start()
        for k in range(1, Z_SIZE):
            self.go(self.mods, own, self.m, k - 1, self.r.z_peers[k - 1])
        keep.wait()

    def to_x(self):
        z, y, x, c = self.r.spot
        mine, other = self.halves()
        self.arrive(self.small_c, self.v, 0)
        self.small_c[...] = self.small_c[...] + self.own[mine]
        self.go(self.small_c, self.small_x, self.v, 1, self.r.across_x)
        slot = x * C_SIZE + c
        for k in range(1, Z_SIZE):
            self.arrive(self.mods_all.at[(z - k) % Z_SIZE, y, slot], self.m, k - 1)
        ref = self.mods_all.at[:, y, slot]
        self.go(ref, ref, self.m, 3, self.r.across_y)

    def to_y(self):
        z, y, x, c = self.r.spot
        self.arrive(self.small_x, self.v, 1)
        self.small_x[...] = self.small_x[...] + self.small_c[...]
        self.go(self.small_x, self.small_y, self.v, 2, self.r.across_y)
        slot = x * C_SIZE + c
        self.arrive(self.mods_all.at[:, 1 - y, slot], self.m, 3)
        ref = self.mods_all.at[:, :, slot]
        self.go(ref, ref, self.m, 4, self.r.across_x)

    def to_z(self):
        z, y, x, c = self.r.spot
        self.arrive(self.small_y, self.v, 2)
        self.small_z[z] = self.small_y[...] + self.small_x[...]
        own = self.small_z.at[z]
        for k in range(1, Z_SIZE):
            self.go(own, own, self.v, 2 + k, self.r.z_peers[k - 1])
        self.arrive(self.mods_all.at[:, :, (1 - x) * C_SIZE + c], self.m, 4)
        for k in range(X_SIZE):
            ref = self.mods_all.at[:, :, k * C_SIZE + c]
            self.go(ref, ref, self.m, 5 + k, self.r.sibling)

    def to_c(self):
        z, y, x, c = self.r.spot
        mine, other = self.halves()
        for k in range(1, Z_SIZE):
            self.arrive(self.small_z.at[(z - k) % Z_SIZE], self.v, 2 + k)
        self.total[mine] = (self.small_z[0] + self.small_z[1]) + (self.small_z[2] + self.small_z[3])
        self.go(self.total.at[mine], self.total.at[mine], self.v, 6, self.r.sibling)
        for k in range(X_SIZE):
            self.arrive(self.mods_all.at[:, :, k * C_SIZE + 1 - c], self.m, 5 + k)

    def last(self):
        mine, other = self.halves()
        self.arrive(self.total.at[other], self.v, 6)


def backward_kernel(
    groups, count_all, x_last, mods, biases, picked, wanted, head_w, head_b, full,
    x_h, proj_h, att_h, branch_a_h, middle_h, branch_b_h,
    finals, mods_all, sums_out,
    w_v, grad_x, x_v, proj_v, att_v, branch, middle, mixed, grad_b, active, grad_hidden, grad_mixed,
    grad_projected, stage, mods_acc, mods_tile, mods_low, sums,
    held, from_c, from_x, from_y, from_z, from_fin, small_c, small_x, small_y, small_z,
    w_sem, load_sem, last_sem, keep_sem, c_s, c_r, x_s, x_r, y_s, y_r, z_s, z_r, e_s, e_r, f_s, f_r,
    v_s, v_r, m_s, m_r, local, cred_c, cred_x, cred_y, cred_z, cred_e,
):
    tokens = x_last.shape[0]
    images = mods.shape[0]
    owners = full.shape[1]
    shard, deep = D // owners, FF // owners
    count = 4 + FF_BLOCKS
    per = D // deep
    slots = w_v.shape[0]
    spot = place()
    pace = Pace()
    reduction = Reduction(
        pace, groups, shard, spot, (held, from_c, from_x, from_y, from_z, from_fin),
        {"c": (c_s, c_r), "x": (x_s, x_r), "y": (y_s, y_r), "z": (z_s, z_r), "e": (e_s, e_r), "f": (f_s, f_r), "keep": keep_sem},
        {"c": cred_c, "x": cred_x, "y": cred_y, "z": cred_z, "e": cred_e}, finals,
    )
    order = [i for b in range(FF_BLOCKS) for i in (4 + b, count + b)] + [3, 0, 1, 2]
    order = [(layer, index) for layer in reversed(range(LAYERS)) for index in order]

    def load(at):
        layer, index = order[at]
        slot = at % slots
        target = w_v.at[slot]
        if index < count:
            return pltpu.make_async_copy(
                full.at[layer, :, pl.ds(index * shard, shard)], target.reshape(owners, shard, D), w_sem.at[slot]
            )
        return pltpu.make_async_copy(
            full.at[layer, pl.ds((index - count) * per, per), pl.ds(count * shard, deep)],
            target.reshape(per, deep, D),
            w_sem.at[slot],
        )

    def fetch(at):
        if at < len(order):
            load(at).start()

    def weight(at):
        load(at).wait()
        return w_v.at[at % slots]

    def total(values):
        return jnp.sum(values, axis=0, keepdims=True)

    last_copy = pltpu.make_async_copy(x_last, grad_x, last_sem)
    last_copy.start()
    for at in range(slots):
        fetch(at)
    meet(reduction.peers())
    sums[...] = jnp.zeros_like(sums)
    mods_acc[...] = jnp.zeros_like(mods_acc)
    last_copy.wait()
    final = 6 * LAYERS
    modulate(grad_x, mods, final, final + 1, mixed, tokens)
    picks, wide = wanted.shape[1], head_w.shape[1]
    strip = PDIM // PATCH
    pixel = lax.broadcasted_iota(jnp.int32, (picks, wide), 0)
    entry = lax.broadcasted_iota(jnp.int32, (picks, wide), 1)
    select = (entry == pixel // (picks // PATCH) * strip + pixel % strip).astype(jnp.float32)
    target = jnp.dot(wanted[...], select, precision=HIGHEST, preferred_element_type=jnp.float32)
    error = dot_nn(mixed[...], head_w[...]) + head_b[...] - target
    grad_low = (error * (2.0 / count_all)).astype(jnp.bfloat16)
    sums[pl.ds(PDIM, PDIM)] = dot_tn(grad_low, mixed[...])[:PDIM]
    lane = lax.broadcasted_iota(jnp.int32, (1, wide), 1)
    sums[pl.ds(2 * PDIM, 1), pl.ds(0, wide)] = jnp.where(
        lane == PDIM, jnp.sum(error * error), total(grad_low.astype(jnp.float32))
    )
    for i in range(D // TILE):
        grad_mixed[:, columns(i)] = dot_nt(grad_low, head_w[columns(i)])

    def head(rows, image):
        grad = grad_mixed[rows]
        normed, inverse = centre(grad_x[rows])
        mods_acc[image, final] += total(grad)
        mods_acc[image, final + 1] += total(grad * normed)
        grad = grad * (1.0 + mods[image, final + 1])
        grad_x[rows] = inverse * (
            grad - jnp.mean(grad, axis=-1, keepdims=True) - normed * jnp.mean(grad * normed, axis=-1, keepdims=True)
        )

    row_blocks(tokens, head)
    busy = [[], []]
    turn = [0]

    def weight_grad(layer, left, right, index):
        slot = turn[0] % 2
        turn[0] += 1
        for wait in busy[slot]:
            wait()

        def body(i):
            cut = block_at(i, D // 2)
            value = dot_tn(left[:, cut], right[...]).astype(jnp.bfloat16)
            stage[slot, cut] = value

        each(2, body)
        half = shard // 2
        if index < count:
            group = next(g for g, entry in enumerate(groups) if entry[0] <= index * half < entry[0] + entry[1])
            view = stage.at[slot].reshape(Z_SIZE, Y_SIZE, 1, shard, D)
            busy[slot] = [
                reduction.put(layer, group, view, index * half, 1, 0, (index * half - groups[group][0]) // half)
            ]
            if index * half == groups[group][0] + groups[group][1] - half:
                reduction.begin(layer, group)
        else:
            block = index - count
            busy[slot] = []
            for group, (first, rows, _) in enumerate(groups):
                if first >= count * half:
                    squares = rows // half
                    view = stage.at[slot].reshape(1, Y_SIZE, deep // shard, shard, D)
                    view = view.at[:, :, pl.ds((first - count * half) // half, squares)]
                    busy[slot].append(reduction.put(layer, group, view, first, squares, block, block))
                    if block == FF_BLOCKS - 1:
                        reduction.begin(layer, group)
        pace.spend(1.3)

    for layer in reversed(range(LAYERS)):
        base = 6 * layer
        at = (LAYERS - 1 - layer) * (count + FF_BLOCKS)
        bias_row = 3 * PDIM + layer * (4 + FF_BLOCKS)

        def bias_add(k, values, cut=slice(None), bias_row=bias_row):
            sums[pl.ds(bias_row + k, 1), cut] += total(values)

        saved = [
            (branch_b_h, branch), (middle_h, middle), (att_h, att_v), (proj_h, proj_v), (x_h, x_v), (branch_a_h, branch),
        ]
        copies = [
            pltpu.make_async_copy(source.at[layer], target, load_sem.at[i])
            for i, (source, target) in enumerate(saved)
        ]
        for copy in copies[:-1]:
            copy.start()
        copies[0].wait()
        copies[1].wait()

        def enter(rows, image, base=base, bias_add=bias_add):
            grad = grad_x[rows]
            low = (mods[image, base + 5] * grad).astype(jnp.bfloat16)
            grad_b[rows] = low
            bias_add(3 + FF_BLOCKS, low.astype(jnp.float32))
            mods_acc[image, base + 5] += total(grad * branch[rows])
            normed, _ = centre(middle[rows])
            mixed[rows] = (normed * (1.0 + mods[image, base + 4]) + mods[image, base + 3]).astype(jnp.bfloat16)

        row_blocks(tokens, enter)
        pace.spend(1.8)
        copies[-1].start()
        for block in range(FF_BLOCKS):
            w_one, w_two = weight(at), weight(at + 1)

            def expand(i, block=block, w_one=w_one, w_two=w_two, layer=layer, bias_add=bias_add):
                hidden = dot_nn(mixed[...], w_one[:, columns(i)]) + biases[layer, 3 + block, :, columns(i)]
                square = hidden * hidden
                inner = jnp.tanh(GELU_A * (hidden + GELU_B * hidden * square))
                active[:, columns(i)] = (0.5 * hidden * (1.0 + inner)).astype(jnp.bfloat16)
                slope = 0.5 * (1.0 + inner) + 0.5 * hidden * (1.0 - inner * inner) * (
                    GELU_A * (1.0 + 3.0 * GELU_B * square)
                )
                low = (slope * dot_nt(grad_b[...], w_two[columns(i)])).astype(jnp.bfloat16)
                grad_hidden[:, columns(i)] = low
                bias_add(3 + block, low.astype(jnp.float32), columns(i))

            each(D // TILE, expand)
            pace.spend(3.6)
            weight_grad(layer, active, grad_b, count + block)

            def back(i, block=block, w_one=w_one):
                value = dot_nt(grad_hidden[...], w_one[columns(i)])
                if block == 0:
                    grad_mixed[:, columns(i)] = value
                else:
                    grad_mixed[:, columns(i)] += value

            each(D // TILE, back)
            pace.spend(1.0)
            fetch(at + slots)
            fetch(at + slots + 1)
            weight_grad(layer, mixed, grad_hidden, 4 + block)
            at += 2
        for copy in copies[2:]:
            copy.wait()

        def leave(rows, image, base=base, bias_add=bias_add):
            grad = grad_mixed[rows]
            normed, inverse = centre(middle[rows])
            mods_acc[image, base + 3] += total(grad)
            mods_acc[image, base + 4] += total(grad * normed)
            grad = grad * (1.0 + mods[image, base + 4])
            grad = grad_x[rows] + inverse * (
                grad - jnp.mean(grad, axis=-1, keepdims=True) - normed * jnp.mean(grad * normed, axis=-1, keepdims=True)
            )
            middle[rows] = grad
            low = (mods[image, base + 2] * grad).astype(jnp.bfloat16)
            grad_b[rows] = low
            bias_add(2, low.astype(jnp.float32))
            mods_acc[image, base + 2] += total(grad * branch[rows])
            normed, _ = centre(x_v[rows])
            mixed[rows] = (normed * (1.0 + mods[image, base + 1]) + mods[image, base]).astype(jnp.bfloat16)

        row_blocks(tokens, leave)
        pace.spend(2.6)
        w_proj = weight(at)

        def through(i, w_proj=w_proj):
            active[:, columns(i)] = dot_nt(grad_b[...], w_proj[columns(i)]).astype(jnp.bfloat16)

        each(D // TILE, through)
        pace.spend(0.9)
        fetch(at + slots)
        weight_grad(layer, att_v, grad_b, 3)
        for image in range(images):
            for pair in range(0, HEADS // 2, 2):
                attention_backward(proj_v, active, grad_projected, image, pair, 2)
                pace.spend(2.1)
        for p in range(3):
            w_part = weight(at + 1 + p)

            def into(i, p=p, w_part=w_part):
                value = dot_nt(grad_projected[p], w_part[columns(i)])
                if p == 0:
                    grad_mixed[:, columns(i)] = value
                else:
                    grad_mixed[:, columns(i)] += value

            weight_grad(layer, mixed, grad_projected.at[p], p)
            each(D // TILE, into)
            pace.spend(1.0)
            fetch(at + 1 + p + slots)

        def last(rows, image, base=base, bias_add=bias_add):
            grad = grad_mixed[rows]
            normed, inverse = centre(x_v[rows])
            mods_acc[image, base] += total(grad)
            mods_acc[image, base + 1] += total(grad * normed)
            grad = grad * (1.0 + mods[image, base + 1])
            grad_x[rows] = middle[rows] + inverse * (
                grad - jnp.mean(grad, axis=-1, keepdims=True) - normed * jnp.mean(grad * normed, axis=-1, keepdims=True)
            )
            bias_add(0, grad_projected[0, rows].astype(jnp.float32))
            bias_add(1, grad_projected[2, rows].astype(jnp.float32))

        row_blocks(tokens, last)
        pace.spend(2.2)

    def patch(rows, image):
        low = grad_x[rows].astype(jnp.bfloat16)
        grad_b[rows] = low
        sums[pl.ds(2 * PDIM + 8, 1)] += total(low.astype(jnp.float32))

    row_blocks(tokens, patch)
    value = dot_tn(picked[...], grad_b[...])
    for u in range(PATCH):
        first = u * strip * GRID
        part = value[first : first + strip]
        for j in range(1, GRID):
            part = part + value[first + j * strip : first + (j + 1) * strip]
        sums[pl.ds(u * strip, strip)] = part
    mods_tile[...] = jnp.zeros_like(mods_tile)
    entries = mods.shape[1]
    for image in range(images):
        for k in range(entries):
            mods_tile[pl.ds(image * entries + k, 1)] = mods_acc[image, k]
    mods_low[...] = mods_tile[...].astype(jnp.bfloat16)
    small = Sums(
        reduction, sums, sums_out, small_c, small_x, small_y, small_z, mods_low, mods_all, (v_s, v_r), (m_s, m_r), local
    )
    pace.add(pace.now, small.run)
    pace.drain()
    reduction.finish()
    for waits in busy:
        for wait in waits:
            wait()


def run_backward(count_all, x_last, mods, biases, picked, wanted, head_w, head_b, full, kept):
    tokens = x_last.shape[0]
    images, entries = mods.shape[:2]
    layers, owners, height, width = full.shape
    shard = D // owners
    count = 4 + FF_BLOCKS
    piece = shard // 2
    sizes = [(2, 1), (1, 1), (1, 1), (2, 2), (2, 1), (2, 2), (2, 1)]
    groups = []
    for squares, thirds in sizes:
        first = sum(group[1] for group in groups)
        groups.append((first, squares * piece, thirds * piece // 3))
    half = height // 2
    part = sum(group[2] for group in groups)
    most = half - part
    wide, low = jnp.float32, jnp.bfloat16
    vmem, anywhere = pl.BlockSpec(memory_space=pltpu.VMEM), pl.BlockSpec(memory_space=pl.ANY)
    rows = (tokens, D)
    dma, regular = pltpu.SemaphoreType.DMA, pltpu.SemaphoreType.REGULAR
    number = len(groups)
    sum_rows = 3 * PDIM + LAYERS * count
    mod_rows = -(-images * entries // 16) * 16
    pair = [dma((layers, number))] * 2
    return pl.pallas_call(
        partial(backward_kernel, groups, count_all),
        out_shape=[
            jax.ShapeDtypeStruct((layers, 2, half, width), wide),
            jax.ShapeDtypeStruct((Z_SIZE, Y_SIZE, X_SIZE * C_SIZE, mod_rows, D), low),
            jax.ShapeDtypeStruct((sum_rows, D), wide),
        ],
        in_specs=[anywhere] + [vmem] * 6 + [anywhere] * 7,
        out_specs=[vmem] * 3,
        scratch_shapes=[
            pltpu.VMEM((4, D, D), low),
            pltpu.VMEM(rows, wide),
            pltpu.VMEM(rows, wide),
            pltpu.VMEM((3,) + rows, low),
            pltpu.VMEM(rows, low),
            pltpu.VMEM(rows, wide),
            pltpu.VMEM(rows, wide),
            pltpu.VMEM(rows, low),
            pltpu.VMEM(rows, low),
            pltpu.VMEM(rows, low),
            pltpu.VMEM(rows, low),
            pltpu.VMEM(rows, wide),
            pltpu.VMEM((3,) + rows, low),
            pltpu.VMEM((2, D, D), low),
            pltpu.VMEM((images, entries, 1, D), wide),
            pltpu.VMEM((mod_rows, D), wide),
            pltpu.VMEM((mod_rows, D), low),
            pltpu.VMEM((sum_rows, D), wide),
            pltpu.VMEM((Z_SIZE, Y_SIZE, half, D), low),
            pltpu.VMEM((Z_SIZE, Y_SIZE, half, D), low),
            pltpu.VMEM((Z_SIZE, Y_SIZE, part, D), low),
            pltpu.VMEM((Z_SIZE, most, D), low),
            pltpu.VMEM((Z_SIZE - 1, most, D), low),
            pltpu.VMEM((most, D), low),
            pltpu.VMEM((sum_rows // 2, D), wide),
            pltpu.VMEM((sum_rows // 2, D), wide),
            pltpu.VMEM((sum_rows // 2, D), wide),
            pltpu.VMEM((Z_SIZE, sum_rows // 2, D), wide),
            dma((4,)),
            dma((6,)),
            dma,
            dma((layers, number, FF_BLOCKS)),
            dma((layers, number, FF_BLOCKS)),
            dma((layers, number, FF_BLOCKS)),
            *pair,
            *pair,
            dma((layers, number, Z_SIZE - 1)),
            dma((layers, number, Z_SIZE - 1)),
            *pair,
            *pair,
            dma((7,)),
            dma((7,)),
            dma((7,)),
            dma((7,)),
            dma,
            regular((number,)),
            regular((number,)),
            regular((number,)),
            regular((number, Z_SIZE - 1)),
            regular((number,)),
        ],
        compiler_params=pltpu.CompilerParams(
            collective_id=3, has_side_effects=True, vmem_limit_bytes=63 * 2**20
        ),
        name="blocks_backward",
    )(x_last, mods, biases, picked, wanted, head_w, head_b, full, *kept)


def exchange_kernel(cond, stats, cond_all, total, pieces, c_s, c_r, p_s, p_r, g_s, g_r, r_s, r_r):
    dp, rep = lax.axis_index("dp"), lax.axis_index("rep")
    dps, reps = Z_SIZE * Y_SIZE, X_SIZE * C_SIZE
    dp_peers = [((dp + k) % dps, rep) for k in range(1, dps)]
    rep_peers = [(dp, (rep + k) % reps) for k in range(1, reps)]
    meet(dp_peers + rep_peers)
    quarter = stats.shape[0] // reps
    size = quarter // dps
    copies = []

    def go(source, target, sems, index, peer):
        copy = push(source, target, sems[0].at[index], sems[1].at[index], peer)
        copy.start()
        copies.append(copy)
        return copy

    def part(owner):
        return pl.ds(pl.multiple_of(rep * quarter + owner * size, 8), size)

    first = [go(stats.at[part(peer[0])], pieces.at[dp], (p_s, p_r), k, peer) for k, peer in enumerate(dp_peers)]
    spread = [go(cond, cond_all.at[dp], (c_s, c_r), k, peer) for k, peer in enumerate(dp_peers)]
    cond_all[dp] = cond[...]
    pieces[dp] = stats[part(dp)]
    for copy in first:
        copy.wait_recv()
    value = pieces[0]
    for k in range(1, dps):
        value = value + pieces[k]
    total[part(dp)] = value
    own = total.at[part(dp)]
    second = [go(own, own, (g_s, g_r), k, peer) for k, peer in enumerate(dp_peers)]
    for copy in second:
        copy.wait_recv()
    own = total.at[pl.ds(pl.multiple_of(rep * quarter, 8), quarter)]
    third = [go(own, own, (r_s, r_r), k, peer) for k, peer in enumerate(rep_peers)]
    for copy in third + spread:
        copy.wait_recv()
    for copy in copies:
        copy.wait_send()


def exchange(cond, stats):
    dps, reps = Z_SIZE * Y_SIZE, X_SIZE * C_SIZE
    vmem = pl.BlockSpec(memory_space=pltpu.VMEM)
    dma = pltpu.SemaphoreType.DMA
    return pl.pallas_call(
        exchange_kernel,
        out_shape=[
            jax.ShapeDtypeStruct((dps,) + cond.shape, cond.dtype),
            jax.ShapeDtypeStruct(stats.shape, stats.dtype),
        ],
        in_specs=[vmem, vmem],
        out_specs=[vmem, vmem],
        scratch_shapes=[pltpu.VMEM((dps, stats.shape[0] // (dps * reps), LANES), stats.dtype)]
        + [dma((dps - 1,))] * 6
        + [dma((reps - 1,))] * 2,
        compiler_params=pltpu.CompilerParams(collective_id=4, has_side_effects=True),
        name="exchange_sums",
    )(cond, stats)


def line_up_kernel(offsets, *refs):
    pieces, (first, tail), out, spread = refs[: len(offsets)], refs[len(offsets) : -2], refs[-2], refs[-1]
    ways = D // LANES
    for piece, offset in zip(pieces, offsets):
        rows = piece.shape[0]
        for k in range(ways):
            out[pl.ds(ways * offset + k, rows, stride=ways)] = piece[:, k * LANES : (k + 1) * LANES]
    rows = tail.shape[0] * ways
    for k in range(ways):
        spread[pl.ds(k, tail.shape[0], stride=ways)] = tail[:, k * LANES : (k + 1) * LANES]
    moved = pltpu.roll(spread[...], PDIM, 1)
    lane = lax.broadcasted_iota(jnp.int32, (rows, LANES), 1)
    spread[pl.ds(1, rows - 1)] = moved[: rows - 1]
    spread[pl.ds(0, 1)] = first[...]
    start = out.shape[0] - rows - 1
    out[pl.ds(start, rows)] = jnp.where(lane >= PDIM, moved, spread[...])
    out[pl.ds(start + rows, 1)] = moved[rows - 1 :]


def line_up(pieces, first, tail):
    offsets, at = [], 0
    for piece in pieces:
        offsets.append(at)
        at += piece.shape[0]
    ways = D // LANES
    vmem = pl.BlockSpec(memory_space=pltpu.VMEM)
    count = (at + tail.shape[0]) * ways + 1
    return pl.pallas_call(
        partial(line_up_kernel, offsets),
        out_shape=jax.ShapeDtypeStruct((count, LANES), jnp.float32),
        in_specs=[vmem] * (len(pieces) + 2),
        out_specs=vmem,
        scratch_shapes=[pltpu.VMEM((tail.shape[0] * ways, LANES), jnp.float32)],
        compiler_params=pltpu.CompilerParams(vmem_limit_bytes=32 * 2**20),
        name="line_up",
    )(*pieces, first, tail)


def unpack_shard(packed, rows):
    count = FF // D
    blocks = [packed[:, rows * i : rows * (i + 1)] for i in range(4 + count)]
    return (
        jnp.concatenate(blocks[:3], axis=-1),
        blocks[3],
        jnp.concatenate(blocks[4:], axis=-1),
        packed[:, rows * (4 + count) :],
    )


def local(
    latents,
    noise_field,
    timesteps,
    labels,
    drop_mask,
    roster,
    w_qkv,
    w_proj,
    w_fc1,
    w_fc2,
    w_mod,
    row_qkv,
    col_qkv,
    row_proj,
    col_proj,
    row_fc1,
    col_fc1,
    row_fc2,
    col_fc2,
    row_mod,
    col_mod,
    small,
    small_second,
):
    pieces = unpack(small)
    dp_size, rep_size = lax.axis_size("dp"), lax.axis_size("rep")
    everyone = dp_size * rep_size
    number = latents.shape[0] * latents.shape[1]
    count_all = number * everyone * GRID * GRID * PDIM
    rows_mod = w_mod.shape[0]
    first_row = lax.axis_index("dp") * rows_mod
    places = position_table()
    patch_low = pieces["patch_w"].astype(jnp.bfloat16)
    time1_low = pieces["time1_w"].astype(jnp.bfloat16)
    time2_low = pieces["time2_w"].astype(jnp.bfloat16)
    head_low = pieces["head_w"].astype(jnp.bfloat16)
    mod_shard = w_mod.astype(jnp.bfloat16)

    direct = (dp_size, rep_size) == (Z_SIZE * Y_SIZE, X_SIZE * C_SIZE) and rows_mod % 96 == 0
    picker = (timesteps.reshape(-1)[:, None] == jnp.arange(STEPS_T)[None, :]).astype(jnp.float32)
    factors = jnp.dot(picker, roster.T, precision=HIGHEST)
    noise_flat = noise_field.reshape(number, -1)
    noised = factors[:, 0:1] * latents.reshape(number, -1) + factors[:, 1:2] * noise_flat
    own_ids = jnp.stack([timesteps, labels, drop_mask]).reshape(3, number)
    if direct:
        tile = jnp.pad(own_ids.T.astype(jnp.float32), ((0, 8 - number), (0, LANES - 3)))
        column = jnp.arange(2 * LANES)[None, None, :] % LANES // (PATCH * CHAN)
        own_place = column == jnp.arange(GRID)[None, :, None]

        def pick(values):
            values = values.reshape(number * GRID, 1, PATCH * LANES)
            return jnp.where(own_place, values, jnp.zeros_like(values)).reshape(-1, PATCH * LANES)

        picked, wanted = pick(noised.astype(jnp.bfloat16)), pick(noise_flat)
        rows_at, places_of = 0, {}
        for piece_name, piece_dims in layout()[:8]:
            height = math.prod(piece_dims) // D
            places_of[piece_name] = (rows_at, height)
            rows_at += height
        biases = pieces["block_b"].reshape(LAYERS, -1, 1, D)
        x_last, packed_full, mods, all_ids, hidden_t, condition, *kept_blocks = run_forward(
            picked,
            places,
            tile,
            w_qkv,
            w_proj,
            w_fc1,
            w_fc2,
            w_mod,
            small[: rows_at * D].reshape(-1, LANES),
            places_of,
            biases,
            number,
        )
        all_ids = all_ids[:, :number, :3].reshape(-1, 3).T.astype(jnp.int32)
        hidden_t = hidden_t.reshape(everyone, 8, D)[:, :number].reshape(-1, D)
        condition = condition.reshape(everyone, 8, D)[:, :number].reshape(-1, D)
    else:
        all_ids = lax.all_gather(own_ids, ("dp", "rep"), axis=0, tiled=False)
        all_ids = all_ids.transpose(1, 0, 2).reshape(3, everyone * number)
    features = time_features(all_ids[0]).astype(jnp.bfloat16)
    if not direct:
        hidden_t = product(features, time1_low) + pieces["time1_b"]
    silu_t = jax.nn.silu(hidden_t).astype(jnp.bfloat16)
    chosen = jnp.where(all_ids[2] == 1, CLASSES, all_ids[1])
    onehot = (chosen[:, None] == jnp.arange(CLASSES + 1)[None, :]).astype(jnp.float32)
    if not direct:
        condition = (
            product(silu_t, time2_low)
            + pieces["time2_b"]
            + jnp.dot(onehot, pieces["class_tab"], precision=HIGHEST)
        )
    silu_c = jax.nn.silu(condition).astype(jnp.bfloat16)
    silu_rows = lax.dynamic_slice_in_dim(silu_c, first_row, rows_mod, axis=1)
    if not direct:
        tokens = patchify(noised).astype(jnp.bfloat16)
        target = patchify(noise_flat).reshape(-1, PDIM)
        residual = (product(tokens.reshape(-1, PDIM), patch_low) + pieces["patch_b"]).reshape(
            number, GRID * GRID, D
        ) + places
        group_rows = lax.dynamic_index_in_dim(
            silu_rows.reshape(dp_size, rep_size, number, rows_mod),
            lax.axis_index("rep"),
            axis=1,
            keepdims=False,
        ).reshape(dp_size * number, rows_mod)
        mod_part = product(group_rows, mod_shard)
        mod_sum = lax.psum_scatter(mod_part, "dp", scatter_dimension=0, tiled=True)
        modulation = mod_sum + pieces["mod_b"]
    if direct:
        head_wide = jnp.pad(head_low, ((0, 0), (0, LANES - PDIM)))
        head_shift = jnp.pad(pieces["head_b"], (0, LANES - PDIM))[None]
        finals, mod_all, sums = run_backward(
            count_all, x_last, mods, biases, picked, wanted, head_wide, head_shift, packed_full, kept_blocks
        )
        finals = finals.reshape(LAYERS, C_SIZE, -1, rows_mod // C_SIZE, D).transpose(0, 2, 1, 3, 4)
        grad_qkv, grad_proj, grad_fc1, grad_fc2 = unpack_shard(finals.reshape(LAYERS, -1, D), rows_mod)
        grad_mod = mod_all.reshape(everyone, -1, D)[:, : number * (MOD // D)].reshape(-1, MOD)
        loss_total = sums[2 * PDIM, PDIM]
    else:
        kept_all = []
        gathered_all = []
        spans_all = []
        for layer_index in range(LAYERS):
            weights = tuple(
                lax.all_gather(w[layer_index].astype(jnp.bfloat16), "dp", axis=0, tiled=True)
                for w in (w_qkv, w_proj, w_fc1, w_fc2)
            )
            spans = [
                modulation[:, None, D * (6 * layer_index + i) : D * (6 * layer_index + i + 1)]
                for i in range(6)
            ]
            residual, kept = layer_forward(residual, spans, weights, pieces["block_b"][layer_index])
            kept_all.append(kept)
            gathered_all.append(weights)
            spans_all.append(spans)
        final_shift = modulation[:, None, 6 * D * LAYERS : 6 * D * LAYERS + D]
        final_scale = modulation[:, None, 6 * D * LAYERS + D :]
        normed_f, inverse_f = norm_rows(residual)
        final_in = (normed_f * (1.0 + final_scale) + final_shift).astype(jnp.bfloat16).reshape(-1, D)
        output = product(final_in, head_low) + pieces["head_b"]
        error = output - target
        loss_own = jnp.sum(error * error)
        grad_output = (error * (2.0 / count_all)).astype(jnp.bfloat16)
        grad_head = product(final_in.T, grad_output)
        grad_head_b = jnp.sum(grad_output.astype(jnp.float32), axis=0)
        grad_final = product(grad_output, head_low.T).reshape(number, GRID * GRID, D)
        final_grads = [jnp.sum(grad_final, axis=1), jnp.sum(grad_final * normed_f, axis=1)]
        grad_res = norm_back(grad_final * (1.0 + final_scale), normed_f, inverse_f)
        layer_spans = [None] * LAYERS
        bias_grads = [None] * LAYERS
        block_grads = [None] * LAYERS
        for layer_index in reversed(range(LAYERS)):
            grad_res, grads, grad_bias, grad_spans = layer_backward(
                grad_res, spans_all[layer_index], gathered_all[layer_index], kept_all[layer_index]
            )
            layer_spans[layer_index] = grad_spans
            bias_grads[layer_index] = grad_bias
            block_grads[layer_index] = tuple(
                lax.psum_scatter(g, "dp", scatter_dimension=0, tiled=True) for g in grads
            )

        grad_start = grad_res.reshape(-1, D).astype(jnp.bfloat16)
        grad_patch = product(tokens.reshape(-1, PDIM).T, grad_start)
        grad_patch_b = jnp.sum(grad_start.astype(jnp.float32), axis=0)
        own_sums = jnp.concatenate(
            [
                grad_patch.reshape(-1),
                grad_patch_b,
                grad_head.reshape(-1),
                jnp.stack(bias_grads).reshape(-1),
                grad_head_b,
                loss_own[None],
            ]
        )
        own_mod = jnp.concatenate(layer_spans + final_grads, axis=-1).astype(jnp.bfloat16)
        grad_qkv, grad_proj, grad_fc1, grad_fc2 = lax.psum(
            tuple(jnp.stack([block_grads[i][k] for i in range(LAYERS)]) for k in range(4)), "rep"
        )
        grad_mod = lax.all_gather(own_mod, ("dp", "rep"), axis=0, tiled=True)
        summed = lax.psum(own_sums, ("dp", "rep"))
        cut_patch = (PDIM + 1) * D
        cut_head = cut_patch + D * PDIM
        cut_bias = cut_head + LAYERS * (4 * D + FF)
        loss_total = summed[cut_bias + PDIM]
        sum_patch = summed[:cut_patch]
        sum_head = jnp.append(summed[cut_patch:cut_head], summed[cut_bias : cut_bias + PDIM])
        sum_bias = summed[cut_head:cut_bias]

    grad_wmod = product(silu_rows.T, grad_mod)
    grad_mod_b = jnp.sum(grad_mod.astype(jnp.float32), axis=0)
    beta = 1.0 - STEP ** (-0.8)
    kinds = [
        (w_qkv, grad_qkv, row_qkv, col_qkv),
        (w_proj, grad_proj, row_proj, col_proj),
        (w_fc1, grad_fc1, row_fc1, col_fc1),
        (w_fc2, grad_fc2, row_fc2, col_fc2),
        (w_mod[None], grad_wmod[None], row_mod[None], col_mod[None]),
    ]
    firsts = []
    for weight, grad, row, col in kinds:
        square = grad * grad
        row_new = beta * row + (1.0 - beta) * jnp.mean(square + EPS_ONE, axis=-1)
        firsts.append(
            (
                row_new,
                jnp.sum(square + EPS_ONE, axis=-2),
                jnp.sum(square / row_new[:, :, None], axis=-2),
                jnp.sum(row_new, axis=-1),
                jnp.sum(weight * weight, axis=(-2, -1)),
            )
        )
    stats = jnp.concatenate([entry[k].reshape(-1) for k in range(1, 5) for entry in firsts])
    cond_own = product(grad_mod, mod_shard.T)
    if direct:
        cond_tile = jnp.pad(cond_own, ((0, 0), (0, -rows_mod % LANES)))
        stats_tile = jnp.pad(stats, (0, -stats.size % (everyone * 8 * LANES))).reshape(-1, LANES)
        cond_all, shared = exchange(cond_tile, stats_tile)
        cond_rows = cond_all[:, :, :rows_mod].transpose(1, 0, 2).reshape(-1, D)
        shared = shared.reshape(-1)
    else:
        cond_rows = lax.all_gather(cond_own, "dp", axis=1, tiled=True)
        shared = lax.psum(stats, "dp")
    _, silu_pull = jax.vjp(jax.nn.silu, condition)
    grad_cond = silu_pull(cond_rows)[0].astype(jnp.bfloat16)
    grad_class = jnp.dot(onehot.T, grad_cond.astype(jnp.float32), precision=HIGHEST)
    grad_time2 = product(silu_t.T, grad_cond)
    grad_time2_b = jnp.sum(grad_cond.astype(jnp.float32), axis=0)
    _, silu_time_pull = jax.vjp(jax.nn.silu, hidden_t)
    grad_hidden_t = silu_time_pull(product(grad_cond, time2_low.T))[0].astype(jnp.bfloat16)
    grad_time1 = product(features.T, grad_hidden_t)
    grad_time1_b = jnp.sum(grad_hidden_t.astype(jnp.float32), axis=0)
    if direct:
        lined = line_up(
            [
                sums[:PDIM],
                sums[2 * PDIM + 8 :][:1],
                grad_time1,
                grad_time1_b[None],
                grad_time2,
                grad_time2_b[None],
                grad_class,
                grad_mod_b.reshape(-1, D),
                sums[PDIM : 2 * PDIM].T.reshape(-1, D),
            ],
            sums[2 * PDIM : 2 * PDIM + 1, :LANES],
            sums[3 * PDIM :],
        )
        small_grad = lined.reshape(-1)[: small.shape[0]]
    else:
        small_grad = jnp.concatenate(
            [
                sum_patch,
                grad_time1.reshape(-1),
                grad_time1_b,
                grad_time2.reshape(-1),
                grad_time2_b,
                grad_class.reshape(-1),
                grad_mod_b,
                sum_head,
                sum_bias,
            ]
        )
    rows_dp = dp_size
    parts = []
    offset = 0
    for k in range(1, 5):
        for entry in firsts:
            parts.append(shared[offset : offset + entry[k].size].reshape(entry[k].shape))
            offset += entry[k].size
    seconds = []
    for index, kind in enumerate(kinds):
        weight, grad, row, col = kind
        rows_all = weight.shape[1] * rows_dp
        col_count = weight.shape[2]
        col_sum, over_rows, row_sum, weight_sq = (parts[index + len(kinds) * k] for k in range(4))
        row_mean = row_sum / rows_all
        weight_rms = jnp.sqrt(weight_sq / (rows_all * col_count))
        col_new = beta * col + (1.0 - beta) * col_sum / rows_all
        update_sq = row_mean * jnp.sum(over_rows / col_new, axis=-1)
        estimate = firsts[index][0][:, :, None] * col_new[:, None, :] / row_mean[:, None, None]
        update = grad * lax.rsqrt(estimate)
        seconds.append((update, col_new, weight_rms, update_sq / (rows_all * col_count)))
    results = []
    for kind, first, second in zip(kinds, firsts, seconds):
        weight, grad = (kind[0], kind[1])
        update, col_new, weight_rms, update_ms = second
        update_rms = jnp.sqrt(update_ms)
        update = update / jnp.maximum(1.0, update_rms / CLIP)[:, None, None]
        new_weight = weight - (RATE * jnp.maximum(0.001, weight_rms))[:, None, None] * update
        results.append((new_weight, grad, first[0], col_new, new_weight.astype(jnp.bfloat16)))
    square = small_grad * small_grad + EPS_ONE
    small_second_new = beta * small_second + (1.0 - beta) * square
    update = small_grad * lax.rsqrt(small_second_new)
    update = update / jnp.maximum(1.0, jnp.sqrt(jnp.mean(update * update)) / CLIP)
    small_new = small - RATE * jnp.maximum(0.001, jnp.sqrt(jnp.mean(small * small))) * update
    mod_result = results[4]
    return (
        loss_total,
        results[0][0],
        results[0][1],
        results[0][2],
        results[0][3],
        results[0][4],
        results[1][0],
        results[1][1],
        results[1][2],
        results[1][3],
        results[1][4],
        results[2][0],
        results[2][1],
        results[2][2],
        results[2][3],
        results[2][4],
        results[3][0],
        results[3][1],
        results[3][2],
        results[3][3],
        results[3][4],
        mod_result[0][0],
        mod_result[1][0],
        mod_result[2][0],
        mod_result[3][0],
        mod_result[4][0],
        small_grad,
        small_second_new,
        small_new,
        small_new.astype(jnp.bfloat16),
    )


def solution(mesh):
    in_specs = (
        P(None, ("dp", "rep"), None),
        P(None, ("dp", "rep"), None),
        P(None, ("dp", "rep")),
        P(None, ("dp", "rep")),
        P(None, ("dp", "rep")),
        P(),
        P(None, "dp", None),
        P(None, "dp", None),
        P(None, "dp", None),
        P(None, "dp", None),
        P("dp", None),
        P(None, "dp"),
        P(),
        P(None, "dp"),
        P(),
        P(None, "dp"),
        P(),
        P(None, "dp"),
        P(),
        P("dp"),
        P(),
        P(),
        P(),
    )
    out_specs = (
        P(),
        P(None, "dp", None),
        P(None, "dp", None),
        P(None, "dp"),
        P(),
        P(None, "dp", None),
        P(None, "dp", None),
        P(None, "dp", None),
        P(None, "dp"),
        P(),
        P(None, "dp", None),
        P(None, "dp", None),
        P(None, "dp", None),
        P(None, "dp"),
        P(),
        P(None, "dp", None),
        P(None, "dp", None),
        P(None, "dp", None),
        P(None, "dp"),
        P(),
        P(None, "dp", None),
        P("dp", None),
        P("dp", None),
        P("dp"),
        P(),
        P("dp", None),
        P(),
        P(),
        P(),
        P(),
    )
    return jax.shard_map(local, mesh=mesh, in_specs=in_specs, out_specs=out_specs, check_vma=False)
```

```python
from functools import partial
import math

import jax
import jax.numpy as jnp
from jax import lax
from jax.experimental import pallas as pl
from jax.experimental.pallas import tpu as pltpu
from jax.sharding import PartitionSpec as P

D = 768
HEADS = 12
FF = 3072
FREQ = 256
CLASSES = 32
GRID = 16
PATCH = 2
CHAN = 4
LAYERS = 2
MICRO = 2
STEPS_T = 1000
STEP = 10
PDIM = 16
MOD = 10752


HIGHEST = lax.Precision.HIGHEST
EPS_NORM = 1e-06
EPS_ONE = 1e-30
CLIP = 0.5
RATE = 0.6


def product(left, right):
    return jnp.dot(left, right, preferred_element_type=jnp.float32)


def layout():
    return [
        ("patch_w", (PDIM, D)),
        ("patch_b", (D,)),
        ("time1_w", (FREQ, D)),
        ("time1_b", (D,)),
        ("time2_w", (D, D)),
        ("time2_b", (D,)),
        ("class_tab", (CLASSES + 1, D)),
        ("mod_b", (MOD,)),
        ("head_w", (D, PDIM)),
        ("head_b", (PDIM,)),
        ("block_b", (LAYERS, 4 * D + FF)),
    ]


def unpack(small):
    pieces = {}
    offset = 0
    for piece_name, piece_dims in layout():
        piece_size = math.prod(piece_dims)
        pieces[piece_name] = small[offset : offset + piece_size].reshape(piece_dims)
        offset += piece_size
    return pieces


def position_table():
    quarter = D // 4
    omega = jnp.exp(-math.log(10000.0) * jnp.arange(quarter, dtype=jnp.float32) / quarter)
    places = jnp.arange(GRID * GRID, dtype=jnp.int32)
    across = (places // GRID).astype(jnp.float32)[:, None] * omega
    downward = (places % GRID).astype(jnp.float32)[:, None] * omega
    return jnp.concatenate(
        [jnp.sin(across), jnp.cos(across), jnp.sin(downward), jnp.cos(downward)], axis=1
    )


def time_features(timesteps):
    half_count = FREQ // 2
    frequency = jnp.exp(-math.log(10000.0) * jnp.arange(half_count, dtype=jnp.float32) / half_count)
    angles = timesteps.astype(jnp.float32)[:, None] * frequency
    return jnp.concatenate([jnp.cos(angles), jnp.sin(angles)], axis=1)


def patchify(flat):
    number = flat.shape[0]
    blocks = flat.reshape(number, GRID, PATCH, GRID, PATCH, CHAN).transpose(0, 1, 3, 2, 4, 5)
    return blocks.reshape(number, GRID * GRID, PDIM)


def norm_rows(values):
    centered = values - jnp.mean(values, axis=-1, keepdims=True)
    inverse = lax.rsqrt(jnp.mean(centered * centered, axis=-1, keepdims=True) + EPS_NORM)
    return (centered * inverse, inverse)


def norm_back(grad, normed, inverse):
    return inverse * (
        grad
        - jnp.mean(grad, axis=-1, keepdims=True)
        - normed * jnp.mean(grad * normed, axis=-1, keepdims=True)
    )


def layer_forward(residual, spans, weights, biases):
    number, seq_tokens = (residual.shape[0], residual.shape[1])
    scaling = 1.0 / math.sqrt(D // HEADS)
    blank_bias = jnp.zeros((D,), jnp.float32)
    qkv_bias = jnp.concatenate([biases[:D], blank_bias, biases[D : 2 * D]])
    normed_a, inverse_a = norm_rows(residual)
    mixed_a = (normed_a * (1.0 + spans[1]) + spans[0]).astype(jnp.bfloat16)
    projected = (product(mixed_a.reshape(-1, D), weights[0]) + qkv_bias).astype(jnp.bfloat16)
    projected = projected.reshape(number, seq_tokens, 3, HEADS, D // HEADS)
    scores = (
        jnp.einsum(
            "bqhd,bkhd->bhqk",
            projected[:, :, 0],
            projected[:, :, 1],
            preferred_element_type=jnp.float32,
        )
        * scaling
    )
    total_lse = jax.nn.logsumexp(scores, axis=-1, keepdims=True)
    attention = jnp.exp(scores - total_lse).astype(jnp.bfloat16)
    attended = jnp.einsum(
        "bhqk,bkhd->bqhd", attention, projected[:, :, 2], preferred_element_type=jnp.float32
    )
    attended = attended.astype(jnp.bfloat16).reshape(-1, D)
    branch_a = product(attended, weights[1]) + biases[2 * D : 3 * D]
    middle = residual + spans[2] * branch_a.reshape(number, seq_tokens, D)
    normed_b, inverse_b = norm_rows(middle)
    mixed_b = (normed_b * (1.0 + spans[4]) + spans[3]).astype(jnp.bfloat16)
    hidden = product(mixed_b.reshape(-1, D), weights[2]) + biases[3 * D : 3 * D + FF]
    activated = jax.nn.gelu(hidden, approximate=True).astype(jnp.bfloat16)
    branch_b = product(activated, weights[3]) + biases[3 * D + FF :]
    result = middle + spans[5] * branch_b.reshape(number, seq_tokens, D)
    kept = (
        normed_a,
        inverse_a,
        mixed_a,
        projected,
        total_lse,
        attended,
        branch_a,
        normed_b,
        inverse_b,
        mixed_b,
        hidden,
        activated,
        branch_b,
    )
    return (result, kept)


def layer_backward(grad_out, spans, weights, kept):
    (
        normed_a,
        inverse_a,
        mixed_a,
        projected,
        total_lse,
        attended,
        branch_a,
        normed_b,
        inverse_b,
        mixed_b,
        hidden,
        activated,
        branch_b,
    ) = kept
    number, seq_tokens = (grad_out.shape[0], grad_out.shape[1])
    scaling = 1.0 / math.sqrt(D // HEADS)
    grad_b = (spans[5] * grad_out).reshape(-1, D).astype(jnp.bfloat16)
    gate_b = jnp.sum(grad_out * branch_b.reshape(number, seq_tokens, D), axis=1)
    grad_fc2 = product(activated.T, grad_b)
    bias_fc2 = jnp.sum(grad_b.astype(jnp.float32), axis=0)
    _, gelu_pull = jax.vjp(partial(jax.nn.gelu, approximate=True), hidden)
    grad_hidden = gelu_pull(product(grad_b, weights[3].T))[0].astype(jnp.bfloat16)
    grad_fc1 = product(mixed_b.reshape(-1, D).T, grad_hidden)
    bias_fc1 = jnp.sum(grad_hidden.astype(jnp.float32), axis=0)
    grad_mixed = product(grad_hidden, weights[2].T).reshape(number, seq_tokens, D)
    shift_b = jnp.sum(grad_mixed, axis=1)
    scale_b = jnp.sum(grad_mixed * normed_b, axis=1)
    grad_mid = grad_out + norm_back(grad_mixed * (1.0 + spans[4]), normed_b, inverse_b)
    grad_a = (spans[2] * grad_mid).reshape(-1, D).astype(jnp.bfloat16)
    gate_a = jnp.sum(grad_mid * branch_a.reshape(number, seq_tokens, D), axis=1)
    grad_proj = product(attended.T, grad_a)
    bias_proj = jnp.sum(grad_a.astype(jnp.float32), axis=0)
    grad_att = (
        product(grad_a, weights[1].T)
        .astype(jnp.bfloat16)
        .reshape(number, seq_tokens, HEADS, D // HEADS)
    )
    query, keys, values = (projected[:, :, 0], projected[:, :, 1], projected[:, :, 2])
    scores = (
        jnp.einsum("bqhd,bkhd->bhqk", query, keys, preferred_element_type=jnp.float32) * scaling
    )
    attention = jnp.exp(scores - total_lse)
    grad_values = jnp.einsum(
        "bhqk,bqhd->bkhd",
        attention.astype(jnp.bfloat16),
        grad_att,
        preferred_element_type=jnp.float32,
    )
    grad_weights = jnp.einsum(
        "bqhd,bkhd->bhqk", grad_att, values, preferred_element_type=jnp.float32
    )
    inner = jnp.sum(attention * grad_weights, axis=-1, keepdims=True)
    grad_scores = (attention * (grad_weights - inner)).astype(jnp.bfloat16)
    grad_query = (
        jnp.einsum("bhqk,bkhd->bqhd", grad_scores, keys, preferred_element_type=jnp.float32)
        * scaling
    )
    grad_keys = (
        jnp.einsum("bhqk,bqhd->bkhd", grad_scores, query, preferred_element_type=jnp.float32)
        * scaling
    )
    grad_projected = (
        jnp.stack([grad_query, grad_keys, grad_values], axis=2)
        .reshape(-1, 3 * D)
        .astype(jnp.bfloat16)
    )
    grad_qkv = product(mixed_a.reshape(-1, D).T, grad_projected)
    bias_sums = jnp.sum(grad_projected.astype(jnp.float32), axis=0)
    grad_mixed_a = product(grad_projected, weights[0].T).reshape(number, seq_tokens, D)
    shift_a = jnp.sum(grad_mixed_a, axis=1)
    scale_a = jnp.sum(grad_mixed_a * normed_a, axis=1)
    grad_in = grad_mid + norm_back(grad_mixed_a * (1.0 + spans[1]), normed_a, inverse_a)
    grad_spans = jnp.concatenate([shift_a, scale_a, gate_a, shift_b, scale_b, gate_b], axis=-1)
    grad_bias = jnp.concatenate([bias_sums[:D], bias_sums[2 * D :], bias_proj, bias_fc1, bias_fc2])
    return (grad_in, (grad_qkv, grad_proj, grad_fc1, grad_fc2), grad_bias, grad_spans)


MESH_IDS = pl.DeviceIdType.MESH
Z_SIZE, Y_SIZE, X_SIZE, C_SIZE = 4, 2, 2, 2
LANES = 128


def place():
    dp, rep = lax.axis_index("dp"), lax.axis_index("rep")
    return (dp // Y_SIZE, dp % Y_SIZE, rep // C_SIZE, rep % C_SIZE)


def device(z, y, x, c):
    return (z * Y_SIZE + y, x * C_SIZE + c)


def meet(peers):
    barrier = pltpu.get_barrier_semaphore()
    for peer in peers:
        pl.semaphore_signal(barrier, inc=1, device_id=peer, device_id_type=MESH_IDS)
    pl.semaphore_wait(barrier, len(peers))


def push(source, target, send, receive, peer):
    return pltpu.make_async_remote_copy(
        src_ref=source,
        dst_ref=target,
        send_sem=send,
        recv_sem=receive,
        device_id=peer,
        device_id_type=MESH_IDS,
    )


GELU_A, GELU_B = 0.79788456, 0.044715
FF_BLOCKS = FF // D
TILE = 256
ROWS = 64


def centre(values):
    centered = values - jnp.mean(values, axis=-1, keepdims=True)
    inverse = lax.rsqrt(jnp.mean(centered * centered, axis=-1, keepdims=True) + EPS_NORM)
    return centered * inverse, inverse


def dot_nn(left, right):
    return lax.dot_general(left, right, (((1,), (0,)), ((), ())), preferred_element_type=jnp.float32)


def dot_nt(left, right):
    return lax.dot_general(left, right, (((1,), (1,)), ((), ())), preferred_element_type=jnp.float32)


def dot_tn(left, right):
    return lax.dot_general(left, right, (((0,), (0,)), ((), ())), preferred_element_type=jnp.float32)


def each(count, body):
    if count <= 3:
        for i in range(count):
            body(i)
        return
    lax.fori_loop(0, count, lambda i, carry: (body(i), carry)[1], 0)


def row_blocks(tokens, body, step=ROWS):
    each(tokens // step, lambda i: body(pl.ds(pl.multiple_of(i * step, step), step), i // (GRID * GRID // step)))


def modulate(source, mods, shift, scale, target, tokens):
    def body(rows, image):
        normed, _ = centre(source[rows])
        target[rows] = (normed * (1.0 + mods[image, scale]) + mods[image, shift]).astype(jnp.bfloat16)

    row_blocks(tokens, body)


def block_at(i, size):
    return pl.ds(i * size if isinstance(i, int) else pl.multiple_of(i * size, size), size)


def columns(i):
    return block_at(i, TILE)


def head_lanes(head):
    lane = lax.broadcasted_iota(jnp.int32, (GRID * GRID, 2 * D // HEADS), 1)
    return lane // (D // HEADS) == head


def softmax(query, keys):
    scores = dot_nt(query, keys) * (1.0 / math.sqrt(D // HEADS))
    powers = jnp.exp(scores - jnp.max(scores, axis=-1, keepdims=True))
    return powers * (1.0 / jnp.sum(powers, axis=-1, keepdims=True))


def pick(lanes, values):
    return jnp.where(lanes, values, jnp.zeros_like(values))


def attention_forward(projected, attended, images, first_pair, pairs):
    size, width = GRID * GRID, 2 * D // HEADS

    def body(i, image):
        rows, lanes = block_at(image, size), block_at(first_pair + i, width)
        query, keys, values = (projected[p, rows, lanes] for p in range(3))
        first = head_lanes(0)
        outs = []
        for own in (first, jnp.logical_not(first)):
            weights = softmax(pick(own, query), keys).astype(jnp.bfloat16)
            outs.append(dot_nn(weights, values))
        attended[rows, lanes] = jnp.where(first, outs[0], outs[1]).astype(jnp.bfloat16)

    each(pairs, lambda i: [body(i, image) for image in range(images)])


def attention_backward(projected, grad_attended, grad_projected, image, first_pair, pairs):
    size, width = GRID * GRID, 2 * D // HEADS
    scaling = 1.0 / math.sqrt(D // HEADS)

    def body(i):
        rows, lanes = block_at(image, size), block_at(first_pair + i, width)
        query, keys, values = (projected[p, rows, lanes] for p in range(3))
        grad_out = grad_attended[rows, lanes]
        first = head_lanes(0)
        outs = []
        for own in (first, jnp.logical_not(first)):
            weights = softmax(pick(own, query), keys)
            grad_values = dot_tn(weights.astype(jnp.bfloat16), grad_out)
            grad_weights = dot_nt(pick(own, grad_out), values)
            inner = jnp.sum(weights * grad_weights, axis=-1, keepdims=True)
            grad_scores = (weights * (grad_weights - inner)).astype(jnp.bfloat16)
            outs.append(
                (dot_nn(grad_scores, keys) * scaling, dot_tn(grad_scores, query) * scaling, grad_values)
            )
        for p in range(3):
            grad_projected[p, rows, lanes] = jnp.where(first, outs[0][p], outs[1][p]).astype(jnp.bfloat16)

    each(pairs, body)


def whole(block):
    return block.reshape(D, block.shape[-1])


class Pace:
    LATENCY = 2.2

    def __init__(self, rate=48e3, along_z=4):
        self.rate, self.along_z = rate, along_z
        self.now = 0.0
        self.free = {}
        self.entries = []

    def send(self, link, count):
        rate = 10 * self.rate if link == "c" else self.rate
        self.free[link] = max(self.now, self.free.get(link, 0.0)) + count / rate
        return self.free[link] + self.LATENCY

    def add(self, ready, run):
        self.entries.append([ready, len(self.entries), run])

    def serve(self, entry):
        cost, ready = entry[2]()
        self.now += cost
        if ready is None:
            self.entries.remove(entry)
        else:
            entry[0] = ready

    def spend(self, cost):
        self.now += cost
        while self.entries:
            entry = min(self.entries, key=lambda e: e[:2])
            if entry[0] > self.now:
                return
            self.serve(entry)

    def next(self):
        entry = min(self.entries, key=lambda e: e[:2])
        self.now = max(self.now, entry[0])
        self.serve(entry)

    def until(self, done):
        while not done():
            self.next()

    def drain(self):
        while self.entries:
            self.next()


class Gather:
    def __init__(self, pace, groups, spot, packed, full, semaphores, prepare, loads):
        self.pace, self.groups, self.spot = pace, groups, spot
        self.packed = packed
        layers, owners, height, width = full.shape
        self.full = full.reshape(layers, Z_SIZE, Y_SIZE, height, width)
        self.sems, self.prepare, self.loads = semaphores, prepare, loads
        z, y, x, c = spot
        self.z_peers = [device((z + k) % Z_SIZE, y, x, c) for k in range(1, Z_SIZE)]
        self.across_y, self.across_x = device(z, 1 - y, x, c), device(z, y, 1 - x, c)
        self.sibling = device(z, y, x, 1 - c)
        self.done, self.copies, self.keeps = set(), [], {}
        self.waiting = list(range(len(groups)))

    def rows(self, group, third, count, core):
        _, first, size = self.groups[group]
        step = size // 6
        return pl.ds(pl.multiple_of(first + core * 3 * step + third * step, 16), count * step)

    def size(self, group, count):
        return self.groups[group][2] // 6 * count * D * 2

    def sem(self, name, group, *index):
        send, receive = self.sems[name]
        return send.at[(group,) + index], receive.at[(group,) + index]

    def go(self, source, target, sems, peer):
        copy = push(source, target, sems[0], sems[1], peer)
        copy.start()
        self.copies.append(copy)

    def arrive(self, ref, sems):
        push(ref, ref, sems[0], sems[1], self.across_y).wait_recv()

    def start(self):
        z, y, x, c = self.spot
        group = self.waiting.pop(0)
        layer = self.groups[group][0]
        self.prepare(group)
        own = self.packed.at[layer, self.rows(group, x, 2, c)]
        target = self.full.at[layer, z, y, self.rows(group, x, 2, c)]
        for k in range(1, Z_SIZE):
            self.go(own, target, self.sem("z", group, k - 1), self.z_peers[k - 1])
        keep = pltpu.make_async_copy(own, target, self.sems["keep"].at[group])
        keep.start()
        self.keeps[group] = keep
        stages = [self.on_z, self.on_y, self.on_x, self.on_c]
        self.pace.add(
            self.pace.send("z", 4 * self.size(group, 2)), lambda: (0.6, stages.pop(0)(group, layer))
        )
        return 1.4, self.pace.free["z"] - 9.0 if self.waiting else None

    def on_z(self, group, layer):
        z, y, x, c = self.spot
        self.keeps[group].wait()
        both, third = self.rows(group, x, 2, c), self.rows(group, 2 * x, 1, c)
        for k in range(1, Z_SIZE):
            self.arrive(self.full.at[layer, (z - k) % Z_SIZE, y, both], self.sem("z", group, k - 1))
        ref = self.full.at[layer, :, y, both]
        self.go(ref, ref, self.sem("y", group), self.across_y)
        part = self.full.at[layer, :, y, third]
        self.go(part, part, self.sem("x", group, 0), self.across_x)
        self.go(ref, ref, self.sem("c", group, 0), self.sibling)
        self.x_ready = self.pace.send("x", 4 * self.size(group, 1))
        return self.pace.send("y", 4 * self.size(group, 2))

    def on_y(self, group, layer):
        z, y, x, c = self.spot
        ref = self.full.at[layer, :, 1 - y, self.rows(group, x, 2, c)]
        self.arrive(ref, self.sem("y", group))
        part = self.full.at[layer, :, 1 - y, self.rows(group, 2 * x, 1, c)]
        self.go(part, part, self.sem("x", group, 1), self.across_x)
        self.go(ref, ref, self.sem("c", group, 1), self.sibling)
        return self.pace.send("x", 4 * self.size(group, 1))

    def on_x(self, group, layer):
        z, y, x, c = self.spot
        third = self.rows(group, 2 - 2 * x, 1, c)
        for k, side in enumerate((y, 1 - y)):
            self.arrive(self.full.at[layer, :, side, third], self.sem("x", group, k))
        ref = self.full.at[layer, :, :, third]
        self.go(ref, ref, self.sem("c", group, 2), self.sibling)
        return self.pace.send("c", 8 * self.size(group, 1))

    def on_c(self, group, layer):
        z, y, x, c = self.spot
        for k, side in enumerate((y, 1 - y)):
            self.arrive(self.full.at[layer, :, side, self.rows(group, x, 2, 1 - c)], self.sem("c", group, k))
        third = self.rows(group, 2 - 2 * x, 1, 1 - c)
        self.arrive(self.full.at[layer, :, :, third], self.sem("c", group, 2))
        self.done.add(group)
        self.loads(group)
        return None

    def finish(self):
        for copy in self.copies:
            copy.wait_send()


def silu(values):
    return values / (1.0 + jnp.exp(-values))


def conditions(ids, time1_w, time1_b, time2_w, time2_b, class_tab, hidden_t, condition):
    rows, half = ids.shape[0], FREQ // 2
    k = lax.broadcasted_iota(jnp.int32, (1, half), 1).astype(jnp.float32)
    angles = ids[:, 0:1] * jnp.exp(-math.log(10000.0) * k / half)
    features = jnp.concatenate([jnp.cos(angles), jnp.sin(angles)], axis=1).astype(jnp.bfloat16)
    hidden = dot_nn(features, time1_w[...]) + time1_b
    hidden_t[...] = hidden
    chosen = jnp.where(ids[:, 2:3] == 1.0, float(CLASSES), ids[:, 1:2])
    lane = lax.broadcasted_iota(jnp.int32, (rows, class_tab.shape[0]), 1).astype(jnp.float32)
    picked = jnp.dot(
        (lane == chosen).astype(jnp.float32), class_tab, precision=HIGHEST, preferred_element_type=jnp.float32
    )
    condition[...] = dot_nn(silu(hidden).astype(jnp.bfloat16), time2_w[...]) + time2_b + picked


def forward_kernel(
    groups, places_of, picked, places, ids, w_qkv, w_proj, w_fc1, w_fc2, w_mod, small, biases,
    out, full, mods, ids_all, hidden_t, condition, x_h, proj_h, att_h, branch_a_h, middle_h, branch_b_h,
    w_in, w_out, x_v, proj_v, att_v, branch_a, middle, branch_b, mixed, active,
    mod_part, mod_y, mod_z, packed, raw, time1_w, time2_w, raw_sem, out_sem,
    w_sem, save_sem, i_s, i_r, z_s, z_r, y_s, y_r, x_s, x_r, c_s, c_r, keep_sem, my_s, my_r, mz_s, mz_r,
):
    tokens = picked.shape[0]
    images, entries = mods.shape[:2]
    shard, deep = w_in.shape[3], w_out.shape[3]
    ways = D // LANES
    count = 4 + FF_BLOCKS
    spot = place()
    z, y, x, c = spot
    dps, reps = Z_SIZE * Y_SIZE, X_SIZE * C_SIZE
    dp, rep = z * Y_SIZE + y, x * C_SIZE + c
    pace = Pace()

    def load(layer, index):
        if index < count:
            return pltpu.make_async_copy(
                full.at[layer, :, pl.ds(index * shard, shard)], w_in.at[layer, index], w_sem.at[layer, index]
            )
        block = index - count
        per = D // deep
        return pltpu.make_async_copy(
            full.at[layer, pl.ds(block * per, per), pl.ds(count * shard, deep)],
            w_out.at[layer, block],
            w_sem.at[layer, index],
        )

    def loads(group):
        layer, first, size = groups[group]
        for index in range(count):
            if first <= index * shard < first + size:
                load(layer, index).start()
        ends = {g for g, (at, begin, _) in enumerate(groups) if at == layer and begin >= count * shard}
        if group in ends and ends <= gather.done:
            for block in range(FF_BLOCKS):
                load(layer, count + block).start()

    def square(layer, index):
        if index < 3:
            return w_qkv.at[layer, :, pl.ds(index * D, D)]
        if index == 3:
            return w_proj.at[layer]
        if index < count:
            return w_fc1.at[layer, :, pl.ds((index - 4) * D, D)]
        return w_fc2.at[layer, pl.ds((index - count) * shard, shard)]

    def fetch(group):
        if group < len(groups):
            layer, first, size = groups[group]
            slot = group % raw.shape[0]
            for k in range(size // shard):
                pltpu.make_async_copy(square(layer, first // shard + k), raw.at[slot, k], raw_sem.at[slot, k]).start()

    def prepare(group):
        layer, first, size = groups[group]
        slot = group % raw.shape[0]
        for k in range(size // shard):
            pltpu.make_async_copy(square(layer, first // shard + k), raw.at[slot, k], raw_sem.at[slot, k]).wait()
            packed[layer, pl.ds(first + k * shard, shard)] = raw[slot, k].astype(jnp.bfloat16)
        fetch(group + raw.shape[0])

    gather = Gather(
        pace, groups, spot, packed, full,
        {"z": (z_s, z_r), "y": (y_s, y_r), "x": (x_s, x_r), "c": (c_s, c_r), "keep": keep_sem}, prepare, loads,
    )
    for group in range(raw.shape[0]):
        fetch(group)

    def rows_of(name, k, first=0, size=None):
        at, height = places_of[name]
        return small[pl.ds((at + first) * ways + k, size or height, stride=ways)]

    def piece(name):
        return jnp.concatenate([rows_of(name, k) for k in range(ways)], axis=1)
    offsets = [(i, j) for i in range(dps) for j in range(reps) if i or j]
    everyone = [((dp + i) % dps, (rep + j) % reps) for i, j in offsets]
    meet(everyone)
    mine = dp * reps + rep
    id_copies = [push(ids, ids_all.at[mine], i_s.at[n], i_r.at[n], peer) for n, peer in enumerate(everyone)]
    for copy in id_copies:
        copy.start()
    ids_all[mine] = ids[...]
    ready = []

    def mods_start():
        for copy in id_copies:
            copy.wait_recv()
        for k in range(ways):
            lanes = pl.ds(k * LANES, LANES)
            time1_w[:, lanes] = rows_of("time1_w", k).astype(jnp.bfloat16)
            time2_w[:, lanes] = rows_of("time2_w", k).astype(jnp.bfloat16)
        conditions(
            ids_all[...].reshape(dps * reps * 8, LANES), time1_w, piece("time1_b"), time2_w, piece("time2_b"),
            piece("class_tab"), hidden_t, condition,
        )
        chosen = [condition[pl.ds(pl.multiple_of((d * reps + rep) * 8, 8), 8)] for d in range(dps)]
        group_c = silu(jnp.concatenate(chosen, axis=0)).astype(jnp.bfloat16)
        rows_mod = w_mod.shape[0]
        entry = lax.broadcasted_iota(jnp.int32, (D, rows_mod), 0)
        lane = lax.broadcasted_iota(jnp.int32, (D, rows_mod), 1)
        select = (entry == lane + dp * rows_mod).astype(jnp.bfloat16)
        own = dot_nn(group_c, select).astype(jnp.bfloat16)
        for k in range(entries):
            value = dot_nn(own, w_mod[:, k * D : (k + 1) * D].astype(jnp.bfloat16))
            for d in range(dps):
                for image in range(images):
                    row = 8 * d + image
                    mod_part[d // Y_SIZE, d % Y_SIZE, pl.ds(image * entries + k, 1)] = value[row : row + 1]
        gather.go(mod_part.at[:, 1 - y], mod_y, (my_s, my_r), gather.across_y)
        return 9.0, pace.send("y", 4 * mod_part.shape[2] * D * 4)

    def mods_across():
        gather.arrive(mod_y, (my_s, my_r))
        for k in range(Z_SIZE):
            mod_y[k] = mod_y[k] + mod_part[k, y]
        for k in range(1, Z_SIZE):
            peer = (z + k) % Z_SIZE
            gather.go(mod_y.at[peer], mod_z.at[z], (mz_s.at[k - 1], mz_r.at[k - 1]), gather.z_peers[k - 1])
        return 1.5, pace.send("z", 4 * mod_part.shape[2] * D * 4)

    def mods_end():
        mod_z[z] = mod_y[z]
        for k in range(1, Z_SIZE):
            gather.arrive(mod_z.at[(z - k) % Z_SIZE], (mz_s.at[k - 1], mz_r.at[k - 1]))
        value = (mod_z[0] + mod_z[1]) + (mod_z[2] + mod_z[3])
        shift = piece("mod_b")
        for image in range(images):
            for k in range(entries):
                row = image * entries + k
                mods[image, k] = value[row : row + 1] + shift[k : k + 1]
        ready.append(True)
        return 1.0, None

    steps = [mods_start, mods_across, mods_end]
    pace.now = 8.0
    for _ in range(2):
        gather.start()
    pace.add(pace.now + 3.0, lambda: steps.pop(0)())
    pace.add(pace.free["z"] - 9.0, gather.start)

    def need(layer, which):
        index = min(which, count)
        last = (index if index < count else count + deep // shard - 1) * shard
        first = min(last, index * shard)
        wanted = {
            g for g, (at, begin, size) in enumerate(groups) if at == layer and first < begin + size and begin <= last
        }
        pace.until(lambda: wanted <= gather.done)
        load(layer, which).wait()

    patch_w = piece("patch_w").astype(jnp.bfloat16)
    strip = PDIM // PATCH
    weights = jnp.concatenate([patch_w[u * strip : (u + 1) * strip] for u in range(PATCH) for _ in range(GRID)], axis=0)
    shift = piece("patch_b")
    for image in range(images):
        rows = pl.ds(image * GRID * GRID, GRID * GRID)
        x_v[rows] = dot_nn(picked[rows], weights) + shift + places[...]
    pace.spend(1.5)
    saves = {}

    def save(layer, source, target, index):
        copy = pltpu.make_async_copy(source, target.at[layer], save_sem.at[layer, index])
        copy.start()
        saves[index] = copy

    def reuse(index):
        copy = saves.pop(index, None)
        if copy is not None:
            copy.wait()

    for layer in range(LAYERS):
        base = 6 * layer
        save(layer, x_v, x_h, 0)
        pace.until(lambda: ready)
        modulate(x_v, mods, base, base + 1, mixed, tokens)
        pace.spend(1.0)
        reuse(1)
        for p in range(3):
            need(layer, p)

            def project(i, p=p, layer=layer):
                value = dot_nn(mixed[...], whole(w_in[layer, p, :, :, columns(i)]))
                if p != 1:
                    value = value + biases[layer, p // 2, :, columns(i)]
                proj_v[p, :, columns(i)] = value.astype(jnp.bfloat16)

            each(D // TILE, project)
            pace.spend(1.1)
        save(layer, proj_v, proj_h, 1)
        reuse(2)
        for pair in range(0, HEADS // 2, 2):
            attention_forward(proj_v, att_v, images, pair, 2)
            pace.spend(2.3)
        save(layer, att_v, att_h, 2)
        reuse(3)
        reuse(4)
        need(layer, 3)

        def first_branch(i, layer=layer, base=base):
            value = dot_nn(att_v[...], whole(w_in[layer, 3, :, :, columns(i)]))
            value = value + biases[layer, 2, :, columns(i)]
            branch_a[:, columns(i)] = value
            for image in range(images):
                rows = pl.ds(image * GRID * GRID, GRID * GRID)
                part = value[image * GRID * GRID : (image + 1) * GRID * GRID]
                middle[rows, columns(i)] = x_v[rows, columns(i)] + mods[image, base + 2, :, columns(i)] * part

        each(D // TILE, first_branch)
        save(layer, branch_a, branch_a_h, 3)
        save(layer, middle, middle_h, 4)
        modulate(middle, mods, base + 3, base + 4, mixed, tokens)
        pace.spend(2.3)
        for block in range(FF_BLOCKS):
            need(layer, 4 + block)

            def expand(i, block=block, layer=layer):
                hidden = dot_nn(mixed[...], whole(w_in[layer, 4 + block, :, :, columns(i)]))
                hidden = hidden + biases[layer, 3 + block, :, columns(i)]
                inner = jnp.tanh(GELU_A * (hidden + GELU_B * hidden * hidden * hidden))
                active[block, :, columns(i)] = (0.5 * hidden * (1.0 + inner)).astype(jnp.bfloat16)

            each(D // TILE, expand)
            pace.spend(2.2)
        reuse(5)
        for block in range(FF_BLOCKS):
            need(layer, count + block)

            def contract(i, block=block, layer=layer):
                value = dot_nn(active[block], whole(w_out[layer, block, :, :, columns(i)]))
                if block == 0:
                    branch_b[:, columns(i)] = value + biases[layer, 3 + FF_BLOCKS, :, columns(i)]
                else:
                    branch_b[:, columns(i)] += value

            each(D // TILE, contract)
            pace.spend(1.1)
        save(layer, branch_b, branch_b_h, 5)
        reuse(0)

        def finish(rows, image, base=base):
            x_v[rows] = middle[rows] + mods[image, base + 5] * branch_b[rows]

        row_blocks(tokens, finish)
        pace.spend(1.0)
    last = pltpu.make_async_copy(x_v, out, out_sem)
    last.start()
    pace.drain()
    for copy in saves.values():
        copy.wait()
    last.wait()
    gather.finish()
    for copy in id_copies:
        copy.wait_send()


def run_forward(picked, places, ids, w_qkv, w_proj, w_fc1, w_fc2, w_mod, small, places_of, biases, images):
    tokens = picked.shape[0]
    layers = w_qkv.shape[0]
    owners, everyone = Z_SIZE * Y_SIZE, Z_SIZE * Y_SIZE * X_SIZE * C_SIZE
    shard, deep = D // owners, FF // owners
    height, width = (4 + FF_BLOCKS) * shard + deep, D
    wide, low = jnp.float32, jnp.bfloat16
    entries = MOD // D
    mod_rows = -(-images * entries // 8) * 8
    keep = [
        ((tokens, D), wide), ((3, tokens, D), low), ((tokens, D), low),
        ((tokens, D), wide), ((tokens, D), wide), ((tokens, D), wide),
    ]
    groups = [(layer, first, 2 * shard) for layer in range(layers) for first in range(0, height, 2 * shard)]
    number = len(groups)
    dma = pltpu.SemaphoreType.DMA
    vmem, anywhere = pl.BlockSpec(memory_space=pltpu.VMEM), pl.BlockSpec(memory_space=pl.ANY)
    outs = [
        jax.ShapeDtypeStruct((tokens, D), wide),
        jax.ShapeDtypeStruct((layers, owners, height, width), low),
        jax.ShapeDtypeStruct((images, entries, 1, D), wide),
        jax.ShapeDtypeStruct((everyone,) + ids.shape, wide),
        jax.ShapeDtypeStruct((everyone * ids.shape[0], D), wide),
        jax.ShapeDtypeStruct((everyone * ids.shape[0], D), wide),
    ]
    return pl.pallas_call(
        partial(forward_kernel, groups, places_of),
        out_shape=outs + [jax.ShapeDtypeStruct((layers,) + shape, kind) for shape, kind in keep],
        in_specs=[vmem] * 3 + [anywhere] * 4 + [vmem] * 3,
        out_specs=[anywhere, anywhere, vmem, vmem, vmem, vmem] + [anywhere] * len(keep),
        scratch_shapes=[
            pltpu.VMEM((layers, 4 + FF_BLOCKS, owners, shard, D), low),
            pltpu.VMEM((layers, FF_BLOCKS, D // deep, deep, D), low),
        ]
        + [pltpu.VMEM(shape, kind) for shape, kind in keep]
        + [
            pltpu.VMEM((tokens, D), low),
            pltpu.VMEM((FF_BLOCKS, tokens, D), low),
            pltpu.VMEM((Z_SIZE, Y_SIZE, mod_rows, D), wide),
            pltpu.VMEM((Z_SIZE, mod_rows, D), wide),
            pltpu.VMEM((Z_SIZE, mod_rows, D), wide),
            pltpu.VMEM((layers, height, width), low),
            pltpu.VMEM((3, 2, shard, D), wide),
            pltpu.VMEM((FREQ, D), low),
            pltpu.VMEM((D, D), low),
            dma((3, 2)),
            dma,
            dma((layers, 4 + 2 * FF_BLOCKS)),
            dma((layers, len(keep))),
            dma((everyone - 1,)),
            dma((everyone - 1,)),
            dma((number, Z_SIZE - 1)),
            dma((number, Z_SIZE - 1)),
            dma((number,)),
            dma((number,)),
            dma((number, 2)),
            dma((number, 2)),
            dma((number, 3)),
            dma((number, 3)),
            dma((number,)),
            dma,
            dma,
            dma((Z_SIZE - 1,)),
            dma((Z_SIZE - 1,)),
        ],
        compiler_params=pltpu.CompilerParams(
            collective_id=2, has_side_effects=True, vmem_limit_bytes=63 * 2**20
        ),
        name="blocks_forward",
    )(picked, places, ids, w_qkv, w_proj, w_fc1, w_fc2, w_mod, small, biases)


class Reduction:
    COSTS = (0.6, 0.4, 0.8, 0.5, 0.4, 0.1)

    def __init__(self, pace, groups, shard, spot, buffers, semaphores, credits, finals):
        self.pace, self.groups, self.shard, self.spot = pace, groups, shard, spot
        self.held, self.from_c, self.from_x, self.from_y, self.from_z, self.from_fin = buffers
        self.sems, self.credits, self.finals = semaphores, credits, finals
        z, y, x, c = spot
        self.z_peers = [device((z + k) % Z_SIZE, y, x, c) for k in range(1, Z_SIZE)]
        self.z_before = [device((z - k) % Z_SIZE, y, x, c) for k in range(1, Z_SIZE)]
        self.across_y, self.across_x = device(z, 1 - y, x, c), device(z, y, 1 - x, c)
        self.sibling = device(z, y, x, 1 - c)
        self.started, self.kept, self.filled, self.busy = {}, {}, {}, {}
        self.at_half = [first for first, _, _ in groups]
        self.halves = [rows for _, rows, _ in groups]
        self.parts = [part for _, _, part in groups]
        most = [rows - part for _, rows, part in groups]
        self.at_part = [sum(self.parts[:g]) for g in range(len(groups))]
        self.at_most = [sum(most[:g]) for g in range(len(groups))]

    def peers(self):
        return self.z_peers + [self.across_y, self.across_x, self.sibling]

    def go(self, key, source, target, sems, peer):
        copy = push(source, target, sems[0], sems[1], peer)
        copy.start()
        self.started.setdefault(key, []).append(copy)

    def arrive(self, ref, sems):
        push(ref, ref, sems[0], sems[1], self.across_y).wait_recv()

    def sem(self, name, layer, *index):
        send, receive = self.sems[name]
        return send.at[(layer,) + index], receive.at[(layer,) + index]

    def give(self, layer, name, peer, *index):
        if layer == LAYERS - 1:
            pl.semaphore_signal(
                self.credits[name].at[index], inc=1, device_id=peer, device_id_type=MESH_IDS
            )

    def take(self, layer, name, *index):
        if layer != LAYERS - 1:
            pl.semaphore_wait(self.credits[name].at[index], 1)

    def put(self, layer, group, stage, first, squares, owner_z, slot):
        c = self.spot[3]
        half = self.shard // 2
        if (layer, group) not in self.filled:
            while (layer + 1, group) in self.busy:
                self.pace.spend(0.5)
            for copy in self.started.pop((layer + 1, group), []):
                copy.wait_send()
            self.take(layer, "c", group)
            self.filled[layer, group] = []
        rows = pl.ds(first, squares * half)
        theirs = stage.at[:, :, :, pl.ds(pl.multiple_of((1 - c) * half, 16), half)]
        ours = stage.at[:, :, :, pl.ds(pl.multiple_of(c * half, 16), half)]
        zs = stage.shape[0]

        def view(ref):
            pieces = ref.reshape(Z_SIZE, Y_SIZE, ref.shape[2] // half, half, D)
            return pieces.at[pl.ds(owner_z, zs), :, pl.ds(first // half, squares)]

        sems = self.sem("c", layer, group, slot)
        send = push(theirs, view(self.from_c), sems[0], sems[1], self.sibling)
        keep = pltpu.make_async_copy(ours, view(self.held), self.sems["keep"].at[layer, group, slot])
        send.start()
        keep.start()
        self.filled[layer, group].append((slot, owner_z, zs, rows))
        self.kept[layer, group, slot] = keep
        self.ready = self.pace.send("c", zs * Y_SIZE * squares * half * D * 2)

        def free():
            send.wait_send()
            self.keep_wait(layer, group, slot)

        return free

    def begin(self, layer, group):
        stages = [self.on_c, self.on_x, self.on_y, self.on_z, self.on_fin, self.on_last]
        costs = list(self.COSTS)
        self.busy[layer, group] = True

        def run():
            ready = stages.pop(0)(layer, group)
            if not stages:
                del self.busy[layer, group]
            return costs.pop(0), ready

        self.pace.add(self.ready, run)

    def keep_wait(self, *key):
        keep = self.kept.pop(key, None)
        if keep is not None:
            keep.wait()

    def add(self, target, extra):
        def body(owner):
            total = target[owner].astype(jnp.float32) + extra[owner].astype(jnp.float32)
            target[owner] = total.astype(jnp.bfloat16)

        each(Z_SIZE, body)

    def on_c(self, layer, group):
        z, y, x, c = self.spot
        half, part = self.halves[group], self.parts[group]
        first = self.at_half[group]
        for slot, owner_z, zs, rows in self.filled[layer, group]:
            self.keep_wait(layer, group, slot)
            self.arrive(self.from_c.at[pl.ds(owner_z, zs), :, rows], self.sem("c", layer, group, slot))
        theirs = pl.ds(pl.multiple_of(first + (1 - x) * (half - part), 16), part)
        ours = pl.ds(pl.multiple_of(first + x * part, 16), half - part)
        for side in range(Y_SIZE):
            self.add(self.held.at[:, side, theirs], self.from_c.at[:, side, theirs])
        target = self.from_x.at[:, :, pl.ds(self.at_part[group], part)]
        self.take(layer, "x", group)
        self.go((layer, group), self.held.at[:, :, theirs], target, self.sem("x", layer, group), self.across_x)
        for side in range(Y_SIZE):
            self.add(self.held.at[:, side, ours], self.from_c.at[:, side, ours])
        self.give(layer, "c", self.sibling, group)
        return self.pace.send("x", 8 * part * D * 2)

    def on_x(self, layer, group):
        z, y, x, c = self.spot
        half, part = self.halves[group], self.parts[group]
        first = self.at_half[group]
        got = self.from_x.at[:, :, pl.ds(self.at_part[group], part)]
        self.arrive(got, self.sem("x", layer, group))
        ours = pl.ds(pl.multiple_of(first + x * (half - part), 16), part)
        for side in (1 - y, y):
            self.add(self.held.at[:, side, ours], self.from_x.at[:, side, pl.ds(self.at_part[group], part)])
        self.give(layer, "x", self.across_x, group)
        most = pl.ds(pl.multiple_of(first + x * part, 16), half - part)
        self.take(layer, "y", group)
        self.go(
            (layer, group), self.held.at[:, 1 - y, most], self.from_y.at[:, pl.ds(self.at_most[group], half - part)],
            self.sem("y", layer, group), self.across_y,
        )
        return self.pace.send("y", 4 * (half - part) * D * 2)

    def on_y(self, layer, group):
        z, y, x, c = self.spot
        half, part = self.halves[group], self.parts[group]
        got = self.from_y.at[:, pl.ds(self.at_most[group], half - part)]
        self.arrive(got, self.sem("y", layer, group))
        most = pl.ds(pl.multiple_of(self.at_half[group] + x * part, 16), half - part)
        self.add(self.held.at[:, y, most], got)
        self.give(layer, "y", self.across_y, group)
        for k in range(1, Z_SIZE):
            self.take(layer, "z", group, k - 1)
            self.go(
                (layer, group), self.held.at[(z + k) % Z_SIZE, y, most],
                self.from_z.at[k - 1, pl.ds(self.at_most[group], half - part)],
                self.sem("z", layer, group, k - 1), self.z_peers[k - 1],
            )
        return self.pace.send("z", self.pace.along_z * (half - part) * D * 2)

    def on_z(self, layer, group):
        z, y, x, c = self.spot
        half, part = self.halves[group], self.parts[group]
        most = pl.ds(pl.multiple_of(self.at_half[group] + x * part, 16), half - part)
        got = pl.ds(self.at_most[group], half - part)
        for k in range(1, Z_SIZE):
            self.arrive(self.from_z.at[k - 1, got], self.sem("z", layer, group, k - 1))
        total = self.held[z, y, most].astype(jnp.float32)
        for k in range(1, Z_SIZE):
            total = total + self.from_z[k - 1, got].astype(jnp.float32)
        self.held[z, y, most] = total.astype(jnp.bfloat16)
        for k in range(1, Z_SIZE):
            self.give(layer, "z", self.z_before[k - 1], group, k - 1)
        self.take(layer, "e", group)
        self.go((layer, group), self.held.at[z, y, most], self.from_fin.at[got], self.sem("e", layer, group), self.across_x)
        return self.pace.send("x", (half - part) * D * 2)

    def on_fin(self, layer, group):
        z, y, x, c = self.spot
        half, part = self.halves[group], self.parts[group]
        middle = half - 2 * part
        base, start = self.at_most[group], self.at_half[group]
        self.arrive(self.from_fin.at[pl.ds(base, half - part)], self.sem("e", layer, group))
        wide = jnp.float32

        def span(begin, size):
            return pl.ds(pl.multiple_of(begin, 16), size)

        ours, theirs = span(start + x * (half - part), part), span(start + (1 - x) * (half - part), part)
        both = span(start + part, middle)
        self.finals[layer, c, ours] = self.held[z, y, ours].astype(wide)
        self.finals[layer, c, theirs] = self.from_fin[span(base + (1 - x) * middle, part)].astype(wide)
        self.finals[layer, c, both] = self.held[z, y, both].astype(wide) + self.from_fin[
            span(base + x * part, middle)
        ].astype(wide)
        self.give(layer, "e", self.across_x, group)
        ref = self.finals.at[layer, c, pl.ds(start, half)]
        self.go((layer, group), ref, ref, self.sem("f", layer, group), self.sibling)
        return self.pace.send("c", half * D * 4)

    def on_last(self, layer, group):
        c = self.spot[3]
        ref = self.finals.at[layer, 1 - c, pl.ds(self.at_half[group], self.halves[group])]
        self.arrive(ref, self.sem("f", layer, group))
        return None

    def finish(self):
        for copies in self.started.values():
            for copy in copies:
                copy.wait_send()


class Sums:
    def __init__(self, reduction, own, total, small_c, small_x, small_y, small_z, mods, mods_all, sems, mod_sems, local):
        self.r = reduction
        self.own, self.total = own, total
        self.small_c, self.small_x, self.small_y, self.small_z = small_c, small_x, small_y, small_z
        self.mods, self.mods_all, self.v, self.m, self.local = mods, mods_all, sems, mod_sems, local
        self.stages = [self.first, self.to_x, self.to_y, self.to_z, self.to_c, self.last]

    def sem(self, pair, index):
        return pair[0].at[index], pair[1].at[index]

    def go(self, ref, target, pair, index, peer):
        self.r.go("sums", ref, target, self.sem(pair, index), peer)

    def arrive(self, ref, pair, index):
        self.r.arrive(ref, self.sem(pair, index))

    def run(self):
        self.stages.pop(0)()
        return 1.0, self.r.pace.now + 7.0 if self.stages else None

    def halves(self):
        span = self.small_c.shape[0]
        c = self.r.spot[3]
        return [pl.ds(pl.multiple_of(i * span, 8), span) for i in (c, 1 - c)]

    def first(self):
        z, y, x, c = self.r.spot
        mine, other = self.halves()
        self.go(self.own.at[other], self.small_c, self.v, 0, self.r.sibling)
        own = self.mods_all.at[z, y, x * C_SIZE + c]
        keep = pltpu.make_async_copy(self.mods, own, self.local)
        keep.start()
        for k in range(1, Z_SIZE):
            self.go(self.mods, own, self.m, k - 1, self.r.z_peers[k - 1])
        keep.wait()

    def to_x(self):
        z, y, x, c = self.r.spot
        mine, other = self.halves()
        self.arrive(self.small_c, self.v, 0)
        self.small_c[...] = self.small_c[...] + self.own[mine]
        self.go(self.small_c, self.small_x, self.v, 1, self.r.across_x)
        slot = x * C_SIZE + c
        for k in range(1, Z_SIZE):
            self.arrive(self.mods_all.at[(z - k) % Z_SIZE, y, slot], self.m, k - 1)
        ref = self.mods_all.at[:, y, slot]
        self.go(ref, ref, self.m, 3, self.r.across_y)

    def to_y(self):
        z, y, x, c = self.r.spot
        self.arrive(self.small_x, self.v, 1)
        self.small_x[...] = self.small_x[...] + self.small_c[...]
        self.go(self.small_x, self.small_y, self.v, 2, self.r.across_y)
        slot = x * C_SIZE + c
        self.arrive(self.mods_all.at[:, 1 - y, slot], self.m, 3)
        ref = self.mods_all.at[:, :, slot]
        self.go(ref, ref, self.m, 4, self.r.across_x)

    def to_z(self):
        z, y, x, c = self.r.spot
        self.arrive(self.small_y, self.v, 2)
        self.small_z[z] = self.small_y[...] + self.small_x[...]
        own = self.small_z.at[z]
        for k in range(1, Z_SIZE):
            self.go(own, own, self.v, 2 + k, self.r.z_peers[k - 1])
        self.arrive(self.mods_all.at[:, :, (1 - x) * C_SIZE + c], self.m, 4)
        for k in range(X_SIZE):
            ref = self.mods_all.at[:, :, k * C_SIZE + c]
            self.go(ref, ref, self.m, 5 + k, self.r.sibling)

    def to_c(self):
        z, y, x, c = self.r.spot
        mine, other = self.halves()
        for k in range(1, Z_SIZE):
            self.arrive(self.small_z.at[(z - k) % Z_SIZE], self.v, 2 + k)
        self.total[mine] = (self.small_z[0] + self.small_z[1]) + (self.small_z[2] + self.small_z[3])
        self.go(self.total.at[mine], self.total.at[mine], self.v, 6, self.r.sibling)
        for k in range(X_SIZE):
            self.arrive(self.mods_all.at[:, :, k * C_SIZE + 1 - c], self.m, 5 + k)

    def last(self):
        mine, other = self.halves()
        self.arrive(self.total.at[other], self.v, 6)


def backward_kernel(
    groups, count_all, x_last, mods, biases, picked, wanted, head_w, head_b, full,
    x_h, proj_h, att_h, branch_a_h, middle_h, branch_b_h,
    finals, mods_all, sums_out,
    w_v, grad_x, x_v, proj_v, att_v, branch, middle, mixed, grad_b, active, grad_hidden, grad_mixed,
    grad_projected, stage, mods_acc, mods_tile, mods_low, sums,
    held, from_c, from_x, from_y, from_z, from_fin, small_c, small_x, small_y, small_z,
    w_sem, load_sem, last_sem, keep_sem, c_s, c_r, x_s, x_r, y_s, y_r, z_s, z_r, e_s, e_r, f_s, f_r,
    v_s, v_r, m_s, m_r, local, cred_c, cred_x, cred_y, cred_z, cred_e,
):
    tokens = x_last.shape[0]
    images = mods.shape[0]
    owners = full.shape[1]
    shard, deep = D // owners, FF // owners
    count = 4 + FF_BLOCKS
    per = D // deep
    slots = w_v.shape[0]
    spot = place()
    pace = Pace(52e3, 3.3)
    reduction = Reduction(
        pace, groups, shard, spot, (held, from_c, from_x, from_y, from_z, from_fin),
        {"c": (c_s, c_r), "x": (x_s, x_r), "y": (y_s, y_r), "z": (z_s, z_r), "e": (e_s, e_r), "f": (f_s, f_r), "keep": keep_sem},
        {"c": cred_c, "x": cred_x, "y": cred_y, "z": cred_z, "e": cred_e}, finals,
    )
    order = [i for b in range(FF_BLOCKS) for i in (4 + b, count + b)] + [3, 0, 1, 2]
    order = [(layer, index) for layer in reversed(range(LAYERS)) for index in order]

    def load(at):
        layer, index = order[at]
        slot = at % slots
        target = w_v.at[slot]
        if index < count:
            return pltpu.make_async_copy(
                full.at[layer, :, pl.ds(index * shard, shard)], target.reshape(owners, shard, D), w_sem.at[slot]
            )
        return pltpu.make_async_copy(
            full.at[layer, pl.ds((index - count) * per, per), pl.ds(count * shard, deep)],
            target.reshape(per, deep, D),
            w_sem.at[slot],
        )

    def fetch(at):
        if at < len(order):
            load(at).start()

    def weight(at):
        load(at).wait()
        return w_v.at[at % slots]

    def total(values):
        return jnp.sum(values, axis=0, keepdims=True)

    last_copy = pltpu.make_async_copy(x_last, grad_x, last_sem)
    last_copy.start()
    for at in range(slots):
        fetch(at)
    meet(reduction.peers())
    sums[...] = jnp.zeros_like(sums)
    mods_acc[...] = jnp.zeros_like(mods_acc)
    last_copy.wait()
    final = 6 * LAYERS
    modulate(grad_x, mods, final, final + 1, mixed, tokens)
    picks, wide = wanted.shape[1], head_w.shape[1]
    strip = PDIM // PATCH
    pixel = lax.broadcasted_iota(jnp.int32, (picks, wide), 0)
    entry = lax.broadcasted_iota(jnp.int32, (picks, wide), 1)
    select = (entry == pixel // (picks // PATCH) * strip + pixel % strip).astype(jnp.float32)
    target = jnp.dot(wanted[...], select, precision=HIGHEST, preferred_element_type=jnp.float32)
    error = dot_nn(mixed[...], head_w[...]) + head_b[...] - target
    grad_low = (error * (2.0 / count_all)).astype(jnp.bfloat16)
    sums[pl.ds(PDIM, PDIM)] = dot_tn(grad_low, mixed[...])[:PDIM]
    lane = lax.broadcasted_iota(jnp.int32, (1, wide), 1)
    sums[pl.ds(2 * PDIM, 1), pl.ds(0, wide)] = jnp.where(
        lane == PDIM, jnp.sum(error * error), total(grad_low.astype(jnp.float32))
    )
    for i in range(D // TILE):
        grad_mixed[:, columns(i)] = dot_nt(grad_low, head_w[columns(i)])

    def head(rows, image):
        grad = grad_mixed[rows]
        normed, inverse = centre(grad_x[rows])
        mods_acc[image, final] += total(grad)
        mods_acc[image, final + 1] += total(grad * normed)
        grad = grad * (1.0 + mods[image, final + 1])
        grad_x[rows] = inverse * (
            grad - jnp.mean(grad, axis=-1, keepdims=True) - normed * jnp.mean(grad * normed, axis=-1, keepdims=True)
        )

    row_blocks(tokens, head)
    busy = [[], []]
    turn = [0]

    def weight_grad(layer, left, right, index):
        slot = turn[0] % 2
        turn[0] += 1
        for wait in busy[slot]:
            wait()

        def body(i):
            cut = block_at(i, D // 2)
            value = dot_tn(left[:, cut], right[...]).astype(jnp.bfloat16)
            stage[slot, cut] = value

        each(2, body)
        half = shard // 2
        if index < count:
            group = next(g for g, entry in enumerate(groups) if entry[0] <= index * half < entry[0] + entry[1])
            view = stage.at[slot].reshape(Z_SIZE, Y_SIZE, 1, shard, D)
            busy[slot] = [
                reduction.put(layer, group, view, index * half, 1, 0, (index * half - groups[group][0]) // half)
            ]
            if index * half == groups[group][0] + groups[group][1] - half:
                reduction.begin(layer, group)
        else:
            block = index - count
            busy[slot] = []
            for group, (first, rows, _) in enumerate(groups):
                if first >= count * half:
                    squares = rows // half
                    view = stage.at[slot].reshape(1, Y_SIZE, deep // shard, shard, D)
                    view = view.at[:, :, pl.ds((first - count * half) // half, squares)]
                    busy[slot].append(reduction.put(layer, group, view, first, squares, block, block))
                    if block == FF_BLOCKS - 1:
                        reduction.begin(layer, group)
        pace.spend(1.3)

    for layer in reversed(range(LAYERS)):
        base = 6 * layer
        at = (LAYERS - 1 - layer) * (count + FF_BLOCKS)
        bias_row = 3 * PDIM + layer * (4 + FF_BLOCKS)

        def bias_add(k, values, cut=slice(None), bias_row=bias_row):
            sums[pl.ds(bias_row + k, 1), cut] += total(values)

        saved = [
            (branch_b_h, branch), (middle_h, middle), (att_h, att_v), (proj_h, proj_v), (x_h, x_v), (branch_a_h, branch),
        ]
        copies = [
            pltpu.make_async_copy(source.at[layer], target, load_sem.at[i])
            for i, (source, target) in enumerate(saved)
        ]
        for copy in copies[:-1]:
            copy.start()
        copies[0].wait()
        copies[1].wait()

        def enter(rows, image, base=base, bias_add=bias_add):
            grad = grad_x[rows]
            low = (mods[image, base + 5] * grad).astype(jnp.bfloat16)
            grad_b[rows] = low
            bias_add(3 + FF_BLOCKS, low.astype(jnp.float32))
            mods_acc[image, base + 5] += total(grad * branch[rows])
            normed, _ = centre(middle[rows])
            mixed[rows] = (normed * (1.0 + mods[image, base + 4]) + mods[image, base + 3]).astype(jnp.bfloat16)

        row_blocks(tokens, enter)
        pace.spend(1.8)
        copies[-1].start()
        for block in range(FF_BLOCKS):
            w_one, w_two = weight(at), weight(at + 1)

            def expand(i, block=block, w_one=w_one, w_two=w_two, layer=layer, bias_add=bias_add):
                hidden = dot_nn(mixed[...], w_one[:, columns(i)]) + biases[layer, 3 + block, :, columns(i)]
                square = hidden * hidden
                inner = jnp.tanh(GELU_A * (hidden + GELU_B * hidden * square))
                active[:, columns(i)] = (0.5 * hidden * (1.0 + inner)).astype(jnp.bfloat16)
                slope = 0.5 * (1.0 + inner) + 0.5 * hidden * (1.0 - inner * inner) * (
                    GELU_A * (1.0 + 3.0 * GELU_B * square)
                )
                low = (slope * dot_nt(grad_b[...], w_two[columns(i)])).astype(jnp.bfloat16)
                grad_hidden[:, columns(i)] = low
                bias_add(3 + block, low.astype(jnp.float32), columns(i))

            each(D // TILE, expand)
            pace.spend(3.6)
            weight_grad(layer, active, grad_b, count + block)

            def back(i, block=block, w_one=w_one):
                value = dot_nt(grad_hidden[...], w_one[columns(i)])
                if block == 0:
                    grad_mixed[:, columns(i)] = value
                else:
                    grad_mixed[:, columns(i)] += value

            each(D // TILE, back)
            pace.spend(1.0)
            fetch(at + slots)
            fetch(at + slots + 1)
            weight_grad(layer, mixed, grad_hidden, 4 + block)
            at += 2
        for copy in copies[2:]:
            copy.wait()

        def leave(rows, image, base=base, bias_add=bias_add):
            grad = grad_mixed[rows]
            normed, inverse = centre(middle[rows])
            mods_acc[image, base + 3] += total(grad)
            mods_acc[image, base + 4] += total(grad * normed)
            grad = grad * (1.0 + mods[image, base + 4])
            grad = grad_x[rows] + inverse * (
                grad - jnp.mean(grad, axis=-1, keepdims=True) - normed * jnp.mean(grad * normed, axis=-1, keepdims=True)
            )
            middle[rows] = grad
            low = (mods[image, base + 2] * grad).astype(jnp.bfloat16)
            grad_b[rows] = low
            bias_add(2, low.astype(jnp.float32))
            mods_acc[image, base + 2] += total(grad * branch[rows])
            normed, _ = centre(x_v[rows])
            mixed[rows] = (normed * (1.0 + mods[image, base + 1]) + mods[image, base]).astype(jnp.bfloat16)

        row_blocks(tokens, leave)
        pace.spend(2.6)
        w_proj = weight(at)

        def through(i, w_proj=w_proj):
            active[:, columns(i)] = dot_nt(grad_b[...], w_proj[columns(i)]).astype(jnp.bfloat16)

        each(D // TILE, through)
        pace.spend(0.9)
        fetch(at + slots)
        weight_grad(layer, att_v, grad_b, 3)
        for image in range(images):
            for pair in range(0, HEADS // 2, 2):
                attention_backward(proj_v, active, grad_projected, image, pair, 2)
                pace.spend(2.1)
        for p in range(3):
            w_part = weight(at + 1 + p)

            def into(i, p=p, w_part=w_part):
                value = dot_nt(grad_projected[p], w_part[columns(i)])
                if p == 0:
                    grad_mixed[:, columns(i)] = value
                else:
                    grad_mixed[:, columns(i)] += value

            weight_grad(layer, mixed, grad_projected.at[p], p)
            each(D // TILE, into)
            pace.spend(1.0)
            fetch(at + 1 + p + slots)

        def last(rows, image, base=base, bias_add=bias_add):
            grad = grad_mixed[rows]
            normed, inverse = centre(x_v[rows])
            mods_acc[image, base] += total(grad)
            mods_acc[image, base + 1] += total(grad * normed)
            grad = grad * (1.0 + mods[image, base + 1])
            grad_x[rows] = middle[rows] + inverse * (
                grad - jnp.mean(grad, axis=-1, keepdims=True) - normed * jnp.mean(grad * normed, axis=-1, keepdims=True)
            )
            bias_add(0, grad_projected[0, rows].astype(jnp.float32))
            bias_add(1, grad_projected[2, rows].astype(jnp.float32))

        row_blocks(tokens, last)
        pace.spend(2.2)

    def patch(rows, image):
        low = grad_x[rows].astype(jnp.bfloat16)
        grad_b[rows] = low
        sums[pl.ds(2 * PDIM + 8, 1)] += total(low.astype(jnp.float32))

    row_blocks(tokens, patch)
    value = dot_tn(picked[...], grad_b[...])
    for u in range(PATCH):
        first = u * strip * GRID
        part = value[first : first + strip]
        for j in range(1, GRID):
            part = part + value[first + j * strip : first + (j + 1) * strip]
        sums[pl.ds(u * strip, strip)] = part
    mods_tile[...] = jnp.zeros_like(mods_tile)
    entries = mods.shape[1]
    for image in range(images):
        for k in range(entries):
            mods_tile[pl.ds(image * entries + k, 1)] = mods_acc[image, k]
    mods_low[...] = mods_tile[...].astype(jnp.bfloat16)
    small = Sums(
        reduction, sums, sums_out, small_c, small_x, small_y, small_z, mods_low, mods_all, (v_s, v_r), (m_s, m_r), local
    )
    pace.add(pace.now, small.run)
    pace.drain()
    reduction.finish()
    for waits in busy:
        for wait in waits:
            wait()


def run_backward(count_all, x_last, mods, biases, picked, wanted, head_w, head_b, full, kept):
    tokens = x_last.shape[0]
    images, entries = mods.shape[:2]
    layers, owners, height, width = full.shape
    shard = D // owners
    count = 4 + FF_BLOCKS
    piece = shard // 2
    sizes = [(2, 1), (1, 1), (1, 1), (2, 2), (2, 1), (2, 2), (2, 1)]
    groups = []
    for squares, thirds in sizes:
        first = sum(group[1] for group in groups)
        groups.append((first, squares * piece, thirds * piece // 3))
    half = height // 2
    part = sum(group[2] for group in groups)
    most = half - part
    wide, low = jnp.float32, jnp.bfloat16
    vmem, anywhere = pl.BlockSpec(memory_space=pltpu.VMEM), pl.BlockSpec(memory_space=pl.ANY)
    rows = (tokens, D)
    dma, regular = pltpu.SemaphoreType.DMA, pltpu.SemaphoreType.REGULAR
    number = len(groups)
    sum_rows = 3 * PDIM + LAYERS * count
    mod_rows = -(-images * entries // 16) * 16
    pair = [dma((layers, number))] * 2
    return pl.pallas_call(
        partial(backward_kernel, groups, count_all),
        out_shape=[
            jax.ShapeDtypeStruct((layers, 2, half, width), wide),
            jax.ShapeDtypeStruct((Z_SIZE, Y_SIZE, X_SIZE * C_SIZE, mod_rows, D), low),
            jax.ShapeDtypeStruct((sum_rows, D), wide),
        ],
        in_specs=[anywhere] + [vmem] * 6 + [anywhere] * 7,
        out_specs=[vmem] * 3,
        scratch_shapes=[
            pltpu.VMEM((4, D, D), low),
            pltpu.VMEM(rows, wide),
            pltpu.VMEM(rows, wide),
            pltpu.VMEM((3,) + rows, low),
            pltpu.VMEM(rows, low),
            pltpu.VMEM(rows, wide),
            pltpu.VMEM(rows, wide),
            pltpu.VMEM(rows, low),
            pltpu.VMEM(rows, low),
            pltpu.VMEM(rows, low),
            pltpu.VMEM(rows, low),
            pltpu.VMEM(rows, wide),
            pltpu.VMEM((3,) + rows, low),
            pltpu.VMEM((2, D, D), low),
            pltpu.VMEM((images, entries, 1, D), wide),
            pltpu.VMEM((mod_rows, D), wide),
            pltpu.VMEM((mod_rows, D), low),
            pltpu.VMEM((sum_rows, D), wide),
            pltpu.VMEM((Z_SIZE, Y_SIZE, half, D), low),
            pltpu.VMEM((Z_SIZE, Y_SIZE, half, D), low),
            pltpu.VMEM((Z_SIZE, Y_SIZE, part, D), low),
            pltpu.VMEM((Z_SIZE, most, D), low),
            pltpu.VMEM((Z_SIZE - 1, most, D), low),
            pltpu.VMEM((most, D), low),
            pltpu.VMEM((sum_rows // 2, D), wide),
            pltpu.VMEM((sum_rows // 2, D), wide),
            pltpu.VMEM((sum_rows // 2, D), wide),
            pltpu.VMEM((Z_SIZE, sum_rows // 2, D), wide),
            dma((4,)),
            dma((6,)),
            dma,
            dma((layers, number, FF_BLOCKS)),
            dma((layers, number, FF_BLOCKS)),
            dma((layers, number, FF_BLOCKS)),
            *pair,
            *pair,
            dma((layers, number, Z_SIZE - 1)),
            dma((layers, number, Z_SIZE - 1)),
            *pair,
            *pair,
            dma((7,)),
            dma((7,)),
            dma((7,)),
            dma((7,)),
            dma,
            regular((number,)),
            regular((number,)),
            regular((number,)),
            regular((number, Z_SIZE - 1)),
            regular((number,)),
        ],
        compiler_params=pltpu.CompilerParams(
            collective_id=3, has_side_effects=True, vmem_limit_bytes=63 * 2**20
        ),
        name="blocks_backward",
    )(x_last, mods, biases, picked, wanted, head_w, head_b, full, *kept)


KINDS = [("qkv", 0, 3), ("proj", 3, 1), ("fc1", 4, FF // D), ("fc2", 4 + FF // D, 1)]


def statistics_kernel(
    finals, mods_all, silu_rows, w_qkv, w_proj, w_fc1, w_fc2, w_mod,
    row_qkv, row_proj, row_fc1, row_fc2, row_mod,
    cond_all, mod_b_grad, picked, stats, qkv_row, proj_row, fc1_row, fc2_row, mod_row,
    mod_grad, lined, sums, pieces, cond, c_s, c_r, p_s, p_r, g_s, g_r, r_s, r_r,
):
    dp, rep = lax.axis_index("dp"), lax.axis_index("rep")
    dps, reps = Z_SIZE * Y_SIZE, X_SIZE * C_SIZE
    dp_peers = [((dp + k) % dps, rep) for k in range(1, dps)]
    rep_peers = [(dp, (rep + k) % reps) for k in range(1, reps)]
    barrier = pltpu.get_barrier_semaphore()
    for peer in dp_peers + rep_peers:
        pl.semaphore_signal(barrier, inc=1, device_id=peer, device_id_type=MESH_IDS)
    beta = 1.0 - STEP ** (-0.8)
    shard, half = w_mod.shape[0], w_mod.shape[0] // 2
    entries, images = picked.shape[0], picked.shape[1]
    ways = D // LANES
    per = 5 + FF_BLOCKS
    mats = [(w_qkv, row_qkv, qkv_row), (w_proj, row_proj, proj_row), (w_fc1, row_fc1, fc1_row), (w_fc2, row_fc2, fc2_row)]
    columns_all = LAYERS * per + entries
    scalars = LAYERS * len(KINDS) + 1
    at_row, at_weight = 2 * columns_all, 2 * columns_all + scalars

    def over_rows(values):
        return jnp.sum(values, axis=0, keepdims=True)

    def over_all(values):
        return jnp.sum(jnp.sum(values, axis=1, keepdims=True), axis=0, keepdims=True)

    stats[...] = jnp.zeros_like(stats)
    lined[...] = jnp.zeros_like(lined)
    cond[...] = jnp.zeros_like(cond)

    number = mods_all.shape[0] // (dps * reps)
    here = images // (dps * reps)
    row = lax.broadcasted_iota(jnp.int32, (images, mods_all.shape[0]), 0)
    at = lax.broadcasted_iota(jnp.int32, (images, mods_all.shape[0]), 1)
    back = jnp.zeros((images, shard), jnp.float32)
    for k in range(entries):
        wanted = row // here * number + row % here * entries + k
        picked[k] = dot_nn((at == wanted).astype(jnp.bfloat16), mods_all[...]).astype(jnp.bfloat16)
        mod_b_grad[pl.ds(k, 1)] = over_rows(picked[k].astype(jnp.float32))
        back = back + dot_nt(picked[k], w_mod[:, k * D : (k + 1) * D].astype(jnp.bfloat16))
    cond[:, pl.ds(0, shard)] = back

    def first_pass(blocks, rows, row_old, width, row_out, weights, stat):
        total = jnp.zeros((rows, 1), jnp.float32)
        for grad, _ in blocks:
            value = grad()
            total = total + jnp.sum(value * value + EPS_ONE, axis=1, keepdims=True)
        factor = beta * row_old + (1.0 - beta) * (total / width)
        row_out(factor)
        inverse = 1.0 / factor
        for grad, index in blocks:
            value = grad()
            value = value * value
            stats[pl.ds(index, 1)] += over_rows(value + EPS_ONE)
            stats[pl.ds(columns_all + index, 1)] += over_rows(value * inverse)
        stats[pl.ds(at_row + stat, 1)] += over_rows(factor)
        for weight in weights:
            stats[pl.ds(at_weight + stat, 1), pl.ds(0, 1)] += over_all(weight() * weight())

    def block(layer, index, core):
        return lambda: finals[layer, core, pl.ds(index * half, half)]

    for layer in range(LAYERS):
        for kind, (name, first, count) in enumerate(KINDS):
            weight, row_old, row_new = mats[kind]
            stat = layer * len(KINDS) + kind
            tall = weight.shape[1] // shard
            for part in range(tall):
                for core in range(C_SIZE):
                    rows = pl.ds(part * shard + core * half, half)
                    blocks, weights = [], []
                    for j in range(count):
                        grad = block(layer, first + part + j, core)
                        cut = pl.ds(j * D, D)
                        blocks.append((grad, layer * per + first + j))
                        weights.append(lambda rows=rows, cut=cut, weight=weight, layer=layer: weight[layer, rows, cut])

                    def keep(value, rows=rows, row_new=row_new, layer=layer):
                        row_new[layer, rows] = value

                    first_pass(blocks, half, row_old[layer, rows], count * D, keep, weights, stat)
    blocks, weights = [], []
    for k in range(entries):
        cut = pl.ds(k * D, D)
        mod_grad[:, cut] = dot_tn(silu_rows[...], picked[k])
        blocks.append((lambda cut=cut: mod_grad[:, cut], LAYERS * per + k))
        weights.append(lambda cut=cut: w_mod[:, cut])

    def keep_mod(value):
        mod_row[...] = value

    first_pass(blocks, shard, row_mod[...], entries * D, keep_mod, weights, scalars - 1)

    for k in range(ways):
        lined[pl.ds(k, stats.shape[0], stride=ways)] = stats[:, k * LANES : (k + 1) * LANES]
    quarter = lined.shape[0] // reps
    size = quarter // dps
    copies = []

    def go(source, target, sems, index, peer):
        copy = push(source, target, sems[0].at[index], sems[1].at[index], peer)
        copy.start()
        copies.append(copy)
        return copy

    def part_of(owner):
        return pl.ds(pl.multiple_of(rep * quarter + owner * size, 8), size)

    pl.semaphore_wait(barrier, len(dp_peers + rep_peers))
    first = [go(lined.at[part_of(peer[0])], pieces.at[dp], (p_s, p_r), k, peer) for k, peer in enumerate(dp_peers)]
    spread = [go(cond, cond_all.at[dp], (c_s, c_r), k, peer) for k, peer in enumerate(dp_peers)]
    cond_all[dp] = cond[...]
    pieces[dp] = lined[part_of(dp)]
    for copy in first:
        copy.wait_recv()
    value = pieces[0]
    for k in range(1, dps):
        value = value + pieces[k]
    sums[part_of(dp)] = value
    own = sums.at[part_of(dp)]
    second = [go(own, own, (g_s, g_r), k, peer) for k, peer in enumerate(dp_peers)]
    for copy in second:
        copy.wait_recv()
    own = sums.at[pl.ds(pl.multiple_of(rep * quarter, 8), quarter)]
    third = [go(own, own, (r_s, r_r), k, peer) for k, peer in enumerate(rep_peers)]
    for copy in third + spread:
        copy.wait_recv()
    for k in range(ways):
        stats[:, pl.ds(k * LANES, LANES)] = sums[pl.ds(k, stats.shape[0], stride=ways)]

    for copy in copies:
        copy.wait_send()


def update_kernel(
    finals, picked, stats, silu_rows, w_qkv, w_proj, w_fc1, w_fc2, w_mod,
    row_qkv, row_proj, row_fc1, row_fc2, row_mod, col_qkv, col_proj, col_fc1, col_fc2, col_mod,
    qkv_new, qkv_grad, qkv_col, qkv_low,
    proj_new, proj_grad, proj_col, proj_low,
    fc1_new, fc1_grad, fc1_col, fc1_low,
    fc2_new, fc2_grad, fc2_col, fc2_low,
    mod_new, mod_grad, mod_col, mod_low,
):
    dps = Z_SIZE * Y_SIZE
    beta = 1.0 - STEP ** (-0.8)
    shard, half = w_mod.shape[0], w_mod.shape[0] // 2
    entries = picked.shape[0]
    per = 5 + FF_BLOCKS
    mats = [
        (w_qkv, row_qkv, col_qkv, qkv_new, qkv_grad, qkv_col, qkv_low),
        (w_proj, row_proj, col_proj, proj_new, proj_grad, proj_col, proj_low),
        (w_fc1, row_fc1, col_fc1, fc1_new, fc1_grad, fc1_col, fc1_low),
        (w_fc2, row_fc2, col_fc2, fc2_new, fc2_grad, fc2_col, fc2_low),
    ]
    columns_all = LAYERS * per + entries
    scalars = LAYERS * len(KINDS) + 1
    at_row, at_weight = 2 * columns_all, 2 * columns_all + scalars

    def scale_of(indices, col_old, col_new, stat, rows_all):
        width = len(indices) * D
        row_mean = stats[pl.ds(at_row + stat, 1), pl.ds(0, 1)] / rows_all
        weight_rms = jnp.sqrt(stats[pl.ds(at_weight + stat, 1), pl.ds(0, 1)] / (rows_all * width))
        update_sq = jnp.zeros((1, 1), jnp.float32)
        sides = []
        for j, index in enumerate(indices):
            cut = slice(j * D, (j + 1) * D)
            value = beta * col_old[:, cut] + (1.0 - beta) * (stats[pl.ds(index, 1)] / rows_all)
            col_new(j, value)
            update_sq = update_sq + jnp.sum(stats[pl.ds(columns_all + index, 1)] / value, axis=1, keepdims=True)
            sides.append(lax.rsqrt(value))
        update_rms = jnp.sqrt(row_mean * update_sq / (rows_all * width))
        rate = RATE * jnp.maximum(0.001, weight_rms) / jnp.maximum(1.0, update_rms / CLIP)
        return row_mean, rate, sides

    for layer in range(LAYERS):
        for kind, (name, first_square, count) in enumerate(KINDS):
            weight, row_new, col_old, new, grad_out, col_new, low = mats[kind]
            indices = [layer * per + first_square + j for j in range(count)]

            def put(j, value, col_new=col_new, layer=layer):
                col_new[layer, :, pl.ds(j * D, D)] = value

            row_mean, rate, sides = scale_of(
                indices, col_old[layer], put, layer * len(KINDS) + kind, float(weight.shape[1] * dps)
            )
            for step in range(weight.shape[1] // half):
                rows = pl.ds(step * half, half)
                left = rate * lax.rsqrt(row_new[layer, rows] / row_mean)
                for j in range(count):
                    cut = pl.ds(j * D, D)
                    index = first_square + step // C_SIZE + j
                    grad = finals[layer, step % C_SIZE, pl.ds(index * half, half)]
                    grad_out[layer, rows, cut] = grad
                    value = weight[layer, rows, cut] - grad * left * sides[j]
                    new[layer, rows, cut] = value
                    low[layer, rows, cut] = value.astype(jnp.bfloat16)

    def put_mod(j, value):
        mod_col[:, pl.ds(j * D, D)] = value

    indices = [LAYERS * per + k for k in range(entries)]
    row_mean, rate, sides = scale_of(indices, col_mod[...], put_mod, scalars - 1, float(shard * dps))
    left = rate * lax.rsqrt(row_mod[...] / row_mean)
    for k in range(entries):
        cut = pl.ds(k * D, D)
        grad = dot_tn(silu_rows[...], picked[k])
        mod_grad[:, cut] = grad
        value = w_mod[:, cut] - grad * left * sides[k]
        mod_new[:, cut] = value
        mod_low[:, cut] = value.astype(jnp.bfloat16)


def run_update(finals, mods_all, silu_rows, kinds, w_mod, row_mod, col_mod):
    dps, reps = Z_SIZE * Y_SIZE, X_SIZE * C_SIZE
    wide, low = jnp.float32, jnp.bfloat16
    images, shard = silu_rows.shape
    entries = w_mod.shape[1] // D
    vmem = pl.BlockSpec(memory_space=pltpu.VMEM)
    dma = pltpu.SemaphoreType.DMA
    weights, rows, cols, outs = [], [], [], []
    for weight, row, col in kinds + [(w_mod, row_mod, col_mod)]:
        weights.append(weight)
        rows.append(row[..., None])
        cols.append(col[..., None, :])
        outs += [
            jax.ShapeDtypeStruct(weight.shape, wide),
            jax.ShapeDtypeStruct(weight.shape, wide),
            jax.ShapeDtypeStruct(cols[-1].shape, wide),
            jax.ShapeDtypeStruct(weight.shape, low),
        ]
    used = 2 * (LAYERS * (5 + FF_BLOCKS) + entries) + 2 * (LAYERS * len(KINDS) + 1)
    height = -(-used // 8) * 8
    lined = -(-height * D // LANES // (8 * dps * reps)) * 8 * dps * reps
    cond_all, mod_b_grad, picked, stats, *rows_new = pl.pallas_call(
        statistics_kernel,
        out_shape=[
            jax.ShapeDtypeStruct((dps, images, LANES), wide),
            jax.ShapeDtypeStruct((entries, D), wide),
            jax.ShapeDtypeStruct((entries, images, D), low),
            jax.ShapeDtypeStruct((height, D), wide),
        ]
        + [jax.ShapeDtypeStruct(row.shape, wide) for row in rows],
        in_specs=[vmem] * (3 + 2 * len(weights)),
        out_specs=[vmem] * (4 + len(rows)),
        scratch_shapes=[
            pltpu.VMEM(w_mod.shape, wide),
            pltpu.VMEM((lined, LANES), wide),
            pltpu.VMEM((lined, LANES), wide),
            pltpu.VMEM((dps, lined // (dps * reps), LANES), wide),
            pltpu.VMEM((images, LANES), wide),
        ]
        + [dma((dps - 1,))] * 6
        + [dma((reps - 1,))] * 2,
        compiler_params=pltpu.CompilerParams(
            collective_id=4, has_side_effects=True, vmem_limit_bytes=48 * 2**20
        ),
        name="statistics",
    )(finals, mods_all, silu_rows, *weights, *rows)
    results = pl.pallas_call(
        update_kernel,
        out_shape=outs,
        in_specs=[vmem] * (4 + 3 * len(weights)),
        out_specs=[vmem] * len(outs),
        compiler_params=pltpu.CompilerParams(vmem_limit_bytes=58 * 2**20),
        name="update_weights",
    )(finals, picked, stats, silu_rows, *weights, *rows_new, *cols)
    groups = [results[4 * i : 4 * i + 4] for i in range(len(weights))]
    return cond_all, mod_b_grad, [
        (new, grad, row[..., 0], col.reshape(col.shape[:-2] + col.shape[-1:]), rounded)
        for (new, grad, col, rounded), row in zip(groups, rows_new)
    ]


def line_up_kernel(offsets, *refs):
    pieces, (first, tail), out, spread = refs[: len(offsets)], refs[len(offsets) : -2], refs[-2], refs[-1]
    ways = D // LANES
    for piece, offset in zip(pieces, offsets):
        rows = piece.shape[0]
        for k in range(ways):
            out[pl.ds(ways * offset + k, rows, stride=ways)] = piece[:, k * LANES : (k + 1) * LANES]
    rows = tail.shape[0] * ways
    for k in range(ways):
        spread[pl.ds(k, tail.shape[0], stride=ways)] = tail[:, k * LANES : (k + 1) * LANES]
    moved = pltpu.roll(spread[...], PDIM, 1)
    lane = lax.broadcasted_iota(jnp.int32, (rows, LANES), 1)
    spread[pl.ds(1, rows - 1)] = moved[: rows - 1]
    spread[pl.ds(0, 1)] = first[...]
    start = out.shape[0] - rows - 1
    out[pl.ds(start, rows)] = jnp.where(lane >= PDIM, moved, spread[...])
    out[pl.ds(start + rows, 1)] = moved[rows - 1 :]


def line_up(pieces, first, tail):
    offsets, at = [], 0
    for piece in pieces:
        offsets.append(at)
        at += piece.shape[0]
    ways = D // LANES
    vmem = pl.BlockSpec(memory_space=pltpu.VMEM)
    count = (at + tail.shape[0]) * ways + 1
    return pl.pallas_call(
        partial(line_up_kernel, offsets),
        out_shape=jax.ShapeDtypeStruct((count, LANES), jnp.float32),
        in_specs=[vmem] * (len(pieces) + 2),
        out_specs=vmem,
        scratch_shapes=[pltpu.VMEM((tail.shape[0] * ways, LANES), jnp.float32)],
        compiler_params=pltpu.CompilerParams(vmem_limit_bytes=32 * 2**20),
        name="line_up",
    )(*pieces, first, tail)


def local(
    latents,
    noise_field,
    timesteps,
    labels,
    drop_mask,
    roster,
    w_qkv,
    w_proj,
    w_fc1,
    w_fc2,
    w_mod,
    row_qkv,
    col_qkv,
    row_proj,
    col_proj,
    row_fc1,
    col_fc1,
    row_fc2,
    col_fc2,
    row_mod,
    col_mod,
    small,
    small_second,
):
    pieces = unpack(small)
    dp_size, rep_size = lax.axis_size("dp"), lax.axis_size("rep")
    everyone = dp_size * rep_size
    number = latents.shape[0] * latents.shape[1]
    count_all = number * everyone * GRID * GRID * PDIM
    rows_mod = w_mod.shape[0]
    first_row = lax.axis_index("dp") * rows_mod
    places = position_table()
    patch_low = pieces["patch_w"].astype(jnp.bfloat16)
    time1_low = pieces["time1_w"].astype(jnp.bfloat16)
    time2_low = pieces["time2_w"].astype(jnp.bfloat16)
    head_low = pieces["head_w"].astype(jnp.bfloat16)
    mod_shard = w_mod.astype(jnp.bfloat16)

    direct = (dp_size, rep_size) == (Z_SIZE * Y_SIZE, X_SIZE * C_SIZE) and rows_mod % 96 == 0
    picker = (timesteps.reshape(-1)[:, None] == jnp.arange(STEPS_T)[None, :]).astype(jnp.float32)
    factors = jnp.dot(picker, roster.T, precision=HIGHEST)
    noise_flat = noise_field.reshape(number, -1)
    noised = factors[:, 0:1] * latents.reshape(number, -1) + factors[:, 1:2] * noise_flat
    own_ids = jnp.stack([timesteps, labels, drop_mask]).reshape(3, number)
    if direct:
        tile = jnp.pad(own_ids.T.astype(jnp.float32), ((0, 8 - number), (0, LANES - 3)))
        column = jnp.arange(2 * LANES)[None, None, :] % LANES // (PATCH * CHAN)
        own_place = column == jnp.arange(GRID)[None, :, None]

        def pick(values):
            values = values.reshape(number * GRID, 1, PATCH * LANES)
            return jnp.where(own_place, values, jnp.zeros_like(values)).reshape(-1, PATCH * LANES)

        picked, wanted = pick(noised.astype(jnp.bfloat16)), pick(noise_flat)
        rows_at, places_of = 0, {}
        for piece_name, piece_dims in layout()[:8]:
            height = math.prod(piece_dims) // D
            places_of[piece_name] = (rows_at, height)
            rows_at += height
        biases = pieces["block_b"].reshape(LAYERS, -1, 1, D)
        x_last, packed_full, mods, all_ids, hidden_t, condition, *kept_blocks = run_forward(
            picked,
            places,
            tile,
            w_qkv,
            w_proj,
            w_fc1,
            w_fc2,
            w_mod,
            small[: rows_at * D].reshape(-1, LANES),
            places_of,
            biases,
            number,
        )
        all_ids = all_ids[:, :number, :3].reshape(-1, 3).T.astype(jnp.int32)
        hidden_t = hidden_t.reshape(everyone, 8, D)[:, :number].reshape(-1, D)
        condition = condition.reshape(everyone, 8, D)[:, :number].reshape(-1, D)
    else:
        all_ids = lax.all_gather(own_ids, ("dp", "rep"), axis=0, tiled=False)
        all_ids = all_ids.transpose(1, 0, 2).reshape(3, everyone * number)
    features = time_features(all_ids[0]).astype(jnp.bfloat16)
    if not direct:
        hidden_t = product(features, time1_low) + pieces["time1_b"]
    silu_t = jax.nn.silu(hidden_t).astype(jnp.bfloat16)
    chosen = jnp.where(all_ids[2] == 1, CLASSES, all_ids[1])
    onehot = (chosen[:, None] == jnp.arange(CLASSES + 1)[None, :]).astype(jnp.float32)
    if not direct:
        condition = (
            product(silu_t, time2_low)
            + pieces["time2_b"]
            + jnp.dot(onehot, pieces["class_tab"], precision=HIGHEST)
        )
    silu_c = jax.nn.silu(condition).astype(jnp.bfloat16)
    silu_rows = lax.dynamic_slice_in_dim(silu_c, first_row, rows_mod, axis=1)
    if not direct:
        tokens = patchify(noised).astype(jnp.bfloat16)
        target = patchify(noise_flat).reshape(-1, PDIM)
        residual = (product(tokens.reshape(-1, PDIM), patch_low) + pieces["patch_b"]).reshape(
            number, GRID * GRID, D
        ) + places
        group_rows = lax.dynamic_index_in_dim(
            silu_rows.reshape(dp_size, rep_size, number, rows_mod),
            lax.axis_index("rep"),
            axis=1,
            keepdims=False,
        ).reshape(dp_size * number, rows_mod)
        mod_part = product(group_rows, mod_shard)
        mod_sum = lax.psum_scatter(mod_part, "dp", scatter_dimension=0, tiled=True)
        modulation = mod_sum + pieces["mod_b"]
    if direct:
        head_wide = jnp.pad(head_low, ((0, 0), (0, LANES - PDIM)))
        head_shift = jnp.pad(pieces["head_b"], (0, LANES - PDIM))[None]
        finals, mod_all, sums = run_backward(
            count_all, x_last, mods, biases, picked, wanted, head_wide, head_shift, packed_full, kept_blocks
        )
        loss_total = sums[2 * PDIM, PDIM]
    else:
        kept_all = []
        gathered_all = []
        spans_all = []
        for layer_index in range(LAYERS):
            weights = tuple(
                lax.all_gather(w[layer_index].astype(jnp.bfloat16), "dp", axis=0, tiled=True)
                for w in (w_qkv, w_proj, w_fc1, w_fc2)
            )
            spans = [
                modulation[:, None, D * (6 * layer_index + i) : D * (6 * layer_index + i + 1)]
                for i in range(6)
            ]
            residual, kept = layer_forward(residual, spans, weights, pieces["block_b"][layer_index])
            kept_all.append(kept)
            gathered_all.append(weights)
            spans_all.append(spans)
        final_shift = modulation[:, None, 6 * D * LAYERS : 6 * D * LAYERS + D]
        final_scale = modulation[:, None, 6 * D * LAYERS + D :]
        normed_f, inverse_f = norm_rows(residual)
        final_in = (normed_f * (1.0 + final_scale) + final_shift).astype(jnp.bfloat16).reshape(-1, D)
        output = product(final_in, head_low) + pieces["head_b"]
        error = output - target
        loss_own = jnp.sum(error * error)
        grad_output = (error * (2.0 / count_all)).astype(jnp.bfloat16)
        grad_head = product(final_in.T, grad_output)
        grad_head_b = jnp.sum(grad_output.astype(jnp.float32), axis=0)
        grad_final = product(grad_output, head_low.T).reshape(number, GRID * GRID, D)
        final_grads = [jnp.sum(grad_final, axis=1), jnp.sum(grad_final * normed_f, axis=1)]
        grad_res = norm_back(grad_final * (1.0 + final_scale), normed_f, inverse_f)
        layer_spans = [None] * LAYERS
        bias_grads = [None] * LAYERS
        block_grads = [None] * LAYERS
        for layer_index in reversed(range(LAYERS)):
            grad_res, grads, grad_bias, grad_spans = layer_backward(
                grad_res, spans_all[layer_index], gathered_all[layer_index], kept_all[layer_index]
            )
            layer_spans[layer_index] = grad_spans
            bias_grads[layer_index] = grad_bias
            block_grads[layer_index] = tuple(
                lax.psum_scatter(g, "dp", scatter_dimension=0, tiled=True) for g in grads
            )

        grad_start = grad_res.reshape(-1, D).astype(jnp.bfloat16)
        grad_patch = product(tokens.reshape(-1, PDIM).T, grad_start)
        grad_patch_b = jnp.sum(grad_start.astype(jnp.float32), axis=0)
        own_sums = jnp.concatenate(
            [
                grad_patch.reshape(-1),
                grad_patch_b,
                grad_head.reshape(-1),
                jnp.stack(bias_grads).reshape(-1),
                grad_head_b,
                loss_own[None],
            ]
        )
        own_mod = jnp.concatenate(layer_spans + final_grads, axis=-1).astype(jnp.bfloat16)
        grad_qkv, grad_proj, grad_fc1, grad_fc2 = lax.psum(
            tuple(jnp.stack([block_grads[i][k] for i in range(LAYERS)]) for k in range(4)), "rep"
        )
        grad_mod = lax.all_gather(own_mod, ("dp", "rep"), axis=0, tiled=True)
        summed = lax.psum(own_sums, ("dp", "rep"))
        cut_patch = (PDIM + 1) * D
        cut_head = cut_patch + D * PDIM
        cut_bias = cut_head + LAYERS * (4 * D + FF)
        loss_total = summed[cut_bias + PDIM]
        sum_patch = summed[:cut_patch]
        sum_head = jnp.append(summed[cut_patch:cut_head], summed[cut_bias : cut_bias + PDIM])
        sum_bias = summed[cut_head:cut_bias]

    beta = 1.0 - STEP ** (-0.8)
    if direct:
        kinds = [
            (w_qkv, row_qkv, col_qkv),
            (w_proj, row_proj, col_proj),
            (w_fc1, row_fc1, col_fc1),
            (w_fc2, row_fc2, col_fc2),
        ]
        cond_all, grad_mod_b, results = run_update(
            finals, mod_all.reshape(-1, D), silu_rows, kinds, w_mod, row_mod, col_mod
        )
        cond_rows = cond_all[:, :, :rows_mod].transpose(1, 0, 2).reshape(-1, D)
        results[4] = tuple(entry[None] for entry in results[4])
    else:
        grad_wmod = product(silu_rows.T, grad_mod)
        grad_mod_b = jnp.sum(grad_mod.astype(jnp.float32), axis=0)
        kinds = [
            (w_qkv, grad_qkv, row_qkv, col_qkv),
            (w_proj, grad_proj, row_proj, col_proj),
            (w_fc1, grad_fc1, row_fc1, col_fc1),
            (w_fc2, grad_fc2, row_fc2, col_fc2),
            (w_mod[None], grad_wmod[None], row_mod[None], col_mod[None]),
        ]
        firsts = []
        for weight, grad, row, col in kinds:
            square = grad * grad
            row_new = beta * row + (1.0 - beta) * jnp.mean(square + EPS_ONE, axis=-1)
            firsts.append(
                (
                    row_new,
                    jnp.sum(square + EPS_ONE, axis=-2),
                    jnp.sum(square / row_new[:, :, None], axis=-2),
                    jnp.sum(row_new, axis=-1),
                    jnp.sum(weight * weight, axis=(-2, -1)),
                )
            )
        stats = jnp.concatenate([entry[k].reshape(-1) for k in range(1, 5) for entry in firsts])
        cond_rows = lax.all_gather(product(grad_mod, mod_shard.T), "dp", axis=1, tiled=True)
        shared = lax.psum(stats, "dp")
        rows_dp = dp_size
        parts = []
        offset = 0
        for k in range(1, 5):
            for entry in firsts:
                parts.append(shared[offset : offset + entry[k].size].reshape(entry[k].shape))
                offset += entry[k].size
        seconds = []
        for index, kind in enumerate(kinds):
            weight, grad, row, col = kind
            rows_all = weight.shape[1] * rows_dp
            col_count = weight.shape[2]
            col_sum, over_rows, row_sum, weight_sq = (parts[index + len(kinds) * k] for k in range(4))
            row_mean = row_sum / rows_all
            weight_rms = jnp.sqrt(weight_sq / (rows_all * col_count))
            col_new = beta * col + (1.0 - beta) * col_sum / rows_all
            update_sq = row_mean * jnp.sum(over_rows / col_new, axis=-1)
            estimate = firsts[index][0][:, :, None] * col_new[:, None, :] / row_mean[:, None, None]
            update = grad * lax.rsqrt(estimate)
            seconds.append((update, col_new, weight_rms, update_sq / (rows_all * col_count)))
        results = []
        for kind, first, second in zip(kinds, firsts, seconds):
            weight, grad = (kind[0], kind[1])
            update, col_new, weight_rms, update_ms = second
            update_rms = jnp.sqrt(update_ms)
            update = update / jnp.maximum(1.0, update_rms / CLIP)[:, None, None]
            new_weight = weight - (RATE * jnp.maximum(0.001, weight_rms))[:, None, None] * update
            results.append((new_weight, grad, first[0], col_new, new_weight.astype(jnp.bfloat16)))
    _, silu_pull = jax.vjp(jax.nn.silu, condition)
    grad_cond = silu_pull(cond_rows)[0].astype(jnp.bfloat16)
    grad_class = jnp.dot(onehot.T, grad_cond.astype(jnp.float32), precision=HIGHEST)
    grad_time2 = product(silu_t.T, grad_cond)
    grad_time2_b = jnp.sum(grad_cond.astype(jnp.float32), axis=0)
    _, silu_time_pull = jax.vjp(jax.nn.silu, hidden_t)
    grad_hidden_t = silu_time_pull(product(grad_cond, time2_low.T))[0].astype(jnp.bfloat16)
    grad_time1 = product(features.T, grad_hidden_t)
    grad_time1_b = jnp.sum(grad_hidden_t.astype(jnp.float32), axis=0)
    if direct:
        lined = line_up(
            [
                sums[:PDIM],
                sums[2 * PDIM + 8 :][:1],
                grad_time1,
                grad_time1_b[None],
                grad_time2,
                grad_time2_b[None],
                grad_class,
                grad_mod_b,
                sums[PDIM : 2 * PDIM].T.reshape(-1, D),
            ],
            sums[2 * PDIM : 2 * PDIM + 1, :LANES],
            sums[3 * PDIM :],
        )
        small_grad = lined.reshape(-1)[: small.shape[0]]
    else:
        small_grad = jnp.concatenate(
            [
                sum_patch,
                grad_time1.reshape(-1),
                grad_time1_b,
                grad_time2.reshape(-1),
                grad_time2_b,
                grad_class.reshape(-1),
                grad_mod_b,
                sum_head,
                sum_bias,
            ]
        )
    square = small_grad * small_grad + EPS_ONE
    small_second_new = beta * small_second + (1.0 - beta) * square
    update = small_grad * lax.rsqrt(small_second_new)
    update = update / jnp.maximum(1.0, jnp.sqrt(jnp.mean(update * update)) / CLIP)
    small_new = small - RATE * jnp.maximum(0.001, jnp.sqrt(jnp.mean(small * small))) * update
    mod_result = results[4]
    return (
        loss_total,
        results[0][0],
        results[0][1],
        results[0][2],
        results[0][3],
        results[0][4],
        results[1][0],
        results[1][1],
        results[1][2],
        results[1][3],
        results[1][4],
        results[2][0],
        results[2][1],
        results[2][2],
        results[2][3],
        results[2][4],
        results[3][0],
        results[3][1],
        results[3][2],
        results[3][3],
        results[3][4],
        mod_result[0][0],
        mod_result[1][0],
        mod_result[2][0],
        mod_result[3][0],
        mod_result[4][0],
        small_grad,
        small_second_new,
        small_new,
        small_new.astype(jnp.bfloat16),
    )


def solution(mesh):
    in_specs = (
        P(None, ("dp", "rep"), None),
        P(None, ("dp", "rep"), None),
        P(None, ("dp", "rep")),
        P(None, ("dp", "rep")),
        P(None, ("dp", "rep")),
        P(),
        P(None, "dp", None),
        P(None, "dp", None),
        P(None, "dp", None),
        P(None, "dp", None),
        P("dp", None),
        P(None, "dp"),
        P(),
        P(None, "dp"),
        P(),
        P(None, "dp"),
        P(),
        P(None, "dp"),
        P(),
        P("dp"),
        P(),
        P(),
        P(),
    )
    out_specs = (
        P(),
        P(None, "dp", None),
        P(None, "dp", None),
        P(None, "dp"),
        P(),
        P(None, "dp", None),
        P(None, "dp", None),
        P(None, "dp", None),
        P(None, "dp"),
        P(),
        P(None, "dp", None),
        P(None, "dp", None),
        P(None, "dp", None),
        P(None, "dp"),
        P(),
        P(None, "dp", None),
        P(None, "dp", None),
        P(None, "dp", None),
        P(None, "dp"),
        P(),
        P(None, "dp", None),
        P("dp", None),
        P("dp", None),
        P("dp"),
        P(),
        P("dp", None),
        P(),
        P(),
        P(),
        P(),
    )
    return jax.shard_map(local, mesh=mesh, in_specs=in_specs, out_specs=out_specs, check_vma=False)
```

```python
from functools import partial
import math

import jax
import jax.numpy as jnp
from jax import lax
from jax.experimental import pallas as pl
from jax.experimental.pallas import tpu as pltpu
from jax.sharding import PartitionSpec as P

D = 768
HEADS = 12
FF = 3072
FREQ = 256
CLASSES = 32
GRID = 16
PATCH = 2
CHAN = 4
LAYERS = 2
MICRO = 2
STEPS_T = 1000
STEP = 10
PDIM = 16
MOD = 10752


HIGHEST = lax.Precision.HIGHEST
EPS_NORM = 1e-06
EPS_ONE = 1e-30
CLIP = 0.5
RATE = 0.6


def product(left, right):
    return jnp.dot(left, right, preferred_element_type=jnp.float32)


def layout():
    return [
        ("patch_w", (PDIM, D)),
        ("patch_b", (D,)),
        ("time1_w", (FREQ, D)),
        ("time1_b", (D,)),
        ("time2_w", (D, D)),
        ("time2_b", (D,)),
        ("class_tab", (CLASSES + 1, D)),
        ("mod_b", (MOD,)),
        ("head_w", (D, PDIM)),
        ("head_b", (PDIM,)),
        ("block_b", (LAYERS, 4 * D + FF)),
    ]


def unpack(small):
    pieces = {}
    offset = 0
    for piece_name, piece_dims in layout():
        piece_size = math.prod(piece_dims)
        pieces[piece_name] = small[offset : offset + piece_size].reshape(piece_dims)
        offset += piece_size
    return pieces


def position_table():
    quarter = D // 4
    omega = jnp.exp(-math.log(10000.0) * jnp.arange(quarter, dtype=jnp.float32) / quarter)
    places = jnp.arange(GRID * GRID, dtype=jnp.int32)
    across = (places // GRID).astype(jnp.float32)[:, None] * omega
    downward = (places % GRID).astype(jnp.float32)[:, None] * omega
    return jnp.concatenate(
        [jnp.sin(across), jnp.cos(across), jnp.sin(downward), jnp.cos(downward)], axis=1
    )


def time_features(timesteps):
    half_count = FREQ // 2
    frequency = jnp.exp(-math.log(10000.0) * jnp.arange(half_count, dtype=jnp.float32) / half_count)
    angles = timesteps.astype(jnp.float32)[:, None] * frequency
    return jnp.concatenate([jnp.cos(angles), jnp.sin(angles)], axis=1)


def patchify(flat):
    number = flat.shape[0]
    blocks = flat.reshape(number, GRID, PATCH, GRID, PATCH, CHAN).transpose(0, 1, 3, 2, 4, 5)
    return blocks.reshape(number, GRID * GRID, PDIM)


def norm_rows(values):
    centered = values - jnp.mean(values, axis=-1, keepdims=True)
    inverse = lax.rsqrt(jnp.mean(centered * centered, axis=-1, keepdims=True) + EPS_NORM)
    return (centered * inverse, inverse)


def norm_back(grad, normed, inverse):
    return inverse * (
        grad
        - jnp.mean(grad, axis=-1, keepdims=True)
        - normed * jnp.mean(grad * normed, axis=-1, keepdims=True)
    )


def layer_forward(residual, spans, weights, biases):
    number, seq_tokens = (residual.shape[0], residual.shape[1])
    scaling = 1.0 / math.sqrt(D // HEADS)
    blank_bias = jnp.zeros((D,), jnp.float32)
    qkv_bias = jnp.concatenate([biases[:D], blank_bias, biases[D : 2 * D]])
    normed_a, inverse_a = norm_rows(residual)
    mixed_a = (normed_a * (1.0 + spans[1]) + spans[0]).astype(jnp.bfloat16)
    projected = (product(mixed_a.reshape(-1, D), weights[0]) + qkv_bias).astype(jnp.bfloat16)
    projected = projected.reshape(number, seq_tokens, 3, HEADS, D // HEADS)
    scores = (
        jnp.einsum(
            "bqhd,bkhd->bhqk",
            projected[:, :, 0],
            projected[:, :, 1],
            preferred_element_type=jnp.float32,
        )
        * scaling
    )
    total_lse = jax.nn.logsumexp(scores, axis=-1, keepdims=True)
    attention = jnp.exp(scores - total_lse).astype(jnp.bfloat16)
    attended = jnp.einsum(
        "bhqk,bkhd->bqhd", attention, projected[:, :, 2], preferred_element_type=jnp.float32
    )
    attended = attended.astype(jnp.bfloat16).reshape(-1, D)
    branch_a = product(attended, weights[1]) + biases[2 * D : 3 * D]
    middle = residual + spans[2] * branch_a.reshape(number, seq_tokens, D)
    normed_b, inverse_b = norm_rows(middle)
    mixed_b = (normed_b * (1.0 + spans[4]) + spans[3]).astype(jnp.bfloat16)
    hidden = product(mixed_b.reshape(-1, D), weights[2]) + biases[3 * D : 3 * D + FF]
    activated = jax.nn.gelu(hidden, approximate=True).astype(jnp.bfloat16)
    branch_b = product(activated, weights[3]) + biases[3 * D + FF :]
    result = middle + spans[5] * branch_b.reshape(number, seq_tokens, D)
    kept = (
        normed_a,
        inverse_a,
        mixed_a,
        projected,
        total_lse,
        attended,
        branch_a,
        normed_b,
        inverse_b,
        mixed_b,
        hidden,
        activated,
        branch_b,
    )
    return (result, kept)


def layer_backward(grad_out, spans, weights, kept):
    (
        normed_a,
        inverse_a,
        mixed_a,
        projected,
        total_lse,
        attended,
        branch_a,
        normed_b,
        inverse_b,
        mixed_b,
        hidden,
        activated,
        branch_b,
    ) = kept
    number, seq_tokens = (grad_out.shape[0], grad_out.shape[1])
    scaling = 1.0 / math.sqrt(D // HEADS)
    grad_b = (spans[5] * grad_out).reshape(-1, D).astype(jnp.bfloat16)
    gate_b = jnp.sum(grad_out * branch_b.reshape(number, seq_tokens, D), axis=1)
    grad_fc2 = product(activated.T, grad_b)
    bias_fc2 = jnp.sum(grad_b.astype(jnp.float32), axis=0)
    _, gelu_pull = jax.vjp(partial(jax.nn.gelu, approximate=True), hidden)
    grad_hidden = gelu_pull(product(grad_b, weights[3].T))[0].astype(jnp.bfloat16)
    grad_fc1 = product(mixed_b.reshape(-1, D).T, grad_hidden)
    bias_fc1 = jnp.sum(grad_hidden.astype(jnp.float32), axis=0)
    grad_mixed = product(grad_hidden, weights[2].T).reshape(number, seq_tokens, D)
    shift_b = jnp.sum(grad_mixed, axis=1)
    scale_b = jnp.sum(grad_mixed * normed_b, axis=1)
    grad_mid = grad_out + norm_back(grad_mixed * (1.0 + spans[4]), normed_b, inverse_b)
    grad_a = (spans[2] * grad_mid).reshape(-1, D).astype(jnp.bfloat16)
    gate_a = jnp.sum(grad_mid * branch_a.reshape(number, seq_tokens, D), axis=1)
    grad_proj = product(attended.T, grad_a)
    bias_proj = jnp.sum(grad_a.astype(jnp.float32), axis=0)
    grad_att = (
        product(grad_a, weights[1].T)
        .astype(jnp.bfloat16)
        .reshape(number, seq_tokens, HEADS, D // HEADS)
    )
    query, keys, values = (projected[:, :, 0], projected[:, :, 1], projected[:, :, 2])
    scores = (
        jnp.einsum("bqhd,bkhd->bhqk", query, keys, preferred_element_type=jnp.float32) * scaling
    )
    attention = jnp.exp(scores - total_lse)
    grad_values = jnp.einsum(
        "bhqk,bqhd->bkhd",
        attention.astype(jnp.bfloat16),
        grad_att,
        preferred_element_type=jnp.float32,
    )
    grad_weights = jnp.einsum(
        "bqhd,bkhd->bhqk", grad_att, values, preferred_element_type=jnp.float32
    )
    inner = jnp.sum(attention * grad_weights, axis=-1, keepdims=True)
    grad_scores = (attention * (grad_weights - inner)).astype(jnp.bfloat16)
    grad_query = (
        jnp.einsum("bhqk,bkhd->bqhd", grad_scores, keys, preferred_element_type=jnp.float32)
        * scaling
    )
    grad_keys = (
        jnp.einsum("bhqk,bqhd->bkhd", grad_scores, query, preferred_element_type=jnp.float32)
        * scaling
    )
    grad_projected = (
        jnp.stack([grad_query, grad_keys, grad_values], axis=2)
        .reshape(-1, 3 * D)
        .astype(jnp.bfloat16)
    )
    grad_qkv = product(mixed_a.reshape(-1, D).T, grad_projected)
    bias_sums = jnp.sum(grad_projected.astype(jnp.float32), axis=0)
    grad_mixed_a = product(grad_projected, weights[0].T).reshape(number, seq_tokens, D)
    shift_a = jnp.sum(grad_mixed_a, axis=1)
    scale_a = jnp.sum(grad_mixed_a * normed_a, axis=1)
    grad_in = grad_mid + norm_back(grad_mixed_a * (1.0 + spans[1]), normed_a, inverse_a)
    grad_spans = jnp.concatenate([shift_a, scale_a, gate_a, shift_b, scale_b, gate_b], axis=-1)
    grad_bias = jnp.concatenate([bias_sums[:D], bias_sums[2 * D :], bias_proj, bias_fc1, bias_fc2])
    return (grad_in, (grad_qkv, grad_proj, grad_fc1, grad_fc2), grad_bias, grad_spans)


MESH_IDS = pl.DeviceIdType.MESH
Z_SIZE, Y_SIZE, X_SIZE, C_SIZE = 4, 2, 2, 2
LANES = 128


def place():
    dp, rep = lax.axis_index("dp"), lax.axis_index("rep")
    return (dp // Y_SIZE, dp % Y_SIZE, rep // C_SIZE, rep % C_SIZE)


def device(z, y, x, c):
    return (z * Y_SIZE + y, x * C_SIZE + c)


def meet(peers):
    barrier = pltpu.get_barrier_semaphore()
    for peer in peers:
        pl.semaphore_signal(barrier, inc=1, device_id=peer, device_id_type=MESH_IDS)
    pl.semaphore_wait(barrier, len(peers))


def push(source, target, send, receive, peer):
    return pltpu.make_async_remote_copy(
        src_ref=source,
        dst_ref=target,
        send_sem=send,
        recv_sem=receive,
        device_id=peer,
        device_id_type=MESH_IDS,
    )


GELU_A, GELU_B = 0.79788456, 0.044715
FF_BLOCKS = FF // D
TILE = 256
ROWS = 64


def centre(values):
    centered = values - jnp.mean(values, axis=-1, keepdims=True)
    inverse = lax.rsqrt(jnp.mean(centered * centered, axis=-1, keepdims=True) + EPS_NORM)
    return centered * inverse, inverse


def dot_nn(left, right):
    return lax.dot_general(left, right, (((1,), (0,)), ((), ())), preferred_element_type=jnp.float32)


def dot_nt(left, right):
    return lax.dot_general(left, right, (((1,), (1,)), ((), ())), preferred_element_type=jnp.float32)


def dot_tn(left, right):
    return lax.dot_general(left, right, (((0,), (0,)), ((), ())), preferred_element_type=jnp.float32)


def each(count, body):
    if count <= 3:
        for i in range(count):
            body(i)
        return
    lax.fori_loop(0, count, lambda i, carry: (body(i), carry)[1], 0)


def row_blocks(tokens, body, step=ROWS):
    each(tokens // step, lambda i: body(pl.ds(pl.multiple_of(i * step, step), step), i // (GRID * GRID // step)))


def modulate(source, mods, shift, scale, target, tokens):
    def body(rows, image):
        normed, _ = centre(source[rows])
        target[rows] = (normed * (1.0 + mods[image, scale]) + mods[image, shift]).astype(jnp.bfloat16)

    row_blocks(tokens, body)


def block_at(i, size):
    return pl.ds(i * size if isinstance(i, int) else pl.multiple_of(i * size, size), size)


def columns(i):
    return block_at(i, TILE)


def head_lanes(head):
    lane = lax.broadcasted_iota(jnp.int32, (GRID * GRID, 2 * D // HEADS), 1)
    return lane // (D // HEADS) == head


def softmax(query, keys):
    scores = dot_nt(query, keys) * (1.0 / math.sqrt(D // HEADS))
    powers = jnp.exp(scores - jnp.max(scores, axis=-1, keepdims=True))
    return powers * (1.0 / jnp.sum(powers, axis=-1, keepdims=True))


def pick(lanes, values):
    return jnp.where(lanes, values, jnp.zeros_like(values))


def attention_forward(projected, attended, images, first_pair, pairs):
    size, width = GRID * GRID, 2 * D // HEADS

    def body(i, image):
        rows, lanes = block_at(image, size), block_at(first_pair + i, width)
        query, keys, values = (projected[p, rows, lanes] for p in range(3))
        first = head_lanes(0)
        outs = []
        for own in (first, jnp.logical_not(first)):
            weights = softmax(pick(own, query), keys).astype(jnp.bfloat16)
            outs.append(dot_nn(weights, values))
        attended[rows, lanes] = jnp.where(first, outs[0], outs[1]).astype(jnp.bfloat16)

    each(pairs, lambda i: [body(i, image) for image in range(images)])


def attention_backward(projected, grad_attended, grad_projected, image, first_pair, pairs):
    size, width = GRID * GRID, 2 * D // HEADS
    scaling = 1.0 / math.sqrt(D // HEADS)

    def body(i):
        rows, lanes = block_at(image, size), block_at(first_pair + i, width)
        query, keys, values = (projected[p, rows, lanes] for p in range(3))
        grad_out = grad_attended[rows, lanes]
        first = head_lanes(0)
        outs = []
        for own in (first, jnp.logical_not(first)):
            weights = softmax(pick(own, query), keys)
            grad_values = dot_tn(weights.astype(jnp.bfloat16), grad_out)
            grad_weights = dot_nt(pick(own, grad_out), values)
            inner = jnp.sum(weights * grad_weights, axis=-1, keepdims=True)
            grad_scores = (weights * (grad_weights - inner)).astype(jnp.bfloat16)
            outs.append(
                (dot_nn(grad_scores, keys) * scaling, dot_tn(grad_scores, query) * scaling, grad_values)
            )
        for p in range(3):
            grad_projected[p, rows, lanes] = jnp.where(first, outs[0][p], outs[1][p]).astype(jnp.bfloat16)

    each(pairs, body)


def whole(block):
    return block.reshape(D, block.shape[-1])


class Pace:
    LATENCY = 2.2

    def __init__(self, rate=48e3, along_z=4):
        self.rate, self.along_z = rate, along_z
        self.now = 0.0
        self.free = {}
        self.entries = []

    def send(self, link, count):
        rate = 10 * self.rate if link == "c" else self.rate
        self.free[link] = max(self.now, self.free.get(link, 0.0)) + count / rate
        return self.free[link] + self.LATENCY

    def add(self, ready, run):
        self.entries.append([ready, len(self.entries), run])

    def serve(self, entry):
        cost, ready = entry[2]()
        self.now += cost
        if ready is None:
            self.entries.remove(entry)
        else:
            entry[0] = ready

    def spend(self, cost):
        self.now += cost
        while self.entries:
            entry = min(self.entries, key=lambda e: e[:2])
            if entry[0] > self.now:
                return
            self.serve(entry)

    def next(self):
        entry = min(self.entries, key=lambda e: e[:2])
        self.now = max(self.now, entry[0])
        self.serve(entry)

    def until(self, done):
        while not done():
            self.next()

    def drain(self):
        while self.entries:
            self.next()


class Gather:
    def __init__(self, pace, groups, spot, packed, full, semaphores, prepare, loads):
        self.pace, self.groups, self.spot = pace, groups, spot
        self.packed = packed
        layers, owners, height, width = full.shape
        self.full = full.reshape(layers, Z_SIZE, Y_SIZE, height, width)
        self.sems, self.prepare, self.loads = semaphores, prepare, loads
        z, y, x, c = spot
        self.z_peers = [device((z + k) % Z_SIZE, y, x, c) for k in range(1, Z_SIZE)]
        self.across_y, self.across_x = device(z, 1 - y, x, c), device(z, y, 1 - x, c)
        self.sibling = device(z, y, x, 1 - c)
        self.done, self.copies, self.keeps = set(), [], {}
        self.waiting = list(range(len(groups)))

    def rows(self, group, third, count, core):
        _, first, size = self.groups[group]
        step = size // 6
        return pl.ds(pl.multiple_of(first + core * 3 * step + third * step, 16), count * step)

    def size(self, group, count):
        return self.groups[group][2] // 6 * count * D * 2

    def sem(self, name, group, *index):
        send, receive = self.sems[name]
        return send.at[(group,) + index], receive.at[(group,) + index]

    def go(self, source, target, sems, peer):
        copy = push(source, target, sems[0], sems[1], peer)
        copy.start()
        self.copies.append(copy)

    def arrive(self, ref, sems):
        push(ref, ref, sems[0], sems[1], self.across_y).wait_recv()

    def start(self):
        z, y, x, c = self.spot
        group = self.waiting.pop(0)
        layer = self.groups[group][0]
        self.prepare(group)
        own = self.packed.at[layer, self.rows(group, x, 2, c)]
        target = self.full.at[layer, z, y, self.rows(group, x, 2, c)]
        for k in range(1, Z_SIZE):
            self.go(own, target, self.sem("z", group, k - 1), self.z_peers[k - 1])
        keep = pltpu.make_async_copy(own, target, self.sems["keep"].at[group])
        keep.start()
        self.keeps[group] = keep
        stages = [self.on_z, self.on_y, self.on_x, self.on_c]
        self.pace.add(
            self.pace.send("z", 4 * self.size(group, 2)), lambda: (0.6, stages.pop(0)(group, layer))
        )
        return 1.4, self.pace.free["z"] - 9.0 if self.waiting else None

    def on_z(self, group, layer):
        z, y, x, c = self.spot
        self.keeps[group].wait()
        both, third = self.rows(group, x, 2, c), self.rows(group, 2 * x, 1, c)
        for k in range(1, Z_SIZE):
            self.arrive(self.full.at[layer, (z - k) % Z_SIZE, y, both], self.sem("z", group, k - 1))
        ref = self.full.at[layer, :, y, both]
        self.go(ref, ref, self.sem("y", group), self.across_y)
        part = self.full.at[layer, :, y, third]
        self.go(part, part, self.sem("x", group, 0), self.across_x)
        self.go(ref, ref, self.sem("c", group, 0), self.sibling)
        self.x_ready = self.pace.send("x", 4 * self.size(group, 1))
        return self.pace.send("y", 4 * self.size(group, 2))

    def on_y(self, group, layer):
        z, y, x, c = self.spot
        ref = self.full.at[layer, :, 1 - y, self.rows(group, x, 2, c)]
        self.arrive(ref, self.sem("y", group))
        part = self.full.at[layer, :, 1 - y, self.rows(group, 2 * x, 1, c)]
        self.go(part, part, self.sem("x", group, 1), self.across_x)
        self.go(ref, ref, self.sem("c", group, 1), self.sibling)
        return self.pace.send("x", 4 * self.size(group, 1))

    def on_x(self, group, layer):
        z, y, x, c = self.spot
        third = self.rows(group, 2 - 2 * x, 1, c)
        for k, side in enumerate((y, 1 - y)):
            self.arrive(self.full.at[layer, :, side, third], self.sem("x", group, k))
        ref = self.full.at[layer, :, :, third]
        self.go(ref, ref, self.sem("c", group, 2), self.sibling)
        return self.pace.send("c", 8 * self.size(group, 1))

    def on_c(self, group, layer):
        z, y, x, c = self.spot
        for k, side in enumerate((y, 1 - y)):
            self.arrive(self.full.at[layer, :, side, self.rows(group, x, 2, 1 - c)], self.sem("c", group, k))
        third = self.rows(group, 2 - 2 * x, 1, 1 - c)
        self.arrive(self.full.at[layer, :, :, third], self.sem("c", group, 2))
        self.done.add(group)
        self.loads(group)
        return None

    def finish(self):
        for copy in self.copies:
            copy.wait_send()


def silu(values):
    return values / (1.0 + jnp.exp(-values))


def conditions(ids, time1_w, time1_b, time2_w, time2_b, class_tab, hidden_t, condition):
    rows, half = ids.shape[0], FREQ // 2
    k = lax.broadcasted_iota(jnp.int32, (1, half), 1).astype(jnp.float32)
    angles = ids[:, 0:1] * jnp.exp(-math.log(10000.0) * k / half)
    features = jnp.concatenate([jnp.cos(angles), jnp.sin(angles)], axis=1).astype(jnp.bfloat16)
    hidden = dot_nn(features, time1_w[...]) + time1_b
    hidden_t[...] = hidden
    chosen = jnp.where(ids[:, 2:3] == 1.0, float(CLASSES), ids[:, 1:2])
    lane = lax.broadcasted_iota(jnp.int32, (rows, class_tab.shape[0]), 1).astype(jnp.float32)
    picked = jnp.dot(
        (lane == chosen).astype(jnp.float32), class_tab, precision=HIGHEST, preferred_element_type=jnp.float32
    )
    condition[...] = dot_nn(silu(hidden).astype(jnp.bfloat16), time2_w[...]) + time2_b + picked


def forward_kernel(
    groups, places_of, picked, places, ids, w_qkv, w_proj, w_fc1, w_fc2, w_mod, small, biases,
    out, full, mods, ids_all, hidden_t, condition, time2_w, x_h, proj_h, att_h, branch_a_h, middle_h, branch_b_h,
    w_in, w_out, x_v, proj_v, att_v, branch_a, middle, branch_b, mixed, active,
    mod_part, mod_y, mod_z, packed, raw, time1_w, raw_sem, out_sem,
    w_sem, save_sem, i_s, i_r, z_s, z_r, y_s, y_r, x_s, x_r, c_s, c_r, keep_sem, my_s, my_r, mz_s, mz_r,
):
    tokens = picked.shape[0]
    images, entries = mods.shape[:2]
    shard, deep = w_in.shape[3], w_out.shape[3]
    ways = D // LANES
    count = 4 + FF_BLOCKS
    spot = place()
    z, y, x, c = spot
    dps, reps = Z_SIZE * Y_SIZE, X_SIZE * C_SIZE
    dp, rep = z * Y_SIZE + y, x * C_SIZE + c
    pace = Pace()

    def load(layer, index):
        if index < count:
            return pltpu.make_async_copy(
                full.at[layer, :, pl.ds(index * shard, shard)], w_in.at[layer, index], w_sem.at[layer, index]
            )
        block = index - count
        per = D // deep
        return pltpu.make_async_copy(
            full.at[layer, pl.ds(block * per, per), pl.ds(count * shard, deep)],
            w_out.at[layer, block],
            w_sem.at[layer, index],
        )

    def loads(group):
        layer, first, size = groups[group]
        for index in range(count):
            if first <= index * shard < first + size:
                load(layer, index).start()
        ends = {g for g, (at, begin, _) in enumerate(groups) if at == layer and begin >= count * shard}
        if group in ends and ends <= gather.done:
            for block in range(FF_BLOCKS):
                load(layer, count + block).start()

    def square(layer, index):
        if index < 3:
            return w_qkv.at[layer, :, pl.ds(index * D, D)]
        if index == 3:
            return w_proj.at[layer]
        if index < count:
            return w_fc1.at[layer, :, pl.ds((index - 4) * D, D)]
        return w_fc2.at[layer, pl.ds((index - count) * shard, shard)]

    def fetch(group):
        if group < len(groups):
            layer, first, size = groups[group]
            slot = group % raw.shape[0]
            for k in range(size // shard):
                pltpu.make_async_copy(square(layer, first // shard + k), raw.at[slot, k], raw_sem.at[slot, k]).start()

    def prepare(group):
        layer, first, size = groups[group]
        slot = group % raw.shape[0]
        for k in range(size // shard):
            pltpu.make_async_copy(square(layer, first // shard + k), raw.at[slot, k], raw_sem.at[slot, k]).wait()
            packed[layer, pl.ds(first + k * shard, shard)] = raw[slot, k].astype(jnp.bfloat16)
        fetch(group + raw.shape[0])

    gather = Gather(
        pace, groups, spot, packed, full,
        {"z": (z_s, z_r), "y": (y_s, y_r), "x": (x_s, x_r), "c": (c_s, c_r), "keep": keep_sem}, prepare, loads,
    )
    for group in range(raw.shape[0]):
        fetch(group)

    def rows_of(name, k, first=0, size=None):
        at, height = places_of[name]
        return small[pl.ds((at + first) * ways + k, size or height, stride=ways)]

    def piece(name):
        return jnp.concatenate([rows_of(name, k) for k in range(ways)], axis=1)
    offsets = [(i, j) for i in range(dps) for j in range(reps) if i or j]
    everyone = [((dp + i) % dps, (rep + j) % reps) for i, j in offsets]
    meet(everyone)
    mine = dp * reps + rep
    id_copies = [push(ids, ids_all.at[mine], i_s.at[n], i_r.at[n], peer) for n, peer in enumerate(everyone)]
    for copy in id_copies:
        copy.start()
    ids_all[mine] = ids[...]
    ready = []

    def mods_start():
        for copy in id_copies:
            copy.wait_recv()
        for k in range(ways):
            lanes = pl.ds(k * LANES, LANES)
            time1_w[:, lanes] = rows_of("time1_w", k).astype(jnp.bfloat16)
            time2_w[:, lanes] = rows_of("time2_w", k).astype(jnp.bfloat16)
        conditions(
            ids_all[...].reshape(dps * reps * 8, LANES), time1_w, piece("time1_b"), time2_w, piece("time2_b"),
            piece("class_tab"), hidden_t, condition,
        )
        chosen = [condition[pl.ds(pl.multiple_of((d * reps + rep) * 8, 8), 8)] for d in range(dps)]
        group_c = silu(jnp.concatenate(chosen, axis=0)).astype(jnp.bfloat16)
        rows_mod = w_mod.shape[0]
        entry = lax.broadcasted_iota(jnp.int32, (D, rows_mod), 0)
        lane = lax.broadcasted_iota(jnp.int32, (D, rows_mod), 1)
        select = (entry == lane + dp * rows_mod).astype(jnp.bfloat16)
        own = dot_nn(group_c, select).astype(jnp.bfloat16)
        for k in range(entries):
            value = dot_nn(own, w_mod[:, k * D : (k + 1) * D].astype(jnp.bfloat16))
            for d in range(dps):
                for image in range(images):
                    row = 8 * d + image
                    mod_part[d // Y_SIZE, d % Y_SIZE, pl.ds(image * entries + k, 1)] = value[row : row + 1]
        gather.go(mod_part.at[:, 1 - y], mod_y, (my_s, my_r), gather.across_y)
        return 9.0, pace.send("y", 4 * mod_part.shape[2] * D * 4)

    def mods_across():
        gather.arrive(mod_y, (my_s, my_r))
        for k in range(Z_SIZE):
            mod_y[k] = mod_y[k] + mod_part[k, y]
        for k in range(1, Z_SIZE):
            peer = (z + k) % Z_SIZE
            gather.go(mod_y.at[peer], mod_z.at[z], (mz_s.at[k - 1], mz_r.at[k - 1]), gather.z_peers[k - 1])
        return 1.5, pace.send("z", 4 * mod_part.shape[2] * D * 4)

    def mods_end():
        mod_z[z] = mod_y[z]
        for k in range(1, Z_SIZE):
            gather.arrive(mod_z.at[(z - k) % Z_SIZE], (mz_s.at[k - 1], mz_r.at[k - 1]))
        value = (mod_z[0] + mod_z[1]) + (mod_z[2] + mod_z[3])
        shift = piece("mod_b")
        for image in range(images):
            for k in range(entries):
                row = image * entries + k
                mods[image, k] = value[row : row + 1] + shift[k : k + 1]
        ready.append(True)
        return 1.0, None

    steps = [mods_start, mods_across, mods_end]
    pace.now = 8.0
    for _ in range(2):
        gather.start()
    pace.add(pace.now + 3.0, lambda: steps.pop(0)())
    pace.add(pace.free["z"] - 9.0, gather.start)

    def need(layer, which):
        index = min(which, count)
        last = (index if index < count else count + deep // shard - 1) * shard
        first = min(last, index * shard)
        wanted = {
            g for g, (at, begin, size) in enumerate(groups) if at == layer and first < begin + size and begin <= last
        }
        pace.until(lambda: wanted <= gather.done)
        load(layer, which).wait()

    patch_w = piece("patch_w").astype(jnp.bfloat16)
    strip = PDIM // PATCH
    weights = jnp.concatenate([patch_w[u * strip : (u + 1) * strip] for u in range(PATCH) for _ in range(GRID)], axis=0)
    shift = piece("patch_b")
    for image in range(images):
        rows = pl.ds(image * GRID * GRID, GRID * GRID)
        x_v[rows] = dot_nn(picked[rows], weights) + shift + places[...]
    pace.spend(1.5)
    saves = {}

    def save(layer, source, target, index):
        copy = pltpu.make_async_copy(source, target.at[layer], save_sem.at[layer, index])
        copy.start()
        saves[index] = copy

    def reuse(index):
        copy = saves.pop(index, None)
        if copy is not None:
            copy.wait()

    for layer in range(LAYERS):
        base = 6 * layer
        save(layer, x_v, x_h, 0)
        pace.until(lambda: ready)
        modulate(x_v, mods, base, base + 1, mixed, tokens)
        pace.spend(1.0)
        reuse(1)
        for p in range(3):
            need(layer, p)

            def project(i, p=p, layer=layer):
                value = dot_nn(mixed[...], whole(w_in[layer, p, :, :, columns(i)]))
                if p != 1:
                    value = value + biases[layer, p // 2, :, columns(i)]
                proj_v[p, :, columns(i)] = value.astype(jnp.bfloat16)

            each(D // TILE, project)
            pace.spend(1.1)
        save(layer, proj_v, proj_h, 1)
        reuse(2)
        for pair in range(0, HEADS // 2, 2):
            attention_forward(proj_v, att_v, images, pair, 2)
            pace.spend(2.3)
        save(layer, att_v, att_h, 2)
        reuse(3)
        reuse(4)
        need(layer, 3)

        def first_branch(i, layer=layer, base=base):
            value = dot_nn(att_v[...], whole(w_in[layer, 3, :, :, columns(i)]))
            value = value + biases[layer, 2, :, columns(i)]
            branch_a[:, columns(i)] = value
            for image in range(images):
                rows = pl.ds(image * GRID * GRID, GRID * GRID)
                part = value[image * GRID * GRID : (image + 1) * GRID * GRID]
                middle[rows, columns(i)] = x_v[rows, columns(i)] + mods[image, base + 2, :, columns(i)] * part

        each(D // TILE, first_branch)
        save(layer, branch_a, branch_a_h, 3)
        save(layer, middle, middle_h, 4)
        modulate(middle, mods, base + 3, base + 4, mixed, tokens)
        pace.spend(2.3)
        for block in range(FF_BLOCKS):
            need(layer, 4 + block)

            def expand(i, block=block, layer=layer):
                hidden = dot_nn(mixed[...], whole(w_in[layer, 4 + block, :, :, columns(i)]))
                hidden = hidden + biases[layer, 3 + block, :, columns(i)]
                inner = jnp.tanh(GELU_A * (hidden + GELU_B * hidden * hidden * hidden))
                active[block, :, columns(i)] = (0.5 * hidden * (1.0 + inner)).astype(jnp.bfloat16)

            each(D // TILE, expand)
            pace.spend(2.2)
        reuse(5)
        for block in range(FF_BLOCKS):
            need(layer, count + block)

            def contract(i, block=block, layer=layer):
                value = dot_nn(active[block], whole(w_out[layer, block, :, :, columns(i)]))
                if block == 0:
                    branch_b[:, columns(i)] = value + biases[layer, 3 + FF_BLOCKS, :, columns(i)]
                else:
                    branch_b[:, columns(i)] += value

            each(D // TILE, contract)
            pace.spend(1.1)
        save(layer, branch_b, branch_b_h, 5)
        reuse(0)

        def finish(rows, image, base=base):
            x_v[rows] = middle[rows] + mods[image, base + 5] * branch_b[rows]

        row_blocks(tokens, finish)
        pace.spend(1.0)
    last = pltpu.make_async_copy(x_v, out, out_sem)
    last.start()
    pace.drain()
    for copy in saves.values():
        copy.wait()
    last.wait()
    gather.finish()
    for copy in id_copies:
        copy.wait_send()


def run_forward(picked, places, ids, w_qkv, w_proj, w_fc1, w_fc2, w_mod, small, places_of, biases, images):
    tokens = picked.shape[0]
    layers = w_qkv.shape[0]
    owners, everyone = Z_SIZE * Y_SIZE, Z_SIZE * Y_SIZE * X_SIZE * C_SIZE
    shard, deep = D // owners, FF // owners
    height, width = (4 + FF_BLOCKS) * shard + deep, D
    wide, low = jnp.float32, jnp.bfloat16
    entries = MOD // D
    mod_rows = -(-images * entries // 8) * 8
    keep = [
        ((tokens, D), wide), ((3, tokens, D), low), ((tokens, D), low),
        ((tokens, D), wide), ((tokens, D), wide), ((tokens, D), wide),
    ]
    groups = [(layer, first, 2 * shard) for layer in range(layers) for first in range(0, height, 2 * shard)]
    number = len(groups)
    dma = pltpu.SemaphoreType.DMA
    vmem, anywhere = pl.BlockSpec(memory_space=pltpu.VMEM), pl.BlockSpec(memory_space=pl.ANY)
    outs = [
        jax.ShapeDtypeStruct((tokens, D), wide),
        jax.ShapeDtypeStruct((layers, owners, height, width), low),
        jax.ShapeDtypeStruct((images, entries, 1, D), wide),
        jax.ShapeDtypeStruct((everyone,) + ids.shape, wide),
        jax.ShapeDtypeStruct((everyone * ids.shape[0], D), wide),
        jax.ShapeDtypeStruct((everyone * ids.shape[0], D), wide),
        jax.ShapeDtypeStruct((D, D), low),
    ]
    return pl.pallas_call(
        partial(forward_kernel, groups, places_of),
        out_shape=outs + [jax.ShapeDtypeStruct((layers,) + shape, kind) for shape, kind in keep],
        in_specs=[vmem] * 3 + [anywhere] * 4 + [vmem] * 3,
        out_specs=[anywhere, anywhere, vmem, vmem, vmem, vmem, vmem] + [anywhere] * len(keep),
        scratch_shapes=[
            pltpu.VMEM((layers, 4 + FF_BLOCKS, owners, shard, D), low),
            pltpu.VMEM((layers, FF_BLOCKS, D // deep, deep, D), low),
        ]
        + [pltpu.VMEM(shape, kind) for shape, kind in keep]
        + [
            pltpu.VMEM((tokens, D), low),
            pltpu.VMEM((FF_BLOCKS, tokens, D), low),
            pltpu.VMEM((Z_SIZE, Y_SIZE, mod_rows, D), wide),
            pltpu.VMEM((Z_SIZE, mod_rows, D), wide),
            pltpu.VMEM((Z_SIZE, mod_rows, D), wide),
            pltpu.VMEM((layers, height, width), low),
            pltpu.VMEM((3, 2, shard, D), wide),
            pltpu.VMEM((FREQ, D), low),
            dma((3, 2)),
            dma,
            dma((layers, 4 + 2 * FF_BLOCKS)),
            dma((layers, len(keep))),
            dma((everyone - 1,)),
            dma((everyone - 1,)),
            dma((number, Z_SIZE - 1)),
            dma((number, Z_SIZE - 1)),
            dma((number,)),
            dma((number,)),
            dma((number, 2)),
            dma((number, 2)),
            dma((number, 3)),
            dma((number, 3)),
            dma((number,)),
            dma,
            dma,
            dma((Z_SIZE - 1,)),
            dma((Z_SIZE - 1,)),
        ],
        compiler_params=pltpu.CompilerParams(
            collective_id=2, has_side_effects=True, vmem_limit_bytes=63 * 2**20
        ),
        name="blocks_forward",
    )(picked, places, ids, w_qkv, w_proj, w_fc1, w_fc2, w_mod, small, biases)


class Reduction:
    COSTS = (0.6, 0.4, 0.8, 0.5, 0.4, 0.1)

    def __init__(self, pace, groups, shard, spot, buffers, semaphores, credits, finals):
        self.pace, self.groups, self.shard, self.spot = pace, groups, shard, spot
        self.held, self.from_c, self.from_x, self.from_y, self.from_z, self.from_fin = buffers
        self.sems, self.credits, self.finals = semaphores, credits, finals
        z, y, x, c = spot
        self.z_peers = [device((z + k) % Z_SIZE, y, x, c) for k in range(1, Z_SIZE)]
        self.z_before = [device((z - k) % Z_SIZE, y, x, c) for k in range(1, Z_SIZE)]
        self.across_y, self.across_x = device(z, 1 - y, x, c), device(z, y, 1 - x, c)
        self.sibling = device(z, y, x, 1 - c)
        self.started, self.kept, self.filled, self.busy = {}, {}, {}, {}
        self.at_half = [first for first, _, _ in groups]
        self.halves = [rows for _, rows, _ in groups]
        self.parts = [part for _, _, part in groups]
        most = [rows - part for _, rows, part in groups]
        self.at_part = [sum(self.parts[:g]) for g in range(len(groups))]
        self.at_most = [sum(most[:g]) for g in range(len(groups))]

    def peers(self):
        return self.z_peers + [self.across_y, self.across_x, self.sibling]

    def go(self, key, source, target, sems, peer):
        copy = push(source, target, sems[0], sems[1], peer)
        copy.start()
        self.started.setdefault(key, []).append(copy)

    def arrive(self, ref, sems):
        push(ref, ref, sems[0], sems[1], self.across_y).wait_recv()

    def sem(self, name, layer, *index):
        send, receive = self.sems[name]
        return send.at[(layer,) + index], receive.at[(layer,) + index]

    def give(self, layer, name, peer, *index):
        if layer == LAYERS - 1:
            pl.semaphore_signal(
                self.credits[name].at[index], inc=1, device_id=peer, device_id_type=MESH_IDS
            )

    def take(self, layer, name, *index):
        if layer != LAYERS - 1:
            pl.semaphore_wait(self.credits[name].at[index], 1)

    def put(self, layer, group, stage, first, squares, owner_z, slot):
        c = self.spot[3]
        half = self.shard // 2
        if (layer, group) not in self.filled:
            while (layer + 1, group) in self.busy:
                self.pace.spend(0.5)
            for copy in self.started.pop((layer + 1, group), []):
                copy.wait_send()
            self.take(layer, "c", group)
            self.filled[layer, group] = []
        rows = pl.ds(first, squares * half)
        theirs = stage.at[:, :, :, pl.ds(pl.multiple_of((1 - c) * half, 16), half)]
        ours = stage.at[:, :, :, pl.ds(pl.multiple_of(c * half, 16), half)]
        zs = stage.shape[0]

        def view(ref):
            pieces = ref.reshape(Z_SIZE, Y_SIZE, ref.shape[2] // half, half, D)
            return pieces.at[pl.ds(owner_z, zs), :, pl.ds(first // half, squares)]

        sems = self.sem("c", layer, group, slot)
        send = push(theirs, view(self.from_c), sems[0], sems[1], self.sibling)
        keep = pltpu.make_async_copy(ours, view(self.held), self.sems["keep"].at[layer, group, slot])
        send.start()
        keep.start()
        self.filled[layer, group].append((slot, owner_z, zs, rows))
        self.kept[layer, group, slot] = keep
        self.ready = self.pace.send("c", zs * Y_SIZE * squares * half * D * 2)

        def free():
            send.wait_send()
            self.keep_wait(layer, group, slot)

        return free

    def begin(self, layer, group):
        stages = [self.on_c, self.on_x, self.on_y, self.on_z, self.on_fin, self.on_last]
        costs = list(self.COSTS)
        self.busy[layer, group] = True

        def run():
            ready = stages.pop(0)(layer, group)
            if not stages:
                del self.busy[layer, group]
            return costs.pop(0), ready

        self.pace.add(self.ready, run)

    def keep_wait(self, *key):
        keep = self.kept.pop(key, None)
        if keep is not None:
            keep.wait()

    def add(self, target, extra):
        def body(owner):
            total = target[owner].astype(jnp.float32) + extra[owner].astype(jnp.float32)
            target[owner] = total.astype(jnp.bfloat16)

        each(Z_SIZE, body)

    def on_c(self, layer, group):
        z, y, x, c = self.spot
        half, part = self.halves[group], self.parts[group]
        first = self.at_half[group]
        for slot, owner_z, zs, rows in self.filled[layer, group]:
            self.keep_wait(layer, group, slot)
            self.arrive(self.from_c.at[pl.ds(owner_z, zs), :, rows], self.sem("c", layer, group, slot))
        theirs = pl.ds(pl.multiple_of(first + (1 - x) * (half - part), 16), part)
        ours = pl.ds(pl.multiple_of(first + x * part, 16), half - part)
        for side in range(Y_SIZE):
            self.add(self.held.at[:, side, theirs], self.from_c.at[:, side, theirs])
        target = self.from_x.at[:, :, pl.ds(self.at_part[group], part)]
        self.take(layer, "x", group)
        self.go((layer, group), self.held.at[:, :, theirs], target, self.sem("x", layer, group), self.across_x)
        for side in range(Y_SIZE):
            self.add(self.held.at[:, side, ours], self.from_c.at[:, side, ours])
        self.give(layer, "c", self.sibling, group)
        return self.pace.send("x", 8 * part * D * 2)

    def on_x(self, layer, group):
        z, y, x, c = self.spot
        half, part = self.halves[group], self.parts[group]
        first = self.at_half[group]
        got = self.from_x.at[:, :, pl.ds(self.at_part[group], part)]
        self.arrive(got, self.sem("x", layer, group))
        ours = pl.ds(pl.multiple_of(first + x * (half - part), 16), part)
        for side in (1 - y, y):
            self.add(self.held.at[:, side, ours], self.from_x.at[:, side, pl.ds(self.at_part[group], part)])
        self.give(layer, "x", self.across_x, group)
        most = pl.ds(pl.multiple_of(first + x * part, 16), half - part)
        self.take(layer, "y", group)
        self.go(
            (layer, group), self.held.at[:, 1 - y, most], self.from_y.at[:, pl.ds(self.at_most[group], half - part)],
            self.sem("y", layer, group), self.across_y,
        )
        return self.pace.send("y", 4 * (half - part) * D * 2)

    def on_y(self, layer, group):
        z, y, x, c = self.spot
        half, part = self.halves[group], self.parts[group]
        got = self.from_y.at[:, pl.ds(self.at_most[group], half - part)]
        self.arrive(got, self.sem("y", layer, group))
        most = pl.ds(pl.multiple_of(self.at_half[group] + x * part, 16), half - part)
        self.add(self.held.at[:, y, most], got)
        self.give(layer, "y", self.across_y, group)
        for k in range(1, Z_SIZE):
            self.take(layer, "z", group, k - 1)
            self.go(
                (layer, group), self.held.at[(z + k) % Z_SIZE, y, most],
                self.from_z.at[k - 1, pl.ds(self.at_most[group], half - part)],
                self.sem("z", layer, group, k - 1), self.z_peers[k - 1],
            )
        return self.pace.send("z", self.pace.along_z * (half - part) * D * 2)

    def on_z(self, layer, group):
        z, y, x, c = self.spot
        half, part = self.halves[group], self.parts[group]
        most = pl.ds(pl.multiple_of(self.at_half[group] + x * part, 16), half - part)
        got = pl.ds(self.at_most[group], half - part)
        for k in range(1, Z_SIZE):
            self.arrive(self.from_z.at[k - 1, got], self.sem("z", layer, group, k - 1))
        total = self.held[z, y, most].astype(jnp.float32)
        for k in range(1, Z_SIZE):
            total = total + self.from_z[k - 1, got].astype(jnp.float32)
        self.held[z, y, most] = total.astype(jnp.bfloat16)
        for k in range(1, Z_SIZE):
            self.give(layer, "z", self.z_before[k - 1], group, k - 1)
        self.take(layer, "e", group)
        self.go((layer, group), self.held.at[z, y, most], self.from_fin.at[got], self.sem("e", layer, group), self.across_x)
        return self.pace.send("x", (half - part) * D * 2)

    def on_fin(self, layer, group):
        z, y, x, c = self.spot
        half, part = self.halves[group], self.parts[group]
        middle = half - 2 * part
        base, start = self.at_most[group], self.at_half[group]
        self.arrive(self.from_fin.at[pl.ds(base, half - part)], self.sem("e", layer, group))
        wide = jnp.float32

        def span(begin, size):
            return pl.ds(pl.multiple_of(begin, 16), size)

        ours, theirs = span(start + x * (half - part), part), span(start + (1 - x) * (half - part), part)
        both = span(start + part, middle)
        self.finals[layer, c, ours] = self.held[z, y, ours].astype(wide)
        self.finals[layer, c, theirs] = self.from_fin[span(base + (1 - x) * middle, part)].astype(wide)
        self.finals[layer, c, both] = self.held[z, y, both].astype(wide) + self.from_fin[
            span(base + x * part, middle)
        ].astype(wide)
        self.give(layer, "e", self.across_x, group)
        ref = self.finals.at[layer, c, pl.ds(start, half)]
        self.go((layer, group), ref, ref, self.sem("f", layer, group), self.sibling)
        return self.pace.send("c", half * D * 4)

    def on_last(self, layer, group):
        c = self.spot[3]
        ref = self.finals.at[layer, 1 - c, pl.ds(self.at_half[group], self.halves[group])]
        self.arrive(ref, self.sem("f", layer, group))
        return None

    def finish(self):
        for copies in self.started.values():
            for copy in copies:
                copy.wait_send()


class Sums:
    def __init__(self, reduction, own, total, small_c, small_x, small_y, small_z, mods, mods_all, sems, mod_sems, local):
        self.r = reduction
        self.own, self.total = own, total
        self.small_c, self.small_x, self.small_y, self.small_z = small_c, small_x, small_y, small_z
        self.mods, self.mods_all, self.v, self.m, self.local = mods, mods_all, sems, mod_sems, local
        self.stages = [self.first, self.to_x, self.to_y, self.to_z, self.to_c, self.last]

    def sem(self, pair, index):
        return pair[0].at[index], pair[1].at[index]

    def go(self, ref, target, pair, index, peer):
        self.r.go("sums", ref, target, self.sem(pair, index), peer)

    def arrive(self, ref, pair, index):
        self.r.arrive(ref, self.sem(pair, index))

    def run(self):
        self.stages.pop(0)()
        return 1.0, self.r.pace.now + 7.0 if self.stages else None

    def halves(self):
        span = self.small_c.shape[0]
        c = self.r.spot[3]
        return [pl.ds(pl.multiple_of(i * span, 8), span) for i in (c, 1 - c)]

    def first(self):
        z, y, x, c = self.r.spot
        mine, other = self.halves()
        self.go(self.own.at[other], self.small_c, self.v, 0, self.r.sibling)
        own = self.mods_all.at[z, y, x * C_SIZE + c]
        keep = pltpu.make_async_copy(self.mods, own, self.local)
        keep.start()
        for k in range(1, Z_SIZE):
            self.go(self.mods, own, self.m, k - 1, self.r.z_peers[k - 1])
        keep.wait()

    def to_x(self):
        z, y, x, c = self.r.spot
        mine, other = self.halves()
        self.arrive(self.small_c, self.v, 0)
        self.small_c[...] = self.small_c[...] + self.own[mine]
        self.go(self.small_c, self.small_x, self.v, 1, self.r.across_x)
        slot = x * C_SIZE + c
        for k in range(1, Z_SIZE):
            self.arrive(self.mods_all.at[(z - k) % Z_SIZE, y, slot], self.m, k - 1)
        ref = self.mods_all.at[:, y, slot]
        self.go(ref, ref, self.m, 3, self.r.across_y)

    def to_y(self):
        z, y, x, c = self.r.spot
        self.arrive(self.small_x, self.v, 1)
        self.small_x[...] = self.small_x[...] + self.small_c[...]
        self.go(self.small_x, self.small_y, self.v, 2, self.r.across_y)
        slot = x * C_SIZE + c
        self.arrive(self.mods_all.at[:, 1 - y, slot], self.m, 3)
        ref = self.mods_all.at[:, :, slot]
        self.go(ref, ref, self.m, 4, self.r.across_x)

    def to_z(self):
        z, y, x, c = self.r.spot
        self.arrive(self.small_y, self.v, 2)
        self.small_z[z] = self.small_y[...] + self.small_x[...]
        own = self.small_z.at[z]
        for k in range(1, Z_SIZE):
            self.go(own, own, self.v, 2 + k, self.r.z_peers[k - 1])
        self.arrive(self.mods_all.at[:, :, (1 - x) * C_SIZE + c], self.m, 4)
        for k in range(X_SIZE):
            ref = self.mods_all.at[:, :, k * C_SIZE + c]
            self.go(ref, ref, self.m, 5 + k, self.r.sibling)

    def to_c(self):
        z, y, x, c = self.r.spot
        mine, other = self.halves()
        for k in range(1, Z_SIZE):
            self.arrive(self.small_z.at[(z - k) % Z_SIZE], self.v, 2 + k)
        self.total[mine] = (self.small_z[0] + self.small_z[1]) + (self.small_z[2] + self.small_z[3])
        self.go(self.total.at[mine], self.total.at[mine], self.v, 6, self.r.sibling)
        for k in range(X_SIZE):
            self.arrive(self.mods_all.at[:, :, k * C_SIZE + 1 - c], self.m, 5 + k)

    def last(self):
        mine, other = self.halves()
        self.arrive(self.total.at[other], self.v, 6)


def backward_kernel(
    groups, count_all, x_last, mods, biases, picked, wanted, head_w, head_b, full,
    x_h, proj_h, att_h, branch_a_h, middle_h, branch_b_h,
    finals, mods_all, sums_out,
    w_v, grad_x, x_v, proj_v, att_v, branch, middle, mixed, grad_b, active, grad_hidden, grad_mixed,
    grad_projected, stage, mods_acc, mods_tile, mods_low, sums,
    held, from_c, from_x, from_y, from_z, from_fin, small_c, small_x, small_y, small_z,
    w_sem, load_sem, last_sem, keep_sem, c_s, c_r, x_s, x_r, y_s, y_r, z_s, z_r, e_s, e_r, f_s, f_r,
    v_s, v_r, m_s, m_r, local, cred_c, cred_x, cred_y, cred_z, cred_e,
):
    tokens = x_last.shape[0]
    images = mods.shape[0]
    owners = full.shape[1]
    shard, deep = D // owners, FF // owners
    count = 4 + FF_BLOCKS
    per = D // deep
    slots = w_v.shape[0]
    spot = place()
    pace = Pace(52e3, 3.3)
    reduction = Reduction(
        pace, groups, shard, spot, (held, from_c, from_x, from_y, from_z, from_fin),
        {"c": (c_s, c_r), "x": (x_s, x_r), "y": (y_s, y_r), "z": (z_s, z_r), "e": (e_s, e_r), "f": (f_s, f_r), "keep": keep_sem},
        {"c": cred_c, "x": cred_x, "y": cred_y, "z": cred_z, "e": cred_e}, finals,
    )
    order = [i for b in range(FF_BLOCKS) for i in (4 + b, count + b)] + [3, 0, 1, 2]
    order = [(layer, index) for layer in reversed(range(LAYERS)) for index in order]

    def load(at):
        layer, index = order[at]
        slot = at % slots
        target = w_v.at[slot]
        if index < count:
            return pltpu.make_async_copy(
                full.at[layer, :, pl.ds(index * shard, shard)], target.reshape(owners, shard, D), w_sem.at[slot]
            )
        return pltpu.make_async_copy(
            full.at[layer, pl.ds((index - count) * per, per), pl.ds(count * shard, deep)],
            target.reshape(per, deep, D),
            w_sem.at[slot],
        )

    def fetch(at):
        if at < len(order):
            load(at).start()

    def weight(at):
        load(at).wait()
        return w_v.at[at % slots]

    def total(values):
        return jnp.sum(values, axis=0, keepdims=True)

    last_copy = pltpu.make_async_copy(x_last, grad_x, last_sem)
    last_copy.start()
    for at in range(slots):
        fetch(at)
    meet(reduction.peers())
    sums[...] = jnp.zeros_like(sums)
    mods_acc[...] = jnp.zeros_like(mods_acc)
    last_copy.wait()
    final = 6 * LAYERS
    modulate(grad_x, mods, final, final + 1, mixed, tokens)
    picks, wide = wanted.shape[1], head_w.shape[1]
    strip = PDIM // PATCH
    pixel = lax.broadcasted_iota(jnp.int32, (picks, wide), 0)
    entry = lax.broadcasted_iota(jnp.int32, (picks, wide), 1)
    select = (entry == pixel // (picks // PATCH) * strip + pixel % strip).astype(jnp.float32)
    target = jnp.dot(wanted[...], select, precision=HIGHEST, preferred_element_type=jnp.float32)
    error = dot_nn(mixed[...], head_w[...]) + head_b[...] - target
    grad_low = (error * (2.0 / count_all)).astype(jnp.bfloat16)
    sums[pl.ds(PDIM, PDIM)] = dot_tn(grad_low, mixed[...])[:PDIM]
    lane = lax.broadcasted_iota(jnp.int32, (1, wide), 1)
    sums[pl.ds(2 * PDIM, 1), pl.ds(0, wide)] = jnp.where(
        lane == PDIM, jnp.sum(error * error), total(grad_low.astype(jnp.float32))
    )
    for i in range(D // TILE):
        grad_mixed[:, columns(i)] = dot_nt(grad_low, head_w[columns(i)])

    def head(rows, image):
        grad = grad_mixed[rows]
        normed, inverse = centre(grad_x[rows])
        mods_acc[image, final] += total(grad)
        mods_acc[image, final + 1] += total(grad * normed)
        grad = grad * (1.0 + mods[image, final + 1])
        grad_x[rows] = inverse * (
            grad - jnp.mean(grad, axis=-1, keepdims=True) - normed * jnp.mean(grad * normed, axis=-1, keepdims=True)
        )

    row_blocks(tokens, head)
    busy = [[], []]
    turn = [0]

    def weight_grad(layer, left, right, index):
        slot = turn[0] % 2
        turn[0] += 1
        for wait in busy[slot]:
            wait()

        def body(i):
            cut = block_at(i, D // 2)
            value = dot_tn(left[:, cut], right[...]).astype(jnp.bfloat16)
            stage[slot, cut] = value

        each(2, body)
        half = shard // 2
        if index < count:
            group = next(g for g, entry in enumerate(groups) if entry[0] <= index * half < entry[0] + entry[1])
            view = stage.at[slot].reshape(Z_SIZE, Y_SIZE, 1, shard, D)
            busy[slot] = [
                reduction.put(layer, group, view, index * half, 1, 0, (index * half - groups[group][0]) // half)
            ]
            if index * half == groups[group][0] + groups[group][1] - half:
                reduction.begin(layer, group)
        else:
            block = index - count
            busy[slot] = []
            for group, (first, rows, _) in enumerate(groups):
                if first >= count * half:
                    squares = rows // half
                    view = stage.at[slot].reshape(1, Y_SIZE, deep // shard, shard, D)
                    view = view.at[:, :, pl.ds((first - count * half) // half, squares)]
                    busy[slot].append(reduction.put(layer, group, view, first, squares, block, block))
                    if block == FF_BLOCKS - 1:
                        reduction.begin(layer, group)
        pace.spend(1.3)

    for layer in reversed(range(LAYERS)):
        base = 6 * layer
        at = (LAYERS - 1 - layer) * (count + FF_BLOCKS)
        bias_row = 3 * PDIM + layer * (4 + FF_BLOCKS)

        def bias_add(k, values, cut=slice(None), bias_row=bias_row):
            sums[pl.ds(bias_row + k, 1), cut] += total(values)

        saved = [
            (branch_b_h, branch), (middle_h, middle), (att_h, att_v), (proj_h, proj_v), (x_h, x_v), (branch_a_h, branch),
        ]
        copies = [
            pltpu.make_async_copy(source.at[layer], target, load_sem.at[i])
            for i, (source, target) in enumerate(saved)
        ]
        for copy in copies[:-1]:
            copy.start()
        copies[0].wait()
        copies[1].wait()

        def enter(rows, image, base=base, bias_add=bias_add):
            grad = grad_x[rows]
            low = (mods[image, base + 5] * grad).astype(jnp.bfloat16)
            grad_b[rows] = low
            bias_add(3 + FF_BLOCKS, low.astype(jnp.float32))
            mods_acc[image, base + 5] += total(grad * branch[rows])
            normed, _ = centre(middle[rows])
            mixed[rows] = (normed * (1.0 + mods[image, base + 4]) + mods[image, base + 3]).astype(jnp.bfloat16)

        row_blocks(tokens, enter)
        pace.spend(1.8)
        copies[-1].start()
        for block in range(FF_BLOCKS):
            w_one, w_two = weight(at), weight(at + 1)

            def expand(i, block=block, w_one=w_one, w_two=w_two, layer=layer, bias_add=bias_add):
                hidden = dot_nn(mixed[...], w_one[:, columns(i)]) + biases[layer, 3 + block, :, columns(i)]
                square = hidden * hidden
                inner = jnp.tanh(GELU_A * (hidden + GELU_B * hidden * square))
                active[:, columns(i)] = (0.5 * hidden * (1.0 + inner)).astype(jnp.bfloat16)
                slope = 0.5 * (1.0 + inner) + 0.5 * hidden * (1.0 - inner * inner) * (
                    GELU_A * (1.0 + 3.0 * GELU_B * square)
                )
                low = (slope * dot_nt(grad_b[...], w_two[columns(i)])).astype(jnp.bfloat16)
                grad_hidden[:, columns(i)] = low
                bias_add(3 + block, low.astype(jnp.float32), columns(i))

            each(D // TILE, expand)
            pace.spend(3.6)
            weight_grad(layer, active, grad_b, count + block)

            def back(i, block=block, w_one=w_one):
                value = dot_nt(grad_hidden[...], w_one[columns(i)])
                if block == 0:
                    grad_mixed[:, columns(i)] = value
                else:
                    grad_mixed[:, columns(i)] += value

            each(D // TILE, back)
            pace.spend(1.0)
            fetch(at + slots)
            fetch(at + slots + 1)
            weight_grad(layer, mixed, grad_hidden, 4 + block)
            at += 2
        for copy in copies[2:]:
            copy.wait()

        def leave(rows, image, base=base, bias_add=bias_add):
            grad = grad_mixed[rows]
            normed, inverse = centre(middle[rows])
            mods_acc[image, base + 3] += total(grad)
            mods_acc[image, base + 4] += total(grad * normed)
            grad = grad * (1.0 + mods[image, base + 4])
            grad = grad_x[rows] + inverse * (
                grad - jnp.mean(grad, axis=-1, keepdims=True) - normed * jnp.mean(grad * normed, axis=-1, keepdims=True)
            )
            middle[rows] = grad
            low = (mods[image, base + 2] * grad).astype(jnp.bfloat16)
            grad_b[rows] = low
            bias_add(2, low.astype(jnp.float32))
            mods_acc[image, base + 2] += total(grad * branch[rows])
            normed, _ = centre(x_v[rows])
            mixed[rows] = (normed * (1.0 + mods[image, base + 1]) + mods[image, base]).astype(jnp.bfloat16)

        row_blocks(tokens, leave)
        pace.spend(2.6)
        w_proj = weight(at)

        def through(i, w_proj=w_proj):
            active[:, columns(i)] = dot_nt(grad_b[...], w_proj[columns(i)]).astype(jnp.bfloat16)

        each(D // TILE, through)
        pace.spend(0.9)
        fetch(at + slots)
        weight_grad(layer, att_v, grad_b, 3)
        for image in range(images):
            for pair in range(0, HEADS // 2, 2):
                attention_backward(proj_v, active, grad_projected, image, pair, 2)
                pace.spend(2.1)
        for p in range(3):
            w_part = weight(at + 1 + p)

            def into(i, p=p, w_part=w_part):
                value = dot_nt(grad_projected[p], w_part[columns(i)])
                if p == 0:
                    grad_mixed[:, columns(i)] = value
                else:
                    grad_mixed[:, columns(i)] += value

            weight_grad(layer, mixed, grad_projected.at[p], p)
            each(D // TILE, into)
            pace.spend(1.0)
            fetch(at + 1 + p + slots)

        def last(rows, image, base=base, bias_add=bias_add):
            grad = grad_mixed[rows]
            normed, inverse = centre(x_v[rows])
            mods_acc[image, base] += total(grad)
            mods_acc[image, base + 1] += total(grad * normed)
            grad = grad * (1.0 + mods[image, base + 1])
            grad_x[rows] = middle[rows] + inverse * (
                grad - jnp.mean(grad, axis=-1, keepdims=True) - normed * jnp.mean(grad * normed, axis=-1, keepdims=True)
            )
            bias_add(0, grad_projected[0, rows].astype(jnp.float32))
            bias_add(1, grad_projected[2, rows].astype(jnp.float32))

        row_blocks(tokens, last)
        pace.spend(2.2)

    def patch(rows, image):
        low = grad_x[rows].astype(jnp.bfloat16)
        grad_b[rows] = low
        sums[pl.ds(2 * PDIM + 8, 1)] += total(low.astype(jnp.float32))

    row_blocks(tokens, patch)
    value = dot_tn(picked[...], grad_b[...])
    for u in range(PATCH):
        first = u * strip * GRID
        part = value[first : first + strip]
        for j in range(1, GRID):
            part = part + value[first + j * strip : first + (j + 1) * strip]
        sums[pl.ds(u * strip, strip)] = part
    mods_tile[...] = jnp.zeros_like(mods_tile)
    entries = mods.shape[1]
    for image in range(images):
        for k in range(entries):
            mods_tile[pl.ds(image * entries + k, 1)] = mods_acc[image, k]
    mods_low[...] = mods_tile[...].astype(jnp.bfloat16)
    small = Sums(
        reduction, sums, sums_out, small_c, small_x, small_y, small_z, mods_low, mods_all, (v_s, v_r), (m_s, m_r), local
    )
    pace.add(pace.now, small.run)
    pace.drain()
    reduction.finish()
    for waits in busy:
        for wait in waits:
            wait()


def run_backward(count_all, x_last, mods, biases, picked, wanted, head_w, head_b, full, kept):
    tokens = x_last.shape[0]
    images, entries = mods.shape[:2]
    layers, owners, height, width = full.shape
    shard = D // owners
    count = 4 + FF_BLOCKS
    piece = shard // 2
    sizes = [(2, 1), (1, 1), (1, 1), (2, 2), (2, 1), (2, 2), (2, 1)]
    groups = []
    for squares, thirds in sizes:
        first = sum(group[1] for group in groups)
        groups.append((first, squares * piece, thirds * piece // 3))
    half = height // 2
    part = sum(group[2] for group in groups)
    most = half - part
    wide, low = jnp.float32, jnp.bfloat16
    vmem, anywhere = pl.BlockSpec(memory_space=pltpu.VMEM), pl.BlockSpec(memory_space=pl.ANY)
    rows = (tokens, D)
    dma, regular = pltpu.SemaphoreType.DMA, pltpu.SemaphoreType.REGULAR
    number = len(groups)
    sum_rows = 3 * PDIM + LAYERS * count
    mod_rows = -(-images * entries // 16) * 16
    pair = [dma((layers, number))] * 2
    return pl.pallas_call(
        partial(backward_kernel, groups, count_all),
        out_shape=[
            jax.ShapeDtypeStruct((layers, 2, half, width), wide),
            jax.ShapeDtypeStruct((Z_SIZE, Y_SIZE, X_SIZE * C_SIZE, mod_rows, D), low),
            jax.ShapeDtypeStruct((sum_rows, D), wide),
        ],
        in_specs=[anywhere] + [vmem] * 6 + [anywhere] * 7,
        out_specs=[vmem] * 3,
        scratch_shapes=[
            pltpu.VMEM((4, D, D), low),
            pltpu.VMEM(rows, wide),
            pltpu.VMEM(rows, wide),
            pltpu.VMEM((3,) + rows, low),
            pltpu.VMEM(rows, low),
            pltpu.VMEM(rows, wide),
            pltpu.VMEM(rows, wide),
            pltpu.VMEM(rows, low),
            pltpu.VMEM(rows, low),
            pltpu.VMEM(rows, low),
            pltpu.VMEM(rows, low),
            pltpu.VMEM(rows, wide),
            pltpu.VMEM((3,) + rows, low),
            pltpu.VMEM((2, D, D), low),
            pltpu.VMEM((images, entries, 1, D), wide),
            pltpu.VMEM((mod_rows, D), wide),
            pltpu.VMEM((mod_rows, D), low),
            pltpu.VMEM((sum_rows, D), wide),
            pltpu.VMEM((Z_SIZE, Y_SIZE, half, D), low),
            pltpu.VMEM((Z_SIZE, Y_SIZE, half, D), low),
            pltpu.VMEM((Z_SIZE, Y_SIZE, part, D), low),
            pltpu.VMEM((Z_SIZE, most, D), low),
            pltpu.VMEM((Z_SIZE - 1, most, D), low),
            pltpu.VMEM((most, D), low),
            pltpu.VMEM((sum_rows // 2, D), wide),
            pltpu.VMEM((sum_rows // 2, D), wide),
            pltpu.VMEM((sum_rows // 2, D), wide),
            pltpu.VMEM((Z_SIZE, sum_rows // 2, D), wide),
            dma((4,)),
            dma((6,)),
            dma,
            dma((layers, number, FF_BLOCKS)),
            dma((layers, number, FF_BLOCKS)),
            dma((layers, number, FF_BLOCKS)),
            *pair,
            *pair,
            dma((layers, number, Z_SIZE - 1)),
            dma((layers, number, Z_SIZE - 1)),
            *pair,
            *pair,
            dma((7,)),
            dma((7,)),
            dma((7,)),
            dma((7,)),
            dma,
            regular((number,)),
            regular((number,)),
            regular((number,)),
            regular((number, Z_SIZE - 1)),
            regular((number,)),
        ],
        compiler_params=pltpu.CompilerParams(
            collective_id=3, has_side_effects=True, vmem_limit_bytes=63 * 2**20
        ),
        name="blocks_backward",
    )(x_last, mods, biases, picked, wanted, head_w, head_b, full, *kept)


KINDS = [("qkv", 0, 3), ("proj", 3, 1), ("fc1", 4, FF // D), ("fc2", 4 + FF // D, 1)]


def statistics_kernel(
    finals, mods_all, silu_rows, w_qkv, w_proj, w_fc1, w_fc2, w_mod,
    row_qkv, row_proj, row_fc1, row_fc2, row_mod,
    cond_all, mod_b_grad, picked, stats, qkv_row, proj_row, fc1_row, fc2_row, mod_row,
    mod_grad, lined, sums, pieces, cond, c_s, c_r, p_s, p_r, g_s, g_r, r_s, r_r,
):
    dp, rep = lax.axis_index("dp"), lax.axis_index("rep")
    dps, reps = Z_SIZE * Y_SIZE, X_SIZE * C_SIZE
    dp_peers = [((dp + k) % dps, rep) for k in range(1, dps)]
    rep_peers = [(dp, (rep + k) % reps) for k in range(1, reps)]
    barrier = pltpu.get_barrier_semaphore()
    for peer in dp_peers + rep_peers:
        pl.semaphore_signal(barrier, inc=1, device_id=peer, device_id_type=MESH_IDS)
    beta = 1.0 - STEP ** (-0.8)
    shard, half = w_mod.shape[0], w_mod.shape[0] // 2
    entries, images = picked.shape[0], picked.shape[1]
    ways = D // LANES
    per = 5 + FF_BLOCKS
    mats = [(w_qkv, row_qkv, qkv_row), (w_proj, row_proj, proj_row), (w_fc1, row_fc1, fc1_row), (w_fc2, row_fc2, fc2_row)]
    columns_all = LAYERS * per + entries
    scalars = LAYERS * len(KINDS) + 1
    at_row, at_weight = 2 * columns_all, 2 * columns_all + scalars

    def over_rows(values):
        return jnp.sum(values, axis=0, keepdims=True)

    def over_all(values):
        return jnp.sum(jnp.sum(values, axis=1, keepdims=True), axis=0, keepdims=True)

    stats[...] = jnp.zeros_like(stats)
    lined[...] = jnp.zeros_like(lined)
    cond[...] = jnp.zeros_like(cond)

    number = mods_all.shape[0] // (dps * reps)
    here = images // (dps * reps)
    row = lax.broadcasted_iota(jnp.int32, (images, mods_all.shape[0]), 0)
    at = lax.broadcasted_iota(jnp.int32, (images, mods_all.shape[0]), 1)
    back = jnp.zeros((images, shard), jnp.float32)
    for k in range(entries):
        wanted = row // here * number + row % here * entries + k
        picked[k] = dot_nn((at == wanted).astype(jnp.bfloat16), mods_all[...]).astype(jnp.bfloat16)
        mod_b_grad[pl.ds(k, 1)] = over_rows(picked[k].astype(jnp.float32))
        back = back + dot_nt(picked[k], w_mod[:, k * D : (k + 1) * D].astype(jnp.bfloat16))
    cond[:, pl.ds(0, shard)] = back

    def first_pass(blocks, rows, row_old, width, row_out, weights, stat):
        total = jnp.zeros((rows, 1), jnp.float32)
        for grad, _ in blocks:
            value = grad()
            total = total + jnp.sum(value * value + EPS_ONE, axis=1, keepdims=True)
        factor = beta * row_old + (1.0 - beta) * (total / width)
        row_out(factor)
        inverse = 1.0 / factor
        for grad, index in blocks:
            value = grad()
            value = value * value
            stats[pl.ds(index, 1)] += over_rows(value + EPS_ONE)
            stats[pl.ds(columns_all + index, 1)] += over_rows(value * inverse)
        stats[pl.ds(at_row + stat, 1)] += over_rows(factor)
        for weight in weights:
            stats[pl.ds(at_weight + stat, 1), pl.ds(0, 1)] += over_all(weight() * weight())

    def block(layer, index, core):
        return lambda: finals[layer, core, pl.ds(index * half, half)]

    for layer in range(LAYERS):
        for kind, (name, first, count) in enumerate(KINDS):
            weight, row_old, row_new = mats[kind]
            stat = layer * len(KINDS) + kind
            tall = weight.shape[1] // shard
            for part in range(tall):
                for core in range(C_SIZE):
                    rows = pl.ds(part * shard + core * half, half)
                    blocks, weights = [], []
                    for j in range(count):
                        grad = block(layer, first + part + j, core)
                        cut = pl.ds(j * D, D)
                        blocks.append((grad, layer * per + first + j))
                        weights.append(lambda rows=rows, cut=cut, weight=weight, layer=layer: weight[layer, rows, cut])

                    def keep(value, rows=rows, row_new=row_new, layer=layer):
                        row_new[layer, rows] = value

                    first_pass(blocks, half, row_old[layer, rows], count * D, keep, weights, stat)
    blocks, weights = [], []
    for k in range(entries):
        cut = pl.ds(k * D, D)
        mod_grad[:, cut] = dot_tn(silu_rows[...], picked[k])
        blocks.append((lambda cut=cut: mod_grad[:, cut], LAYERS * per + k))
        weights.append(lambda cut=cut: w_mod[:, cut])

    def keep_mod(value):
        mod_row[...] = value

    first_pass(blocks, shard, row_mod[...], entries * D, keep_mod, weights, scalars - 1)

    for k in range(ways):
        lined[pl.ds(k, stats.shape[0], stride=ways)] = stats[:, k * LANES : (k + 1) * LANES]
    quarter = lined.shape[0] // reps
    size = quarter // dps
    copies = []

    def go(source, target, sems, index, peer):
        copy = push(source, target, sems[0].at[index], sems[1].at[index], peer)
        copy.start()
        copies.append(copy)
        return copy

    def part_of(owner):
        return pl.ds(pl.multiple_of(rep * quarter + owner * size, 8), size)

    pl.semaphore_wait(barrier, len(dp_peers + rep_peers))
    first = [go(lined.at[part_of(peer[0])], pieces.at[dp], (p_s, p_r), k, peer) for k, peer in enumerate(dp_peers)]
    spread = [go(cond, cond_all.at[dp], (c_s, c_r), k, peer) for k, peer in enumerate(dp_peers)]
    cond_all[dp] = cond[...]
    pieces[dp] = lined[part_of(dp)]
    for copy in first:
        copy.wait_recv()
    value = pieces[0]
    for k in range(1, dps):
        value = value + pieces[k]
    sums[part_of(dp)] = value
    own = sums.at[part_of(dp)]
    second = [go(own, own, (g_s, g_r), k, peer) for k, peer in enumerate(dp_peers)]
    for copy in second:
        copy.wait_recv()
    own = sums.at[pl.ds(pl.multiple_of(rep * quarter, 8), quarter)]
    third = [go(own, own, (r_s, r_r), k, peer) for k, peer in enumerate(rep_peers)]
    for copy in third + spread:
        copy.wait_recv()
    for k in range(ways):
        stats[:, pl.ds(k * LANES, LANES)] = sums[pl.ds(k, stats.shape[0], stride=ways)]

    for copy in copies:
        copy.wait_send()


def update_kernel(
    finals, picked, stats, silu_rows, w_qkv, w_proj, w_fc1, w_fc2, w_mod,
    row_qkv, row_proj, row_fc1, row_fc2, row_mod, col_qkv, col_proj, col_fc1, col_fc2, col_mod,
    qkv_new, qkv_grad, qkv_col, qkv_low,
    proj_new, proj_grad, proj_col, proj_low,
    fc1_new, fc1_grad, fc1_col, fc1_low,
    fc2_new, fc2_grad, fc2_col, fc2_low,
    mod_new, mod_grad, mod_col, mod_low,
):
    dps = Z_SIZE * Y_SIZE
    beta = 1.0 - STEP ** (-0.8)
    shard, half = w_mod.shape[0], w_mod.shape[0] // 2
    entries = picked.shape[0]
    per = 5 + FF_BLOCKS
    mats = [
        (w_qkv, row_qkv, col_qkv, qkv_new, qkv_grad, qkv_col, qkv_low),
        (w_proj, row_proj, col_proj, proj_new, proj_grad, proj_col, proj_low),
        (w_fc1, row_fc1, col_fc1, fc1_new, fc1_grad, fc1_col, fc1_low),
        (w_fc2, row_fc2, col_fc2, fc2_new, fc2_grad, fc2_col, fc2_low),
    ]
    columns_all = LAYERS * per + entries
    scalars = LAYERS * len(KINDS) + 1
    at_row, at_weight = 2 * columns_all, 2 * columns_all + scalars

    def scale_of(indices, col_old, col_new, stat, rows_all):
        width = len(indices) * D
        row_mean = stats[pl.ds(at_row + stat, 1), pl.ds(0, 1)] / rows_all
        weight_rms = jnp.sqrt(stats[pl.ds(at_weight + stat, 1), pl.ds(0, 1)] / (rows_all * width))
        update_sq = jnp.zeros((1, 1), jnp.float32)
        sides = []
        for j, index in enumerate(indices):
            cut = slice(j * D, (j + 1) * D)
            value = beta * col_old[:, cut] + (1.0 - beta) * (stats[pl.ds(index, 1)] / rows_all)
            col_new(j, value)
            update_sq = update_sq + jnp.sum(stats[pl.ds(columns_all + index, 1)] / value, axis=1, keepdims=True)
            sides.append(lax.rsqrt(value))
        update_rms = jnp.sqrt(row_mean * update_sq / (rows_all * width))
        rate = RATE * jnp.maximum(0.001, weight_rms) / jnp.maximum(1.0, update_rms / CLIP)
        return row_mean, rate, sides

    for layer in range(LAYERS):
        for kind, (name, first_square, count) in enumerate(KINDS):
            weight, row_new, col_old, new, grad_out, col_new, low = mats[kind]
            indices = [layer * per + first_square + j for j in range(count)]

            def put(j, value, col_new=col_new, layer=layer):
                col_new[pl.ds(layer, 1), pl.ds(j * D, D)] = value

            row_mean, rate, sides = scale_of(
                indices, col_old[pl.ds(layer, 1)], put, layer * len(KINDS) + kind, float(weight.shape[1] * dps)
            )
            for step in range(weight.shape[1] // half):
                rows = pl.ds(step * half, half)
                left = rate * lax.rsqrt(row_new[layer, rows] / row_mean)
                for j in range(count):
                    cut = pl.ds(j * D, D)
                    index = first_square + step // C_SIZE + j
                    grad = finals[layer, step % C_SIZE, pl.ds(index * half, half)]
                    grad_out[layer, rows, cut] = grad
                    value = weight[layer, rows, cut] - grad * left * sides[j]
                    new[layer, rows, cut] = value
                    low[layer, rows, cut] = value.astype(jnp.bfloat16)

    def put_mod(j, value):
        mod_col[:, pl.ds(j * D, D)] = value

    indices = [LAYERS * per + k for k in range(entries)]
    row_mean, rate, sides = scale_of(indices, col_mod[...], put_mod, scalars - 1, float(shard * dps))
    left = rate * lax.rsqrt(row_mod[...] / row_mean)
    for k in range(entries):
        cut = pl.ds(k * D, D)
        grad = dot_tn(silu_rows[...], picked[k])
        mod_grad[:, cut] = grad
        value = w_mod[:, cut] - grad * left * sides[k]
        mod_new[:, cut] = value
        mod_low[:, cut] = value.astype(jnp.bfloat16)


def run_update(finals, mods_all, silu_rows, kinds, w_mod, row_mod, col_mod):
    dps, reps = Z_SIZE * Y_SIZE, X_SIZE * C_SIZE
    wide, low = jnp.float32, jnp.bfloat16
    images, shard = silu_rows.shape
    entries = w_mod.shape[1] // D
    vmem = pl.BlockSpec(memory_space=pltpu.VMEM)
    dma = pltpu.SemaphoreType.DMA
    weights, rows, cols, outs = [], [], [], []
    for weight, row, col in kinds + [(w_mod, row_mod, col_mod)]:
        weights.append(weight)
        rows.append(row[..., None])
        cols.append(col.reshape(-1, col.shape[-1]))
        outs += [
            jax.ShapeDtypeStruct(weight.shape, wide),
            jax.ShapeDtypeStruct(weight.shape, wide),
            jax.ShapeDtypeStruct(cols[-1].shape, wide),
            jax.ShapeDtypeStruct(weight.shape, low),
        ]
    used = 2 * (LAYERS * (5 + FF_BLOCKS) + entries) + 2 * (LAYERS * len(KINDS) + 1)
    height = -(-used // 8) * 8
    lined = -(-height * D // LANES // (8 * dps * reps)) * 8 * dps * reps
    cond_all, mod_b_grad, picked, stats, *rows_new = pl.pallas_call(
        statistics_kernel,
        out_shape=[
            jax.ShapeDtypeStruct((dps, images, LANES), wide),
            jax.ShapeDtypeStruct((entries, D), wide),
            jax.ShapeDtypeStruct((entries, images, D), low),
            jax.ShapeDtypeStruct((height, D), wide),
        ]
        + [jax.ShapeDtypeStruct(row.shape, wide) for row in rows],
        in_specs=[vmem] * (3 + 2 * len(weights)),
        out_specs=[vmem] * (4 + len(rows)),
        scratch_shapes=[
            pltpu.VMEM(w_mod.shape, wide),
            pltpu.VMEM((lined, LANES), wide),
            pltpu.VMEM((lined, LANES), wide),
            pltpu.VMEM((dps, lined // (dps * reps), LANES), wide),
            pltpu.VMEM((images, LANES), wide),
        ]
        + [dma((dps - 1,))] * 6
        + [dma((reps - 1,))] * 2,
        compiler_params=pltpu.CompilerParams(
            collective_id=4, has_side_effects=True, vmem_limit_bytes=48 * 2**20
        ),
        name="statistics",
    )(finals, mods_all, silu_rows, *weights, *rows)
    results = pl.pallas_call(
        update_kernel,
        out_shape=outs,
        in_specs=[vmem] * (4 + 3 * len(weights)),
        out_specs=[vmem] * len(outs),
        compiler_params=pltpu.CompilerParams(vmem_limit_bytes=58 * 2**20),
        name="update_weights",
    )(finals, picked, stats, silu_rows, *weights, *rows_new, *cols)
    groups = [results[4 * i : 4 * i + 4] for i in range(len(weights))]
    return cond_all, mod_b_grad, [
        (new, grad, row[..., 0], col.reshape(row.shape[:-2] + col.shape[-1:]), rounded)
        for (new, grad, col, rounded), row in zip(groups, rows_new)
    ]


def line_up_kernel(offsets, *refs):
    pieces, (first, tail), out, spread = refs[: len(offsets)], refs[len(offsets) : -2], refs[-2], refs[-1]
    ways = D // LANES
    for piece, offset in zip(pieces, offsets):
        rows = piece.shape[0]
        for k in range(ways):
            out[pl.ds(ways * offset + k, rows, stride=ways)] = piece[:, k * LANES : (k + 1) * LANES]
    rows = tail.shape[0] * ways
    for k in range(ways):
        spread[pl.ds(k, tail.shape[0], stride=ways)] = tail[:, k * LANES : (k + 1) * LANES]
    moved = pltpu.roll(spread[...], PDIM, 1)
    lane = lax.broadcasted_iota(jnp.int32, (rows, LANES), 1)
    spread[pl.ds(1, rows - 1)] = moved[: rows - 1]
    spread[pl.ds(0, 1)] = first[...]
    start = out.shape[0] - rows - 1
    out[pl.ds(start, rows)] = jnp.where(lane >= PDIM, moved, spread[...])
    out[pl.ds(start + rows, 1)] = moved[rows - 1 :]


def line_up(pieces, first, tail):
    offsets, at = [], 0
    for piece in pieces:
        offsets.append(at)
        at += piece.shape[0]
    ways = D // LANES
    vmem = pl.BlockSpec(memory_space=pltpu.VMEM)
    count = (at + tail.shape[0]) * ways + 1
    return pl.pallas_call(
        partial(line_up_kernel, offsets),
        out_shape=jax.ShapeDtypeStruct((count, LANES), jnp.float32),
        in_specs=[vmem] * (len(pieces) + 2),
        out_specs=vmem,
        scratch_shapes=[pltpu.VMEM((tail.shape[0] * ways, LANES), jnp.float32)],
        compiler_params=pltpu.CompilerParams(vmem_limit_bytes=32 * 2**20),
        name="line_up",
    )(*pieces, first, tail)


def local(
    latents,
    noise_field,
    timesteps,
    labels,
    drop_mask,
    roster,
    w_qkv,
    w_proj,
    w_fc1,
    w_fc2,
    w_mod,
    row_qkv,
    col_qkv,
    row_proj,
    col_proj,
    row_fc1,
    col_fc1,
    row_fc2,
    col_fc2,
    row_mod,
    col_mod,
    small,
    small_second,
):
    pieces = unpack(small)
    dp_size, rep_size = lax.axis_size("dp"), lax.axis_size("rep")
    everyone = dp_size * rep_size
    number = latents.shape[0] * latents.shape[1]
    count_all = number * everyone * GRID * GRID * PDIM
    rows_mod = w_mod.shape[0]
    first_row = lax.axis_index("dp") * rows_mod
    places = position_table()
    patch_low = pieces["patch_w"].astype(jnp.bfloat16)
    time1_low = pieces["time1_w"].astype(jnp.bfloat16)
    time2_low = pieces["time2_w"].astype(jnp.bfloat16)
    head_low = pieces["head_w"].astype(jnp.bfloat16)
    mod_shard = w_mod.astype(jnp.bfloat16)

    direct = (dp_size, rep_size) == (Z_SIZE * Y_SIZE, X_SIZE * C_SIZE) and rows_mod % 96 == 0
    picker = (timesteps.reshape(-1)[:, None] == jnp.arange(STEPS_T)[None, :]).astype(jnp.float32)
    factors = jnp.dot(picker, roster.T, precision=HIGHEST)
    noise_flat = noise_field.reshape(number, -1)
    noised = factors[:, 0:1] * latents.reshape(number, -1) + factors[:, 1:2] * noise_flat
    own_ids = jnp.stack([timesteps, labels, drop_mask]).reshape(3, number)
    if direct:
        tile = jnp.pad(own_ids.T.astype(jnp.float32), ((0, 8 - number), (0, LANES - 3)))
        column = jnp.arange(2 * LANES)[None, None, :] % LANES // (PATCH * CHAN)
        own_place = column == jnp.arange(GRID)[None, :, None]

        def pick(values):
            values = values.reshape(number * GRID, 1, PATCH * LANES)
            return jnp.where(own_place, values, jnp.zeros_like(values)).reshape(-1, PATCH * LANES)

        picked, wanted = pick(noised.astype(jnp.bfloat16)), pick(noise_flat)
        rows_at, places_of = 0, {}
        for piece_name, piece_dims in layout()[:8]:
            height = math.prod(piece_dims) // D
            places_of[piece_name] = (rows_at, height)
            rows_at += height
        biases = pieces["block_b"].reshape(LAYERS, -1, 1, D)
        x_last, packed_full, mods, all_ids, hidden_t, condition, time2_low, *kept_blocks = run_forward(
            picked,
            places,
            tile,
            w_qkv,
            w_proj,
            w_fc1,
            w_fc2,
            w_mod,
            small[: rows_at * D].reshape(-1, LANES),
            places_of,
            biases,
            number,
        )
        all_ids = all_ids[:, :number, :3].reshape(-1, 3).T.astype(jnp.int32)
        hidden_t = hidden_t.reshape(everyone, 8, D)[:, :number].reshape(-1, D)
        condition = condition.reshape(everyone, 8, D)[:, :number].reshape(-1, D)
    else:
        all_ids = lax.all_gather(own_ids, ("dp", "rep"), axis=0, tiled=False)
        all_ids = all_ids.transpose(1, 0, 2).reshape(3, everyone * number)
    features = time_features(all_ids[0]).astype(jnp.bfloat16)
    if not direct:
        hidden_t = product(features, time1_low) + pieces["time1_b"]
    silu_t = jax.nn.silu(hidden_t).astype(jnp.bfloat16)
    chosen = jnp.where(all_ids[2] == 1, CLASSES, all_ids[1])
    onehot = (chosen[:, None] == jnp.arange(CLASSES + 1)[None, :]).astype(jnp.float32)
    if not direct:
        condition = (
            product(silu_t, time2_low)
            + pieces["time2_b"]
            + jnp.dot(onehot, pieces["class_tab"], precision=HIGHEST)
        )
    silu_c = jax.nn.silu(condition).astype(jnp.bfloat16)
    silu_rows = lax.dynamic_slice_in_dim(silu_c, first_row, rows_mod, axis=1)
    if not direct:
        tokens = patchify(noised).astype(jnp.bfloat16)
        target = patchify(noise_flat).reshape(-1, PDIM)
        residual = (product(tokens.reshape(-1, PDIM), patch_low) + pieces["patch_b"]).reshape(
            number, GRID * GRID, D
        ) + places
        group_rows = lax.dynamic_index_in_dim(
            silu_rows.reshape(dp_size, rep_size, number, rows_mod),
            lax.axis_index("rep"),
            axis=1,
            keepdims=False,
        ).reshape(dp_size * number, rows_mod)
        mod_part = product(group_rows, mod_shard)
        mod_sum = lax.psum_scatter(mod_part, "dp", scatter_dimension=0, tiled=True)
        modulation = mod_sum + pieces["mod_b"]
    if direct:
        head_wide = jnp.pad(head_low, ((0, 0), (0, LANES - PDIM)))
        head_shift = jnp.pad(pieces["head_b"], (0, LANES - PDIM))[None]
        finals, mod_all, sums = run_backward(
            count_all, x_last, mods, biases, picked, wanted, head_wide, head_shift, packed_full, kept_blocks
        )
        loss_total = sums[2 * PDIM, PDIM]
    else:
        kept_all = []
        gathered_all = []
        spans_all = []
        for layer_index in range(LAYERS):
            weights = tuple(
                lax.all_gather(w[layer_index].astype(jnp.bfloat16), "dp", axis=0, tiled=True)
                for w in (w_qkv, w_proj, w_fc1, w_fc2)
            )
            spans = [
                modulation[:, None, D * (6 * layer_index + i) : D * (6 * layer_index + i + 1)]
                for i in range(6)
            ]
            residual, kept = layer_forward(residual, spans, weights, pieces["block_b"][layer_index])
            kept_all.append(kept)
            gathered_all.append(weights)
            spans_all.append(spans)
        final_shift = modulation[:, None, 6 * D * LAYERS : 6 * D * LAYERS + D]
        final_scale = modulation[:, None, 6 * D * LAYERS + D :]
        normed_f, inverse_f = norm_rows(residual)
        final_in = (normed_f * (1.0 + final_scale) + final_shift).astype(jnp.bfloat16).reshape(-1, D)
        output = product(final_in, head_low) + pieces["head_b"]
        error = output - target
        loss_own = jnp.sum(error * error)
        grad_output = (error * (2.0 / count_all)).astype(jnp.bfloat16)
        grad_head = product(final_in.T, grad_output)
        grad_head_b = jnp.sum(grad_output.astype(jnp.float32), axis=0)
        grad_final = product(grad_output, head_low.T).reshape(number, GRID * GRID, D)
        final_grads = [jnp.sum(grad_final, axis=1), jnp.sum(grad_final * normed_f, axis=1)]
        grad_res = norm_back(grad_final * (1.0 + final_scale), normed_f, inverse_f)
        layer_spans = [None] * LAYERS
        bias_grads = [None] * LAYERS
        block_grads = [None] * LAYERS
        for layer_index in reversed(range(LAYERS)):
            grad_res, grads, grad_bias, grad_spans = layer_backward(
                grad_res, spans_all[layer_index], gathered_all[layer_index], kept_all[layer_index]
            )
            layer_spans[layer_index] = grad_spans
            bias_grads[layer_index] = grad_bias
            block_grads[layer_index] = tuple(
                lax.psum_scatter(g, "dp", scatter_dimension=0, tiled=True) for g in grads
            )

        grad_start = grad_res.reshape(-1, D).astype(jnp.bfloat16)
        grad_patch = product(tokens.reshape(-1, PDIM).T, grad_start)
        grad_patch_b = jnp.sum(grad_start.astype(jnp.float32), axis=0)
        own_sums = jnp.concatenate(
            [
                grad_patch.reshape(-1),
                grad_patch_b,
                grad_head.reshape(-1),
                jnp.stack(bias_grads).reshape(-1),
                grad_head_b,
                loss_own[None],
            ]
        )
        own_mod = jnp.concatenate(layer_spans + final_grads, axis=-1).astype(jnp.bfloat16)
        grad_qkv, grad_proj, grad_fc1, grad_fc2 = lax.psum(
            tuple(jnp.stack([block_grads[i][k] for i in range(LAYERS)]) for k in range(4)), "rep"
        )
        grad_mod = lax.all_gather(own_mod, ("dp", "rep"), axis=0, tiled=True)
        summed = lax.psum(own_sums, ("dp", "rep"))
        cut_patch = (PDIM + 1) * D
        cut_head = cut_patch + D * PDIM
        cut_bias = cut_head + LAYERS * (4 * D + FF)
        loss_total = summed[cut_bias + PDIM]
        sum_patch = summed[:cut_patch]
        sum_head = jnp.append(summed[cut_patch:cut_head], summed[cut_bias : cut_bias + PDIM])
        sum_bias = summed[cut_head:cut_bias]

    beta = 1.0 - STEP ** (-0.8)
    if direct:
        kinds = [
            (w_qkv, row_qkv, col_qkv),
            (w_proj, row_proj, col_proj),
            (w_fc1, row_fc1, col_fc1),
            (w_fc2, row_fc2, col_fc2),
        ]
        cond_all, grad_mod_b, results = run_update(
            finals, mod_all.reshape(-1, D), silu_rows, kinds, w_mod, row_mod, col_mod
        )
        cond_rows = cond_all[:, :, :rows_mod].transpose(1, 0, 2).reshape(-1, D)
        results[4] = tuple(entry[None] for entry in results[4])
    else:
        grad_wmod = product(silu_rows.T, grad_mod)
        grad_mod_b = jnp.sum(grad_mod.astype(jnp.float32), axis=0)
        kinds = [
            (w_qkv, grad_qkv, row_qkv, col_qkv),
            (w_proj, grad_proj, row_proj, col_proj),
            (w_fc1, grad_fc1, row_fc1, col_fc1),
            (w_fc2, grad_fc2, row_fc2, col_fc2),
            (w_mod[None], grad_wmod[None], row_mod[None], col_mod[None]),
        ]
        firsts = []
        for weight, grad, row, col in kinds:
            square = grad * grad
            row_new = beta * row + (1.0 - beta) * jnp.mean(square + EPS_ONE, axis=-1)
            firsts.append(
                (
                    row_new,
                    jnp.sum(square + EPS_ONE, axis=-2),
                    jnp.sum(square / row_new[:, :, None], axis=-2),
                    jnp.sum(row_new, axis=-1),
                    jnp.sum(weight * weight, axis=(-2, -1)),
                )
            )
        stats = jnp.concatenate([entry[k].reshape(-1) for k in range(1, 5) for entry in firsts])
        cond_rows = lax.all_gather(product(grad_mod, mod_shard.T), "dp", axis=1, tiled=True)
        shared = lax.psum(stats, "dp")
        rows_dp = dp_size
        parts = []
        offset = 0
        for k in range(1, 5):
            for entry in firsts:
                parts.append(shared[offset : offset + entry[k].size].reshape(entry[k].shape))
                offset += entry[k].size
        seconds = []
        for index, kind in enumerate(kinds):
            weight, grad, row, col = kind
            rows_all = weight.shape[1] * rows_dp
            col_count = weight.shape[2]
            col_sum, over_rows, row_sum, weight_sq = (parts[index + len(kinds) * k] for k in range(4))
            row_mean = row_sum / rows_all
            weight_rms = jnp.sqrt(weight_sq / (rows_all * col_count))
            col_new = beta * col + (1.0 - beta) * col_sum / rows_all
            update_sq = row_mean * jnp.sum(over_rows / col_new, axis=-1)
            estimate = firsts[index][0][:, :, None] * col_new[:, None, :] / row_mean[:, None, None]
            update = grad * lax.rsqrt(estimate)
            seconds.append((update, col_new, weight_rms, update_sq / (rows_all * col_count)))
        results = []
        for kind, first, second in zip(kinds, firsts, seconds):
            weight, grad = (kind[0], kind[1])
            update, col_new, weight_rms, update_ms = second
            update_rms = jnp.sqrt(update_ms)
            update = update / jnp.maximum(1.0, update_rms / CLIP)[:, None, None]
            new_weight = weight - (RATE * jnp.maximum(0.001, weight_rms))[:, None, None] * update
            results.append((new_weight, grad, first[0], col_new, new_weight.astype(jnp.bfloat16)))
    _, silu_pull = jax.vjp(jax.nn.silu, condition)
    grad_cond = silu_pull(cond_rows)[0].astype(jnp.bfloat16)
    grad_class = jnp.dot(onehot.T, grad_cond.astype(jnp.float32), precision=HIGHEST)
    grad_time2 = product(silu_t.T, grad_cond)
    grad_time2_b = jnp.sum(grad_cond.astype(jnp.float32), axis=0)
    _, silu_time_pull = jax.vjp(jax.nn.silu, hidden_t)
    grad_hidden_t = silu_time_pull(product(grad_cond, time2_low.T))[0].astype(jnp.bfloat16)
    grad_time1 = product(features.T, grad_hidden_t)
    grad_time1_b = jnp.sum(grad_hidden_t.astype(jnp.float32), axis=0)
    if direct:
        lined = line_up(
            [
                sums[:PDIM],
                sums[2 * PDIM + 8 :][:1],
                grad_time1,
                grad_time1_b[None],
                grad_time2,
                grad_time2_b[None],
                grad_class,
                grad_mod_b,
                sums[PDIM : 2 * PDIM].T.reshape(-1, D),
            ],
            sums[2 * PDIM : 2 * PDIM + 1, :LANES],
            sums[3 * PDIM :],
        )
        small_grad = lined.reshape(-1)[: small.shape[0]]
    else:
        small_grad = jnp.concatenate(
            [
                sum_patch,
                grad_time1.reshape(-1),
                grad_time1_b,
                grad_time2.reshape(-1),
                grad_time2_b,
                grad_class.reshape(-1),
                grad_mod_b,
                sum_head,
                sum_bias,
            ]
        )
    square = small_grad * small_grad + EPS_ONE
    small_second_new = beta * small_second + (1.0 - beta) * square
    update = small_grad * lax.rsqrt(small_second_new)
    update = update / jnp.maximum(1.0, jnp.sqrt(jnp.mean(update * update)) / CLIP)
    small_new = small - RATE * jnp.maximum(0.001, jnp.sqrt(jnp.mean(small * small))) * update
    mod_result = results[4]
    return (
        loss_total,
        results[0][0],
        results[0][1],
        results[0][2],
        results[0][3],
        results[0][4],
        results[1][0],
        results[1][1],
        results[1][2],
        results[1][3],
        results[1][4],
        results[2][0],
        results[2][1],
        results[2][2],
        results[2][3],
        results[2][4],
        results[3][0],
        results[3][1],
        results[3][2],
        results[3][3],
        results[3][4],
        mod_result[0][0],
        mod_result[1][0],
        mod_result[2][0],
        mod_result[3][0],
        mod_result[4][0],
        small_grad,
        small_second_new,
        small_new,
        small_new.astype(jnp.bfloat16),
    )


def solution(mesh):
    in_specs = (
        P(None, ("dp", "rep"), None),
        P(None, ("dp", "rep"), None),
        P(None, ("dp", "rep")),
        P(None, ("dp", "rep")),
        P(None, ("dp", "rep")),
        P(),
        P(None, "dp", None),
        P(None, "dp", None),
        P(None, "dp", None),
        P(None, "dp", None),
        P("dp", None),
        P(None, "dp"),
        P(),
        P(None, "dp"),
        P(),
        P(None, "dp"),
        P(),
        P(None, "dp"),
        P(),
        P("dp"),
        P(),
        P(),
        P(),
    )
    out_specs = (
        P(),
        P(None, "dp", None),
        P(None, "dp", None),
        P(None, "dp"),
        P(),
        P(None, "dp", None),
        P(None, "dp", None),
        P(None, "dp", None),
        P(None, "dp"),
        P(),
        P(None, "dp", None),
        P(None, "dp", None),
        P(None, "dp", None),
        P(None, "dp"),
        P(),
        P(None, "dp", None),
        P(None, "dp", None),
        P(None, "dp", None),
        P(None, "dp"),
        P(),
        P(None, "dp", None),
        P("dp", None),
        P("dp", None),
        P("dp"),
        P(),
        P("dp", None),
        P(),
        P(),
        P(),
        P(),
    )
    return jax.shard_map(local, mesh=mesh, in_specs=in_specs, out_specs=out_specs, check_vma=False)
```
